32 devices in a mesh: expert: 8 (over z, y), dp: 4 (over x, core).
Axes of the slice: x: 2, y: 2, z: 4, core: 2. Of those that a mesh axis runs over, the one named last changes fastest.
Arguments:
- tokens: bfloat16 [1024, 4096], P(('expert', 'dp')), may hold values from -6 to 6
- out_grad: bfloat16 [1024, 4096], P(('expert', 'dp')), may hold values from -6 to 6
- gate_probs: bfloat16 [1024, 8], P(('expert', 'dp')), may hold values from 0.049804688 to 0.5
- route_ids: int32 [1024, 8], P(('expert', 'dp')), may hold values from 0 to 127, all different within a row; in each aligned block of 32 rows (0 to 31, 32 to 63, ...) at most 4 rows name the same one
- w_gate: bfloat16 [8, 1536, 4096], P('expert', 'dp'), may hold values from -0.09375 to 0.09375
- w_up: bfloat16 [8, 1536, 4096], P('expert', 'dp'), may hold values from -0.09375 to 0.09375
- w_down: bfloat16 [8, 1536, 4096], P('expert', 'dp'), may hold values from -0.15625 to 0.15625
Outputs:
- token_grad: bfloat16 [1024, 4096], P(('expert', 'dp'))
- gate_grad: float32 [1024, 8], P(('expert', 'dp'))
- grad_gate: bfloat16 [8, 1536, 4096], P('expert', 'dp')
- grad_up: bfloat16 [8, 1536, 4096], P('expert', 'dp')
- grad_down: bfloat16 [8, 1536, 4096], P('expert', 'dp')
The draws below stay inside these ranges and needn't reach their ends.
Inputs may be any that keep to these rules, and one draw needn't show every extreme that they name: `route_ids`: the 8 ids of a token differ. In each aligned block of 32 rows (the tokens of one device) no id is named by more than 4 rows, a bound that some block reaches.
All inputs are finite; a program needn't handle non-finite values.
Results may differ from the reference program's by a relative error of at most 0.014.
Values may be sent and summed in bfloat16 or wider, within the bound.
No kernel may reach another device: no remote copies, remote signals or barrier semaphores. Data moves between devices by JAX's collectives and lax.ppermute only.
A program may use at most 128 MiB of HBM per device.

```python
import math
import jax
import jax.numpy as jnp
import numpy as np
from jax import lax

D = 4096
FF = 1536
EXPERTS = 128
TOPK = 8
TOK_DEV = 32
CAP = 4
WINDOW = 8
TOKENS = 1024
N_EXPERT = 8
N_DP = 4


def block_scale(key, extent, cuts, low, top_value):
    loudness = 1.0
    for dim, parts in cuts:
        heights = jax.random.uniform(jax.random.fold_in(jax.random.fold_in(key, 6), dim), (parts,), jnp.float32, low / len(cuts), top_value / len(cuts))
        loudness = loudness * jnp.repeat(jnp.exp(heights), extent[dim] // parts).reshape((-1,) + (1,) * (len(extent) - 1 - dim))
    return loudness


def assign_block(key, own, number, rows, number_of, top, bound, skew):
    ranking = jax.random.permutation(key, number_of)
    crowded, usual = portions_of(number_of, rows * top, bound, skew, True), portions_of(number_of, rows * top, bound, skew, False)
    places = jnp.arange(number_of)

    def named(tallies, turn):
        used = int((tallies > 0).sum())
        fixed = max(1, used // 4)
        shifted = fixed + (places - fixed + turn * (used - fixed)) % max(1, number_of - fixed)
        return jnp.zeros((number_of,), jnp.int32).at[ranking[jnp.where(places < fixed, places, shifted)]].set(jnp.asarray(tallies, jnp.int32))

    tallies = jnp.where(number % 4 == 0, named(crowded, number // 4), named(usual, number - number // 4 - 1))
    mixed = jax.random.permutation(jax.random.fold_in(own, 3), number_of)
    donor, sink = mixed[0:number_of // 2 * 2:2], mixed[1:number_of // 2 * 2:2]
    slack = jnp.minimum(tallies[donor] - 1, bound - tallies[sink]) // 2
    slack = jnp.where((donor == ranking[0]) | (sink == ranking[0]) | (tallies[sink] == 0), 0, jnp.maximum(slack, 0))
    shifted = jax.random.randint(jax.random.fold_in(own, 4), (number_of // 2,), 0, 1 << 20) % (slack + 1)
    tallies = tallies.at[donor].add(-shifted).at[sink].add(shifted)
    labels = jnp.searchsorted(jnp.cumsum(tallies), jnp.arange(rows * top), side="right").astype(jnp.int32)
    grid = labels.reshape(top, rows).T
    grid = grid[jax.random.permutation(jax.random.fold_in(own, 1), rows)]
    turn = jax.random.randint(jax.random.fold_in(own, 2), (rows, 1), 0, top)
    return jnp.take_along_axis(grid, (jnp.arange(top)[None, :] + turn) % top, axis=1)


def portions_of(amount, total, bound, lean, full):
    weights = [(1 << 20) // math.isqrt(grade ** lean) + 1 for grade in range(1, amount + 1)]
    largest = bound if full else min(bound, max(-(-total // amount), total * weights[0] // sum(weights)))
    least = 1 if total - largest >= amount - 1 else 0
    given, surplus = [largest] + [least] * (amount - 1), total - largest - least * (amount - 1)
    while surplus > 0:
        candidates = [i for i in range(1, amount) if given[i] < largest] or [i for i in range(1, amount) if given[i] < bound]
        pool, left = sum([weights[i] for i in candidates]), surplus
        for i in candidates:
            more = min(bound - given[i], max(1, left * weights[i] // pool), surplus)
            given[i] = given[i] + more
            surplus = surplus - more
    return np.array(given)


def bell_draw(key, shape, deviation, most, split=(), kind=jnp.bfloat16):
    entries = jax.random.normal(key, shape, jnp.float32) * deviation
    if len(split) > 0:
        entries = block_scale(key, shape, split, -0.22, 0.18) * entries
    return jnp.clip(entries, min=-most, max=most).astype(kind)


def setup_inputs(seed: int = 0) -> dict:
    streams_of = jax.random.split(jax.random.key(seed), 8)
    tokens = bell_draw(streams_of[0], (TOKENS, D), 1.0, 6.0, ((0, 32),))
    out_grad = bell_draw(streams_of[1], (TOKENS, D), 1.0, 6.0, ((0, 32),))
    gate_probs = jnp.clip(jnp.exp(math.log(0.5) - 2.306499 * jax.random.uniform(streams_of[2], (TOKENS, TOPK), jnp.float32) ** block_scale(streams_of[2], (TOKENS, TOPK), ((0, 32),), -0.2, 0.2)), 0.049804688, 0.5).astype(jnp.bfloat16)
    route_ids_keys = jax.random.split(jax.random.fold_in(streams_of[3], 1), TOKENS // TOK_DEV)
    route_ids_turns = jax.random.permutation(jax.random.fold_in(streams_of[3], 3), TOKENS // TOK_DEV)
    route_ids = jax.vmap(lambda own, number: assign_block(jax.random.fold_in(streams_of[3], 2), own, number, TOK_DEV, EXPERTS, TOPK, CAP, 2))(route_ids_keys, route_ids_turns).reshape((TOKENS, TOPK))
    w_gate = bell_draw(streams_of[4], (WINDOW, FF, D), D ** -0.5, 0.09375, ((0, 8), (1, 4)))
    w_up = bell_draw(streams_of[5], (WINDOW, FF, D), D ** -0.5, 0.09375, ((0, 8), (1, 4)))
    w_down = bell_draw(streams_of[6], (WINDOW, FF, D), FF ** -0.5, 0.15625, ((0, 8), (1, 4)))
    return {"tokens": tokens, "out_grad": out_grad, "gate_probs": gate_probs, "route_ids": route_ids, "w_gate": w_gate, "w_up": w_up, "w_down": w_down}


def reference(tokens, out_grad, gate_probs, route_ids, w_gate, w_up, w_down):
    token_total, model_width = tokens.shape
    top_count = route_ids.shape[1]
    pair_total = token_total * top_count
    hidden_units = w_gate.shape[1]
    group_units = hidden_units // N_DP
    per_device = EXPERTS // N_EXPERT
    room = N_EXPERT * N_DP * CAP
    flat_ids = route_ids.reshape(-1)
    active = (flat_ids % per_device) == 0
    target = jnp.where(active, flat_ids // per_device, N_EXPERT).astype(jnp.int32)
    onehot = (target[:, None] == jnp.arange(N_EXPERT, dtype=jnp.int32)[None, :]).astype(jnp.int32)
    slot_rank = jnp.sum((jnp.cumsum(onehot, axis=0) - onehot) * onehot, axis=1).astype(jnp.int32)
    place = jnp.where(active, target * room + slot_rank, N_EXPERT * room).astype(jnp.int32)
    pair_owner = jnp.full((N_EXPERT * room + 1,), pair_total, jnp.int32)
    pair_owner = pair_owner.at[place].set(jnp.arange(pair_total, dtype=jnp.int32))
    pair_owner = pair_owner[: N_EXPERT * room].reshape(N_EXPERT, room)
    gates_flat = gate_probs.reshape(-1).astype(jnp.float32)

    def one_expert(totals, inputs):
        token_acc, gate_acc = totals
        pair_index, gate_weight, up_weight, down_weight = inputs
        occupied = pair_index < pair_total
        safe_index = jnp.where(occupied, pair_index, 0).astype(jnp.int32)
        token_index = (safe_index // top_count).astype(jnp.int32)
        row_tokens = jnp.where(occupied[:, None], tokens[token_index], jnp.zeros_like(tokens[token_index]))
        row_grads = jnp.where(occupied[:, None], out_grad[token_index], jnp.zeros_like(out_grad[token_index]))
        row_gates = jnp.where(occupied, gates_flat[safe_index], jnp.float32(0.0))
        pre_gate = jnp.dot(row_tokens, gate_weight.T, preferred_element_type=jnp.float32)
        pre_up = jnp.dot(row_tokens, up_weight.T, preferred_element_type=jnp.float32)
        back_proj = jnp.dot(row_grads, down_weight.T, preferred_element_type=jnp.float32)
        squash = jax.nn.sigmoid(pre_gate)
        activated = pre_gate * squash
        hidden = (activated * pre_up).astype(jnp.bfloat16)
        gate_terms = jnp.sum(hidden.astype(jnp.float32) * back_proj, axis=1)
        out_scaled = (row_gates[:, None] * row_grads.astype(jnp.float32)).astype(jnp.bfloat16)
        hidden_grad = row_gates[:, None] * back_proj
        up_pre_grad = (hidden_grad * activated).astype(jnp.bfloat16)
        gate_pre_grad = (hidden_grad * pre_up * squash * (1.0 + pre_gate * (1.0 - squash))).astype(jnp.bfloat16)
        grad_down = jnp.dot(hidden.T, out_scaled, preferred_element_type=jnp.float32).astype(jnp.bfloat16)
        grad_gate = jnp.dot(gate_pre_grad.T, row_tokens, preferred_element_type=jnp.float32).astype(jnp.bfloat16)
        grad_up = jnp.dot(up_pre_grad.T, row_tokens, preferred_element_type=jnp.float32).astype(jnp.bfloat16)
        pair_grad = jnp.zeros((room, model_width), jnp.float32)
        for member in range(N_DP):
            low_unit = member * group_units
            high_unit = low_unit + group_units
            partial_value = jnp.dot(gate_pre_grad[:, low_unit:high_unit], gate_weight[low_unit:high_unit], preferred_element_type=jnp.float32)
            partial_value = partial_value + jnp.dot(up_pre_grad[:, low_unit:high_unit], up_weight[low_unit:high_unit], preferred_element_type=jnp.float32)
            rounded = lax.optimization_barrier(partial_value.astype(jnp.bfloat16))
            pair_grad = pair_grad + rounded.astype(jnp.float32)
        pair_grad = jnp.where(occupied[:, None], pair_grad, jnp.float32(0.0))
        token_acc = token_acc.at[token_index].add(pair_grad)
        drop_index = jnp.where(occupied, pair_index, pair_total).astype(jnp.int32)
        gate_acc = gate_acc.at[drop_index].add(gate_terms, mode="drop")
        return (token_acc, gate_acc), (grad_gate, grad_up, grad_down)

    initial = (jnp.zeros((token_total, model_width), jnp.float32), jnp.zeros((pair_total,), jnp.float32))
    finals, weight_grads = lax.scan(one_expert, initial, (pair_owner, w_gate, w_up, w_down))
    token_acc, gate_acc = finals
    return (token_acc.astype(jnp.bfloat16), gate_acc.reshape(token_total, top_count), weight_grads[0], weight_grads[1], weight_grads[2])
```

```python
import functools

import jax
import jax.numpy as jnp
from jax import lax
from jax.experimental import pallas as pl
from jax.experimental.pallas import tpu as pltpu
from jax.sharding import PartitionSpec as P

EXPERTS = 128
CAP = 4
BLOCK = 2 * CAP
LANES = 128

CONTRACT_LAST = (((1,), (1,)), ((), ()))
CONTRACT_FIRST = (((0,), (0,)), ((), ()))


def choice_table(ids, n_targets):
    rows, choices = ids.shape
    width = n_targets * BLOCK
    per_device = EXPERTS // n_targets
    lane = lax.broadcasted_iota(jnp.int32, (rows, width), 1)
    wanted = (lane // BLOCK) * per_device
    slot = lane % BLOCK
    matches = [ids[:, k : k + 1] == wanted for k in range(choices)]
    hit = functools.reduce(jnp.logical_or, matches)
    earlier = lax.broadcasted_iota(jnp.int32, (rows, rows), 1) < lax.broadcasted_iota(
        jnp.int32, (rows, rows), 0
    )
    rank = jnp.dot(
        earlier.astype(jnp.bfloat16), hit.astype(jnp.bfloat16), preferred_element_type=jnp.float32
    ).astype(jnp.int32)
    first = jnp.logical_and(hit, rank == slot)
    second = jnp.logical_and(hit, rank == slot - CAP)
    return matches, first, second


def dispatch_kernel(n_targets, ids_ref, gates_ref, tokens_ref, grads_ref, send_ref):
    matches, first, second = choice_table(ids_ref[...], n_targets)
    gates = gates_ref[...].astype(jnp.float32)
    scale = jnp.zeros(first.shape, jnp.float32)
    for k, match in enumerate(matches):
        scale = scale + jnp.where(match, gates[:, k : k + 1], 0.0)
    pick_tokens = first.astype(jnp.float32).astype(jnp.bfloat16)
    pick_grads = jnp.where(second, scale, 0.0).astype(jnp.bfloat16)
    rows = lax.dot_general(
        pick_tokens, tokens_ref[...], CONTRACT_FIRST, preferred_element_type=jnp.float32
    )
    rows = rows + lax.dot_general(
        pick_grads, grads_ref[...], CONTRACT_FIRST, preferred_element_type=jnp.float32
    )
    send_ref[...] = rows.astype(jnp.bfloat16)


def dispatch(n_targets, route_ids, gate_probs, tokens, out_grad):
    width = tokens.shape[1]
    return pl.pallas_call(
        functools.partial(dispatch_kernel, n_targets),
        out_shape=jax.ShapeDtypeStruct((n_targets * BLOCK, width), jnp.bfloat16),
        compiler_params=pltpu.CompilerParams(vmem_limit_bytes=32 * 2**20),
        name="dispatch",
    )(route_ids, gate_probs, tokens, out_grad)


def expert_kernel(count, *refs):
    pieces = refs[:count]
    weights = refs[count : count + 3]
    parts = refs[count + 3 : 2 * count + 3]
    gate_out, up_out, down_out = refs[2 * count + 3 : 2 * count + 6]
    x_s, w_s, sems = refs[2 * count + 6 :]
    piece_rows = pieces[0].shape[0]
    units, width = weights[0].shape
    half = width // 2
    rows = count * piece_rows
    copies = []
    for i, piece in enumerate(pieces):
        copies.append(
            pltpu.make_async_copy(piece, x_s.at[pl.ds(i * piece_rows, piece_rows)], sems.at[i])
        )
    for i, weight in enumerate(weights):
        copies.append(
            pltpu.make_async_copy(weight, w_s.at[pl.ds(i * units, units)], sems.at[count + i])
        )
    for copy in copies:
        copy.start()
    for copy in copies[:count]:
        copy.wait()
    x = x_s[...]
    projected = []
    for i in range(3):
        copies[count + i].wait()
        projected.append(
            lax.dot_general(
                w_s[pl.ds(i * units, units), :],
                x,
                CONTRACT_LAST,
                preferred_element_type=jnp.float32,
            )
        )
    pre_gate, pre_up, back = projected
    back = pltpu.roll(back, rows - CAP, 1)
    is_token = lax.broadcasted_iota(jnp.int32, (1, rows), 1) % BLOCK < CAP
    squash = 1.0 / (1.0 + jnp.exp(-pre_gate))
    activated = pre_gate * squash
    hidden = jnp.where(is_token, activated * pre_up, 0.0).astype(jnp.bfloat16).astype(jnp.float32)
    gate_terms = jnp.sum(hidden * back, axis=0, keepdims=True)
    up_pre = jnp.where(is_token, back * activated, 0.0)
    gate_pre = jnp.where(
        is_token, back * pre_up * squash * (1.0 + pre_gate * (1.0 - squash)), 0.0
    )
    gate_out[...] = gate_pre.astype(jnp.bfloat16)
    up_out[...] = up_pre.astype(jnp.bfloat16)
    down_out[...] = pltpu.roll(hidden, CAP, 1).astype(jnp.bfloat16)
    both = jnp.concatenate([gate_pre, up_pre], axis=0)
    low = both.T.astype(jnp.bfloat16)
    high = pltpu.roll(both, CAP, 1).T.astype(jnp.bfloat16)
    gate_column = jnp.broadcast_to(gate_terms, (LANES, rows)).T.astype(jnp.bfloat16)
    for i in range(count):
        parts[i][:, half:] = gate_column[i * piece_rows : (i + 1) * piece_rows]
    chunk = 512 if half % 512 == 0 else half

    @pl.loop(0, half // chunk)
    def _(step):
        start = pl.multiple_of(step * chunk, chunk)
        total = jnp.dot(
            low, w_s[: 2 * units, pl.ds(start, chunk)], preferred_element_type=jnp.float32
        )
        total = total + jnp.dot(
            high, w_s[: 2 * units, pl.ds(half + start, chunk)], preferred_element_type=jnp.float32
        )
        total = total.astype(jnp.bfloat16)
        for i in range(count):
            parts[i][:, pl.ds(start, chunk)] = total[i * piece_rows : (i + 1) * piece_rows]


def expert_rows(pieces, weights):
    count = len(pieces)
    piece_rows, width = pieces[0].shape
    units = weights[0].shape[0]
    rows = count * piece_rows
    anywhere = pl.BlockSpec(memory_space=pl.ANY)
    inside = pl.BlockSpec(memory_space=pltpu.VMEM)
    part = jax.ShapeDtypeStruct((piece_rows, width // 2 + LANES), jnp.bfloat16)
    kept = jax.ShapeDtypeStruct((units, rows), jnp.bfloat16)
    outs = pl.pallas_call(
        functools.partial(expert_kernel, count),
        out_shape=[part] * count + [kept] * 3,
        in_specs=[anywhere] * (count + 3),
        out_specs=[inside] * (count + 3),
        scratch_shapes=[
            pltpu.VMEM((rows, width), jnp.bfloat16),
            pltpu.VMEM((3 * units, width), jnp.bfloat16),
            pltpu.SemaphoreType.DMA((count + 3,)),
        ],
        compiler_params=pltpu.CompilerParams(vmem_limit_bytes=56 * 2**20),
        cost_estimate=pl.CostEstimate(
            flops=10 * rows * units * width,
            bytes_accessed=6 * units * width + 3 * rows * width,
            transcendentals=rows * units,
        ),
        name="expert_rows",
    )(*pieces, *weights)
    return outs[:count], outs[count:]


def weight_kernel(count, *refs):
    factors = refs[:3]
    pieces = refs[3 : 3 + count]
    outs = refs[3 + count :]
    x = jnp.concatenate([piece[...] for piece in pieces], axis=0)
    for factor, out in zip(factors, outs):
        out[...] = jnp.dot(factor[...], x, preferred_element_type=jnp.float32).astype(jnp.bfloat16)


def weight_grads(factors, pieces):
    count = len(pieces)
    piece_rows, width = pieces[0].shape
    units, rows = factors[0].shape
    chunk = 512 if width % 512 == 0 else width
    grad = jax.ShapeDtypeStruct((units, width), jnp.bfloat16)
    return pl.pallas_call(
        functools.partial(weight_kernel, count),
        grid=(width // chunk,),
        out_shape=[grad] * 3,
        in_specs=[pl.BlockSpec((units, rows), lambda i: (0, 0))] * 3
        + [pl.BlockSpec((piece_rows, chunk), lambda i: (0, i))] * count,
        out_specs=[pl.BlockSpec((units, chunk), lambda i: (0, i))] * 3,
        compiler_params=pltpu.CompilerParams(vmem_limit_bytes=32 * 2**20),
        cost_estimate=pl.CostEstimate(
            flops=6 * rows * units * width,
            bytes_accessed=6 * units * width + 2 * rows * width,
            transcendentals=0,
        ),
        name="weight_grads",
    )(*factors, *pieces)


def combine_kernel(n_targets, ids_ref, gates_ref, back_ref, token_ref, gate_ref):
    half = token_ref.shape[1] // 2
    token_rows, choices = ids_ref.shape
    matches, first, second = choice_table(ids_ref[...], n_targets)
    pick_first = first.astype(jnp.float32).astype(jnp.bfloat16)
    pick_second = second.astype(jnp.float32).astype(jnp.bfloat16)
    rows = back_ref[:, :half]
    token_ref[:, :half] = jnp.dot(
        pick_first, rows, preferred_element_type=jnp.float32
    ).astype(jnp.bfloat16)
    token_ref[:, half:] = jnp.dot(
        pick_second, rows, preferred_element_type=jnp.float32
    ).astype(jnp.bfloat16)
    lane = lax.broadcasted_iota(jnp.int32, (token_rows, LANES), 1)
    terms = jnp.zeros((token_rows, LANES), jnp.float32)
    for k in range(choices):
        chosen = jnp.logical_and(matches[k], first).astype(jnp.float32).astype(jnp.bfloat16)
        term = jnp.dot(chosen, back_ref[:, half:], preferred_element_type=jnp.float32)
        terms = terms + jnp.where(lane == k, term, 0.0)
    gate_ref[...] = terms[:, :choices] / gates_ref[...].astype(jnp.float32)


def combine(n_targets, route_ids, gate_probs, returned, width):
    token_rows, choices = route_ids.shape
    return pl.pallas_call(
        functools.partial(combine_kernel, n_targets),
        out_shape=[
            jax.ShapeDtypeStruct((token_rows, width), jnp.bfloat16),
            jax.ShapeDtypeStruct((token_rows, choices), jnp.float32),
        ],
        compiler_params=pltpu.CompilerParams(vmem_limit_bytes=32 * 2**20),
        name="combine",
    )(route_ids, gate_probs, returned)


def flip(value, axis, bit):
    size = lax.axis_size(axis)
    return lax.ppermute(value, axis, [(i, i ^ bit) for i in range(size)])


def exchange(value, n_targets):
    rows, width = value.shape
    blocks = value.reshape(n_targets, rows // n_targets, width)
    blocks = lax.all_to_all(blocks, "expert", split_axis=0, concat_axis=0, tiled=True)
    return blocks.reshape(rows, width)


def body(tokens, out_grad, gate_probs, route_ids, w_gate, w_up, w_down):
    n_targets = lax.axis_size("expert")
    n_dp = lax.axis_size("dp")
    width = tokens.shape[1]
    bits = [1 << i for i in range(1, n_dp.bit_length() - 1)] + [1]
    sent = dispatch(n_targets, route_ids, gate_probs, tokens, out_grad)
    held = {0: exchange(sent, n_targets)}
    for bit in bits:
        for mask in list(held):
            held[mask | bit] = flip(held[mask], "dp", bit)
    masks = sorted(held)
    pieces = [held[mask] for mask in masks]
    parts, factors = expert_rows(pieces, (w_gate[0], w_up[0], w_down[0]))
    grad_gate, grad_up, grad_down = weight_grads(factors, pieces)
    sums = dict(zip(masks, parts))
    for bit in reversed(bits):
        for mask in [m for m in sums if m & bit]:
            sums[mask ^ bit] = sums[mask ^ bit] + flip(sums.pop(mask), "dp", bit)
    returned = exchange(sums[0], n_targets)
    token_grad, gate_grad = combine(n_targets, route_ids, gate_probs, returned, width)
    return (token_grad, gate_grad, grad_gate[None], grad_up[None], grad_down[None])


def solution(mesh):
    in_specs = (
        P(("expert", "dp"), None),
        P(("expert", "dp"), None),
        P(("expert", "dp"), None),
        P(("expert", "dp"), None),
        P("expert", "dp", None),
        P("expert", "dp", None),
        P("expert", "dp", None),
    )
    out_specs = (
        P(("expert", "dp"), None),
        P(("expert", "dp"), None),
        P("expert", "dp", None),
        P("expert", "dp", None),
        P("expert", "dp", None),
    )
    return jax.shard_map(body, mesh=mesh, in_specs=in_specs, out_specs=out_specs, check_vma=False)
```

```python
import functools

import jax
import jax.numpy as jnp
from jax import lax
from jax.experimental import pallas as pl
from jax.experimental.pallas import tpu as pltpu
from jax.sharding import PartitionSpec as P

EXPERTS = 128
CAP = 4
BLOCK = 2 * CAP
LANES = 128
MIB = 2**20
SMALL_ROWS = 512
COVER = 12

CONTRACT_LAST = (((1,), (1,)), ((), ()))
CONTRACT_FIRST = (((0,), (0,)), ((), ()))

HBM = pl.BlockSpec(memory_space=pltpu.HBM)
ANY = pl.BlockSpec(memory_space=pl.ANY)
VMEM = pl.BlockSpec(memory_space=pltpu.VMEM)


def as_bf16(mask):
    return mask.astype(jnp.float32).astype(jnp.bfloat16)


def choice_table(ids, n_targets):
    choices, tokens = ids.shape
    height = n_targets * BLOCK
    per_device = EXPERTS // n_targets
    row = lax.broadcasted_iota(jnp.int32, (height, 1), 0)
    wanted = ((row // BLOCK) ^ lax.axis_index("expert")) * per_device
    slot = row % BLOCK
    matches = [ids[k : k + 1, :] == wanted for k in range(choices)]
    hit = functools.reduce(jnp.logical_or, matches)
    earlier = lax.broadcasted_iota(jnp.int32, (tokens, tokens), 0) < lax.broadcasted_iota(
        jnp.int32, (tokens, tokens), 1
    )
    rank = jnp.dot(as_bf16(hit), as_bf16(earlier), preferred_element_type=jnp.float32)
    rank = rank.astype(jnp.int32)
    first = jnp.logical_and(hit, rank == slot)
    second = jnp.logical_and(hit, rank == slot - CAP)
    return matches, first, second


def fetch(sources, targets, sems):
    copies = [
        pltpu.make_async_copy(source, target, sems.at[i])
        for i, (source, target) in enumerate(zip(sources, targets))
    ]
    for copy in copies:
        copy.start()
    for copy in copies:
        copy.wait()


def dispatch_kernel(n_targets, ids_hbm, gates_hbm, tokens_hbm, grads_hbm, *refs):
    outs = refs[:n_targets]
    ids_ref, gates_ref, tokens_ref, grads_ref, sems = refs[n_targets:]
    fetch(
        (ids_hbm, gates_hbm, tokens_hbm, grads_hbm),
        (ids_ref, gates_ref, tokens_ref, grads_ref),
        sems,
    )
    matches, first, second = choice_table(ids_ref[...], n_targets)
    gates = gates_ref[...].astype(jnp.float32)
    scale = jnp.zeros(first.shape, jnp.float32)
    for k, match in enumerate(matches):
        scale = scale + jnp.where(match, gates[k : k + 1, :], 0.0)
    pick_grads = jnp.where(second, scale, 0.0).astype(jnp.bfloat16)
    rows = jnp.dot(as_bf16(first), tokens_ref[...], preferred_element_type=jnp.float32)
    rows = rows + jnp.dot(pick_grads, grads_ref[...], preferred_element_type=jnp.float32)
    for k, out in enumerate(outs):
        out[...] = rows[k * BLOCK : (k + 1) * BLOCK].astype(jnp.bfloat16)


def dispatch(n_targets, ids, gates, tokens, out_grad):
    width = tokens.shape[1]
    arrays = (ids, gates, tokens, out_grad)
    return pl.pallas_call(
        functools.partial(dispatch_kernel, n_targets),
        out_shape=[jax.ShapeDtypeStruct((BLOCK, width), jnp.bfloat16)] * n_targets,
        in_specs=[HBM] * 4,
        out_specs=[VMEM] * n_targets,
        scratch_shapes=[pltpu.VMEM(a.shape, a.dtype) for a in arrays]
        + [pltpu.SemaphoreType.DMA((4,))],
        compiler_params=pltpu.CompilerParams(vmem_limit_bytes=60 * MIB),
        name="dispatch",
    )(*arrays)


def placement_kernel(n_targets, ids_ref, first_ref, second_ref, choice_ref):
    matches, first, second = choice_table(ids_ref[...], n_targets)
    first_ref[...] = as_bf16(first)
    second_ref[...] = as_bf16(second)
    choice = jnp.full(first.shape, -1, jnp.int32)
    for k, match in enumerate(matches):
        choice = jnp.where(jnp.logical_and(match, first), k, choice)
    choice_ref[...] = choice


def placement(n_targets, ids):
    table = (n_targets * BLOCK, ids.shape[1])
    return pl.pallas_call(
        functools.partial(placement_kernel, n_targets),
        out_shape=[
            jax.ShapeDtypeStruct(table, jnp.bfloat16),
            jax.ShapeDtypeStruct(table, jnp.bfloat16),
            jax.ShapeDtypeStruct(table, jnp.int32),
        ],
        in_specs=[VMEM],
        out_specs=[VMEM] * 3,
        compiler_params=pltpu.CompilerParams(vmem_limit_bytes=4 * MIB),
        cost_estimate=pl.CostEstimate(
            flops=COVER * 10**9, bytes_accessed=COVER * 10**6, transcendentals=0
        ),
        name="placement",
    )(ids)


def row_grads(low, high, gate_w, up_w, received, parts, half):
    units = gate_w.shape[0]
    chunk = 512 if half % 512 == 0 else half
    block = parts[0].shape[0]

    @pl.loop(0, half // chunk)
    def _(step):
        near = pl.ds(pl.multiple_of(step * chunk, chunk), chunk)
        far = pl.ds(pl.multiple_of(half + step * chunk, chunk), chunk)
        total = None
        for rows, columns in ((low, near), (high, far)):
            for i, weight in enumerate((gate_w, up_w)):
                term = jnp.dot(
                    rows[:, i * units : (i + 1) * units],
                    weight[:, columns],
                    preferred_element_type=jnp.float32,
                )
                total = term if total is None else total + term
        for i, part in enumerate(parts):
            value = total[i * block : (i + 1) * block]
            if received is not None:
                value = value + received[i][:, near].astype(jnp.float32)
            part[:, near] = value.astype(jnp.bfloat16)


def expert_kernel(count, *refs):
    pieces = refs[:count]
    gate_w, up_w, down_w = refs[count : count + 3]
    part, x_out, gate_out, up_out, down_out, low_out, high_out, gates_out = refs[count + 3 : -1]
    width = gate_w.shape[1]
    half = width // 2
    rows = count * BLOCK
    if rows > SMALL_ROWS:
        spots = [x_out.at[pl.ds(i * BLOCK, BLOCK)] for i in range(count)]
        fetch(pieces, spots, refs[-1])
    else:
        for i in range(0, count, 2):
            x_out[i * BLOCK : (i + 2) * BLOCK, :] = jnp.concatenate(
                [pieces[i][...], pieces[i + 1][...]], axis=0
            )

    def project(weight):
        return lax.dot_general(
            weight[...], x_out[...], CONTRACT_LAST, preferred_element_type=jnp.float32
        )

    pre_gate, pre_up, back = project(gate_w), project(up_w), project(down_w)
    back = pltpu.roll(back, rows - CAP, 1)
    is_token = lax.broadcasted_iota(jnp.int32, (1, rows), 1) % BLOCK < CAP
    squash = 1.0 / (1.0 + jnp.exp(-pre_gate))
    activated = pre_gate * squash
    hidden = jnp.where(is_token, activated * pre_up, 0.0).astype(jnp.bfloat16).astype(jnp.float32)
    gate_terms = jnp.sum(hidden * back, axis=0, keepdims=True)
    up_pre = jnp.where(is_token, back * activated, 0.0)
    gate_pre = jnp.where(
        is_token, back * pre_up * squash * (1.0 + pre_gate * (1.0 - squash)), 0.0
    )
    both = jnp.concatenate([gate_pre, up_pre], axis=0)
    low = both.T.astype(jnp.bfloat16)
    high = pltpu.roll(both, CAP, 1).T.astype(jnp.bfloat16)
    gate_column = jnp.broadcast_to(gate_terms, (LANES, rows)).T.astype(jnp.bfloat16)
    mine = rows // 2
    part[:, half:] = gate_column[mine:]
    row_grads(low[mine:], high[mine:], gate_w, up_w, None, (part,), half)
    low_out[...] = low[:mine]
    high_out[...] = high[:mine]
    gates_out[...] = gate_column[:mine]
    gate_out[...] = gate_pre.astype(jnp.bfloat16)
    up_out[...] = up_pre.astype(jnp.bfloat16)
    down_out[...] = pltpu.roll(hidden, CAP, 1).astype(jnp.bfloat16)


def expert_rows(pieces, weights):
    count = len(pieces)
    width = pieces[0].shape[1]
    units = weights[0].shape[0]
    rows = count * BLOCK
    mine = rows // 2
    shapes = [
        (mine, width // 2 + LANES),
        (rows, width),
        (units, rows),
        (units, rows),
        (units, rows),
        (mine, 2 * units),
        (mine, 2 * units),
        (mine, LANES),
    ]
    return pl.pallas_call(
        functools.partial(expert_kernel, count),
        out_shape=[jax.ShapeDtypeStruct(shape, jnp.bfloat16) for shape in shapes],
        in_specs=[VMEM if rows <= SMALL_ROWS else ANY] * count + [VMEM] * 3,
        out_specs=[VMEM] * len(shapes),
        scratch_shapes=[pltpu.SemaphoreType.DMA((count,))],
        compiler_params=pltpu.CompilerParams(
            vmem_limit_bytes=4 * MIB
            + 2 * sum(height * across for height, across in shapes)
            + 64 * rows * units
        ),
        cost_estimate=pl.CostEstimate(
            flops=8 * rows * units * width,
            bytes_accessed=6 * units * width,
            transcendentals=rows * units,
        ),
        name="expert_rows",
    )(*pieces, *weights)


def own_kernel(groups, low, high, gates, gate_w, up_w, received, *parts):
    half = gate_w.shape[1] // 2
    block = parts[0].shape[0]
    for i, part in enumerate(parts):
        span = pl.ds(i * block, block)
        part[:, half:] = (
            gates[span, :].astype(jnp.float32) + received[span, half:].astype(jnp.float32)
        ).astype(jnp.bfloat16)
    views = [received.at[pl.ds(i * block, block)] for i in range(groups)]
    row_grads(low[...], high[...], gate_w, up_w, views, parts, half)


def own_rows(groups, low, high, gates, gate_w, up_w, received):
    rows, width = received.shape
    units = gate_w.shape[0]
    return pl.pallas_call(
        functools.partial(own_kernel, groups),
        out_shape=[jax.ShapeDtypeStruct((rows // groups, width), jnp.bfloat16)] * groups,
        in_specs=[VMEM] * 6,
        out_specs=[VMEM] * groups,
        compiler_params=pltpu.CompilerParams(vmem_limit_bytes=8 * MIB + 8 * rows * width),
        cost_estimate=pl.CostEstimate(
            flops=4 * rows * units * gate_w.shape[1],
            bytes_accessed=4 * units * gate_w.shape[1],
            transcendentals=0,
        ),
        name="own_rows",
    )(low, high, gates, gate_w, up_w, received)


def add_kernel(count, left, right, *outs):
    for i, out in enumerate(outs):
        span = pl.ds(i * (left.shape[0] // count), left.shape[0] // count)
        out[...] = (
            left[span, :].astype(jnp.float32) + right[span, :].astype(jnp.float32)
        ).astype(jnp.bfloat16)


def add_rows(left, right, count):
    rows, width = left.shape
    return pl.pallas_call(
        functools.partial(add_kernel, count),
        out_shape=[jax.ShapeDtypeStruct((rows // count, width), jnp.bfloat16)] * count,
        in_specs=[VMEM] * 2,
        out_specs=[VMEM] * count,
        compiler_params=pltpu.CompilerParams(vmem_limit_bytes=4 * MIB + 8 * rows * width),
        name="add_rows",
    )(left, right)


def weight_kernel(chunk, factor, x, out, stage, sems):
    copies = []
    for i in range(x.shape[1] // chunk):
        span = pl.ds(i * chunk, chunk)
        stage[:, span] = jnp.dot(
            factor[...], x[:, span], preferred_element_type=jnp.float32
        ).astype(jnp.bfloat16)
        copies.append(pltpu.make_async_copy(stage.at[:, span], out.at[:, span], sems.at[i]))
        copies[-1].start()
    for copy in copies:
        copy.wait()


def weight_grad(factor, x):
    units, rows = factor.shape
    width = x.shape[1]
    chunk = 512 if width % 512 == 0 else width
    return pl.pallas_call(
        functools.partial(weight_kernel, chunk),
        out_shape=jax.ShapeDtypeStruct((units, width), jnp.bfloat16),
        in_specs=[VMEM] * 2,
        out_specs=HBM,
        scratch_shapes=[
            pltpu.VMEM((units, width), jnp.bfloat16),
            pltpu.SemaphoreType.DMA((width // chunk,)),
        ],
        compiler_params=pltpu.CompilerParams(vmem_limit_bytes=12 * MIB),
        cost_estimate=pl.CostEstimate(
            flops=2 * rows * units * width,
            bytes_accessed=2 * units * width,
            transcendentals=0,
        ),
        name="weight_grad",
    )(factor, x)


def combine_kernel(n_targets, first, second, choice_ref, gates_ref, *refs):
    blocks = refs[:n_targets]
    token_ref, gate_ref = refs[n_targets:]
    half = token_ref.shape[1] // 2
    choices, tokens = gates_ref.shape
    back = jnp.concatenate([block[...] for block in blocks], axis=0)
    rows = back[:, :half]
    token_ref[:, :half] = lax.dot_general(
        first[...], rows, CONTRACT_FIRST, preferred_element_type=jnp.float32
    ).astype(jnp.bfloat16)
    token_ref[:, half:] = lax.dot_general(
        second[...], rows, CONTRACT_FIRST, preferred_element_type=jnp.float32
    ).astype(jnp.bfloat16)
    terms = back[:, half : half + tokens].astype(jnp.float32)
    choice = choice_ref[...]
    for k in range(choices):
        chosen = jnp.where(choice == k, terms, 0.0)
        gate = gates_ref[k : k + 1, :].astype(jnp.float32)
        gate_ref[k : k + 1, :] = jnp.sum(chosen, axis=0, keepdims=True) / gate


def combine(n_targets, table, gates, blocks, width):
    choices, tokens = gates.shape
    return pl.pallas_call(
        functools.partial(combine_kernel, n_targets),
        out_shape=[
            jax.ShapeDtypeStruct((tokens, width), jnp.bfloat16),
            jax.ShapeDtypeStruct((choices, tokens), jnp.float32),
        ],
        in_specs=[VMEM] * (4 + n_targets),
        out_specs=[VMEM] * 2,
        compiler_params=pltpu.CompilerParams(
            vmem_limit_bytes=4 * MIB + 16 * n_targets * BLOCK * width
        ),
        name="combine",
    )(*table, gates, *blocks)


def flip(value, axis, bit):
    size = lax.axis_size(axis)
    return lax.ppermute(value, axis, [(i, i ^ bit) for i in range(size)])


def spread(block, bits):
    held = {0: block}
    for bit in bits:
        for mask in list(held):
            held[mask | bit] = flip(held[mask], "dp", bit)
    return held


def body(tokens, out_grad, gate_probs, route_ids, w_gate, w_up, w_down):
    n_targets = lax.axis_size("expert")
    n_dp = lax.axis_size("dp")
    width = tokens.shape[1]
    ids, gates = route_ids.T, gate_probs.T
    far_bits = [1 << i for i in range(1, n_dp.bit_length() - 1)]
    weights = (w_gate[0], w_up[0], w_down[0])

    sent = dispatch(n_targets, ids, gates, tokens, out_grad)
    arrived = [sent[0]] + [flip(sent[k], "expert", k) for k in range(1, n_targets)]
    ids_after, _ = lax.optimization_barrier((ids, sent[0]))
    arrived[-1], *table = lax.optimization_barrier((arrived[-1], *placement(n_targets, ids_after)))
    held = [spread(block, far_bits + [1]) for block in arrived]
    masks = sorted(held[0], key=lambda mask: (mask & 1, mask))
    pieces = [held[k][mask] for mask in masks for k in range(n_targets)]

    part, x, gate_f, up_f, down_f, low, high, gate_column = expert_rows(pieces, weights)
    received = flip(part, "dp", 1)
    grad_gate = weight_grad(gate_f, x)
    received, grad_gate = lax.optimization_barrier((received, grad_gate))
    mine = [mask for mask in masks if not mask & 1]
    sums = dict(
        zip(mine, own_rows(len(mine), low, high, gate_column, weights[0], weights[1], received))
    )
    grad_up = weight_grad(up_f, x)
    for bit in reversed(far_bits):
        moved = {mask: flip(sums.pop(mask), "dp", bit) for mask in list(sums) if mask & bit}
        if bit == far_bits[0]:
            moved, grad_up = lax.optimization_barrier((moved, grad_up))
        for mask, value in moved.items():
            count = n_targets if bit == far_bits[0] else 1
            total = add_rows(sums[mask ^ bit], value, count)
            sums[mask ^ bit] = total if count > 1 else total[0]
    blocks = sums[0]
    returned = [blocks[0]] + [flip(blocks[k], "expert", k) for k in range(1, n_targets)]
    grad_down = weight_grad(down_f, x)
    returned, grad_down = lax.optimization_barrier((returned, grad_down))
    token_grad, gate_grad = combine(n_targets, table, gates, returned, width)
    return (token_grad, gate_grad.T, grad_gate[None], grad_up[None], grad_down[None])


def solution(mesh):
    in_specs = (
        P(("expert", "dp"), None),
        P(("expert", "dp"), None),
        P(("expert", "dp"), None),
        P(("expert", "dp"), None),
        P("expert", "dp", None),
        P("expert", "dp", None),
        P("expert", "dp", None),
    )
    out_specs = (
        P(("expert", "dp"), None),
        P(("expert", "dp"), None),
        P("expert", "dp", None),
        P("expert", "dp", None),
        P("expert", "dp", None),
    )
    return jax.shard_map(body, mesh=mesh, in_specs=in_specs, out_specs=out_specs, check_vma=False)
```

```python
import functools

import jax
import jax.numpy as jnp
from jax import lax
from jax.experimental import pallas as pl
from jax.experimental.pallas import tpu as pltpu
from jax.sharding import PartitionSpec as P

EXPERTS = 128
CAP = 4
BLOCK = 2 * CAP
LANES = 128
MIB = 2**20
COVER = 12

CONTRACT_LAST = (((1,), (1,)), ((), ()))
CONTRACT_FIRST = (((0,), (0,)), ((), ()))

HBM = pl.BlockSpec(memory_space=pltpu.HBM)
VMEM = pl.BlockSpec(memory_space=pltpu.VMEM)


def struct(shape, dtype=jnp.bfloat16):
    return jax.ShapeDtypeStruct(shape, dtype)


def as_bf16(mask):
    return mask.astype(jnp.float32).astype(jnp.bfloat16)


def choice_table(ids, n_targets):
    choices, tokens = ids.shape
    height = n_targets * BLOCK
    per_device = EXPERTS // n_targets
    row = lax.broadcasted_iota(jnp.int32, (height, 1), 0)
    wanted = (row // BLOCK) * per_device
    slot = row % BLOCK
    matches = [ids[k : k + 1, :] == wanted for k in range(choices)]
    hit = functools.reduce(jnp.logical_or, matches)
    earlier = lax.broadcasted_iota(jnp.int32, (tokens, tokens), 0) < lax.broadcasted_iota(
        jnp.int32, (tokens, tokens), 1
    )
    rank = jnp.dot(as_bf16(hit), as_bf16(earlier), preferred_element_type=jnp.float32)
    rank = rank.astype(jnp.int32)
    first = jnp.logical_and(hit, rank == slot)
    second = jnp.logical_and(hit, rank == slot - CAP)
    return matches, first, second


def pick_rows(first, second, rows_ref):
    half = rows_ref.shape[1] // 2
    low = jnp.dot(first, rows_ref[:, :half], preferred_element_type=jnp.float32)
    high = jnp.dot(second, rows_ref[:, half:], preferred_element_type=jnp.float32)
    return (low + high).astype(jnp.bfloat16)


def send_tokens_kernel(n_targets, ids_hbm, tokens_hbm, out, ids_ref, tokens_ref, sems):
    ids_copy = pltpu.make_async_copy(ids_hbm, ids_ref, sems.at[0])
    tokens_copy = pltpu.make_async_copy(tokens_hbm, tokens_ref, sems.at[1])
    ids_copy.start()
    tokens_copy.start()
    ids_copy.wait()
    _, first, second = choice_table(ids_ref[...], n_targets)
    tokens_copy.wait()
    out[...] = pick_rows(as_bf16(first), as_bf16(second), tokens_ref)


def send_tokens(n_targets, ids, tokens):
    return pl.pallas_call(
        functools.partial(send_tokens_kernel, n_targets),
        out_shape=struct((n_targets * BLOCK, tokens.shape[1] // 2)),
        in_specs=[HBM] * 2,
        out_specs=VMEM,
        scratch_shapes=[pltpu.VMEM(a.shape, a.dtype) for a in (ids, tokens)]
        + [pltpu.SemaphoreType.DMA((2,))],
        compiler_params=pltpu.CompilerParams(vmem_limit_bytes=60 * MIB),
        name="send_tokens",
    )(ids, tokens)


def send_grads_kernel(n_targets, ids_ref, gates_ref, grads_ref, out):
    matches, first, second = choice_table(ids_ref[...], n_targets)
    gates = gates_ref[...].astype(jnp.float32)
    scale = jnp.zeros(first.shape, jnp.float32)
    for k, match in enumerate(matches):
        scale = scale + jnp.where(match, gates[k : k + 1, :], 0.0)
    first = jnp.where(first, scale, 0.0).astype(jnp.bfloat16)
    second = jnp.where(second, scale, 0.0).astype(jnp.bfloat16)
    out[...] = pick_rows(first, second, grads_ref)


def send_grads(n_targets, ids, gates, out_grad):
    return pl.pallas_call(
        functools.partial(send_grads_kernel, n_targets),
        out_shape=struct((n_targets * BLOCK, out_grad.shape[1] // 2)),
        in_specs=[VMEM] * 3,
        out_specs=VMEM,
        compiler_params=pltpu.CompilerParams(
            vmem_limit_bytes=4 * MIB + 8 * n_targets * BLOCK * out_grad.shape[1]
        ),
        name="send_grads",
    )(ids, gates, out_grad)


def placement_kernel(n_targets, ids_ref, first_ref, second_ref, choice_ref):
    matches, first, second = choice_table(ids_ref[...], n_targets)
    first_ref[...] = as_bf16(first)
    second_ref[...] = as_bf16(second)
    choice = jnp.full(first.shape, -1, jnp.int32)
    for k, match in enumerate(matches):
        choice = jnp.where(jnp.logical_and(match, first), k, choice)
    choice_ref[...] = choice


def placement(n_targets, ids):
    table = (n_targets * BLOCK, ids.shape[1])
    return pl.pallas_call(
        functools.partial(placement_kernel, n_targets),
        out_shape=[struct(table), struct(table), struct(table, jnp.int32)],
        in_specs=[VMEM],
        out_specs=[VMEM] * 3,
        compiler_params=pltpu.CompilerParams(vmem_limit_bytes=4 * MIB),
        cost_estimate=pl.CostEstimate(
            flops=COVER * 10**9, bytes_accessed=COVER * 10**6, transcendentals=0
        ),
        name="placement",
    )(ids)


def gather_pieces(pieces, out):
    block = pieces[0].shape[0]
    for i, piece in enumerate(pieces):
        out[pl.ds(i * block, block), :] = piece[...]


def project(weight, halves):
    half = halves.shape[1]
    rows = halves.shape[0]
    low = lax.dot_general(
        weight[:, :half], halves[...], CONTRACT_LAST, preferred_element_type=jnp.float32
    )
    high = lax.dot_general(
        weight[:, half:], halves[...], CONTRACT_LAST, preferred_element_type=jnp.float32
    )
    return low + pltpu.roll(high, rows - CAP, 1)


def forward_kernel(count, *refs):
    pieces = refs[:count]
    gate_w, up_w, halves, activated_out, slope_out, hidden_out = refs[count:]
    gather_pieces(pieces, halves)
    pre_gate, pre_up = project(gate_w, halves), project(up_w, halves)
    is_slot = lax.broadcasted_iota(jnp.int32, (1, halves.shape[0]), 1) % BLOCK < CAP
    squash = 1.0 / (1.0 + jnp.exp(-pre_gate))
    activated = jnp.where(is_slot, pre_gate * squash, 0.0)
    slope = pre_up * squash * (1.0 + pre_gate * (1.0 - squash))
    activated_out[...] = activated
    slope_out[...] = jnp.where(is_slot, slope, 0.0)
    hidden_out[...] = (activated * pre_up).astype(jnp.bfloat16)


def forward(pieces, gate_w, up_w):
    count = len(pieces)
    units, width = gate_w.shape
    rows = count * pieces[0].shape[0]
    kept = (units, rows)
    return pl.pallas_call(
        functools.partial(forward_kernel, count),
        out_shape=[
            struct((rows, width // 2)),
            struct(kept, jnp.float32),
            struct(kept, jnp.float32),
            struct(kept),
        ],
        in_specs=[VMEM] * (count + 2),
        out_specs=[VMEM] * 4,
        compiler_params=pltpu.CompilerParams(
            vmem_limit_bytes=4 * MIB + rows * width + 40 * rows * units
        ),
        cost_estimate=pl.CostEstimate(
            flops=4 * rows * units * width,
            bytes_accessed=4 * units * width,
            transcendentals=rows * units,
        ),
        name="forward",
    )(*pieces, gate_w, up_w)


def row_grads(low, high, gate_w, up_w, received, parts, half):
    units = gate_w.shape[0]
    block = parts[0].shape[0]
    chunk = 512 if half % 512 == 0 else half

    @pl.loop(0, half // chunk)
    def _(step):
        near = pl.ds(pl.multiple_of(step * chunk, chunk), chunk)
        far = pl.ds(pl.multiple_of(half + step * chunk, chunk), chunk)
        total = None
        for rows, columns in ((low, near), (high, far)):
            for i, weight in enumerate((gate_w, up_w)):
                term = jnp.dot(
                    rows[:, i * units : (i + 1) * units],
                    weight[:, columns],
                    preferred_element_type=jnp.float32,
                )
                total = term if total is None else total + term
        if received is not None:
            total = total + received[:, near].astype(jnp.float32)
        total = total.astype(jnp.bfloat16)
        for i, part in enumerate(parts):
            part[:, near] = total[i * block : (i + 1) * block]


def backward_kernel(count, *refs):
    pieces = refs[:count]
    activated, slope, hidden, gate_w, up_w, down_w = refs[count : count + 6]
    part, halves, gate_out, up_out, low_out, high_out, gates_out = refs[count + 6 :]
    half = halves.shape[1]
    rows = halves.shape[0]
    mine = rows // 2
    gather_pieces(pieces, halves)
    back = project(down_w, halves)
    gate_terms = jnp.sum(hidden[...].astype(jnp.float32) * back, axis=0, keepdims=True)
    up_pre = back * activated[...]
    gate_pre = back * slope[...]
    both = jnp.concatenate([gate_pre, up_pre], axis=0)
    low = both.T.astype(jnp.bfloat16)
    high = pltpu.roll(both, CAP, 1).T.astype(jnp.bfloat16)
    gate_column = jnp.broadcast_to(gate_terms, (LANES, rows)).T.astype(jnp.bfloat16)
    part[:, half:] = gate_column[mine:]
    row_grads(low[mine:], high[mine:], gate_w, up_w, None, (part,), half)
    low_out[...] = low[:mine]
    high_out[...] = high[:mine]
    gates_out[...] = gate_column[:mine]
    gate_out[...] = gate_pre.astype(jnp.bfloat16)
    up_out[...] = up_pre.astype(jnp.bfloat16)


def backward(pieces, activated, slope, hidden, weights):
    count = len(pieces)
    units, width = weights[0].shape
    rows = count * pieces[0].shape[0]
    mine = rows // 2
    shapes = [
        (mine, width // 2 + LANES),
        (rows, width // 2),
        (units, rows),
        (units, rows),
        (mine, 2 * units),
        (mine, 2 * units),
        (mine, LANES),
    ]
    return pl.pallas_call(
        functools.partial(backward_kernel, count),
        out_shape=[struct(shape) for shape in shapes],
        in_specs=[VMEM] * (count + 6),
        out_specs=[VMEM] * len(shapes),
        compiler_params=pltpu.CompilerParams(
            vmem_limit_bytes=4 * MIB
            + 2 * sum(height * across for height, across in shapes)
            + 40 * rows * units
        ),
        cost_estimate=pl.CostEstimate(
            flops=4 * rows * units * width,
            bytes_accessed=2 * units * width,
            transcendentals=0,
        ),
        name="backward",
    )(*pieces, activated, slope, hidden, *weights)


def own_kernel(low, high, gates, gate_w, up_w, received, *parts):
    half = gate_w.shape[1] // 2
    block = parts[0].shape[0]
    for i, part in enumerate(parts):
        span = pl.ds(i * block, block)
        part[:, half:] = (
            gates[span, :].astype(jnp.float32) + received[span, half:].astype(jnp.float32)
        ).astype(jnp.bfloat16)
    row_grads(low[...], high[...], gate_w, up_w, received, parts, half)


def own_rows(count, low, high, gates, gate_w, up_w, received):
    rows, width = received.shape
    units = gate_w.shape[0]
    return pl.pallas_call(
        own_kernel,
        out_shape=[struct((rows // count, width))] * count,
        in_specs=[VMEM] * 6,
        out_specs=[VMEM] * count,
        compiler_params=pltpu.CompilerParams(vmem_limit_bytes=8 * MIB + 8 * rows * width),
        cost_estimate=pl.CostEstimate(
            flops=4 * rows * units * gate_w.shape[1],
            bytes_accessed=4 * units * gate_w.shape[1],
            transcendentals=0,
        ),
        name="own_rows",
    )(low, high, gates, gate_w, up_w, received)


def add_kernel(left, right, out):
    out[...] = (left[...].astype(jnp.float32) + right[...].astype(jnp.float32)).astype(
        jnp.bfloat16
    )


def add_rows(left, right):
    return pl.pallas_call(
        add_kernel,
        out_shape=struct(right.shape),
        in_specs=[VMEM] * 2,
        out_specs=VMEM,
        compiler_params=pltpu.CompilerParams(vmem_limit_bytes=4 * MIB + 16 * right.size),
        name="add_rows",
    )(left, right)


def weight_kernel(chunk, factor_ref, halves, out, stage, sems):
    half = halves.shape[1]
    low = factor_ref[...]
    high = pltpu.roll(low.astype(jnp.float32), CAP, 1).astype(jnp.bfloat16)
    copies = []
    for factor, base in ((low, 0), (high, half)):
        for start in range(0, half, chunk):
            span = pl.ds(base + start, chunk)
            stage[:, span] = jnp.dot(
                factor, halves[:, pl.ds(start, chunk)], preferred_element_type=jnp.float32
            ).astype(jnp.bfloat16)
            copies.append(
                pltpu.make_async_copy(
                    stage.at[:, span], out.at[:, span], sems.at[len(copies)]
                )
            )
            copies[-1].start()
    for copy in copies:
        copy.wait()


def weight_grad(factor, halves):
    units, rows = factor.shape
    half = halves.shape[1]
    chunk = 512 if half % 512 == 0 else half
    return pl.pallas_call(
        functools.partial(weight_kernel, chunk),
        out_shape=struct((units, 2 * half)),
        in_specs=[VMEM] * 2,
        out_specs=HBM,
        scratch_shapes=[
            pltpu.VMEM((units, 2 * half), jnp.bfloat16),
            pltpu.SemaphoreType.DMA((2 * half // chunk,)),
        ],
        compiler_params=pltpu.CompilerParams(
            vmem_limit_bytes=8 * MIB + 4 * units * half + 8 * units * rows
        ),
        cost_estimate=pl.CostEstimate(
            flops=4 * rows * units * half,
            bytes_accessed=4 * units * half,
            transcendentals=0,
        ),
        name="weight_grad",
    )(factor, halves)


def combine_kernel(first, second, choice_ref, gates_ref, back, token_ref, gate_ref):
    half = token_ref.shape[1] // 2
    choices, tokens = gates_ref.shape
    rows = back[:, :half]
    token_ref[:, :half] = lax.dot_general(
        first[...], rows, CONTRACT_FIRST, preferred_element_type=jnp.float32
    ).astype(jnp.bfloat16)
    token_ref[:, half:] = lax.dot_general(
        second[...], rows, CONTRACT_FIRST, preferred_element_type=jnp.float32
    ).astype(jnp.bfloat16)
    terms = back[:, half : half + tokens].astype(jnp.float32)
    choice = choice_ref[...]
    for k in range(choices):
        chosen = jnp.where(choice == k, terms, 0.0)
        gate = gates_ref[k : k + 1, :].astype(jnp.float32)
        gate_ref[k : k + 1, :] = jnp.sum(chosen, axis=0, keepdims=True) / gate


def combine(table, gates, returned, width):
    choices, tokens = gates.shape
    return pl.pallas_call(
        combine_kernel,
        out_shape=[struct((tokens, width)), struct((choices, tokens), jnp.float32)],
        in_specs=[VMEM] * 5,
        out_specs=[VMEM] * 2,
        compiler_params=pltpu.CompilerParams(vmem_limit_bytes=4 * MIB + 16 * returned.size),
        name="combine",
    )(*table, gates, returned)


def flip(value, axis, bit):
    size = lax.axis_size(axis)
    return lax.ppermute(value, axis, [(i, i ^ bit) for i in range(size)])


def exchange(value):
    n_targets = lax.axis_size("expert")
    rows, width = value.shape
    blocks = value.reshape(n_targets, rows // n_targets, width)
    blocks = lax.all_to_all(blocks, "expert", split_axis=0, concat_axis=0, tiled=True)
    return blocks.reshape(rows, width)


def cross(block, far_bits):
    held = {0: block}
    for bit in far_bits:
        for mask in list(held):
            held[mask | bit] = flip(held[mask], "dp", bit)
    return held


def body(tokens, out_grad, gate_probs, route_ids, w_gate, w_up, w_down):
    n_targets = lax.axis_size("expert")
    n_dp = lax.axis_size("dp")
    width = tokens.shape[1]
    ids, gates = route_ids.T, gate_probs.T
    far_bits = [1 << i for i in range(1, n_dp.bit_length() - 1)]
    weights = (w_gate[0], w_up[0], w_down[0])
    tie = lax.optimization_barrier

    token_rows = send_tokens(n_targets, ids, tokens)
    ids_after, token_rows = tie((ids, token_rows))
    token_rows = exchange(token_rows)
    grad_rows = send_grads(n_targets, ids_after, gates, out_grad)
    table_ids, token_rows = tie((ids_after, token_rows))
    grad_rows, *table = tie((grad_rows, *placement(n_targets, table_ids)))
    grad_rows = exchange(grad_rows)

    token_held = cross(token_rows, far_bits)
    near = sorted(token_held)
    token_near = [token_held[mask] for mask in near]
    token_far = [flip(token_near[0], "dp", 1)]
    grad_rows, *token_near[1:] = tie((grad_rows, *token_near[1:]))
    grad_held = cross(grad_rows, far_bits)
    token_far += [flip(value, "dp", 1) for value in token_near[1:]]
    grad_near = [grad_held[mask] for mask in near]
    token_halves, activated, slope, hidden = forward(
        token_near + token_far, weights[0], weights[1]
    )
    activated, slope, hidden, *grad_near = tie((activated, slope, hidden, *grad_near))
    grad_far = [flip(value, "dp", 1) for value in grad_near]

    part, grad_halves, gate_f, up_f, low, high, gate_column = backward(
        grad_near + grad_far, activated, slope, hidden, weights
    )
    received = flip(part, "dp", 1)
    grad_gate = weight_grad(gate_f, token_halves)
    received, grad_gate = tie((received, grad_gate))
    totals = own_rows(len(near), low, high, gate_column, weights[0], weights[1], received)
    sums = dict(zip(near, totals))
    grad_up = weight_grad(up_f, token_halves)
    for bit in reversed(far_bits):
        moved = {mask: flip(sums.pop(mask), "dp", bit) for mask in list(sums) if mask & bit}
        if bit == far_bits[0]:
            moved, grad_up = tie((moved, grad_up))
        for mask, value in moved.items():
            sums[mask ^ bit] = add_rows(sums[mask ^ bit], value)
    returned = exchange(sums[0])
    grad_down = weight_grad(hidden, grad_halves)
    returned, grad_down = tie((returned, grad_down))
    token_grad, gate_grad = combine(table, gates, returned, width)
    return (token_grad, gate_grad.T, grad_gate[None], grad_up[None], grad_down[None])


def solution(mesh):
    in_specs = (
        P(("expert", "dp"), None),
        P(("expert", "dp"), None),
        P(("expert", "dp"), None),
        P(("expert", "dp"), None),
        P("expert", "dp", None),
        P("expert", "dp", None),
        P("expert", "dp", None),
    )
    out_specs = (
        P(("expert", "dp"), None),
        P(("expert", "dp"), None),
        P("expert", "dp", None),
        P("expert", "dp", None),
        P("expert", "dp", None),
    )
    return jax.shard_map(body, mesh=mesh, in_specs=in_specs, out_specs=out_specs, check_vma=False)
```

```python
import functools

import jax
import jax.numpy as jnp
from jax import lax
from jax.experimental import pallas as pl
from jax.experimental.pallas import tpu as pltpu
from jax.sharding import PartitionSpec as P

EXPERTS = 128
CAP = 4
BLOCK = 2 * CAP
LANES = 128
MIB = 2**20
COVER = 40

CONTRACT_LAST = (((1,), (1,)), ((), ()))
CONTRACT_FIRST = (((0,), (0,)), ((), ()))

HBM = pl.BlockSpec(memory_space=pltpu.HBM)
VMEM = pl.BlockSpec(memory_space=pltpu.VMEM)


def struct(shape, dtype=jnp.bfloat16):
    return jax.ShapeDtypeStruct(shape, dtype)


def as_bf16(mask):
    return mask.astype(jnp.float32).astype(jnp.bfloat16)


def choice_table(ids, n_targets):
    choices, tokens = ids.shape
    height = n_targets * BLOCK
    per_device = EXPERTS // n_targets
    row = lax.broadcasted_iota(jnp.int32, (height, 1), 0)
    wanted = (row // BLOCK) * per_device
    slot = row % BLOCK
    matches = [ids[k : k + 1, :] == wanted for k in range(choices)]
    hit = functools.reduce(jnp.logical_or, matches)
    earlier = lax.broadcasted_iota(jnp.int32, (tokens, tokens), 0) < lax.broadcasted_iota(
        jnp.int32, (tokens, tokens), 1
    )
    rank = jnp.dot(as_bf16(hit), as_bf16(earlier), preferred_element_type=jnp.float32)
    rank = rank.astype(jnp.int32)
    first = jnp.logical_and(hit, rank == slot)
    second = jnp.logical_and(hit, rank == slot - CAP)
    return matches, first, second


def pick_rows(first, second, rows_ref):
    half = rows_ref.shape[1] // 2
    low = jnp.dot(first, rows_ref[:, :half], preferred_element_type=jnp.float32)
    high = jnp.dot(second, rows_ref[:, half:], preferred_element_type=jnp.float32)
    return (low + high).astype(jnp.bfloat16)


def dispatch_kernel(n_targets, *refs):
    sources, (token_out, grad_out), targets, sems = refs[:4], refs[4:6], refs[6:10], refs[10]
    ids_ref, tokens_ref, gates_ref, grads_ref = targets
    copies = [
        pltpu.make_async_copy(source, target, sems.at[i])
        for i, (source, target) in enumerate(zip(sources, targets))
    ]
    for copy in copies:
        copy.start()
    copies[0].wait()
    matches, first, second = choice_table(ids_ref[...], n_targets)
    copies[1].wait()
    token_out[...] = pick_rows(as_bf16(first), as_bf16(second), tokens_ref)
    copies[2].wait()
    gates = gates_ref[...].astype(jnp.float32)
    scale = jnp.zeros(first.shape, jnp.float32)
    for k, match in enumerate(matches):
        scale = scale + jnp.where(match, gates[k : k + 1, :], 0.0)
    first = jnp.where(first, scale, 0.0).astype(jnp.bfloat16)
    second = jnp.where(second, scale, 0.0).astype(jnp.bfloat16)
    copies[3].wait()
    grad_out[...] = pick_rows(first, second, grads_ref)


def dispatch(n_targets, ids, tokens, gates, out_grad):
    arrays = (ids, tokens, gates, out_grad)
    return pl.pallas_call(
        functools.partial(dispatch_kernel, n_targets),
        out_shape=[struct((n_targets * BLOCK, tokens.shape[1] // 2))] * 2,
        in_specs=[HBM] * 4,
        out_specs=[VMEM] * 2,
        scratch_shapes=[pltpu.VMEM(a.shape, a.dtype) for a in arrays]
        + [pltpu.SemaphoreType.DMA((4,))],
        compiler_params=pltpu.CompilerParams(vmem_limit_bytes=60 * MIB),
        name="dispatch",
    )(*arrays)


def placement_kernel(n_targets, ids_ref, first_ref, second_ref, choice_ref):
    matches, first, second = choice_table(ids_ref[...], n_targets)
    first_ref[...] = as_bf16(first)
    second_ref[...] = as_bf16(second)
    choice = jnp.full(first.shape, -1, jnp.int32)
    for k, match in enumerate(matches):
        choice = jnp.where(jnp.logical_and(match, first), k, choice)
    choice_ref[...] = choice


def placement(n_targets, ids):
    table = (n_targets * BLOCK, ids.shape[1])
    return pl.pallas_call(
        functools.partial(placement_kernel, n_targets),
        out_shape=[struct(table), struct(table), struct(table, jnp.int32)],
        in_specs=[VMEM],
        out_specs=[VMEM] * 3,
        compiler_params=pltpu.CompilerParams(vmem_limit_bytes=4 * MIB),
        cost_estimate=pl.CostEstimate(
            flops=COVER * 10**9, bytes_accessed=COVER * 10**6, transcendentals=0
        ),
        name="placement",
    )(ids)


def gather_pieces(pieces, out):
    block = pieces[0].shape[0]
    for i, piece in enumerate(pieces):
        out[pl.ds(i * block, block), :] = piece[...]


def project(weight, halves):
    half = halves.shape[1]
    rows = halves.shape[0]
    low = lax.dot_general(
        weight[:, :half], halves[...], CONTRACT_LAST, preferred_element_type=jnp.float32
    )
    high = lax.dot_general(
        weight[:, half:], halves[...], CONTRACT_LAST, preferred_element_type=jnp.float32
    )
    return low + pltpu.roll(high, rows - CAP, 1)


def forward_kernel(count, *refs):
    pieces = refs[:count]
    gate_w, up_w, halves, activated_out, slope_out, hidden_out = refs[count:]
    gather_pieces(pieces, halves)
    pre_gate, pre_up = project(gate_w, halves), project(up_w, halves)
    is_slot = lax.broadcasted_iota(jnp.int32, (1, halves.shape[0]), 1) % BLOCK < CAP
    squash = 1.0 / (1.0 + jnp.exp(-pre_gate))
    activated = jnp.where(is_slot, pre_gate * squash, 0.0)
    slope = pre_up * squash * (1.0 + pre_gate * (1.0 - squash))
    activated_out[...] = activated
    slope_out[...] = jnp.where(is_slot, slope, 0.0)
    hidden_out[...] = (activated * pre_up).astype(jnp.bfloat16)


def forward(pieces, gate_w, up_w):
    count = len(pieces)
    units, width = gate_w.shape
    rows = count * pieces[0].shape[0]
    kept = (units, rows)
    return pl.pallas_call(
        functools.partial(forward_kernel, count),
        out_shape=[
            struct((rows, width // 2)),
            struct(kept, jnp.float32),
            struct(kept, jnp.float32),
            struct(kept),
        ],
        in_specs=[VMEM] * (count + 2),
        out_specs=[VMEM] * 4,
        compiler_params=pltpu.CompilerParams(
            vmem_limit_bytes=4 * MIB + rows * width + 40 * rows * units
        ),
        cost_estimate=pl.CostEstimate(
            flops=4 * rows * units * width,
            bytes_accessed=4 * units * width,
            transcendentals=rows * units,
        ),
        name="forward",
    )(*pieces, gate_w, up_w)


def row_grads(low, high, gate_w, up_w, received, parts, start, size):
    units, width = gate_w.shape
    block = parts[0].shape[0]
    chunk = 512 if size % 512 == 0 else size

    @pl.loop(0, size // chunk)
    def _(step):
        offset = pl.multiple_of(step * chunk, chunk)
        near = pl.ds(pl.multiple_of(start + offset, chunk), chunk)
        far = pl.ds(pl.multiple_of(width // 2 + start + offset, chunk), chunk)
        here = pl.ds(offset, chunk)
        total = None
        for rows, columns in ((low, near), (high, far)):
            for i, weight in enumerate((gate_w, up_w)):
                term = jnp.dot(
                    rows[:, i * units : (i + 1) * units],
                    weight[:, columns],
                    preferred_element_type=jnp.float32,
                )
                total = term if total is None else total + term
        if received is not None:
            total = total + received[:, here].astype(jnp.float32)
        total = total.astype(jnp.bfloat16)
        for i, part in enumerate(parts):
            part[:, here] = total[i * block : (i + 1) * block]


def backward_kernel(count, *refs):
    pieces = refs[:count]
    activated, slope, hidden, gate_w, up_w, down_w = refs[count : count + 6]
    part, halves, gate_out, up_out, low_out, high_out, gates_out = refs[count + 6 :]
    rows = halves.shape[0]
    mine = rows // 2
    gather_pieces(pieces, halves)
    back = project(down_w, halves)
    gate_terms = jnp.sum(hidden[...].astype(jnp.float32) * back, axis=0, keepdims=True)
    up_pre = back * activated[...]
    gate_pre = back * slope[...]
    both = jnp.concatenate([gate_pre, up_pre], axis=0)
    low = both.T.astype(jnp.bfloat16)
    high = pltpu.roll(both, CAP, 1).T.astype(jnp.bfloat16)
    gate_column = jnp.broadcast_to(gate_terms, (LANES, rows)).T.astype(jnp.bfloat16)
    row_grads(low[mine:], high[mine:], gate_w, up_w, None, (part,), 0, part.shape[1])
    low_out[...] = low
    high_out[...] = high
    gates_out[...] = gate_column
    gate_out[...] = gate_pre.astype(jnp.bfloat16)
    up_out[...] = up_pre.astype(jnp.bfloat16)


def backward(pieces, activated, slope, hidden, weights):
    count = len(pieces)
    units, width = weights[0].shape
    rows = count * pieces[0].shape[0]
    mine = rows // 2
    shapes = [
        (mine, width // 4),
        (rows, width // 2),
        (units, rows),
        (units, rows),
        (rows, 2 * units),
        (rows, 2 * units),
        (rows, LANES),
    ]
    return pl.pallas_call(
        functools.partial(backward_kernel, count),
        out_shape=[struct(shape) for shape in shapes],
        in_specs=[VMEM] * (count + 6),
        out_specs=[VMEM] * len(shapes),
        compiler_params=pltpu.CompilerParams(
            vmem_limit_bytes=4 * MIB
            + 2 * sum(height * across for height, across in shapes)
            + 40 * rows * units
        ),
        cost_estimate=pl.CostEstimate(
            flops=3 * rows * units * width,
            bytes_accessed=2 * units * width,
            transcendentals=0,
        ),
        name="backward",
    )(*pieces, activated, slope, hidden, *weights)


def far_kernel(start, low, high, gates, gate_w, up_w, part):
    span = pl.ds(part.shape[0], part.shape[0])
    size = part.shape[1] - LANES
    part[:, size:] = gates[span, :]
    row_grads(low[span, :], high[span, :], gate_w, up_w, None, (part,), start, size)


def far_rows(start, low, high, gates, gate_w, up_w):
    rows, width = low.shape[0], gate_w.shape[1]
    size = width // 2 - start
    return pl.pallas_call(
        functools.partial(far_kernel, start),
        out_shape=struct((rows // 2, size + LANES)),
        in_specs=[VMEM] * 5,
        out_specs=VMEM,
        compiler_params=pltpu.CompilerParams(vmem_limit_bytes=8 * MIB + 4 * rows * width),
        cost_estimate=pl.CostEstimate(
            flops=4 * rows * low.shape[1] * size, bytes_accessed=4 * rows * size, transcendentals=0
        ),
        name="far_rows",
    )(low, high, gates, gate_w, up_w)


def own_kernel(start, extra, low, high, gates, gate_w, up_w, received, *parts):
    rows, size = received.shape
    size -= extra
    block = parts[0].shape[0]
    if extra:
        for i, part in enumerate(parts):
            span = pl.ds(i * block, block)
            part[:, size:] = (
                gates[span, :].astype(jnp.float32) + received[span, size:].astype(jnp.float32)
            ).astype(jnp.bfloat16)
    row_grads(low[:rows, :], high[:rows, :], gate_w, up_w, received, parts, start, size)


def own_rows(count, start, low, high, gates, gate_w, up_w, received):
    rows, width = received.shape
    return pl.pallas_call(
        functools.partial(own_kernel, start, LANES if start else 0),
        out_shape=[struct((rows // count, width))] * count,
        in_specs=[VMEM] * 6,
        out_specs=[VMEM] * count,
        compiler_params=pltpu.CompilerParams(vmem_limit_bytes=8 * MIB + 16 * rows * width),
        cost_estimate=pl.CostEstimate(
            flops=4 * rows * low.shape[1] * width,
            bytes_accessed=4 * rows * width,
            transcendentals=0,
        ),
        name="own_rows",
    )(low, high, gates, gate_w, up_w, received)


def add_kernel(count, *refs):
    out = refs[-1]
    base = 0
    for left, right in zip(refs[:count], refs[count:-1]):
        total = left[...].astype(jnp.float32) + right[...].astype(jnp.float32)
        out[:, base : base + left.shape[1]] = total.astype(jnp.bfloat16)
        base += left.shape[1]


def add_rows(lefts, rights):
    count = len(lefts)
    rows = lefts[0].shape[0]
    width = sum(left.shape[1] for left in lefts)
    return pl.pallas_call(
        functools.partial(add_kernel, count),
        out_shape=struct((rows, width)),
        in_specs=[VMEM] * 2 * count,
        out_specs=VMEM,
        compiler_params=pltpu.CompilerParams(vmem_limit_bytes=4 * MIB + 16 * rows * width),
        name="add_rows",
    )(*lefts, *rights)


def weight_kernel(chunk, factor_ref, halves, out, stage, sems):
    half = halves.shape[1]
    low = factor_ref[...]
    high = pltpu.roll(low.astype(jnp.float32), CAP, 1).astype(jnp.bfloat16)
    copies = []
    for factor, base in ((low, 0), (high, half)):
        for start in range(0, half, chunk):
            span = pl.ds(base + start, chunk)
            stage[:, span] = jnp.dot(
                factor, halves[:, pl.ds(start, chunk)], preferred_element_type=jnp.float32
            ).astype(jnp.bfloat16)
            copies.append(
                pltpu.make_async_copy(
                    stage.at[:, span], out.at[:, span], sems.at[len(copies)]
                )
            )
            copies[-1].start()
    for copy in copies:
        copy.wait()


def weight_grad(factor, halves):
    units, rows = factor.shape
    half = halves.shape[1]
    chunk = 512 if half % 512 == 0 else half
    return pl.pallas_call(
        functools.partial(weight_kernel, chunk),
        out_shape=struct((units, 2 * half)),
        in_specs=[VMEM] * 2,
        out_specs=HBM,
        scratch_shapes=[
            pltpu.VMEM((units, 2 * half), jnp.bfloat16),
            pltpu.SemaphoreType.DMA((2 * half // chunk,)),
        ],
        compiler_params=pltpu.CompilerParams(
            vmem_limit_bytes=8 * MIB + 4 * units * half + 8 * units * rows
        ),
        cost_estimate=pl.CostEstimate(
            flops=4 * rows * units * half,
            bytes_accessed=4 * units * half,
            transcendentals=0,
        ),
        name="weight_grad",
    )(factor, halves)


def combine_kernel(first, second, choice_ref, gates_ref, back, token_ref, gate_ref):
    half = token_ref.shape[1] // 2
    choices, tokens = gates_ref.shape
    rows = back[:, :half]
    token_ref[:, :half] = lax.dot_general(
        first[...], rows, CONTRACT_FIRST, preferred_element_type=jnp.float32
    ).astype(jnp.bfloat16)
    token_ref[:, half:] = lax.dot_general(
        second[...], rows, CONTRACT_FIRST, preferred_element_type=jnp.float32
    ).astype(jnp.bfloat16)
    terms = back[:, half : half + tokens].astype(jnp.float32)
    choice = choice_ref[...]
    for k in range(choices):
        chosen = jnp.where(choice == k, terms, 0.0)
        gate = gates_ref[k : k + 1, :].astype(jnp.float32)
        gate_ref[k : k + 1, :] = jnp.sum(chosen, axis=0, keepdims=True) / gate


def combine(table, gates, returned, width):
    choices, tokens = gates.shape
    return pl.pallas_call(
        combine_kernel,
        out_shape=[struct((tokens, width)), struct((choices, tokens), jnp.float32)],
        in_specs=[VMEM] * 5,
        out_specs=[VMEM] * 2,
        compiler_params=pltpu.CompilerParams(vmem_limit_bytes=4 * MIB + 16 * returned.size),
        name="combine",
    )(*table, gates, returned)


def flip(value, axis, bit):
    size = lax.axis_size(axis)
    return lax.ppermute(value, axis, [(i, i ^ bit) for i in range(size)])


def exchange(value):
    n_targets = lax.axis_size("expert")
    rows, width = value.shape
    blocks = value.reshape(n_targets, rows // n_targets, width)
    blocks = lax.all_to_all(blocks, "expert", split_axis=0, concat_axis=0, tiled=True)
    return blocks.reshape(rows, width)


def cross(block, far_bits):
    held = {0: block}
    for bit in far_bits:
        for mask in list(held):
            held[mask | bit] = flip(held[mask], "dp", bit)
    return held


def body(tokens, out_grad, gate_probs, route_ids, w_gate, w_up, w_down):
    n_targets = lax.axis_size("expert")
    n_dp = lax.axis_size("dp")
    width = tokens.shape[1]
    ids, gates = route_ids.T, gate_probs.T
    far_bits = [1 << i for i in range(1, n_dp.bit_length() - 1)]
    weights = (w_gate[0], w_up[0], w_down[0])
    tie = lax.optimization_barrier

    token_rows, grad_rows = dispatch(n_targets, ids, tokens, gates, out_grad)
    ids_after, token_rows = tie((ids, token_rows))
    token_rows = exchange(token_rows)
    grad_rows = exchange(grad_rows)
    token_rows, *table = tie((token_rows, *placement(n_targets, ids_after)))

    token_held = cross(token_rows, far_bits)
    near = sorted(token_held)
    token_near = [token_held[mask] for mask in near]
    token_far = [flip(token_near[0], "dp", 1)]
    grad_rows, *token_near[1:] = tie((grad_rows, *token_near[1:]))
    grad_held = cross(grad_rows, far_bits)
    token_far += [flip(value, "dp", 1) for value in token_near[1:]]
    grad_near = [grad_held[mask] for mask in near]
    token_halves, activated, slope, hidden = forward(
        token_near + token_far, weights[0], weights[1]
    )
    activated, slope, hidden, *grad_near[1:] = tie((activated, slope, hidden, *grad_near[1:]))
    grad_far = [flip(value, "dp", 1) for value in grad_near]

    part, grad_halves, gate_f, up_f, low, high, gate_column = backward(
        grad_near + grad_far, activated, slope, hidden, weights
    )
    middle = width // 4
    received = flip(part, "dp", 1)
    other = far_rows(middle, low, high, gate_column, weights[0], weights[1])
    received, other = tie((received, other))
    left = own_rows(len(near), 0, low, high, gate_column, weights[0], weights[1], received)
    received = flip(other, "dp", 1)
    received, left = tie((received, left))
    right = own_rows(len(near), middle, low, high, gate_column, weights[0], weights[1], received)
    lefts, rights = dict(zip(near, left)), dict(zip(near, right))
    for bit in reversed(far_bits):
        masks = [mask for mask in lefts if mask & bit]
        moved_left = {mask: flip(lefts.pop(mask), "dp", bit) for mask in masks}
        moved_right = {mask: flip(rights.pop(mask), "dp", bit) for mask in masks}
        if bit == far_bits[-1]:
            moved_left, rights, gate_f, up_f, hidden = tie(
                (moved_left, rights, gate_f, up_f, hidden)
            )
            grad_gate = weight_grad(gate_f, token_halves)
            moved_right, grad_gate = tie((moved_right, grad_gate))
        for mask in masks:
            terms = (lefts[mask ^ bit], rights[mask ^ bit]), (moved_left[mask], moved_right[mask])
            if bit == far_bits[0]:
                returned = exchange(add_rows(*terms))
            else:
                lefts[mask ^ bit] = add_rows(terms[0][:1], terms[1][:1])
                rights[mask ^ bit] = add_rows(terms[0][1:], terms[1][1:])
    grad_up = weight_grad(up_f, token_halves)
    grad_down = weight_grad(hidden, grad_halves)
    returned, grad_up, grad_down = tie((returned, grad_up, grad_down))
    token_grad, gate_grad = combine(table, gates, returned, width)
    return (token_grad, gate_grad.T, grad_gate[None], grad_up[None], grad_down[None])


def solution(mesh):
    in_specs = (
        P(("expert", "dp"), None),
        P(("expert", "dp"), None),
        P(("expert", "dp"), None),
        P(("expert", "dp"), None),
        P("expert", "dp", None),
        P("expert", "dp", None),
        P("expert", "dp", None),
    )
    out_specs = (
        P(("expert", "dp"), None),
        P(("expert", "dp"), None),
        P("expert", "dp", None),
        P("expert", "dp", None),
        P("expert", "dp", None),
    )
    return jax.shard_map(body, mesh=mesh, in_specs=in_specs, out_specs=out_specs, check_vma=False)
```

```python
import functools

import jax
import jax.numpy as jnp
from jax import lax
from jax.experimental import pallas as pl
from jax.experimental.pallas import tpu as pltpu
from jax.sharding import PartitionSpec as P

EXPERTS = 128
CAP = 4
BLOCK = 2 * CAP
LANES = 128
MIB = 2**20
COVER = 40

CONTRACT_LAST = (((1,), (1,)), ((), ()))
CONTRACT_FIRST = (((0,), (0,)), ((), ()))

HBM = pl.BlockSpec(memory_space=pltpu.HBM)
VMEM = pl.BlockSpec(memory_space=pltpu.VMEM)


def struct(shape, dtype=jnp.bfloat16):
    return jax.ShapeDtypeStruct(shape, dtype)


def as_bf16(mask):
    return mask.astype(jnp.float32).astype(jnp.bfloat16)


def choice_table(ids, n_targets):
    choices, tokens = ids.shape
    height = n_targets * BLOCK
    per_device = EXPERTS // n_targets
    row = lax.broadcasted_iota(jnp.int32, (height, 1), 0)
    wanted = ((row // BLOCK) ^ lax.axis_index("expert")) * per_device
    slot = row % BLOCK
    matches = [ids[k : k + 1, :] == wanted for k in range(choices)]
    hit = functools.reduce(jnp.logical_or, matches)
    earlier = lax.broadcasted_iota(jnp.int32, (tokens, tokens), 0) < lax.broadcasted_iota(
        jnp.int32, (tokens, tokens), 1
    )
    rank = jnp.dot(as_bf16(hit), as_bf16(earlier), preferred_element_type=jnp.float32)
    rank = rank.astype(jnp.int32)
    first = jnp.logical_and(hit, rank == slot)
    second = jnp.logical_and(hit, rank == slot - CAP)
    return matches, first, second


def pick_rows(first, second, rows_ref):
    half = rows_ref.shape[1] // 2
    low = jnp.dot(first, rows_ref[:, :half], preferred_element_type=jnp.float32)
    high = jnp.dot(second, rows_ref[:, half:], preferred_element_type=jnp.float32)
    return (low + high).astype(jnp.bfloat16)


def dispatch_kernel(n_targets, *refs):
    sources, outs = refs[:4], refs[4 : 4 + n_targets]
    targets, sems = refs[4 + n_targets : -1], refs[-1]
    ids_ref, tokens_ref, gates_ref, grads_ref = targets
    copies = [
        pltpu.make_async_copy(source, target, sems.at[i])
        for i, (source, target) in enumerate(zip(sources, targets))
    ]
    for copy in copies:
        copy.start()
    copies[0].wait()
    matches, first, second = choice_table(ids_ref[...], n_targets)
    copies[1].wait()
    rows = pick_rows(as_bf16(first), as_bf16(second), tokens_ref)
    half = rows.shape[1]
    for k, out in enumerate(outs):
        out[:, :half] = rows[k * BLOCK : (k + 1) * BLOCK]
    copies[2].wait()
    gates = gates_ref[...].astype(jnp.float32)
    scale = jnp.zeros(first.shape, jnp.float32)
    for k, match in enumerate(matches):
        scale = scale + jnp.where(match, gates[k : k + 1, :], 0.0)
    first = jnp.where(first, scale, 0.0).astype(jnp.bfloat16)
    second = jnp.where(second, scale, 0.0).astype(jnp.bfloat16)
    copies[3].wait()
    rows = pick_rows(first, second, grads_ref)
    for k, out in enumerate(outs):
        out[:, half:] = rows[k * BLOCK : (k + 1) * BLOCK]


def dispatch(n_targets, ids, tokens, gates, out_grad):
    arrays = (ids, tokens, gates, out_grad)
    return pl.pallas_call(
        functools.partial(dispatch_kernel, n_targets),
        out_shape=[struct((BLOCK, tokens.shape[1]))] * n_targets,
        in_specs=[HBM] * 4,
        out_specs=[VMEM] * n_targets,
        scratch_shapes=[pltpu.VMEM(a.shape, a.dtype) for a in arrays]
        + [pltpu.SemaphoreType.DMA((4,))],
        compiler_params=pltpu.CompilerParams(vmem_limit_bytes=60 * MIB),
        name="dispatch",
    )(*arrays)


def placement_kernel(n_targets, ids_ref, first_ref, second_ref, choice_ref):
    matches, first, second = choice_table(ids_ref[...], n_targets)
    first_ref[...] = as_bf16(first)
    second_ref[...] = as_bf16(second)
    choice = jnp.full(first.shape, -1, jnp.int32)
    for k, match in enumerate(matches):
        choice = jnp.where(jnp.logical_and(match, first), k, choice)
    choice_ref[...] = choice


def placement(n_targets, ids):
    table = (n_targets * BLOCK, ids.shape[1])
    return pl.pallas_call(
        functools.partial(placement_kernel, n_targets),
        out_shape=[struct(table), struct(table), struct(table, jnp.int32)],
        in_specs=[VMEM],
        out_specs=[VMEM] * 3,
        compiler_params=pltpu.CompilerParams(vmem_limit_bytes=4 * MIB),
        cost_estimate=pl.CostEstimate(
            flops=COVER * 10**9, bytes_accessed=COVER * 10**6, transcendentals=0
        ),
        name="placement",
    )(ids)


def pack_kernel(count, *refs):
    blocks, (token_out, grad_out) = refs[:count], refs[count:]
    half = token_out.shape[1]
    for k in range(0, count, 2):
        pair = jnp.concatenate([blocks[k][...], blocks[k + 1][...]], axis=0)
        span = pl.ds(k * BLOCK, 2 * BLOCK)
        token_out[span, :] = pair[:, :half]
        grad_out[span, :] = pair[:, half:]


def pack(blocks):
    count = len(blocks)
    shape = (count * BLOCK, blocks[0].shape[1] // 2)
    return pl.pallas_call(
        functools.partial(pack_kernel, count),
        out_shape=[struct(shape)] * 2,
        in_specs=[VMEM] * count,
        out_specs=[VMEM] * 2,
        compiler_params=pltpu.CompilerParams(
            vmem_limit_bytes=4 * MIB + 16 * shape[0] * shape[1]
        ),
        name="pack",
    )(*blocks)


def gather_pieces(pieces, out):
    block = pieces[0].shape[0]
    for i, piece in enumerate(pieces):
        out[pl.ds(i * block, block), :] = piece[...]


def project(weight, halves):
    half = halves.shape[1]
    rows = halves.shape[0]
    low = lax.dot_general(
        weight[:, :half], halves[...], CONTRACT_LAST, preferred_element_type=jnp.float32
    )
    high = lax.dot_general(
        weight[:, half:], halves[...], CONTRACT_LAST, preferred_element_type=jnp.float32
    )
    return low + pltpu.roll(high, rows - CAP, 1)


def forward_kernel(count, *refs):
    pieces = refs[:count]
    gate_w, up_w, halves, activated_out, slope_out, hidden_out = refs[count:]
    gather_pieces(pieces, halves)
    pre_gate, pre_up = project(gate_w, halves), project(up_w, halves)
    is_slot = lax.broadcasted_iota(jnp.int32, (1, halves.shape[0]), 1) % BLOCK < CAP
    squash = 1.0 / (1.0 + jnp.exp(-pre_gate))
    activated = jnp.where(is_slot, pre_gate * squash, 0.0)
    slope = pre_up * squash * (1.0 + pre_gate * (1.0 - squash))
    activated_out[...] = activated
    slope_out[...] = jnp.where(is_slot, slope, 0.0)
    hidden_out[...] = (activated * pre_up).astype(jnp.bfloat16)


def forward(pieces, gate_w, up_w):
    count = len(pieces)
    units, width = gate_w.shape
    rows = count * pieces[0].shape[0]
    kept = (units, rows)
    return pl.pallas_call(
        functools.partial(forward_kernel, count),
        out_shape=[
            struct((rows, width // 2)),
            struct(kept, jnp.float32),
            struct(kept, jnp.float32),
            struct(kept),
        ],
        in_specs=[VMEM] * (count + 2),
        out_specs=[VMEM] * 4,
        compiler_params=pltpu.CompilerParams(
            vmem_limit_bytes=4 * MIB + rows * width + 40 * rows * units
        ),
        cost_estimate=pl.CostEstimate(
            flops=4 * rows * units * width,
            bytes_accessed=4 * units * width,
            transcendentals=rows * units,
        ),
        name="forward",
    )(*pieces, gate_w, up_w)


def row_grads(low, high, gate_w, up_w, received, parts, start, size):
    units, width = gate_w.shape
    block = parts[0].shape[0]
    chunk = 512 if size % 512 == 0 else size

    @pl.loop(0, size // chunk)
    def _(step):
        offset = pl.multiple_of(step * chunk, chunk)
        near = pl.ds(pl.multiple_of(start + offset, chunk), chunk)
        far = pl.ds(pl.multiple_of(width // 2 + start + offset, chunk), chunk)
        here = pl.ds(offset, chunk)
        total = None
        for rows, columns in ((low, near), (high, far)):
            for i, weight in enumerate((gate_w, up_w)):
                term = jnp.dot(
                    rows[:, i * units : (i + 1) * units],
                    weight[:, columns],
                    preferred_element_type=jnp.float32,
                )
                total = term if total is None else total + term
        if received is not None:
            total = total + received[:, here].astype(jnp.float32)
        total = total.astype(jnp.bfloat16)
        for i, part in enumerate(parts):
            part[:, here] = total[i * block : (i + 1) * block]


def backward_kernel(count, *refs):
    pieces = refs[:count]
    activated, slope, hidden, gate_w, up_w, down_w = refs[count : count + 6]
    part, halves, gate_out, up_out, low_out, high_out, gates_out = refs[count + 6 :]
    rows = halves.shape[0]
    mine = rows // 2
    gather_pieces(pieces, halves)
    back = project(down_w, halves)
    gate_terms = jnp.sum(hidden[...].astype(jnp.float32) * back, axis=0, keepdims=True)
    up_pre = back * activated[...]
    gate_pre = back * slope[...]
    both = jnp.concatenate([gate_pre, up_pre], axis=0)
    low = both.T.astype(jnp.bfloat16)
    high = pltpu.roll(both, CAP, 1).T.astype(jnp.bfloat16)
    gate_column = jnp.broadcast_to(gate_terms, (LANES, rows)).T.astype(jnp.bfloat16)
    row_grads(low[mine:], high[mine:], gate_w, up_w, None, (part,), 0, part.shape[1])
    low_out[...] = low
    high_out[...] = high
    gates_out[...] = gate_column
    gate_out[...] = gate_pre.astype(jnp.bfloat16)
    up_out[...] = up_pre.astype(jnp.bfloat16)


def backward(pieces, activated, slope, hidden, weights):
    count = len(pieces)
    units, width = weights[0].shape
    rows = count * pieces[0].shape[0]
    mine = rows // 2
    shapes = [
        (mine, width // 4),
        (rows, width // 2),
        (units, rows),
        (units, rows),
        (rows, 2 * units),
        (rows, 2 * units),
        (rows, LANES),
    ]
    return pl.pallas_call(
        functools.partial(backward_kernel, count),
        out_shape=[struct(shape) for shape in shapes],
        in_specs=[VMEM] * (count + 6),
        out_specs=[VMEM] * len(shapes),
        compiler_params=pltpu.CompilerParams(
            vmem_limit_bytes=4 * MIB
            + 2 * sum(height * across for height, across in shapes)
            + 40 * rows * units
        ),
        cost_estimate=pl.CostEstimate(
            flops=3 * rows * units * width,
            bytes_accessed=2 * units * width,
            transcendentals=0,
        ),
        name="backward",
    )(*pieces, activated, slope, hidden, *weights)


def far_kernel(start, low, high, gates, gate_w, up_w, part):
    span = pl.ds(part.shape[0], part.shape[0])
    size = part.shape[1] - LANES
    part[:, size:] = gates[span, :]
    row_grads(low[span, :], high[span, :], gate_w, up_w, None, (part,), start, size)


def far_rows(start, low, high, gates, gate_w, up_w):
    rows, width = low.shape[0], gate_w.shape[1]
    size = width // 2 - start
    return pl.pallas_call(
        functools.partial(far_kernel, start),
        out_shape=struct((rows // 2, size + LANES)),
        in_specs=[VMEM] * 5,
        out_specs=VMEM,
        compiler_params=pltpu.CompilerParams(vmem_limit_bytes=8 * MIB + 4 * rows * width),
        cost_estimate=pl.CostEstimate(
            flops=4 * rows * low.shape[1] * size, bytes_accessed=4 * rows * size, transcendentals=0
        ),
        name="far_rows",
    )(low, high, gates, gate_w, up_w)


def own_kernel(start, extra, low, high, gates, gate_w, up_w, received, *parts):
    rows, size = received.shape
    size -= extra
    block = parts[0].shape[0]
    if extra:
        for i, part in enumerate(parts):
            span = pl.ds(i * block, block)
            part[:, size:] = (
                gates[span, :].astype(jnp.float32) + received[span, size:].astype(jnp.float32)
            ).astype(jnp.bfloat16)
    row_grads(low[:rows, :], high[:rows, :], gate_w, up_w, received, parts, start, size)


def own_rows(count, start, low, high, gates, gate_w, up_w, received):
    rows, width = received.shape
    return pl.pallas_call(
        functools.partial(own_kernel, start, LANES if start else 0),
        out_shape=[struct((rows // count, width))] * count,
        in_specs=[VMEM] * 6,
        out_specs=[VMEM] * count,
        compiler_params=pltpu.CompilerParams(vmem_limit_bytes=8 * MIB + 16 * rows * width),
        cost_estimate=pl.CostEstimate(
            flops=4 * rows * low.shape[1] * width,
            bytes_accessed=4 * rows * width,
            transcendentals=0,
        ),
        name="own_rows",
    )(low, high, gates, gate_w, up_w, received)


def add_kernel(count, *refs):
    lefts, rights, outs = refs[:count], refs[count : 2 * count], refs[2 * count :]
    block = outs[0].shape[0]
    base = 0
    for left, right in zip(lefts, rights):
        total = (left[...].astype(jnp.float32) + right[...].astype(jnp.float32)).astype(
            jnp.bfloat16
        )
        for i, out in enumerate(outs):
            out[:, base : base + left.shape[1]] = total[i * block : (i + 1) * block]
        base += left.shape[1]


def add_rows(lefts, rights, blocks=1):
    count = len(lefts)
    rows = lefts[0].shape[0]
    width = sum(left.shape[1] for left in lefts)
    return pl.pallas_call(
        functools.partial(add_kernel, count),
        out_shape=[struct((rows // blocks, width))] * blocks,
        in_specs=[VMEM] * 2 * count,
        out_specs=[VMEM] * blocks,
        compiler_params=pltpu.CompilerParams(vmem_limit_bytes=4 * MIB + 16 * rows * width),
        name="add_rows",
    )(*lefts, *rights)


def weight_kernel(chunk, *refs):
    gate_f, up_f, down_f, token_halves, grad_halves = refs[:5]
    outs, stages, sems = refs[5:8], refs[8:11], refs[11]
    half = token_halves.shape[1]
    jobs = ((gate_f, token_halves), (up_f, token_halves), (down_f, grad_halves))
    factors = []
    for factor, _ in jobs:
        low = factor[...]
        high = pltpu.roll(low.astype(jnp.float32), CAP, 1).astype(jnp.bfloat16)
        factors.append((low, high))
    copies = []
    for start in range(0, half, chunk):
        for (_, halves), pair, out, stage in zip(jobs, factors, outs, stages):
            for factor, base in zip(pair, (0, half)):
                span = pl.ds(base + start, chunk)
                stage[:, span] = jnp.dot(
                    factor, halves[:, pl.ds(start, chunk)], preferred_element_type=jnp.float32
                ).astype(jnp.bfloat16)
                copy = pltpu.make_async_copy(
                    stage.at[:, span], out.at[:, span], sems.at[len(copies)]
                )
                copy.start()
                copies.append(copy)
    for copy in copies:
        copy.wait()


def weight_grads(factors, token_halves, grad_halves):
    units, rows = factors[0].shape
    half = token_halves.shape[1]
    chunk = 512 if half % 512 == 0 else half
    shape = (units, 2 * half)
    return pl.pallas_call(
        functools.partial(weight_kernel, chunk),
        out_shape=[struct(shape)] * 3,
        in_specs=[VMEM] * 5,
        out_specs=[HBM] * 3,
        scratch_shapes=[pltpu.VMEM(shape, jnp.bfloat16)] * 3
        + [pltpu.SemaphoreType.DMA((6 * half // chunk,))],
        compiler_params=pltpu.CompilerParams(
            vmem_limit_bytes=6 * MIB + 12 * units * half + 16 * units * rows
        ),
        cost_estimate=pl.CostEstimate(
            flops=12 * rows * units * half,
            bytes_accessed=12 * units * half,
            transcendentals=0,
        ),
        name="weight_grads",
    )(*factors, token_halves, grad_halves)


def combine_kernel(n_targets, first, second, choice_ref, gates_ref, *refs):
    blocks, (token_ref, gate_ref) = refs[:n_targets], refs[n_targets:]
    order = offsets(n_targets)
    back = jnp.concatenate([blocks[order.index(k)][...] for k in range(n_targets)], axis=0)
    half = token_ref.shape[1] // 2
    choices, tokens = gates_ref.shape
    rows = back[:, :half]
    token_ref[:, :half] = lax.dot_general(
        first[...], rows, CONTRACT_FIRST, preferred_element_type=jnp.float32
    ).astype(jnp.bfloat16)
    token_ref[:, half:] = lax.dot_general(
        second[...], rows, CONTRACT_FIRST, preferred_element_type=jnp.float32
    ).astype(jnp.bfloat16)
    terms = back[:, half : half + tokens].astype(jnp.float32)
    choice = choice_ref[...]
    for k in range(choices):
        chosen = jnp.where(choice == k, terms, 0.0)
        gate = gates_ref[k : k + 1, :].astype(jnp.float32)
        gate_ref[k : k + 1, :] = jnp.sum(chosen, axis=0, keepdims=True) / gate


def combine(table, gates, blocks, width):
    n_targets = len(blocks)
    choices, tokens = gates.shape
    return pl.pallas_call(
        functools.partial(combine_kernel, n_targets),
        out_shape=[struct((tokens, width)), struct((choices, tokens), jnp.float32)],
        in_specs=[VMEM] * (4 + n_targets),
        out_specs=[VMEM] * 2,
        compiler_params=pltpu.CompilerParams(
            vmem_limit_bytes=4 * MIB + 16 * n_targets * BLOCK * width
        ),
        name="combine",
    )(*table, gates, *blocks)


def flip(value, axis, bit):
    size = lax.axis_size(axis)
    return lax.ppermute(value, axis, [(i, i ^ bit) for i in range(size)])


def offsets(count):
    near, far = list(range(1, count // 2)), list(range(count // 2, count))
    return [0] + near[:1] + far + near[1:]


def exchange(blocks):
    order = offsets(len(blocks))
    return [flip(block, "expert", k) if k else block for k, block in zip(order, blocks)]


def cross(block, far_bits):
    held = {0: block}
    for bit in far_bits:
        for mask in list(held):
            held[mask | bit] = flip(held[mask], "dp", bit)
    return held


def body(tokens, out_grad, gate_probs, route_ids, w_gate, w_up, w_down):
    n_targets = lax.axis_size("expert")
    n_dp = lax.axis_size("dp")
    width = tokens.shape[1]
    ids, gates = route_ids.T, gate_probs.T
    far_bits = [1 << i for i in range(1, n_dp.bit_length() - 1)]
    weights = (w_gate[0], w_up[0], w_down[0])
    tie = lax.optimization_barrier

    sent = dispatch(n_targets, ids, tokens, gates, out_grad)
    ids_after, *sent = tie((ids, *sent))
    arrived = exchange([sent[k] for k in offsets(n_targets)])
    arrived[0], *table = tie((arrived[0], *placement(n_targets, ids_after)))
    token_rows, grad_rows = pack(arrived)

    token_held = cross(token_rows, far_bits)
    near = sorted(token_held)
    token_near = [token_held[mask] for mask in near]
    token_far = [flip(value, "dp", 1) for value in token_near]
    grad_held = cross(grad_rows, far_bits)
    grad_near = [grad_held[mask] for mask in near]
    token_halves, activated, slope, hidden = forward(
        token_near + token_far, weights[0], weights[1]
    )
    activated, slope, hidden, *grad_near[1:] = tie((activated, slope, hidden, *grad_near[1:]))
    grad_far = [flip(value, "dp", 1) for value in grad_near]

    part, grad_halves, gate_f, up_f, low, high, gate_column = backward(
        grad_near + grad_far, activated, slope, hidden, weights
    )
    middle = width // 4
    received = flip(part, "dp", 1)
    other = far_rows(middle, low, high, gate_column, weights[0], weights[1])
    received, other = tie((received, other))
    left = own_rows(len(near), 0, low, high, gate_column, weights[0], weights[1], received)
    received = flip(other, "dp", 1)
    received, left = tie((received, left))
    right = own_rows(len(near), middle, low, high, gate_column, weights[0], weights[1], received)
    lefts, rights = dict(zip(near, left)), dict(zip(near, right))
    for bit in reversed(far_bits):
        masks = [mask for mask in lefts if mask & bit]
        moved_left = {mask: flip(lefts.pop(mask), "dp", bit) for mask in masks}
        moved_right = {mask: flip(rights.pop(mask), "dp", bit) for mask in masks}
        if bit == far_bits[-1]:
            moved_left, rights, gate_f, up_f, hidden = tie(
                (moved_left, rights, gate_f, up_f, hidden)
            )
            grads = weight_grads((gate_f, up_f, hidden), token_halves, grad_halves)
            moved_right, grads = tie((moved_right, grads))
        for mask in masks:
            terms = (lefts[mask ^ bit], rights[mask ^ bit]), (moved_left[mask], moved_right[mask])
            if bit == far_bits[0]:
                returned = exchange(add_rows(*terms, n_targets))
            else:
                lefts[mask ^ bit] = add_rows(terms[0][:1], terms[1][:1])[0]
                rights[mask ^ bit] = add_rows(terms[0][1:], terms[1][1:])[0]
    token_grad, gate_grad = combine(table, gates, returned, width)
    return (token_grad, gate_grad.T, *(grad[None] for grad in grads))


def solution(mesh):
    in_specs = (
        P(("expert", "dp"), None),
        P(("expert", "dp"), None),
        P(("expert", "dp"), None),
        P(("expert", "dp"), None),
        P("expert", "dp", None),
        P("expert", "dp", None),
        P("expert", "dp", None),
    )
    out_specs = (
        P(("expert", "dp"), None),
        P(("expert", "dp"), None),
        P("expert", "dp", None),
        P("expert", "dp", None),
        P("expert", "dp", None),
    )
    return jax.shard_map(body, mesh=mesh, in_specs=in_specs, out_specs=out_specs, check_vma=False)
```

```python
import functools

import jax
import jax.numpy as jnp
from jax import lax
from jax.experimental import pallas as pl
from jax.experimental.pallas import tpu as pltpu
from jax.sharding import PartitionSpec as P

EXPERTS = 128
CAP = 4
BLOCK = 2 * CAP
LANES = 128
MIB = 2**20
COVER = 40

CONTRACT_LAST = (((1,), (1,)), ((), ()))
CONTRACT_FIRST = (((0,), (0,)), ((), ()))

HBM = pl.BlockSpec(memory_space=pltpu.HBM)
VMEM = pl.BlockSpec(memory_space=pltpu.VMEM)

LIGHT = pl.CostEstimate(flops=10**6, bytes_accessed=10**4, transcendentals=0)


def struct(shape, dtype=jnp.bfloat16):
    return jax.ShapeDtypeStruct(shape, dtype)


def as_bf16(mask):
    return mask.astype(jnp.float32).astype(jnp.bfloat16)


def choice_table(ids, n_targets):
    choices, tokens = ids.shape
    height = n_targets * BLOCK
    per_device = EXPERTS // n_targets
    row = lax.broadcasted_iota(jnp.int32, (height, 1), 0)
    wanted = ((row // BLOCK) ^ lax.axis_index("expert")) * per_device
    slot = row % BLOCK
    matches = [ids[k : k + 1, :] == wanted for k in range(choices)]
    hit = functools.reduce(jnp.logical_or, matches)
    earlier = lax.broadcasted_iota(jnp.int32, (tokens, tokens), 0) < lax.broadcasted_iota(
        jnp.int32, (tokens, tokens), 1
    )
    rank = jnp.dot(as_bf16(hit), as_bf16(earlier), preferred_element_type=jnp.float32)
    rank = rank.astype(jnp.int32)
    first = jnp.logical_and(hit, rank == slot)
    second = jnp.logical_and(hit, rank == slot - CAP)
    return matches, first, second


def pick_rows(first, second, rows_ref):
    half = rows_ref.shape[1] // 2
    low = jnp.dot(first, rows_ref[:, :half], preferred_element_type=jnp.float32)
    high = jnp.dot(second, rows_ref[:, half:], preferred_element_type=jnp.float32)
    return (low + high).astype(jnp.bfloat16)


def dispatch_kernel(n_targets, *refs):
    sources, outs = refs[:4], refs[4 : 4 + n_targets]
    targets, sems = refs[4 + n_targets : -1], refs[-1]
    ids_ref, tokens_ref, gates_ref, grads_ref = targets
    copies = [
        pltpu.make_async_copy(source, target, sems.at[i])
        for i, (source, target) in enumerate(zip(sources, targets))
    ]
    for copy in copies:
        copy.start()
    copies[0].wait()
    matches, first, second = choice_table(ids_ref[...], n_targets)
    copies[1].wait()
    rows = pick_rows(as_bf16(first), as_bf16(second), tokens_ref)
    half = rows.shape[1]
    for k, out in enumerate(outs):
        out[:, :half] = rows[k * BLOCK : (k + 1) * BLOCK]
    copies[2].wait()
    gates = gates_ref[...].astype(jnp.float32)
    scale = jnp.zeros(first.shape, jnp.float32)
    for k, match in enumerate(matches):
        scale = scale + jnp.where(match, gates[k : k + 1, :], 0.0)
    first = jnp.where(first, scale, 0.0).astype(jnp.bfloat16)
    second = jnp.where(second, scale, 0.0).astype(jnp.bfloat16)
    copies[3].wait()
    rows = pick_rows(first, second, grads_ref)
    for k, out in enumerate(outs):
        out[:, half:] = rows[k * BLOCK : (k + 1) * BLOCK]


def dispatch(n_targets, ids, tokens, gates, out_grad):
    arrays = (ids, tokens, gates, out_grad)
    return pl.pallas_call(
        functools.partial(dispatch_kernel, n_targets),
        out_shape=[struct((BLOCK, tokens.shape[1]))] * n_targets,
        in_specs=[HBM] * 4,
        out_specs=[VMEM] * n_targets,
        scratch_shapes=[pltpu.VMEM(a.shape, a.dtype) for a in arrays]
        + [pltpu.SemaphoreType.DMA((4,))],
        compiler_params=pltpu.CompilerParams(vmem_limit_bytes=60 * MIB),
        name="dispatch",
    )(*arrays)


def placement_kernel(n_targets, ids_ref, first_ref, second_ref, choice_ref):
    matches, first, second = choice_table(ids_ref[...], n_targets)
    first_ref[...] = as_bf16(first)
    second_ref[...] = as_bf16(second)
    choice = jnp.full(first.shape, -1, jnp.int32)
    for k, match in enumerate(matches):
        choice = jnp.where(jnp.logical_and(match, first), k, choice)
    choice_ref[...] = choice


def placement(n_targets, ids):
    table = (n_targets * BLOCK, ids.shape[1])
    return pl.pallas_call(
        functools.partial(placement_kernel, n_targets),
        out_shape=[struct(table), struct(table), struct(table, jnp.int32)],
        in_specs=[VMEM],
        out_specs=[VMEM] * 3,
        compiler_params=pltpu.CompilerParams(vmem_limit_bytes=4 * MIB),
        cost_estimate=pl.CostEstimate(
            flops=COVER * 10**9, bytes_accessed=COVER * 10**6, transcendentals=0
        ),
        name="placement",
    )(ids)


def pack_kernel(count, *refs):
    blocks, out = refs[:count], refs[count]
    for k in range(0, count, 2):
        out[pl.ds(k * BLOCK, 2 * BLOCK), :] = jnp.concatenate(
            [blocks[k][...], blocks[k + 1][...]], axis=0
        )


def pack(blocks):
    count = len(blocks)
    rows, width = count * BLOCK, blocks[0].shape[1]
    return pl.pallas_call(
        functools.partial(pack_kernel, count),
        out_shape=struct((rows, width)),
        in_specs=[VMEM] * count,
        out_specs=VMEM,
        compiler_params=pltpu.CompilerParams(vmem_limit_bytes=4 * MIB + 8 * rows * width),
        name="pack",
    )(*blocks)


def gather_pieces(pieces, start, out):
    base = 0
    for piece in pieces:
        rows = piece.shape[0]
        out[pl.ds(base, rows), :] = piece[:, start : start + out.shape[1]]
        base += rows


def project(weight, halves):
    half = halves.shape[1]
    rows = halves.shape[0]
    low = lax.dot_general(
        weight[:, :half], halves[...], CONTRACT_LAST, preferred_element_type=jnp.float32
    )
    high = lax.dot_general(
        weight[:, half:], halves[...], CONTRACT_LAST, preferred_element_type=jnp.float32
    )
    return low + pltpu.roll(high, rows - CAP, 1)


def forward_kernel(count, *refs):
    pieces = refs[:count]
    gate_w, up_w, halves, activated_out, slope_out, hidden_out = refs[count:]
    gather_pieces(pieces, 0, halves)
    pre_gate, pre_up = project(gate_w, halves), project(up_w, halves)
    is_slot = lax.broadcasted_iota(jnp.int32, (1, halves.shape[0]), 1) % BLOCK < CAP
    squash = 1.0 / (1.0 + jnp.exp(-pre_gate))
    activated = jnp.where(is_slot, pre_gate * squash, 0.0)
    slope = pre_up * squash * (1.0 + pre_gate * (1.0 - squash))
    activated_out[...] = activated
    slope_out[...] = jnp.where(is_slot, slope, 0.0)
    hidden_out[...] = (activated * pre_up).astype(jnp.bfloat16)


def forward(pieces, gate_w, up_w):
    count = len(pieces)
    units, width = gate_w.shape
    rows = sum(piece.shape[0] for piece in pieces)
    kept = (units, rows)
    return pl.pallas_call(
        functools.partial(forward_kernel, count),
        out_shape=[
            struct((rows, width // 2)),
            struct(kept, jnp.float32),
            struct(kept, jnp.float32),
            struct(kept),
        ],
        in_specs=[VMEM] * (count + 2),
        out_specs=[VMEM] * 4,
        compiler_params=pltpu.CompilerParams(
            vmem_limit_bytes=4 * MIB + rows * width + 40 * rows * units
        ),
        cost_estimate=LIGHT,
        name="forward",
    )(*pieces, gate_w, up_w)


def row_grads(low, high, gate_w, up_w, received, parts, start, size):
    units, width = gate_w.shape
    block = parts[0].shape[0]
    chunk = 512 if size % 512 == 0 else size

    @pl.loop(0, size // chunk)
    def _(step):
        offset = pl.multiple_of(step * chunk, chunk)
        near = pl.ds(pl.multiple_of(start + offset, chunk), chunk)
        far = pl.ds(pl.multiple_of(width // 2 + start + offset, chunk), chunk)
        here = pl.ds(offset, chunk)
        total = None
        for rows, columns in ((low, near), (high, far)):
            for i, weight in enumerate((gate_w, up_w)):
                term = jnp.dot(
                    rows[:, i * units : (i + 1) * units],
                    weight[:, columns],
                    preferred_element_type=jnp.float32,
                )
                total = term if total is None else total + term
        if received is not None:
            total = total + received[:, here].astype(jnp.float32)
        total = total.astype(jnp.bfloat16)
        for i, part in enumerate(parts):
            part[:, here] = total[i * block : (i + 1) * block]


def backward_kernel(count, *refs):
    pieces = refs[:count]
    activated, slope, hidden, gate_w, up_w, down_w = refs[count : count + 6]
    part, halves, gate_out, up_out, low_out, high_out, gates_out = refs[count + 6 :]
    rows = halves.shape[0]
    mine = rows // 2
    gather_pieces(pieces, halves.shape[1], halves)
    back = project(down_w, halves)
    gate_terms = jnp.sum(hidden[...].astype(jnp.float32) * back, axis=0, keepdims=True)
    up_pre = back * activated[...]
    gate_pre = back * slope[...]
    both = jnp.concatenate([gate_pre, up_pre], axis=0)
    low = both.T.astype(jnp.bfloat16)
    high = pltpu.roll(both, CAP, 1).T.astype(jnp.bfloat16)
    gate_column = jnp.broadcast_to(gate_terms, (LANES, rows)).T.astype(jnp.bfloat16)
    row_grads(low[mine:], high[mine:], gate_w, up_w, None, (part,), 0, part.shape[1])
    low_out[...] = low
    high_out[...] = high
    gates_out[...] = gate_column
    gate_out[...] = gate_pre.astype(jnp.bfloat16)
    up_out[...] = up_pre.astype(jnp.bfloat16)


def backward(pieces, activated, slope, hidden, weights):
    count = len(pieces)
    units, width = weights[0].shape
    rows = sum(piece.shape[0] for piece in pieces)
    mine = rows // 2
    shapes = [
        (mine, width // 4),
        (rows, width // 2),
        (units, rows),
        (units, rows),
        (rows, 2 * units),
        (rows, 2 * units),
        (rows, LANES),
    ]
    return pl.pallas_call(
        functools.partial(backward_kernel, count),
        out_shape=[struct(shape) for shape in shapes],
        in_specs=[VMEM] * (count + 6),
        out_specs=[VMEM] * len(shapes),
        compiler_params=pltpu.CompilerParams(
            vmem_limit_bytes=4 * MIB
            + 2 * sum(height * across for height, across in shapes)
            + 40 * rows * units
        ),
        cost_estimate=LIGHT,
        name="backward",
    )(*pieces, activated, slope, hidden, *weights)


def far_kernel(start, low, high, gates, gate_w, up_w, part):
    span = pl.ds(part.shape[0], part.shape[0])
    size = part.shape[1] - LANES
    part[:, size:] = gates[span, :]
    row_grads(low[span, :], high[span, :], gate_w, up_w, None, (part,), start, size)


def far_rows(start, low, high, gates, gate_w, up_w):
    rows, width = low.shape[0], gate_w.shape[1]
    size = width // 2 - start
    return pl.pallas_call(
        functools.partial(far_kernel, start),
        out_shape=struct((rows // 2, size + LANES)),
        in_specs=[VMEM] * 5,
        out_specs=VMEM,
        compiler_params=pltpu.CompilerParams(vmem_limit_bytes=8 * MIB + 4 * rows * width),
        cost_estimate=LIGHT,
        name="far_rows",
    )(low, high, gates, gate_w, up_w)


def own_kernel(start, extra, low, high, gates, gate_w, up_w, received, *parts):
    rows, size = received.shape
    size -= extra
    block = parts[0].shape[0]
    if extra:
        for i, part in enumerate(parts):
            span = pl.ds(i * block, block)
            part[:, size:] = (
                gates[span, :].astype(jnp.float32) + received[span, size:].astype(jnp.float32)
            ).astype(jnp.bfloat16)
    row_grads(low[:rows, :], high[:rows, :], gate_w, up_w, received, parts, start, size)


def own_rows(count, start, low, high, gates, gate_w, up_w, received):
    rows, width = received.shape
    return pl.pallas_call(
        functools.partial(own_kernel, start, LANES if start else 0),
        out_shape=[struct((rows // count, width))] * count,
        in_specs=[VMEM] * 6,
        out_specs=[VMEM] * count,
        compiler_params=pltpu.CompilerParams(vmem_limit_bytes=8 * MIB + 16 * rows * width),
        cost_estimate=LIGHT,
        name="own_rows",
    )(low, high, gates, gate_w, up_w, received)


def add_kernel(count, *refs):
    lefts, rights, outs = refs[:count], refs[count : 2 * count], refs[2 * count :]
    block = outs[0].shape[0]
    base = 0
    for left, right in zip(lefts, rights):
        total = (left[...].astype(jnp.float32) + right[...].astype(jnp.float32)).astype(
            jnp.bfloat16
        )
        for i, out in enumerate(outs):
            out[:, base : base + left.shape[1]] = total[i * block : (i + 1) * block]
        base += left.shape[1]


def add_rows(lefts, rights, blocks=1):
    count = len(lefts)
    rows = lefts[0].shape[0]
    width = sum(left.shape[1] for left in lefts)
    return pl.pallas_call(
        functools.partial(add_kernel, count),
        out_shape=[struct((rows // blocks, width))] * blocks,
        in_specs=[VMEM] * 2 * count,
        out_specs=[VMEM] * blocks,
        compiler_params=pltpu.CompilerParams(vmem_limit_bytes=4 * MIB + 16 * rows * width),
        name="add_rows",
    )(*lefts, *rights)


def weight_kernel(chunk, *refs):
    gate_f, up_f, down_f, token_halves, grad_halves = refs[:5]
    outs, stages, sems = refs[5:8], refs[8:11], refs[11]
    half = token_halves.shape[1]
    jobs = ((gate_f, token_halves), (up_f, token_halves), (down_f, grad_halves))
    factors = []
    for factor, _ in jobs:
        low = factor[...]
        high = pltpu.roll(low.astype(jnp.float32), CAP, 1).astype(jnp.bfloat16)
        factors.append((low, high))
    copies = []
    for start in range(0, half, chunk):
        for (_, halves), pair, out, stage in zip(jobs, factors, outs, stages):
            for factor, base in zip(pair, (0, half)):
                span = pl.ds(base + start, chunk)
                stage[:, span] = jnp.dot(
                    factor, halves[:, pl.ds(start, chunk)], preferred_element_type=jnp.float32
                ).astype(jnp.bfloat16)
                copy = pltpu.make_async_copy(
                    stage.at[:, span], out.at[:, span], sems.at[len(copies)]
                )
                copy.start()
                copies.append(copy)
    for copy in copies:
        copy.wait()


def weight_grads(factors, token_halves, grad_halves):
    units, rows = factors[0].shape
    half = token_halves.shape[1]
    chunk = 512 if half % 512 == 0 else half
    shape = (units, 2 * half)
    return pl.pallas_call(
        functools.partial(weight_kernel, chunk),
        out_shape=[struct(shape)] * 3,
        in_specs=[VMEM] * 5,
        out_specs=[HBM] * 3,
        scratch_shapes=[pltpu.VMEM(shape, jnp.bfloat16)] * 3
        + [pltpu.SemaphoreType.DMA((6 * half // chunk,))],
        compiler_params=pltpu.CompilerParams(
            vmem_limit_bytes=6 * MIB + 12 * units * half + 16 * units * rows
        ),
        cost_estimate=LIGHT,
        name="weight_grads",
    )(*factors, token_halves, grad_halves)


def combine_kernel(n_targets, first, second, choice_ref, gates_ref, *refs):
    blocks, (token_ref, gate_ref) = refs[:n_targets], refs[n_targets:]
    order = offsets(n_targets)
    back = jnp.concatenate([blocks[order.index(k)][...] for k in range(n_targets)], axis=0)
    half = token_ref.shape[1] // 2
    choices, tokens = gates_ref.shape
    rows = back[:, :half]
    token_ref[:, :half] = lax.dot_general(
        first[...], rows, CONTRACT_FIRST, preferred_element_type=jnp.float32
    ).astype(jnp.bfloat16)
    token_ref[:, half:] = lax.dot_general(
        second[...], rows, CONTRACT_FIRST, preferred_element_type=jnp.float32
    ).astype(jnp.bfloat16)
    terms = back[:, half : half + tokens].astype(jnp.float32)
    choice = choice_ref[...]
    for k in range(choices):
        chosen = jnp.where(choice == k, terms, 0.0)
        gate = gates_ref[k : k + 1, :].astype(jnp.float32)
        gate_ref[k : k + 1, :] = jnp.sum(chosen, axis=0, keepdims=True) / gate


def combine(table, gates, blocks, width):
    n_targets = len(blocks)
    choices, tokens = gates.shape
    return pl.pallas_call(
        functools.partial(combine_kernel, n_targets),
        out_shape=[struct((tokens, width)), struct((choices, tokens), jnp.float32)],
        in_specs=[VMEM] * (4 + n_targets),
        out_specs=[VMEM] * 2,
        compiler_params=pltpu.CompilerParams(
            vmem_limit_bytes=4 * MIB + 16 * n_targets * BLOCK * width
        ),
        name="combine",
    )(*table, gates, *blocks)


def flip(value, axis, bit):
    size = lax.axis_size(axis)
    return lax.ppermute(value, axis, [(i, i ^ bit) for i in range(size)])


def offsets(count):
    near, far = list(range(1, count // 2)), list(range(count // 2, count))
    order = [0]
    for i, k in enumerate(near):
        order += [k, far[i]]
    return order + far[len(near) :]


def exchange(blocks):
    order = offsets(len(blocks))
    return [flip(block, "expert", k) if k else block for k, block in zip(order, blocks)]


def cross(block, far_bits):
    held = {0: block}
    for bit in far_bits:
        for mask in list(held):
            held[mask | bit] = flip(held[mask], "dp", bit)
    return held


def body(tokens, out_grad, gate_probs, route_ids, w_gate, w_up, w_down):
    n_targets = lax.axis_size("expert")
    n_dp = lax.axis_size("dp")
    width = tokens.shape[1]
    ids, gates = route_ids.T, gate_probs.T
    far_bits = [1 << i for i in range(1, n_dp.bit_length() - 1)]
    weights = (w_gate[0], w_up[0], w_down[0])
    tie = lax.optimization_barrier

    sent = dispatch(n_targets, ids, tokens, gates, out_grad)
    arrived = exchange([sent[k] for k in offsets(n_targets)])
    middle = n_targets // 2
    early = pack(arrived[:middle])
    ids_after, _ = tie((ids, early))
    table, late = tie((placement(n_targets, ids_after), arrived[middle:]))
    held = [cross(group, far_bits) for group in (early, pack(late))]
    near = sorted(held[0])
    others = [{mask: flip(held[0][mask], "dp", 1) for mask in near}]
    others[0], held[1] = tie((others[0], held[1]))
    others.append({mask: flip(held[1][mask], "dp", 1) for mask in near})
    pieces = [group[mask] for groups in (held, others) for mask in near for group in groups]
    token_halves, activated, slope, hidden = forward(pieces, weights[0], weights[1])
    part, grad_halves, gate_f, up_f, low, high, gate_column = backward(
        pieces, activated, slope, hidden, weights
    )
    middle = width // 4
    received = flip(part, "dp", 1)
    other = far_rows(middle, low, high, gate_column, weights[0], weights[1])
    received, other = tie((received, other))
    left = own_rows(len(near), 0, low, high, gate_column, weights[0], weights[1], received)
    received = flip(other, "dp", 1)
    received, left = tie((received, left))
    right = own_rows(len(near), middle, low, high, gate_column, weights[0], weights[1], received)
    lefts, rights = dict(zip(near, left)), dict(zip(near, right))
    for bit in reversed(far_bits):
        masks = [mask for mask in lefts if mask & bit]
        moved_left = {mask: flip(lefts.pop(mask), "dp", bit) for mask in masks}
        moved_right = {mask: flip(rights.pop(mask), "dp", bit) for mask in masks}
        if bit == far_bits[-1]:
            rights, gate_f, up_f, hidden = tie((rights, gate_f, up_f, hidden))
            grads = weight_grads((gate_f, up_f, hidden), token_halves, grad_halves)
            moved_left, moved_right, grads = tie((moved_left, moved_right, grads))
        for mask in masks:
            terms = (lefts[mask ^ bit], rights[mask ^ bit]), (moved_left[mask], moved_right[mask])
            if bit == far_bits[0]:
                returned = exchange(add_rows(*terms, n_targets))
            else:
                lefts[mask ^ bit] = add_rows(terms[0][:1], terms[1][:1])[0]
                rights[mask ^ bit] = add_rows(terms[0][1:], terms[1][1:])[0]
    token_grad, gate_grad = combine(table, gates, returned, width)
    return (token_grad, gate_grad.T, *(grad[None] for grad in grads))


def solution(mesh):
    in_specs = (
        P(("expert", "dp"), None),
        P(("expert", "dp"), None),
        P(("expert", "dp"), None),
        P(("expert", "dp"), None),
        P("expert", "dp", None),
        P("expert", "dp", None),
        P("expert", "dp", None),
    )
    out_specs = (
        P(("expert", "dp"), None),
        P(("expert", "dp"), None),
        P("expert", "dp", None),
        P("expert", "dp", None),
        P("expert", "dp", None),
    )
    return jax.shard_map(body, mesh=mesh, in_specs=in_specs, out_specs=out_specs, check_vma=False)
```

```python
import functools

import jax
import jax.numpy as jnp
from jax import lax
from jax.experimental import pallas as pl
from jax.experimental.pallas import tpu as pltpu
from jax.sharding import PartitionSpec as P

EXPERTS = 128
CAP = 4
BLOCK = 2 * CAP
LANES = 128
MIB = 2**20
COVER = 40

CONTRACT_LAST = (((1,), (1,)), ((), ()))
CONTRACT_FIRST = (((0,), (0,)), ((), ()))

HBM = pl.BlockSpec(memory_space=pltpu.HBM)
VMEM = pl.BlockSpec(memory_space=pltpu.VMEM)

LIGHT = pl.CostEstimate(flops=10**6, bytes_accessed=10**4, transcendentals=0)
SOME = pl.CostEstimate(flops=10**9, bytes_accessed=6 * 10**6, transcendentals=0)


def struct(shape, dtype=jnp.bfloat16):
    return jax.ShapeDtypeStruct(shape, dtype)


def as_bf16(mask):
    return mask.astype(jnp.float32).astype(jnp.bfloat16)


def choice_table(ids, n_targets):
    choices, tokens = ids.shape
    height = n_targets * BLOCK
    per_device = EXPERTS // n_targets
    row = lax.broadcasted_iota(jnp.int32, (height, 1), 0)
    wanted = ((row // BLOCK) ^ lax.axis_index("expert")) * per_device
    slot = row % BLOCK
    matches = [ids[k : k + 1, :] == wanted for k in range(choices)]
    hit = functools.reduce(jnp.logical_or, matches)
    earlier = lax.broadcasted_iota(jnp.int32, (tokens, tokens), 0) < lax.broadcasted_iota(
        jnp.int32, (tokens, tokens), 1
    )
    rank = jnp.dot(as_bf16(hit), as_bf16(earlier), preferred_element_type=jnp.float32)
    rank = rank.astype(jnp.int32)
    first = jnp.logical_and(hit, rank == slot)
    second = jnp.logical_and(hit, rank == slot - CAP)
    return matches, first, second


def pick_rows(first, second, rows_ref):
    half = rows_ref.shape[1] // 2
    low = jnp.dot(first, rows_ref[:, :half], preferred_element_type=jnp.float32)
    high = jnp.dot(second, rows_ref[:, half:], preferred_element_type=jnp.float32)
    return (low + high).astype(jnp.bfloat16)


def dispatch_kernel(n_targets, *refs):
    sources, outs = refs[:4], refs[4 : 4 + n_targets]
    targets, sems = refs[4 + n_targets : -1], refs[-1]
    ids_ref, tokens_ref, gates_ref, grads_ref = targets
    copies = [
        pltpu.make_async_copy(source, target, sems.at[i])
        for i, (source, target) in enumerate(zip(sources, targets))
    ]
    for copy in copies:
        copy.start()
    copies[0].wait()
    matches, first, second = choice_table(ids_ref[...], n_targets)
    copies[1].wait()
    rows = pick_rows(as_bf16(first), as_bf16(second), tokens_ref)
    half = rows.shape[1]
    for k, out in enumerate(outs):
        out[:, :half] = rows[k * BLOCK : (k + 1) * BLOCK]
    copies[2].wait()
    gates = gates_ref[...].astype(jnp.float32)
    scale = jnp.zeros(first.shape, jnp.float32)
    for k, match in enumerate(matches):
        scale = scale + jnp.where(match, gates[k : k + 1, :], 0.0)
    first = jnp.where(first, scale, 0.0).astype(jnp.bfloat16)
    second = jnp.where(second, scale, 0.0).astype(jnp.bfloat16)
    copies[3].wait()
    rows = pick_rows(first, second, grads_ref)
    for k, out in enumerate(outs):
        out[:, half:] = rows[k * BLOCK : (k + 1) * BLOCK]


def dispatch(n_targets, ids, tokens, gates, out_grad):
    arrays = (ids, tokens, gates, out_grad)
    return pl.pallas_call(
        functools.partial(dispatch_kernel, n_targets),
        out_shape=[struct((BLOCK, tokens.shape[1]))] * n_targets,
        in_specs=[HBM] * 4,
        out_specs=[VMEM] * n_targets,
        scratch_shapes=[pltpu.VMEM(a.shape, a.dtype) for a in arrays]
        + [pltpu.SemaphoreType.DMA((4,))],
        compiler_params=pltpu.CompilerParams(vmem_limit_bytes=60 * MIB),
        name="dispatch",
    )(*arrays)


def placement_kernel(n_targets, ids_ref, first_ref, second_ref, choice_ref):
    matches, first, second = choice_table(ids_ref[...], n_targets)
    first_ref[...] = as_bf16(first)
    second_ref[...] = as_bf16(second)
    choice = jnp.full(first.shape, -1, jnp.int32)
    for k, match in enumerate(matches):
        choice = jnp.where(jnp.logical_and(match, first), k, choice)
    choice_ref[...] = choice


def placement(n_targets, ids):
    table = (n_targets * BLOCK, ids.shape[1])
    return pl.pallas_call(
        functools.partial(placement_kernel, n_targets),
        out_shape=[struct(table), struct(table), struct(table, jnp.int32)],
        in_specs=[VMEM],
        out_specs=[VMEM] * 3,
        compiler_params=pltpu.CompilerParams(vmem_limit_bytes=4 * MIB),
        cost_estimate=pl.CostEstimate(
            flops=COVER * 10**9, bytes_accessed=COVER * 10**6, transcendentals=0
        ),
        name="placement",
    )(ids)


def pack_kernel(count, *refs):
    blocks, out = refs[:count], refs[count]
    for k in range(0, count, 2):
        out[pl.ds(k * BLOCK, 2 * BLOCK), :] = jnp.concatenate(
            [blocks[k][...], blocks[k + 1][...]], axis=0
        )


def pack(blocks):
    count = len(blocks)
    rows, width = count * BLOCK, blocks[0].shape[1]
    return pl.pallas_call(
        functools.partial(pack_kernel, count),
        out_shape=struct((rows, width)),
        in_specs=[VMEM] * count,
        out_specs=VMEM,
        compiler_params=pltpu.CompilerParams(vmem_limit_bytes=4 * MIB + 8 * rows * width),
        name="pack",
    )(*blocks)


def gather_pieces(pieces, start, out):
    base = 0
    for piece in pieces:
        rows = piece.shape[0]
        out[pl.ds(base, rows), :] = piece[:, start : start + out.shape[1]]
        base += rows


def project(weight, halves):
    half = halves.shape[1]
    rows = halves.shape[0]
    low = lax.dot_general(
        weight[:, :half], halves[...], CONTRACT_LAST, preferred_element_type=jnp.float32
    )
    high = lax.dot_general(
        weight[:, half:], halves[...], CONTRACT_LAST, preferred_element_type=jnp.float32
    )
    return low + pltpu.roll(high, rows - CAP, 1)


def forward_kernel(count, *refs):
    pieces = refs[:count]
    gate_w, up_w, halves, activated_out, slope_out, hidden_out = refs[count:]
    gather_pieces(pieces, 0, halves)
    pre_gate, pre_up = project(gate_w, halves), project(up_w, halves)
    is_slot = lax.broadcasted_iota(jnp.int32, (1, halves.shape[0]), 1) % BLOCK < CAP
    squash = 1.0 / (1.0 + jnp.exp(-pre_gate))
    activated = jnp.where(is_slot, pre_gate * squash, 0.0)
    slope = pre_up * squash * (1.0 + pre_gate * (1.0 - squash))
    activated_out[...] = activated
    slope_out[...] = jnp.where(is_slot, slope, 0.0)
    hidden_out[...] = (activated * pre_up).astype(jnp.bfloat16)


def forward(pieces, gate_w, up_w):
    count = len(pieces)
    units, width = gate_w.shape
    rows = sum(piece.shape[0] for piece in pieces)
    kept = (units, rows)
    return pl.pallas_call(
        functools.partial(forward_kernel, count),
        out_shape=[
            struct((rows, width // 2)),
            struct(kept, jnp.float32),
            struct(kept, jnp.float32),
            struct(kept),
        ],
        in_specs=[VMEM] * (count + 2),
        out_specs=[VMEM] * 4,
        compiler_params=pltpu.CompilerParams(
            vmem_limit_bytes=4 * MIB + rows * width + 40 * rows * units
        ),
        cost_estimate=LIGHT,
        name="forward",
    )(*pieces, gate_w, up_w)


def row_grads(low, high, gate_w, up_w, received, parts, start, size):
    units, width = gate_w.shape
    block = parts[0].shape[0]
    chunk = 512 if size % 512 == 0 else size

    @pl.loop(0, size // chunk)
    def _(step):
        offset = pl.multiple_of(step * chunk, chunk)
        near = pl.ds(pl.multiple_of(start + offset, chunk), chunk)
        far = pl.ds(pl.multiple_of(width // 2 + start + offset, chunk), chunk)
        here = pl.ds(offset, chunk)
        total = None
        for rows, columns in ((low, near), (high, far)):
            for i, weight in enumerate((gate_w, up_w)):
                term = jnp.dot(
                    rows[:, i * units : (i + 1) * units],
                    weight[:, columns],
                    preferred_element_type=jnp.float32,
                )
                total = term if total is None else total + term
        if received is not None:
            total = total + received[:, here].astype(jnp.float32)
        total = total.astype(jnp.bfloat16)
        for i, part in enumerate(parts):
            part[:, here] = total[i * block : (i + 1) * block]


def backward_kernel(count, *refs):
    pieces = refs[:count]
    activated, slope, hidden, gate_w, up_w, down_w = refs[count : count + 6]
    part, halves, gate_out, up_out, low_out, high_out, gates_out = refs[count + 6 :]
    rows = halves.shape[0]
    mine = rows // 2
    gather_pieces(pieces, halves.shape[1], halves)
    back = project(down_w, halves)
    gate_terms = jnp.sum(hidden[...].astype(jnp.float32) * back, axis=0, keepdims=True)
    up_pre = back * activated[...]
    gate_pre = back * slope[...]
    both = jnp.concatenate([gate_pre, up_pre], axis=0)
    low = both.T.astype(jnp.bfloat16)
    high = pltpu.roll(both, CAP, 1).T.astype(jnp.bfloat16)
    gate_column = jnp.broadcast_to(gate_terms, (LANES, rows)).T.astype(jnp.bfloat16)
    row_grads(low[mine:], high[mine:], gate_w, up_w, None, (part,), 0, part.shape[1])
    low_out[...] = low
    high_out[...] = high
    gates_out[...] = gate_column
    gate_out[...] = gate_pre.astype(jnp.bfloat16)
    up_out[...] = up_pre.astype(jnp.bfloat16)


def backward(pieces, activated, slope, hidden, weights):
    count = len(pieces)
    units, width = weights[0].shape
    rows = sum(piece.shape[0] for piece in pieces)
    mine = rows // 2
    shapes = [
        (mine, width // 4),
        (rows, width // 2),
        (units, rows),
        (units, rows),
        (rows, 2 * units),
        (rows, 2 * units),
        (rows, LANES),
    ]
    return pl.pallas_call(
        functools.partial(backward_kernel, count),
        out_shape=[struct(shape) for shape in shapes],
        in_specs=[VMEM] * (count + 6),
        out_specs=[VMEM] * len(shapes),
        compiler_params=pltpu.CompilerParams(
            vmem_limit_bytes=4 * MIB
            + 2 * sum(height * across for height, across in shapes)
            + 40 * rows * units
        ),
        cost_estimate=LIGHT,
        name="backward",
    )(*pieces, activated, slope, hidden, *weights)


def far_kernel(start, low, high, gates, gate_w, up_w, part):
    span = pl.ds(part.shape[0], part.shape[0])
    size = part.shape[1] - LANES
    part[:, size:] = gates[span, :]
    row_grads(low[span, :], high[span, :], gate_w, up_w, None, (part,), start, size)


def far_rows(start, low, high, gates, gate_w, up_w):
    rows, width = low.shape[0], gate_w.shape[1]
    size = width // 2 - start
    return pl.pallas_call(
        functools.partial(far_kernel, start),
        out_shape=struct((rows // 2, size + LANES)),
        in_specs=[VMEM] * 5,
        out_specs=VMEM,
        compiler_params=pltpu.CompilerParams(vmem_limit_bytes=8 * MIB + 4 * rows * width),
        cost_estimate=LIGHT,
        name="far_rows",
    )(low, high, gates, gate_w, up_w)


def own_kernel(low, high, gates, gate_w, up_w, left, right, *parts):
    rows, size = left.shape
    extra = right.shape[1] - LANES
    block = parts[0].shape[0]
    for i, part in enumerate(parts):
        span = pl.ds(i * block, block)
        part[:, size + extra :] = (
            gates[span, :].astype(jnp.float32) + right[span, extra:].astype(jnp.float32)
        ).astype(jnp.bfloat16)
    low, high = low[:rows, :], high[:rows, :]
    row_grads(low, high, gate_w, up_w, left, parts, 0, size)
    views = [part.at[:, pl.ds(size, extra)] for part in parts]
    row_grads(low, high, gate_w, up_w, right, views, size, extra)


def own_rows(count, low, high, gates, gate_w, up_w, left, right):
    rows = left.shape[0]
    width = left.shape[1] + right.shape[1]
    return pl.pallas_call(
        own_kernel,
        out_shape=[struct((rows // count, width))] * count,
        in_specs=[VMEM] * 7,
        out_specs=[VMEM] * count,
        compiler_params=pltpu.CompilerParams(vmem_limit_bytes=8 * MIB + 16 * rows * width),
        cost_estimate=LIGHT,
        name="own_rows",
    )(low, high, gates, gate_w, up_w, left, right)


def add_kernel(left, right, *outs):
    total = (left[...].astype(jnp.float32) + right[...].astype(jnp.float32)).astype(jnp.bfloat16)
    block = outs[0].shape[0]
    for i, out in enumerate(outs):
        out[...] = total[i * block : (i + 1) * block]


def add_rows(left, right, blocks):
    rows, width = left.shape
    return pl.pallas_call(
        add_kernel,
        out_shape=[struct((rows // blocks, width))] * blocks,
        in_specs=[VMEM] * 2,
        out_specs=[VMEM] * blocks,
        compiler_params=pltpu.CompilerParams(vmem_limit_bytes=4 * MIB + 16 * rows * width),
        name="add_rows",
    )(left, right)


def weight_kernel(chunk, count, *refs):
    factors, halves = refs[:count], refs[count]
    outs, stages, sems = refs[count + 1 : 2 * count + 1], refs[2 * count + 1 : -1], refs[-1]
    half = halves.shape[1]
    pairs = []
    for factor in factors:
        low = factor[...]
        high = pltpu.roll(low.astype(jnp.float32), CAP, 1).astype(jnp.bfloat16)
        pairs.append((low, high))
    copies = []
    for start in range(0, half, chunk):
        for pair, out, stage in zip(pairs, outs, stages):
            for factor, base in zip(pair, (0, half)):
                span = pl.ds(base + start, chunk)
                stage[:, span] = jnp.dot(
                    factor, halves[:, pl.ds(start, chunk)], preferred_element_type=jnp.float32
                ).astype(jnp.bfloat16)
                copy = pltpu.make_async_copy(
                    stage.at[:, span], out.at[:, span], sems.at[len(copies)]
                )
                copy.start()
                copies.append(copy)
    for copy in copies:
        copy.wait()


def weight_grads(factors, halves, cost):
    count = len(factors)
    units, rows = factors[0].shape
    half = halves.shape[1]
    chunk = 512 if half % 512 == 0 else half
    shape = (units, 2 * half)
    return pl.pallas_call(
        functools.partial(weight_kernel, chunk, count),
        out_shape=[struct(shape)] * count,
        in_specs=[VMEM] * (count + 1),
        out_specs=[HBM] * count,
        scratch_shapes=[pltpu.VMEM(shape, jnp.bfloat16)] * count
        + [pltpu.SemaphoreType.DMA((2 * count * half // chunk,))],
        compiler_params=pltpu.CompilerParams(
            vmem_limit_bytes=6 * MIB + 4 * count * units * half + 8 * count * units * rows
        ),
        cost_estimate=cost,
        name="weight_grads",
    )(*factors, halves)


def combine_kernel(n_targets, first, second, choice_ref, gates_ref, *refs):
    blocks, (token_ref, gate_ref) = refs[:n_targets], refs[n_targets:]
    order = offsets(n_targets)
    back = jnp.concatenate([blocks[order.index(k)][...] for k in range(n_targets)], axis=0)
    half = token_ref.shape[1] // 2
    choices, tokens = gates_ref.shape
    rows = back[:, :half]
    token_ref[:, :half] = lax.dot_general(
        first[...], rows, CONTRACT_FIRST, preferred_element_type=jnp.float32
    ).astype(jnp.bfloat16)
    token_ref[:, half:] = lax.dot_general(
        second[...], rows, CONTRACT_FIRST, preferred_element_type=jnp.float32
    ).astype(jnp.bfloat16)
    terms = back[:, half : half + tokens].astype(jnp.float32)
    choice = choice_ref[...]
    for k in range(choices):
        chosen = jnp.where(choice == k, terms, 0.0)
        gate = gates_ref[k : k + 1, :].astype(jnp.float32)
        gate_ref[k : k + 1, :] = jnp.sum(chosen, axis=0, keepdims=True) / gate


def combine(table, gates, blocks, width):
    n_targets = len(blocks)
    choices, tokens = gates.shape
    return pl.pallas_call(
        functools.partial(combine_kernel, n_targets),
        out_shape=[struct((tokens, width)), struct((choices, tokens), jnp.float32)],
        in_specs=[VMEM] * (4 + n_targets),
        out_specs=[VMEM] * 2,
        compiler_params=pltpu.CompilerParams(
            vmem_limit_bytes=4 * MIB + 16 * n_targets * BLOCK * width
        ),
        name="combine",
    )(*table, gates, *blocks)


def flip(value, axis, bit):
    size = lax.axis_size(axis)
    return lax.ppermute(value, axis, [(i, i ^ bit) for i in range(size)])


def offsets(count):
    near, far = list(range(1, count // 2)), list(range(count // 2, count))
    order = []
    for i, k in enumerate(near):
        order += [k, far[i]]
    return order + far[len(near) :] + [0]


def exchange(blocks, order):
    return [flip(block, "expert", k) if k else block for k, block in zip(order, blocks)]


def cross(block, far_bits):
    held = {0: block}
    for bit in far_bits:
        for mask in list(held):
            held[mask | bit] = flip(held[mask], "dp", bit)
    return held


def body(tokens, out_grad, gate_probs, route_ids, w_gate, w_up, w_down):
    n_targets = lax.axis_size("expert")
    n_dp = lax.axis_size("dp")
    width = tokens.shape[1]
    ids, gates = route_ids.T, gate_probs.T
    far_bits = [1 << i for i in range(1, n_dp.bit_length() - 1)]
    weights = (w_gate[0], w_up[0], w_down[0])
    tie = lax.optimization_barrier

    order = offsets(n_targets)
    middle = n_targets // 2
    sent = dispatch(n_targets, ids, tokens, gates, out_grad)
    arrived = exchange([sent[k] for k in order], order)
    early = pack(arrived[:middle])
    ids_after, _ = tie((ids, early))
    table, late = tie((placement(n_targets, ids_after), arrived[middle:]))
    held = [cross(group, far_bits) for group in (early, pack(late))]
    near = sorted(held[0])
    others = [{mask: flip(held[0][mask], "dp", 1) for mask in near}]
    others.append({0: flip(held[1][0], "dp", 1)})
    far_late = {mask: held[1][mask] for mask in near[1:]}
    others, far_late = tie((others, far_late))
    for mask in far_late:
        others[1][mask] = flip(far_late[mask], "dp", 1)
    pieces = [group[mask] for groups in (held, others) for mask in near for group in groups]
    token_halves, activated, slope, hidden = forward(pieces, weights[0], weights[1])
    part, grad_halves, gate_f, up_f, low, high, gate_column = backward(
        pieces, activated, slope, hidden, weights
    )

    received = flip(part, "dp", 1)
    other = far_rows(width // 4, low, high, gate_column, weights[0], weights[1])
    received, other = tie((received, other))
    parts = own_rows(
        2 * len(near), low, high, gate_column, weights[0], weights[1], received, flip(other, "dp", 1)
    )
    sums = [dict(zip(near, parts[i::2])) for i in range(2)]
    gate_f, up_f, _ = tie((gate_f, up_f, parts))
    grad_gate, grad_up = weight_grads((gate_f, up_f), token_halves, LIGHT)
    returned = []
    for group in sums:
        for bit in reversed(far_bits):
            masks = [mask for mask in group if mask & bit]
            moved = {mask: flip(group.pop(mask), "dp", bit) for mask in masks}
            if group is sums[0] and bit == far_bits[-1]:
                moved, grad_gate, grad_up = tie((moved, grad_gate, grad_up))
            for mask in masks:
                blocks = middle if bit == far_bits[0] else 1
                total = add_rows(group[mask ^ bit], moved[mask], blocks)
                group[mask ^ bit] = total if blocks > 1 else total[0]
        returned += list(group[0])
    hidden, _ = tie((hidden, returned[middle:]))
    (grad_down,) = weight_grads((hidden,), grad_halves, SOME)
    returned = exchange(returned, order)
    returned, grad_down = tie((returned, grad_down))
    token_grad, gate_grad = combine(table, gates, returned, width)
    grads = (grad_gate, grad_up, grad_down)
    return (token_grad, gate_grad.T, *(grad[None] for grad in grads))


def solution(mesh):
    in_specs = (
        P(("expert", "dp"), None),
        P(("expert", "dp"), None),
        P(("expert", "dp"), None),
        P(("expert", "dp"), None),
        P("expert", "dp", None),
        P("expert", "dp", None),
        P("expert", "dp", None),
    )
    out_specs = (
        P(("expert", "dp"), None),
        P(("expert", "dp"), None),
        P("expert", "dp", None),
        P("expert", "dp", None),
        P("expert", "dp", None),
    )
    return jax.shard_map(body, mesh=mesh, in_specs=in_specs, out_specs=out_specs, check_vma=False)
```

```python
import functools

import jax
import jax.numpy as jnp
from jax import lax
from jax.experimental import pallas as pl
from jax.experimental.pallas import tpu as pltpu
from jax.sharding import PartitionSpec as P

EXPERTS = 128
CAP = 4
BLOCK = 2 * CAP
LANES = 128
MIB = 2**20
COVER = 40

CONTRACT_LAST = (((1,), (1,)), ((), ()))
CONTRACT_FIRST = (((0,), (0,)), ((), ()))

HBM = pl.BlockSpec(memory_space=pltpu.HBM)
VMEM = pl.BlockSpec(memory_space=pltpu.VMEM)

LIGHT = pl.CostEstimate(flops=10**6, bytes_accessed=10**4, transcendentals=0)


def struct(shape, dtype=jnp.bfloat16):
    return jax.ShapeDtypeStruct(shape, dtype)


def as_bf16(mask):
    return mask.astype(jnp.float32).astype(jnp.bfloat16)


def choice_table(ids, n_targets):
    choices, tokens = ids.shape
    height = n_targets * BLOCK
    per_device = EXPERTS // n_targets
    row = lax.broadcasted_iota(jnp.int32, (height, 1), 0)
    wanted = ((row // BLOCK) ^ lax.axis_index("expert")) * per_device
    slot = row % BLOCK
    matches = [ids[k : k + 1, :] == wanted for k in range(choices)]
    hit = functools.reduce(jnp.logical_or, matches)
    earlier = lax.broadcasted_iota(jnp.int32, (tokens, tokens), 0) < lax.broadcasted_iota(
        jnp.int32, (tokens, tokens), 1
    )
    rank = jnp.dot(as_bf16(hit), as_bf16(earlier), preferred_element_type=jnp.float32)
    rank = rank.astype(jnp.int32)
    first = jnp.logical_and(hit, rank == slot)
    second = jnp.logical_and(hit, rank == slot - CAP)
    return matches, first, second


def pick_rows(first, second, rows_ref):
    half = rows_ref.shape[1] // 2
    low = jnp.dot(first, rows_ref[:, :half], preferred_element_type=jnp.float32)
    high = jnp.dot(second, rows_ref[:, half:], preferred_element_type=jnp.float32)
    return (low + high).astype(jnp.bfloat16)


def dispatch_kernel(n_targets, *refs):
    sources, outs = refs[:4], refs[4 : 4 + n_targets]
    targets, sems = refs[4 + n_targets : -1], refs[-1]
    ids_ref, tokens_ref, gates_ref, grads_ref = targets
    copies = [
        pltpu.make_async_copy(source, target, sems.at[i])
        for i, (source, target) in enumerate(zip(sources, targets))
    ]
    for copy in copies:
        copy.start()
    copies[0].wait()
    matches, first, second = choice_table(ids_ref[...], n_targets)
    copies[1].wait()
    rows = pick_rows(as_bf16(first), as_bf16(second), tokens_ref)
    half = rows.shape[1]
    for k, out in enumerate(outs):
        out[:, :half] = rows[k * BLOCK : (k + 1) * BLOCK]
    copies[2].wait()
    gates = gates_ref[...].astype(jnp.float32)
    scale = jnp.zeros(first.shape, jnp.float32)
    for k, match in enumerate(matches):
        scale = scale + jnp.where(match, gates[k : k + 1, :], 0.0)
    first = jnp.where(first, scale, 0.0).astype(jnp.bfloat16)
    second = jnp.where(second, scale, 0.0).astype(jnp.bfloat16)
    copies[3].wait()
    rows = pick_rows(first, second, grads_ref)
    for k, out in enumerate(outs):
        out[:, half:] = rows[k * BLOCK : (k + 1) * BLOCK]


def dispatch(n_targets, ids, tokens, gates, out_grad):
    arrays = (ids, tokens, gates, out_grad)
    return pl.pallas_call(
        functools.partial(dispatch_kernel, n_targets),
        out_shape=[struct((BLOCK, tokens.shape[1]))] * n_targets,
        in_specs=[HBM] * 4,
        out_specs=[VMEM] * n_targets,
        scratch_shapes=[pltpu.VMEM(a.shape, a.dtype) for a in arrays]
        + [pltpu.SemaphoreType.DMA((4,))],
        compiler_params=pltpu.CompilerParams(vmem_limit_bytes=60 * MIB),
        name="dispatch",
    )(*arrays)


def placement_kernel(n_targets, ids_ref, first_ref, second_ref, choice_ref):
    matches, first, second = choice_table(ids_ref[...], n_targets)
    first_ref[...] = as_bf16(first)
    second_ref[...] = as_bf16(second)
    choice = jnp.full(first.shape, -1, jnp.int32)
    for k, match in enumerate(matches):
        choice = jnp.where(jnp.logical_and(match, first), k, choice)
    choice_ref[...] = choice


def placement(n_targets, ids):
    table = (n_targets * BLOCK, ids.shape[1])
    return pl.pallas_call(
        functools.partial(placement_kernel, n_targets),
        out_shape=[struct(table), struct(table), struct(table, jnp.int32)],
        in_specs=[VMEM],
        out_specs=[VMEM] * 3,
        compiler_params=pltpu.CompilerParams(vmem_limit_bytes=4 * MIB),
        cost_estimate=pl.CostEstimate(
            flops=COVER * 10**9, bytes_accessed=COVER * 10**6, transcendentals=0
        ),
        name="placement",
    )(ids)


def pack_kernel(count, *refs):
    blocks, out = refs[:count], refs[count]
    for k in range(0, count, 2):
        out[pl.ds(k * BLOCK, 2 * BLOCK), :] = jnp.concatenate(
            [blocks[k][...], blocks[k + 1][...]], axis=0
        )


def pack(blocks):
    count = len(blocks)
    rows, width = count * BLOCK, blocks[0].shape[1]
    return pl.pallas_call(
        functools.partial(pack_kernel, count),
        out_shape=struct((rows, width)),
        in_specs=[VMEM] * count,
        out_specs=VMEM,
        compiler_params=pltpu.CompilerParams(vmem_limit_bytes=4 * MIB + 8 * rows * width),
        name="pack",
    )(*blocks)


def gather_pieces(pieces, start, out):
    base = 0
    for piece in pieces:
        rows = piece.shape[0]
        out[pl.ds(base, rows), :] = piece[:, start : start + out.shape[1]]
        base += rows


def project(weight, halves):
    half = halves.shape[1]
    rows = halves.shape[0]
    low = lax.dot_general(
        weight[:, :half], halves[...], CONTRACT_LAST, preferred_element_type=jnp.float32
    )
    high = lax.dot_general(
        weight[:, half:], halves[...], CONTRACT_LAST, preferred_element_type=jnp.float32
    )
    return low + pltpu.roll(high, rows - CAP, 1)


def forward_kernel(count, *refs):
    pieces = refs[:count]
    gate_w, up_w, halves, activated_out, slope_out, hidden_out = refs[count:]
    gather_pieces(pieces, 0, halves)
    pre_gate, pre_up = project(gate_w, halves), project(up_w, halves)
    is_slot = lax.broadcasted_iota(jnp.int32, (1, halves.shape[0]), 1) % BLOCK < CAP
    squash = 1.0 / (1.0 + jnp.exp(-pre_gate))
    activated = jnp.where(is_slot, pre_gate * squash, 0.0)
    slope = pre_up * squash * (1.0 + pre_gate * (1.0 - squash))
    activated_out[...] = activated
    slope_out[...] = jnp.where(is_slot, slope, 0.0)
    hidden_out[...] = (activated * pre_up).astype(jnp.bfloat16)


def forward(pieces, gate_w, up_w):
    count = len(pieces)
    units, width = gate_w.shape
    rows = sum(piece.shape[0] for piece in pieces)
    kept = (units, rows)
    return pl.pallas_call(
        functools.partial(forward_kernel, count),
        out_shape=[
            struct((rows, width // 2)),
            struct(kept, jnp.float32),
            struct(kept, jnp.float32),
            struct(kept),
        ],
        in_specs=[VMEM] * (count + 2),
        out_specs=[VMEM] * 4,
        compiler_params=pltpu.CompilerParams(
            vmem_limit_bytes=4 * MIB + rows * width + 40 * rows * units
        ),
        cost_estimate=LIGHT,
        name="forward",
    )(*pieces, gate_w, up_w)


def row_grads(low, high, gate_w, up_w, received, parts, start, size):
    units, width = gate_w.shape
    block = parts[0].shape[0]
    chunk = 512 if size % 512 == 0 else size

    @pl.loop(0, size // chunk)
    def _(step):
        offset = pl.multiple_of(step * chunk, chunk)
        near = pl.ds(pl.multiple_of(start + offset, chunk), chunk)
        far = pl.ds(pl.multiple_of(width // 2 + start + offset, chunk), chunk)
        here = pl.ds(offset, chunk)
        total = None
        for rows, columns in ((low, near), (high, far)):
            for i, weight in enumerate((gate_w, up_w)):
                term = jnp.dot(
                    rows[:, i * units : (i + 1) * units],
                    weight[:, columns],
                    preferred_element_type=jnp.float32,
                )
                total = term if total is None else total + term
        if received is not None:
            total = total + received[:, here].astype(jnp.float32)
        total = total.astype(jnp.bfloat16)
        for i, part in enumerate(parts):
            part[:, here] = total[i * block : (i + 1) * block]


def backward_kernel(count, *refs):
    pieces = refs[:count]
    activated, slope, hidden, gate_w, up_w, down_w = refs[count : count + 6]
    part, halves, gate_out, up_out, low_out, high_out, gates_out = refs[count + 6 :]
    rows = halves.shape[0]
    mine = rows // 2
    gather_pieces(pieces, halves.shape[1], halves)
    back = project(down_w, halves)
    gate_terms = jnp.sum(hidden[...].astype(jnp.float32) * back, axis=0, keepdims=True)
    up_pre = back * activated[...]
    gate_pre = back * slope[...]
    both = jnp.concatenate([gate_pre, up_pre], axis=0)
    low = both.T.astype(jnp.bfloat16)
    high = pltpu.roll(both, CAP, 1).T.astype(jnp.bfloat16)
    gate_column = jnp.broadcast_to(gate_terms, (LANES, rows)).T.astype(jnp.bfloat16)
    row_grads(low[mine:], high[mine:], gate_w, up_w, None, (part,), 0, part.shape[1])
    low_out[...] = low
    high_out[...] = high
    gates_out[...] = gate_column
    gate_out[...] = gate_pre.astype(jnp.bfloat16)
    up_out[...] = up_pre.astype(jnp.bfloat16)


def backward(pieces, activated, slope, hidden, weights):
    count = len(pieces)
    units, width = weights[0].shape
    rows = sum(piece.shape[0] for piece in pieces)
    mine = rows // 2
    shapes = [
        (mine, width // 4),
        (rows, width // 2),
        (units, rows),
        (units, rows),
        (rows, 2 * units),
        (rows, 2 * units),
        (rows, LANES),
    ]
    return pl.pallas_call(
        functools.partial(backward_kernel, count),
        out_shape=[struct(shape) for shape in shapes],
        in_specs=[VMEM] * (count + 6),
        out_specs=[VMEM] * len(shapes),
        compiler_params=pltpu.CompilerParams(
            vmem_limit_bytes=4 * MIB
            + 2 * sum(height * across for height, across in shapes)
            + 40 * rows * units
        ),
        cost_estimate=LIGHT,
        name="backward",
    )(*pieces, activated, slope, hidden, *weights)


def far_kernel(start, low, high, gates, gate_w, up_w, part):
    span = pl.ds(part.shape[0], part.shape[0])
    size = part.shape[1] - LANES
    part[:, size:] = gates[span, :]
    row_grads(low[span, :], high[span, :], gate_w, up_w, None, (part,), start, size)


def far_rows(start, low, high, gates, gate_w, up_w):
    rows, width = low.shape[0], gate_w.shape[1]
    size = width // 2 - start
    return pl.pallas_call(
        functools.partial(far_kernel, start),
        out_shape=struct((rows // 2, size + LANES)),
        in_specs=[VMEM] * 5,
        out_specs=VMEM,
        compiler_params=pltpu.CompilerParams(vmem_limit_bytes=8 * MIB + 4 * rows * width),
        cost_estimate=LIGHT,
        name="far_rows",
    )(low, high, gates, gate_w, up_w)


def own_first_kernel(low, high, gate_w, up_w, left, out):
    rows, size = left.shape
    row_grads(low[:rows, :], high[:rows, :], gate_w, up_w, left, (out,), 0, size)


def own_first(low, high, gate_w, up_w, left):
    return pl.pallas_call(
        own_first_kernel,
        out_shape=struct(left.shape),
        in_specs=[VMEM] * 5,
        out_specs=VMEM,
        compiler_params=pltpu.CompilerParams(vmem_limit_bytes=8 * MIB + 16 * left.size),
        cost_estimate=LIGHT,
        name="own_first",
    )(low, high, gate_w, up_w, left)


def own_rows_kernel(low, high, gates, gate_w, up_w, left, right, *parts):
    rows, size = left.shape
    extra = right.shape[1] - LANES
    block = parts[0].shape[0]
    for i, part in enumerate(parts):
        span = pl.ds(i * block, block)
        part[:, :size] = left[span, :]
        part[:, size + extra :] = (
            gates[span, :].astype(jnp.float32) + right[span, extra:].astype(jnp.float32)
        ).astype(jnp.bfloat16)
    views = [part.at[:, pl.ds(size, extra)] for part in parts]
    row_grads(low[:rows, :], high[:rows, :], gate_w, up_w, right, views, size, extra)


def own_rows(count, low, high, gates, gate_w, up_w, left, right):
    rows = left.shape[0]
    width = left.shape[1] + right.shape[1]
    return pl.pallas_call(
        own_rows_kernel,
        out_shape=[struct((rows // count, width))] * count,
        in_specs=[VMEM] * 7,
        out_specs=[VMEM] * count,
        compiler_params=pltpu.CompilerParams(vmem_limit_bytes=8 * MIB + 16 * rows * width),
        cost_estimate=LIGHT,
        name="own_rows",
    )(low, high, gates, gate_w, up_w, left, right)


def add_kernel(left, right, out):
    total = left[...].astype(jnp.float32) + right[...].astype(jnp.float32)
    out[...] = total.astype(jnp.bfloat16)


def add_rows(left, right):
    return pl.pallas_call(
        add_kernel,
        out_shape=struct(left.shape),
        in_specs=[VMEM] * 2,
        out_specs=VMEM,
        compiler_params=pltpu.CompilerParams(vmem_limit_bytes=4 * MIB + 16 * left.size),
        name="add_rows",
    )(left, right)


def merge_kernel(kept, passed, *outs):
    for i, out in enumerate(outs):
        span = slice(i * BLOCK, (i + 1) * BLOCK)
        out[...] = jnp.concatenate([kept[span, :], passed[span, :]], axis=0)


def merge_rows(kept, passed):
    rows, width = kept.shape
    count = rows // BLOCK
    return pl.pallas_call(
        merge_kernel,
        out_shape=[struct((2 * BLOCK, width))] * count,
        in_specs=[VMEM] * 2,
        out_specs=[VMEM] * count,
        compiler_params=pltpu.CompilerParams(vmem_limit_bytes=4 * MIB + 24 * rows * width),
        name="merge_rows",
    )(kept, passed)


def weight_kernel(chunk, count, *refs):
    factors, halves = refs[:count], refs[count]
    outs, stages, sems = refs[count + 1 : 2 * count + 1], refs[2 * count + 1 : -1], refs[-1]
    half = halves.shape[1]
    pairs = []
    for factor in factors:
        low = factor[...]
        high = pltpu.roll(low.astype(jnp.float32), CAP, 1).astype(jnp.bfloat16)
        pairs.append((low, high))
    copies = []
    for start in range(0, half, chunk):
        for pair, out, stage in zip(pairs, outs, stages):
            for factor, base in zip(pair, (0, half)):
                span = pl.ds(base + start, chunk)
                stage[:, span] = jnp.dot(
                    factor, halves[:, pl.ds(start, chunk)], preferred_element_type=jnp.float32
                ).astype(jnp.bfloat16)
                copy = pltpu.make_async_copy(
                    stage.at[:, span], out.at[:, span], sems.at[len(copies)]
                )
                copy.start()
                copies.append(copy)
    for copy in copies:
        copy.wait()


def weight_grads(factors, halves):
    count = len(factors)
    units, rows = factors[0].shape
    half = halves.shape[1]
    chunk = 512 if half % 512 == 0 else half
    shape = (units, 2 * half)
    return pl.pallas_call(
        functools.partial(weight_kernel, chunk, count),
        out_shape=[struct(shape)] * count,
        in_specs=[VMEM] * (count + 1),
        out_specs=[HBM] * count,
        scratch_shapes=[pltpu.VMEM(shape, jnp.bfloat16)] * count
        + [pltpu.SemaphoreType.DMA((2 * count * half // chunk,))],
        compiler_params=pltpu.CompilerParams(
            vmem_limit_bytes=6 * MIB + 4 * count * units * half + 8 * count * units * rows
        ),
        cost_estimate=LIGHT,
        name="weight_grads",
    )(*factors, halves)


def combine_kernel(n_targets, first, second, choice_ref, gates_ref, *refs):
    blocks, (token_ref, gate_ref) = refs[: n_targets // 2], refs[n_targets // 2 :]
    even = offsets(n_targets)[1]
    back = jnp.concatenate([blocks[even.index(k)][...] for k in range(0, n_targets, 2)], axis=0)
    half = token_ref.shape[1] // 2
    choices, tokens = gates_ref.shape
    rows = back[:, :half]
    token_ref[:, :half] = lax.dot_general(
        first[...], rows, CONTRACT_FIRST, preferred_element_type=jnp.float32
    ).astype(jnp.bfloat16)
    token_ref[:, half:] = lax.dot_general(
        second[...], rows, CONTRACT_FIRST, preferred_element_type=jnp.float32
    ).astype(jnp.bfloat16)
    terms = back[:, half : half + tokens].astype(jnp.float32)
    choice = choice_ref[...]
    for k in range(choices):
        chosen = jnp.where(choice == k, terms, 0.0)
        gate = gates_ref[k : k + 1, :].astype(jnp.float32)
        gate_ref[k : k + 1, :] = jnp.sum(chosen, axis=0, keepdims=True) / gate


def combine(table, gates, blocks, width):
    n_targets = 2 * len(blocks)
    choices, tokens = gates.shape
    return pl.pallas_call(
        functools.partial(combine_kernel, n_targets),
        out_shape=[struct((tokens, width)), struct((choices, tokens), jnp.float32)],
        in_specs=[VMEM] * (4 + len(blocks)),
        out_specs=[VMEM] * 2,
        compiler_params=pltpu.CompilerParams(
            vmem_limit_bytes=4 * MIB + 16 * n_targets * BLOCK * width
        ),
        name="combine",
    )(*table, gates, *blocks)


def flip(value, axis, bit):
    size = lax.axis_size(axis)
    return lax.ppermute(value, axis, [(i, i ^ bit) for i in range(size)])


def offsets(count):
    even = list(range(count // 2, count, 2)) + list(range(count // 2 - 2, -1, -2))
    return [k ^ 1 for k in even], even


def exchange(blocks, order):
    return [flip(block, "expert", k) if k else block for k, block in zip(order, blocks)]


def cross(block, far_bits):
    held = {0: block}
    for bit in far_bits:
        for mask in list(held):
            held[mask | bit] = flip(held[mask], "dp", bit)
    return held


def body(tokens, out_grad, gate_probs, route_ids, w_gate, w_up, w_down):
    n_targets = lax.axis_size("expert")
    n_dp = lax.axis_size("dp")
    width = tokens.shape[1]
    ids, gates = route_ids.T, gate_probs.T
    far_bits = [1 << i for i in range(1, n_dp.bit_length() - 1)]
    weights = (w_gate[0], w_up[0], w_down[0])
    tie = lax.optimization_barrier

    odd, even = offsets(n_targets)
    middle = n_targets // 2
    sent = dispatch(n_targets, ids, tokens, gates, out_grad)
    arrived = exchange([sent[k] for k in odd + even], odd + even)
    early = pack(arrived[:middle])
    ids_after, _ = tie((ids, early))
    table, late = tie((placement(n_targets, ids_after), arrived[middle:]))
    held = [cross(group, far_bits) for group in (early, pack(late))]
    near = sorted(held[0])
    others = [{mask: flip(held[0][mask], "dp", 1) for mask in near}]
    others.append({0: flip(held[1][0], "dp", 1)})
    far_late = {mask: held[1][mask] for mask in near[1:]}
    others, far_late = tie((others, far_late))
    for mask in far_late:
        others[1][mask] = flip(far_late[mask], "dp", 1)
    pieces = [group[mask] for groups in (held, others) for mask in near for group in groups]
    token_halves, activated, slope, hidden = forward(pieces, weights[0], weights[1])
    part, grad_halves, gate_f, up_f, low, high, gate_column = backward(
        pieces, activated, slope, hidden, weights
    )

    received = flip(part, "dp", 1)
    other = far_rows(width // 4, low, high, gate_column, weights[0], weights[1])
    received, other = tie((received, other))
    left = own_first(low, high, weights[0], weights[1], received)
    right, left = tie((flip(other, "dp", 1), left))
    parts = own_rows(
        2 * len(near), low, high, gate_column, weights[0], weights[1], left, right
    )
    gate_f, up_f, _ = tie((gate_f, up_f, parts))
    grad_gate, grad_up = weight_grads((gate_f, up_f), token_halves)
    sums = []
    for group in range(2):
        held = dict(zip(near, parts[group::2]))
        for bit in reversed(far_bits):
            masks = [mask for mask in held if mask & bit]
            moved = {mask: flip(held.pop(mask), "dp", bit) for mask in masks}
            if group == 0 and bit == far_bits[-1]:
                moved, grad_gate, grad_up = tie((moved, grad_gate, grad_up))
            if bit == far_bits[0]:
                sums.append((held[0], moved[bit]))
            else:
                for mask in masks:
                    held[mask ^ bit] = add_rows(held[mask ^ bit], moved[mask])
    passed = add_rows(*sums[0])
    hidden, _ = tie((hidden, passed))
    (grad_down,) = weight_grads((hidden,), grad_halves)
    kept, passed, grad_down = tie((add_rows(*sums[1]), flip(passed, "expert", 1), grad_down))
    returned = exchange(merge_rows(kept, passed), even)
    token_grad, gate_grad = combine(table, gates, returned, width)
    grads = (grad_gate, grad_up, grad_down)
    return (token_grad, gate_grad.T, *(grad[None] for grad in grads))


def solution(mesh):
    in_specs = (
        P(("expert", "dp"), None),
        P(("expert", "dp"), None),
        P(("expert", "dp"), None),
        P(("expert", "dp"), None),
        P("expert", "dp", None),
        P("expert", "dp", None),
        P("expert", "dp", None),
    )
    out_specs = (
        P(("expert", "dp"), None),
        P(("expert", "dp"), None),
        P("expert", "dp", None),
        P("expert", "dp", None),
        P("expert", "dp", None),
    )
    return jax.shard_map(body, mesh=mesh, in_specs=in_specs, out_specs=out_specs, check_vma=False)
```

```python
import functools

import jax
import jax.numpy as jnp
from jax import lax
from jax.experimental import pallas as pl
from jax.experimental.pallas import tpu as pltpu
from jax.sharding import PartitionSpec as P

EXPERTS = 128
CAP = 4
BLOCK = 2 * CAP
LANES = 128
MIB = 2**20
COVER = 40

CONTRACT_LAST = (((1,), (1,)), ((), ()))
CONTRACT_FIRST = (((0,), (0,)), ((), ()))

HBM = pl.BlockSpec(memory_space=pltpu.HBM)
VMEM = pl.BlockSpec(memory_space=pltpu.VMEM)

LIGHT = pl.CostEstimate(flops=10**6, bytes_accessed=10**4, transcendentals=0)


def struct(shape, dtype=jnp.bfloat16):
    return jax.ShapeDtypeStruct(shape, dtype)


def as_bf16(mask):
    return mask.astype(jnp.float32).astype(jnp.bfloat16)


def choice_table(ids, n_targets):
    choices, tokens = ids.shape
    height = n_targets * BLOCK
    per_device = EXPERTS // n_targets
    row = lax.broadcasted_iota(jnp.int32, (height, 1), 0)
    wanted = ((row // BLOCK) ^ lax.axis_index("expert")) * per_device
    slot = row % BLOCK
    matches = [ids[k : k + 1, :] == wanted for k in range(choices)]
    hit = functools.reduce(jnp.logical_or, matches)
    earlier = lax.broadcasted_iota(jnp.int32, (tokens, tokens), 0) < lax.broadcasted_iota(
        jnp.int32, (tokens, tokens), 1
    )
    rank = jnp.dot(as_bf16(hit), as_bf16(earlier), preferred_element_type=jnp.float32)
    rank = rank.astype(jnp.int32)
    first = jnp.logical_and(hit, rank == slot)
    second = jnp.logical_and(hit, rank == slot - CAP)
    return matches, first, second


def pick_rows(first, second, rows_ref):
    half = rows_ref.shape[1] // 2
    low = jnp.dot(first, rows_ref[:, :half], preferred_element_type=jnp.float32)
    high = jnp.dot(second, rows_ref[:, half:], preferred_element_type=jnp.float32)
    return (low + high).astype(jnp.bfloat16)


def dispatch_kernel(n_targets, *refs):
    sources, outs = refs[:4], refs[4 : 4 + n_targets]
    targets, sems = refs[4 + n_targets : -1], refs[-1]
    ids_ref, tokens_ref, gates_ref, grads_ref = targets
    copies = [
        pltpu.make_async_copy(source, target, sems.at[i])
        for i, (source, target) in enumerate(zip(sources, targets))
    ]
    for copy in copies:
        copy.start()
    copies[0].wait()
    matches, first, second = choice_table(ids_ref[...], n_targets)
    copies[1].wait()
    rows = pick_rows(as_bf16(first), as_bf16(second), tokens_ref)
    half = rows.shape[1]
    for k, out in enumerate(outs):
        out[:, :half] = rows[k * BLOCK : (k + 1) * BLOCK]
    copies[2].wait()
    gates = gates_ref[...].astype(jnp.float32)
    scale = jnp.zeros(first.shape, jnp.float32)
    for k, match in enumerate(matches):
        scale = scale + jnp.where(match, gates[k : k + 1, :], 0.0)
    first = jnp.where(first, scale, 0.0).astype(jnp.bfloat16)
    second = jnp.where(second, scale, 0.0).astype(jnp.bfloat16)
    copies[3].wait()
    rows = pick_rows(first, second, grads_ref)
    for k, out in enumerate(outs):
        out[:, half:] = rows[k * BLOCK : (k + 1) * BLOCK]


def dispatch(n_targets, ids, tokens, gates, out_grad):
    arrays = (ids, tokens, gates, out_grad)
    return pl.pallas_call(
        functools.partial(dispatch_kernel, n_targets),
        out_shape=[struct((BLOCK, tokens.shape[1]))] * n_targets,
        in_specs=[HBM] * 4,
        out_specs=[VMEM] * n_targets,
        scratch_shapes=[pltpu.VMEM(a.shape, a.dtype) for a in arrays]
        + [pltpu.SemaphoreType.DMA((4,))],
        compiler_params=pltpu.CompilerParams(vmem_limit_bytes=60 * MIB),
        name="dispatch",
    )(*arrays)


def placement_kernel(n_targets, ids_ref, first_ref, second_ref, choice_ref):
    matches, first, second = choice_table(ids_ref[...], n_targets)
    first_ref[...] = as_bf16(first)
    second_ref[...] = as_bf16(second)
    choice = jnp.full(first.shape, -1, jnp.int32)
    for k, match in enumerate(matches):
        choice = jnp.where(jnp.logical_and(match, first), k, choice)
    choice_ref[...] = choice


def placement(n_targets, ids):
    table = (n_targets * BLOCK, ids.shape[1])
    return pl.pallas_call(
        functools.partial(placement_kernel, n_targets),
        out_shape=[struct(table), struct(table), struct(table, jnp.int32)],
        in_specs=[VMEM],
        out_specs=[VMEM] * 3,
        compiler_params=pltpu.CompilerParams(vmem_limit_bytes=4 * MIB),
        cost_estimate=pl.CostEstimate(
            flops=COVER * 10**9, bytes_accessed=COVER * 10**6, transcendentals=0
        ),
        name="placement",
    )(ids)


def pack_kernel(count, *refs):
    blocks, out = refs[:count], refs[count]
    for k in range(0, count, 2):
        out[pl.ds(k * BLOCK, 2 * BLOCK), :] = jnp.concatenate(
            [blocks[k][...], blocks[k + 1][...]], axis=0
        )


def pack(blocks):
    count = len(blocks)
    rows, width = count * BLOCK, blocks[0].shape[1]
    return pl.pallas_call(
        functools.partial(pack_kernel, count),
        out_shape=struct((rows, width)),
        in_specs=[VMEM] * count,
        out_specs=VMEM,
        compiler_params=pltpu.CompilerParams(vmem_limit_bytes=4 * MIB + 8 * rows * width),
        name="pack",
    )(*blocks)


def gather_pieces(pieces, start, out):
    base = 0
    for piece in pieces:
        rows = piece.shape[0]
        out[pl.ds(base, rows), :] = piece[:, start : start + out.shape[1]]
        base += rows


def project(weight, halves):
    half = halves.shape[1]
    rows = halves.shape[0]
    low = lax.dot_general(
        weight[:, :half], halves[...], CONTRACT_LAST, preferred_element_type=jnp.float32
    )
    high = lax.dot_general(
        weight[:, half:], halves[...], CONTRACT_LAST, preferred_element_type=jnp.float32
    )
    return low + pltpu.roll(high, rows - CAP, 1)


def forward_kernel(count, *refs):
    pieces = refs[:count]
    gate_w, up_w, halves, activated_out, slope_out, hidden_out = refs[count:]
    gather_pieces(pieces, 0, halves)
    pre_gate, pre_up = project(gate_w, halves), project(up_w, halves)
    is_slot = lax.broadcasted_iota(jnp.int32, (1, halves.shape[0]), 1) % BLOCK < CAP
    squash = 1.0 / (1.0 + jnp.exp(-pre_gate))
    activated = jnp.where(is_slot, pre_gate * squash, 0.0)
    slope = pre_up * squash * (1.0 + pre_gate * (1.0 - squash))
    activated_out[...] = activated
    slope_out[...] = jnp.where(is_slot, slope, 0.0)
    hidden_out[...] = (activated * pre_up).astype(jnp.bfloat16)


def forward(pieces, gate_w, up_w):
    count = len(pieces)
    units, width = gate_w.shape
    rows = sum(piece.shape[0] for piece in pieces)
    kept = (units, rows)
    return pl.pallas_call(
        functools.partial(forward_kernel, count),
        out_shape=[
            struct((rows, width // 2)),
            struct(kept, jnp.float32),
            struct(kept, jnp.float32),
            struct(kept),
        ],
        in_specs=[VMEM] * (count + 2),
        out_specs=[VMEM] * 4,
        compiler_params=pltpu.CompilerParams(
            vmem_limit_bytes=4 * MIB + rows * width + 40 * rows * units
        ),
        cost_estimate=LIGHT,
        name="forward",
    )(*pieces, gate_w, up_w)


def row_grads(low, high, gate_w, up_w, received, parts, start, size):
    units, width = gate_w.shape
    block = parts[0].shape[0]
    chunk = 512 if size % 512 == 0 else size

    @pl.loop(0, size // chunk)
    def _(step):
        offset = pl.multiple_of(step * chunk, chunk)
        near = pl.ds(pl.multiple_of(start + offset, chunk), chunk)
        far = pl.ds(pl.multiple_of(width // 2 + start + offset, chunk), chunk)
        here = pl.ds(offset, chunk)
        total = None
        for rows, columns in ((low, near), (high, far)):
            for i, weight in enumerate((gate_w, up_w)):
                term = jnp.dot(
                    rows[:, i * units : (i + 1) * units],
                    weight[:, columns],
                    preferred_element_type=jnp.float32,
                )
                total = term if total is None else total + term
        if received is not None:
            total = total + received[:, here].astype(jnp.float32)
        total = total.astype(jnp.bfloat16)
        for i, part in enumerate(parts):
            part[:, here] = total[i * block : (i + 1) * block]


def backward_kernel(count, *refs):
    pieces = refs[:count]
    activated, slope, hidden, gate_w, up_w, down_w = refs[count : count + 6]
    part, halves, gate_out, up_out, low_out, high_out, gates_out = refs[count + 6 :]
    rows = halves.shape[0]
    mine = rows // 2
    gather_pieces(pieces, halves.shape[1], halves)
    back = project(down_w, halves)
    gate_terms = jnp.sum(hidden[...].astype(jnp.float32) * back, axis=0, keepdims=True)
    up_pre = back * activated[...]
    gate_pre = back * slope[...]
    both = jnp.concatenate([gate_pre, up_pre], axis=0)
    low = both.T.astype(jnp.bfloat16)
    high = pltpu.roll(both, CAP, 1).T.astype(jnp.bfloat16)
    gate_column = jnp.broadcast_to(gate_terms, (LANES, rows)).T.astype(jnp.bfloat16)
    row_grads(low[mine:], high[mine:], gate_w, up_w, None, (part,), 0, part.shape[1])
    low_out[...] = low
    high_out[...] = high
    gates_out[...] = gate_column
    gate_out[...] = gate_pre.astype(jnp.bfloat16)
    up_out[...] = up_pre.astype(jnp.bfloat16)


def backward(pieces, activated, slope, hidden, weights):
    count = len(pieces)
    units, width = weights[0].shape
    rows = sum(piece.shape[0] for piece in pieces)
    mine = rows // 2
    shapes = [
        (mine, width // 4),
        (rows, width // 2),
        (units, rows),
        (units, rows),
        (rows, 2 * units),
        (rows, 2 * units),
        (rows, LANES),
    ]
    return pl.pallas_call(
        functools.partial(backward_kernel, count),
        out_shape=[struct(shape) for shape in shapes],
        in_specs=[VMEM] * (count + 6),
        out_specs=[VMEM] * len(shapes),
        compiler_params=pltpu.CompilerParams(
            vmem_limit_bytes=4 * MIB
            + 2 * sum(height * across for height, across in shapes)
            + 40 * rows * units
        ),
        cost_estimate=LIGHT,
        name="backward",
    )(*pieces, activated, slope, hidden, *weights)


def far_kernel(start, low, high, gates, gate_w, up_w, part):
    span = pl.ds(part.shape[0], part.shape[0])
    size = part.shape[1] - LANES
    part[:, size:] = gates[span, :]
    row_grads(low[span, :], high[span, :], gate_w, up_w, None, (part,), start, size)


def far_rows(start, low, high, gates, gate_w, up_w):
    rows, width = low.shape[0], gate_w.shape[1]
    size = width // 2 - start
    return pl.pallas_call(
        functools.partial(far_kernel, start),
        out_shape=struct((rows // 2, size + LANES)),
        in_specs=[VMEM] * 5,
        out_specs=VMEM,
        compiler_params=pltpu.CompilerParams(vmem_limit_bytes=8 * MIB + 4 * rows * width),
        cost_estimate=LIGHT,
        name="far_rows",
    )(low, high, gates, gate_w, up_w)


def own_first_kernel(low, high, gate_w, up_w, left, out):
    rows, size = left.shape
    row_grads(low[:rows, :], high[:rows, :], gate_w, up_w, left, (out,), 0, size)


def own_first(low, high, gate_w, up_w, left):
    return pl.pallas_call(
        own_first_kernel,
        out_shape=struct(left.shape),
        in_specs=[VMEM] * 5,
        out_specs=VMEM,
        compiler_params=pltpu.CompilerParams(vmem_limit_bytes=8 * MIB + 16 * left.size),
        cost_estimate=LIGHT,
        name="own_first",
    )(low, high, gate_w, up_w, left)


def own_rows_kernel(low, high, gates, gate_w, up_w, left, right, *parts):
    rows, size = left.shape
    extra = right.shape[1] - LANES
    block = parts[0].shape[0]
    for i, part in enumerate(parts):
        span = pl.ds(i * block, block)
        part[:, :size] = left[span, :]
        part[:, size + extra :] = (
            gates[span, :].astype(jnp.float32) + right[span, extra:].astype(jnp.float32)
        ).astype(jnp.bfloat16)
    views = [part.at[:, pl.ds(size, extra)] for part in parts]
    row_grads(low[:rows, :], high[:rows, :], gate_w, up_w, right, views, size, extra)


def own_rows(count, low, high, gates, gate_w, up_w, left, right):
    rows = left.shape[0]
    width = left.shape[1] + right.shape[1]
    return pl.pallas_call(
        own_rows_kernel,
        out_shape=[struct((rows // count, width))] * count,
        in_specs=[VMEM] * 7,
        out_specs=[VMEM] * count,
        compiler_params=pltpu.CompilerParams(vmem_limit_bytes=8 * MIB + 16 * rows * width),
        cost_estimate=LIGHT,
        name="own_rows",
    )(low, high, gates, gate_w, up_w, left, right)


def add_kernel(left, right, out):
    total = left[...].astype(jnp.float32) + right[...].astype(jnp.float32)
    out[...] = total.astype(jnp.bfloat16)


def add_rows(left, right):
    return pl.pallas_call(
        add_kernel,
        out_shape=struct(left.shape),
        in_specs=[VMEM] * 2,
        out_specs=VMEM,
        compiler_params=pltpu.CompilerParams(vmem_limit_bytes=4 * MIB + 16 * left.size),
        name="add_rows",
    )(left, right)


def merge_kernel(kept, passed, *outs):
    for i, out in enumerate(outs):
        span = slice(i * BLOCK, (i + 1) * BLOCK)
        out[...] = jnp.concatenate([kept[span, :], passed[span, :]], axis=0)


def merge_rows(kept, passed):
    rows, width = kept.shape
    count = rows // BLOCK
    return pl.pallas_call(
        merge_kernel,
        out_shape=[struct((2 * BLOCK, width))] * count,
        in_specs=[VMEM] * 2,
        out_specs=[VMEM] * count,
        compiler_params=pltpu.CompilerParams(vmem_limit_bytes=4 * MIB + 24 * rows * width),
        name="merge_rows",
    )(kept, passed)


def weight_kernel(chunk, count, *refs):
    factors, halves = refs[:count], refs[count]
    outs, stages, sems = refs[count + 1 : 2 * count + 1], refs[2 * count + 1 : -1], refs[-1]
    half = halves.shape[1]
    pairs = []
    for factor in factors:
        low = factor[...]
        high = pltpu.roll(low.astype(jnp.float32), CAP, 1).astype(jnp.bfloat16)
        pairs.append((low, high))
    copies = []
    for start in range(0, half, chunk):
        for pair, out, stage in zip(pairs, outs, stages):
            for factor, base in zip(pair, (0, half)):
                span = pl.ds(base + start, chunk)
                stage[:, span] = jnp.dot(
                    factor, halves[:, pl.ds(start, chunk)], preferred_element_type=jnp.float32
                ).astype(jnp.bfloat16)
                copy = pltpu.make_async_copy(
                    stage.at[:, span], out.at[:, span], sems.at[len(copies)]
                )
                copy.start()
                copies.append(copy)
    for copy in copies:
        copy.wait()


def weight_grads(factors, halves):
    count = len(factors)
    units, rows = factors[0].shape
    half = halves.shape[1]
    chunk = 512 if half % 512 == 0 else half
    shape = (units, 2 * half)
    return pl.pallas_call(
        functools.partial(weight_kernel, chunk, count),
        out_shape=[struct(shape)] * count,
        in_specs=[VMEM] * (count + 1),
        out_specs=[HBM] * count,
        scratch_shapes=[pltpu.VMEM(shape, jnp.bfloat16)] * count
        + [pltpu.SemaphoreType.DMA((2 * count * half // chunk,))],
        compiler_params=pltpu.CompilerParams(
            vmem_limit_bytes=6 * MIB + 4 * count * units * half + 8 * count * units * rows
        ),
        cost_estimate=LIGHT,
        name="weight_grads",
    )(*factors, halves)


def combine_kernel(n_targets, first, second, choice_ref, gates_ref, *refs):
    blocks, (token_ref, gate_ref) = refs[: n_targets // 2], refs[n_targets // 2 :]
    even = offsets(n_targets)[1]
    back = jnp.concatenate([blocks[even.index(k)][...] for k in range(0, n_targets, 2)], axis=0)
    half = token_ref.shape[1] // 2
    choices, tokens = gates_ref.shape
    rows = back[:, :half]
    token_ref[:, :half] = lax.dot_general(
        first[...], rows, CONTRACT_FIRST, preferred_element_type=jnp.float32
    ).astype(jnp.bfloat16)
    token_ref[:, half:] = lax.dot_general(
        second[...], rows, CONTRACT_FIRST, preferred_element_type=jnp.float32
    ).astype(jnp.bfloat16)
    terms = back[:, half : half + tokens].astype(jnp.float32)
    choice = choice_ref[...]
    for k in range(choices):
        chosen = jnp.where(choice == k, terms, 0.0)
        gate = gates_ref[k : k + 1, :].astype(jnp.float32)
        gate_ref[k : k + 1, :] = jnp.sum(chosen, axis=0, keepdims=True) / gate


def combine(table, gates, blocks, width):
    n_targets = 2 * len(blocks)
    choices, tokens = gates.shape
    return pl.pallas_call(
        functools.partial(combine_kernel, n_targets),
        out_shape=[struct((tokens, width)), struct((choices, tokens), jnp.float32)],
        in_specs=[VMEM] * (4 + len(blocks)),
        out_specs=[VMEM] * 2,
        compiler_params=pltpu.CompilerParams(
            vmem_limit_bytes=4 * MIB + 16 * n_targets * BLOCK * width
        ),
        name="combine",
    )(*table, gates, *blocks)


def flip(value, axis, bit):
    size = lax.axis_size(axis)
    return lax.ppermute(value, axis, [(i, i ^ bit) for i in range(size)])


def offsets(count):
    even = []
    for k in range(0, count // 2, 2):
        even += [k, k + count // 2]
    return [k ^ 1 for k in even], even


def exchange(blocks, order):
    return [flip(block, "expert", k) if k else block for k, block in zip(order, blocks)]


def cross(block, far_bits):
    held = {0: block}
    for bit in far_bits:
        for mask in list(held):
            held[mask | bit] = flip(held[mask], "dp", bit)
    return held


def body(tokens, out_grad, gate_probs, route_ids, w_gate, w_up, w_down):
    n_targets = lax.axis_size("expert")
    n_dp = lax.axis_size("dp")
    width = tokens.shape[1]
    ids, gates = route_ids.T, gate_probs.T
    far_bits = [1 << i for i in range(1, n_dp.bit_length() - 1)]
    weights = (w_gate[0], w_up[0], w_down[0])
    tie = lax.optimization_barrier

    odd, even = offsets(n_targets)
    middle = n_targets // 2
    sent = dispatch(n_targets, ids, tokens, gates, out_grad)
    arrived = exchange([sent[k] for k in odd + even], odd + even)
    early = pack(arrived[:middle])
    ids_after, _ = tie((ids, early))
    table, late = tie((placement(n_targets, ids_after), arrived[middle:]))
    late = pack(late)
    early_near, late_near = (cross(value, far_bits) for value in (early, late))
    near = sorted(early_near)
    crossed = {mask: early_near[mask] for mask in near[1:]}
    early, late, crossed = tie((early, late, crossed))
    early_far = {0: flip(early, "dp", 1)}
    for mask, value in crossed.items():
        early_far[mask] = flip(value, "dp", 1)
    late_far = {0: flip(late, "dp", 1)}
    crossed = {mask: late_near[mask] for mask in near[1:]}
    early_far, late_far, crossed = tie((early_far, late_far, crossed))
    for mask, value in crossed.items():
        late_far[mask] = flip(value, "dp", 1)
    pieces = [
        group[mask]
        for groups in ((early_near, late_near), (early_far, late_far))
        for mask in near
        for group in groups
    ]
    token_halves, activated, slope, hidden = forward(pieces, weights[0], weights[1])
    part, grad_halves, gate_f, up_f, low, high, gate_column = backward(
        pieces, activated, slope, hidden, weights
    )

    received = flip(part, "dp", 1)
    other = far_rows(width // 4, low, high, gate_column, weights[0], weights[1])
    received, other = tie((received, other))
    left = own_first(low, high, weights[0], weights[1], received)
    right, left = tie((flip(other, "dp", 1), left))
    parts = own_rows(
        2 * len(near), low, high, gate_column, weights[0], weights[1], left, right
    )
    gate_f, up_f, _ = tie((gate_f, up_f, parts))
    grad_gate, grad_up = weight_grads((gate_f, up_f), token_halves)
    sums = []
    for group in range(2):
        held = dict(zip(near, parts[group::2]))
        for bit in reversed(far_bits):
            masks = [mask for mask in held if mask & bit]
            moved = {mask: flip(held.pop(mask), "dp", bit) for mask in masks}
            if group == 0 and bit == far_bits[-1]:
                moved, grad_gate, grad_up = tie((moved, grad_gate, grad_up))
            if bit == far_bits[0]:
                sums.append((held[0], moved[bit]))
            else:
                for mask in masks:
                    held[mask ^ bit] = add_rows(held[mask ^ bit], moved[mask])
    passed = add_rows(*sums[0])
    hidden, _ = tie((hidden, passed))
    (grad_down,) = weight_grads((hidden,), grad_halves)
    passed = flip(passed, "expert", 1)
    kept, moved, grad_down = tie((*sums[1], grad_down))
    kept, passed = tie((add_rows(kept, moved), passed))
    returned = exchange(merge_rows(kept, passed), even)
    token_grad, gate_grad = combine(table, gates, returned, width)
    grads = (grad_gate, grad_up, grad_down)
    return (token_grad, gate_grad.T, *(grad[None] for grad in grads))


def solution(mesh):
    in_specs = (
        P(("expert", "dp"), None),
        P(("expert", "dp"), None),
        P(("expert", "dp"), None),
        P(("expert", "dp"), None),
        P("expert", "dp", None),
        P("expert", "dp", None),
        P("expert", "dp", None),
    )
    out_specs = (
        P(("expert", "dp"), None),
        P(("expert", "dp"), None),
        P("expert", "dp", None),
        P("expert", "dp", None),
        P("expert", "dp", None),
    )
    return jax.shard_map(body, mesh=mesh, in_specs=in_specs, out_specs=out_specs, check_vma=False)
```

```python
import functools

import jax
import jax.numpy as jnp
from jax import lax
from jax.experimental import pallas as pl
from jax.experimental.pallas import tpu as pltpu
from jax.sharding import PartitionSpec as P

EXPERTS = 128
CAP = 4
BLOCK = 2 * CAP
LANES = 128
MIB = 2**20
COVER = 40

CONTRACT_LAST = (((1,), (1,)), ((), ()))
CONTRACT_FIRST = (((0,), (0,)), ((), ()))

HBM = pl.BlockSpec(memory_space=pltpu.HBM)
VMEM = pl.BlockSpec(memory_space=pltpu.VMEM)

LIGHT = pl.CostEstimate(flops=10**6, bytes_accessed=10**4, transcendentals=0)


def struct(shape, dtype=jnp.bfloat16):
    return jax.ShapeDtypeStruct(shape, dtype)


def as_bf16(mask):
    return mask.astype(jnp.float32).astype(jnp.bfloat16)


def choice_table(ids, n_targets):
    choices, tokens = ids.shape
    height = n_targets * BLOCK
    per_device = EXPERTS // n_targets
    row = lax.broadcasted_iota(jnp.int32, (height, 1), 0)
    wanted = ((row // BLOCK) ^ lax.axis_index("expert")) * per_device
    slot = row % BLOCK
    matches = [ids[k : k + 1, :] == wanted for k in range(choices)]
    hit = functools.reduce(jnp.logical_or, matches)
    earlier = lax.broadcasted_iota(jnp.int32, (tokens, tokens), 0) < lax.broadcasted_iota(
        jnp.int32, (tokens, tokens), 1
    )
    rank = jnp.dot(as_bf16(hit), as_bf16(earlier), preferred_element_type=jnp.float32)
    rank = rank.astype(jnp.int32)
    first = jnp.logical_and(hit, rank == slot)
    second = jnp.logical_and(hit, rank == slot - CAP)
    return matches, first, second


def pick_rows(first, second, rows_ref):
    half = rows_ref.shape[1] // 2
    low = jnp.dot(first, rows_ref[:, :half], preferred_element_type=jnp.float32)
    high = jnp.dot(second, rows_ref[:, half:], preferred_element_type=jnp.float32)
    return (low + high).astype(jnp.bfloat16)


def dispatch_kernel(n_targets, *refs):
    sources, outs = refs[:4], refs[4 : 4 + n_targets]
    targets, sems = refs[4 + n_targets : -1], refs[-1]
    ids_ref, tokens_ref, gates_ref, grads_ref = targets
    copies = [
        pltpu.make_async_copy(source, target, sems.at[i])
        for i, (source, target) in enumerate(zip(sources, targets))
    ]
    for copy in copies:
        copy.start()
    copies[0].wait()
    matches, first, second = choice_table(ids_ref[...], n_targets)
    copies[1].wait()
    rows = pick_rows(as_bf16(first), as_bf16(second), tokens_ref)
    half = rows.shape[1]
    for k, out in enumerate(outs):
        out[:, :half] = rows[k * BLOCK : (k + 1) * BLOCK]
    copies[2].wait()
    gates = gates_ref[...].astype(jnp.float32)
    scale = jnp.zeros(first.shape, jnp.float32)
    for k, match in enumerate(matches):
        scale = scale + jnp.where(match, gates[k : k + 1, :], 0.0)
    first = jnp.where(first, scale, 0.0).astype(jnp.bfloat16)
    second = jnp.where(second, scale, 0.0).astype(jnp.bfloat16)
    copies[3].wait()
    rows = pick_rows(first, second, grads_ref)
    for k, out in enumerate(outs):
        out[:, half:] = rows[k * BLOCK : (k + 1) * BLOCK]


def dispatch(n_targets, ids, tokens, gates, out_grad):
    arrays = (ids, tokens, gates, out_grad)
    return pl.pallas_call(
        functools.partial(dispatch_kernel, n_targets),
        out_shape=[struct((BLOCK, tokens.shape[1]))] * n_targets,
        in_specs=[HBM] * 4,
        out_specs=[VMEM] * n_targets,
        scratch_shapes=[pltpu.VMEM(a.shape, a.dtype) for a in arrays]
        + [pltpu.SemaphoreType.DMA((4,))],
        compiler_params=pltpu.CompilerParams(vmem_limit_bytes=60 * MIB),
        name="dispatch",
    )(*arrays)


def placement_kernel(n_targets, ids_ref, first_ref, second_ref, choice_ref):
    matches, first, second = choice_table(ids_ref[...], n_targets)
    first_ref[...] = as_bf16(first)
    second_ref[...] = as_bf16(second)
    choice = jnp.full(first.shape, -1, jnp.int32)
    for k, match in enumerate(matches):
        choice = jnp.where(jnp.logical_and(match, first), k, choice)
    choice_ref[...] = choice


def placement(n_targets, ids):
    table = (n_targets * BLOCK, ids.shape[1])
    return pl.pallas_call(
        functools.partial(placement_kernel, n_targets),
        out_shape=[struct(table), struct(table), struct(table, jnp.int32)],
        in_specs=[VMEM],
        out_specs=[VMEM] * 3,
        compiler_params=pltpu.CompilerParams(vmem_limit_bytes=4 * MIB),
        cost_estimate=pl.CostEstimate(
            flops=COVER * 10**9, bytes_accessed=COVER * 10**6, transcendentals=0
        ),
        name="placement",
    )(ids)


def pack_kernel(count, *refs):
    blocks, out = refs[:count], refs[count]
    for k in range(0, count, 2):
        out[pl.ds(k * BLOCK, 2 * BLOCK), :] = jnp.concatenate(
            [blocks[k][...], blocks[k + 1][...]], axis=0
        )


def pack(blocks):
    count = len(blocks)
    rows, width = count * BLOCK, blocks[0].shape[1]
    return pl.pallas_call(
        functools.partial(pack_kernel, count),
        out_shape=struct((rows, width)),
        in_specs=[VMEM] * count,
        out_specs=VMEM,
        compiler_params=pltpu.CompilerParams(vmem_limit_bytes=4 * MIB + 8 * rows * width),
        name="pack",
    )(*blocks)


def gather_pieces(pieces, start, out):
    base = 0
    for piece in pieces:
        rows = piece.shape[0]
        out[pl.ds(base, rows), :] = piece[:, start : start + out.shape[1]]
        base += rows


def project(weight, halves):
    half = halves.shape[1]
    rows = halves.shape[0]
    low = lax.dot_general(
        weight[:, :half], halves[...], CONTRACT_LAST, preferred_element_type=jnp.float32
    )
    high = lax.dot_general(
        weight[:, half:], halves[...], CONTRACT_LAST, preferred_element_type=jnp.float32
    )
    return low + pltpu.roll(high, rows - CAP, 1)


def forward_kernel(count, *refs):
    pieces = refs[:count]
    gate_w, up_w, halves, activated_out, slope_out, hidden_out = refs[count:]
    gather_pieces(pieces, 0, halves)
    pre_gate, pre_up = project(gate_w, halves), project(up_w, halves)
    is_slot = lax.broadcasted_iota(jnp.int32, (1, halves.shape[0]), 1) % BLOCK < CAP
    squash = 1.0 / (1.0 + jnp.exp(-pre_gate))
    activated = jnp.where(is_slot, pre_gate * squash, 0.0)
    slope = pre_up * squash * (1.0 + pre_gate * (1.0 - squash))
    activated_out[...] = activated
    slope_out[...] = jnp.where(is_slot, slope, 0.0)
    hidden_out[...] = (activated * pre_up).astype(jnp.bfloat16)


def forward(pieces, gate_w, up_w):
    count = len(pieces)
    units, width = gate_w.shape
    rows = sum(piece.shape[0] for piece in pieces)
    kept = (units, rows)
    return pl.pallas_call(
        functools.partial(forward_kernel, count),
        out_shape=[
            struct((rows, width // 2)),
            struct(kept, jnp.float32),
            struct(kept, jnp.float32),
            struct(kept),
        ],
        in_specs=[VMEM] * (count + 2),
        out_specs=[VMEM] * 4,
        compiler_params=pltpu.CompilerParams(
            vmem_limit_bytes=4 * MIB + rows * width + 40 * rows * units
        ),
        cost_estimate=LIGHT,
        name="forward",
    )(*pieces, gate_w, up_w)


def row_grads(low, high, gate_w, up_w, parts, start):
    units, width = gate_w.shape
    block, size = parts[0].shape
    chunk = 256 if size % 256 == 0 else size

    @pl.loop(0, size // chunk)
    def _(step):
        offset = pl.multiple_of(step * chunk, chunk)
        near = pl.ds(pl.multiple_of(start + offset, chunk), chunk)
        far = pl.ds(pl.multiple_of(width // 2 + start + offset, chunk), chunk)
        total = None
        for rows, columns in ((low, near), (high, far)):
            for i, weight in enumerate((gate_w, up_w)):
                term = jnp.dot(
                    rows[:, i * units : (i + 1) * units],
                    weight[:, columns],
                    preferred_element_type=jnp.float32,
                )
                total = term if total is None else total + term
        total = total.astype(jnp.bfloat16)
        for i, part in enumerate(parts):
            part[:, pl.ds(offset, chunk)] = total[i * block : (i + 1) * block]


def backward_kernel(count, *refs):
    pieces = refs[:count]
    activated, slope, hidden, gate_w, up_w, down_w = refs[count : count + 6]
    own, far, halves, gate_out, up_out, low_out, high_out, gates_out = refs[count + 6 :]
    rows = halves.shape[0]
    gather_pieces(pieces, halves.shape[1], halves)
    back = project(down_w, halves)
    gate_terms = jnp.sum(hidden[...].astype(jnp.float32) * back, axis=0, keepdims=True)
    up_pre = back * activated[...]
    gate_pre = back * slope[...]
    both = jnp.concatenate([gate_pre, up_pre], axis=0)
    low_out[...] = both.T.astype(jnp.bfloat16)
    high_out[...] = pltpu.roll(both, CAP, 1).T.astype(jnp.bfloat16)
    gate_column = jnp.broadcast_to(gate_terms, (LANES, rows)).T.astype(jnp.bfloat16)
    row_grads(low_out, high_out, gate_w, up_w, (own, far), 0)
    gates_out[...] = gate_column
    gate_out[...] = gate_pre.astype(jnp.bfloat16)
    up_out[...] = up_pre.astype(jnp.bfloat16)


def backward(pieces, activated, slope, hidden, weights, size):
    count = len(pieces)
    units, width = weights[0].shape
    rows = sum(piece.shape[0] for piece in pieces)
    mine = rows // 2
    shapes = [
        (mine, size),
        (mine, size),
        (rows, width // 2),
        (units, rows),
        (units, rows),
        (rows, 2 * units),
        (rows, 2 * units),
        (rows, LANES),
    ]
    return pl.pallas_call(
        functools.partial(backward_kernel, count),
        out_shape=[struct(shape) for shape in shapes],
        in_specs=[VMEM] * (count + 6),
        out_specs=[VMEM] * len(shapes),
        compiler_params=pltpu.CompilerParams(
            vmem_limit_bytes=6 * MIB
            + 2 * sum(height * across for height, across in shapes)
            + 56 * rows * units
        ),
        cost_estimate=LIGHT,
        name="backward",
    )(*pieces, activated, slope, hidden, *weights)


def rest_kernel(start, low, high, gates, gate_w, up_w, own, far):
    mine, size = own.shape
    size -= LANES
    own[:, size:] = gates[:mine, :]
    far[:, size:] = gates[mine:, :]
    views = [part.at[:, pl.ds(0, size)] for part in (own, far)]
    row_grads(low, high, gate_w, up_w, views, start)


def rest_rows(start, low, high, gates, gate_w, up_w):
    rows, width = low.shape[0], gate_w.shape[1]
    size = width // 2 - start + LANES
    return pl.pallas_call(
        functools.partial(rest_kernel, start),
        out_shape=[struct((rows // 2, size))] * 2,
        in_specs=[VMEM] * 5,
        out_specs=[VMEM] * 2,
        compiler_params=pltpu.CompilerParams(vmem_limit_bytes=8 * MIB + 4 * rows * width),
        cost_estimate=LIGHT,
        name="rest_rows",
    )(low, high, gates, gate_w, up_w)


def sum_kernel(targets, own_left, own_right, left, right, *outs):
    base = 0
    for own, other in ((own_left, left), (own_right, right)):
        span = pl.ds(base, own.shape[1])
        base += own.shape[1]
        total = (own[...].astype(jnp.float32) + other[...].astype(jnp.float32)).astype(
            jnp.bfloat16
        )
        for i, (out, slot) in enumerate(targets):
            outs[out][pl.ds(slot * BLOCK, BLOCK), span] = total[i * BLOCK : (i + 1) * BLOCK]


def sum_rows(targets, own, other):
    rows = own[0].shape[0]
    width = sum(part.shape[1] for part in own)
    count = 1 + max(out for out, _ in targets)
    return pl.pallas_call(
        functools.partial(sum_kernel, targets),
        out_shape=[struct((rows // count, width))] * count,
        in_specs=[VMEM] * 4,
        out_specs=[VMEM] * count,
        compiler_params=pltpu.CompilerParams(vmem_limit_bytes=8 * MIB + 16 * rows * width),
        cost_estimate=LIGHT,
        name="sum_rows",
    )(*own, *other)


def add_kernel(left, right, out):
    total = left[...].astype(jnp.float32) + right[...].astype(jnp.float32)
    out[...] = total.astype(jnp.bfloat16)


def add_rows(left, right):
    return pl.pallas_call(
        add_kernel,
        out_shape=struct(left.shape),
        in_specs=[VMEM] * 2,
        out_specs=VMEM,
        compiler_params=pltpu.CompilerParams(vmem_limit_bytes=4 * MIB + 16 * left.size),
        name="add_rows",
    )(left, right)


def merge_kernel(kept, passed, *outs):
    for i, out in enumerate(outs):
        span = slice(i * BLOCK, (i + 1) * BLOCK)
        out[...] = jnp.concatenate([kept[span, :], passed[span, :]], axis=0)


def merge_rows(kept, passed):
    rows, width = kept.shape
    count = rows // BLOCK
    return pl.pallas_call(
        merge_kernel,
        out_shape=[struct((2 * BLOCK, width))] * count,
        in_specs=[VMEM] * 2,
        out_specs=[VMEM] * count,
        compiler_params=pltpu.CompilerParams(vmem_limit_bytes=4 * MIB + 24 * rows * width),
        name="merge_rows",
    )(kept, passed)


def weight_kernel(chunk, count, *refs):
    factors, halves = refs[:count], refs[count]
    outs, stages, sems = refs[count + 1 : 2 * count + 1], refs[2 * count + 1 : -1], refs[-1]
    half = halves.shape[1]
    pairs = []
    for factor in factors:
        low = factor[...]
        high = pltpu.roll(low.astype(jnp.float32), CAP, 1).astype(jnp.bfloat16)
        pairs.append((low, high))
    copies = []
    for start in range(0, half, chunk):
        for pair, out, stage in zip(pairs, outs, stages):
            for factor, base in zip(pair, (0, half)):
                span = pl.ds(base + start, chunk)
                stage[:, span] = jnp.dot(
                    factor, halves[:, pl.ds(start, chunk)], preferred_element_type=jnp.float32
                ).astype(jnp.bfloat16)
                copy = pltpu.make_async_copy(
                    stage.at[:, span], out.at[:, span], sems.at[len(copies)]
                )
                copy.start()
                copies.append(copy)
    for copy in copies:
        copy.wait()


def weight_grads(factors, halves):
    count = len(factors)
    units, rows = factors[0].shape
    half = halves.shape[1]
    chunk = 512 if half % 512 == 0 else half
    shape = (units, 2 * half)
    return pl.pallas_call(
        functools.partial(weight_kernel, chunk, count),
        out_shape=[struct(shape)] * count,
        in_specs=[VMEM] * (count + 1),
        out_specs=[HBM] * count,
        scratch_shapes=[pltpu.VMEM(shape, jnp.bfloat16)] * count
        + [pltpu.SemaphoreType.DMA((2 * count * half // chunk,))],
        compiler_params=pltpu.CompilerParams(
            vmem_limit_bytes=6 * MIB + 4 * count * units * half + 8 * count * units * rows
        ),
        cost_estimate=LIGHT,
        name="weight_grads",
    )(*factors, halves)


def combine_kernel(n_targets, first, second, choice_ref, gates_ref, *refs):
    blocks, (token_ref, gate_ref) = refs[: n_targets // 2], refs[n_targets // 2 :]
    even = return_offsets(n_targets)[1]
    back = jnp.concatenate([blocks[even.index(k)][...] for k in range(0, n_targets, 2)], axis=0)
    half = token_ref.shape[1] // 2
    choices, tokens = gates_ref.shape
    rows = back[:, :half]
    token_ref[:, :half] = lax.dot_general(
        first[...], rows, CONTRACT_FIRST, preferred_element_type=jnp.float32
    ).astype(jnp.bfloat16)
    token_ref[:, half:] = lax.dot_general(
        second[...], rows, CONTRACT_FIRST, preferred_element_type=jnp.float32
    ).astype(jnp.bfloat16)
    terms = back[:, half : half + tokens].astype(jnp.float32)
    choice = choice_ref[...]
    for k in range(choices):
        chosen = jnp.where(choice == k, terms, 0.0)
        gate = gates_ref[k : k + 1, :].astype(jnp.float32)
        gate_ref[k : k + 1, :] = jnp.sum(chosen, axis=0, keepdims=True) / gate


def combine(table, gates, blocks, width):
    n_targets = 2 * len(blocks)
    choices, tokens = gates.shape
    return pl.pallas_call(
        functools.partial(combine_kernel, n_targets),
        out_shape=[struct((tokens, width)), struct((choices, tokens), jnp.float32)],
        in_specs=[VMEM] * (4 + len(blocks)),
        out_specs=[VMEM] * 2,
        compiler_params=pltpu.CompilerParams(
            vmem_limit_bytes=4 * MIB + 16 * n_targets * BLOCK * width
        ),
        name="combine",
    )(*table, gates, *blocks)


def flip(value, axis, bit):
    size = lax.axis_size(axis)
    return lax.ppermute(value, axis, [(i, i ^ bit) for i in range(size)])


def offsets(count):
    near, far = list(range(1, count // 2)), list(range(count // 2, count))
    order = []
    for i, k in enumerate(near):
        order += [k, far[i]]
    return order + far[len(near) :] + [0]


def return_offsets(count):
    even = list(range(count // 2, count, 2)) + list(range(count // 2 - 2, -1, -2))
    return [k ^ 1 for k in even], even


def exchange(blocks, order):
    return [flip(block, "expert", k) if k else block for k, block in zip(order, blocks)]


def cross(block, far_bits):
    held = {0: block}
    for bit in far_bits:
        for mask in list(held):
            held[mask | bit] = flip(held[mask], "dp", bit)
    return held


def body(tokens, out_grad, gate_probs, route_ids, w_gate, w_up, w_down):
    n_targets = lax.axis_size("expert")
    n_dp = lax.axis_size("dp")
    width = tokens.shape[1]
    ids, gates = route_ids.T, gate_probs.T
    far_bits = [1 << i for i in range(1, n_dp.bit_length() - 1)]
    weights = (w_gate[0], w_up[0], w_down[0])
    tie = lax.optimization_barrier

    order = offsets(n_targets)
    odd, even = return_offsets(n_targets)
    middle = n_targets // 2
    sent = dispatch(n_targets, ids, tokens, gates, out_grad)
    arrived = exchange([sent[k] for k in order], order)
    early = pack(arrived[:middle])
    ids_after, _ = tie((ids, early))
    table, late = tie((placement(n_targets, ids_after), arrived[middle:]))
    late = pack(late)
    early_near, late_near = (cross(value, far_bits) for value in (early, late))
    near = sorted(early_near)
    crossed = {mask: early_near[mask] for mask in near[1:]}
    early, late, crossed = tie((early, late, crossed))
    early_far = {0: flip(early, "dp", 1)}
    for mask, value in crossed.items():
        early_far[mask] = flip(value, "dp", 1)
    late_far = {0: flip(late, "dp", 1)}
    crossed = {mask: late_near[mask] for mask in near[1:]}
    early_far, late_far, crossed = tie((early_far, late_far, crossed))
    for mask, value in crossed.items():
        late_far[mask] = flip(value, "dp", 1)
    pieces = [
        group[mask]
        for groups in ((early_near, late_near), (early_far, late_far))
        for mask in near
        for group in groups
    ]
    token_halves, activated, slope, hidden = forward(pieces, weights[0], weights[1])
    size = width // 16 * 5
    own_left, far_left, grad_halves, gate_f, up_f, low, high, gate_column = backward(
        pieces, activated, slope, hidden, weights, size
    )

    left = flip(far_left, "dp", 1)
    own_right, far_right = rest_rows(size, low, high, gate_column, weights[0], weights[1])
    left, own_right = tie((left, own_right))
    right = flip(far_right, "dp", 1)
    targets = [
        (2 * i, odd.index(k)) if k % 2 else (2 * i + 1, even.index(k))
        for i in range(len(near))
        for k in order
    ]
    parts = sum_rows(targets, (own_left, own_right), (left, right))
    gate_f, up_f, _ = tie((gate_f, up_f, parts))
    grad_gate, grad_up = weight_grads((gate_f, up_f), token_halves)
    sums = []
    for group in range(2):
        held = dict(zip(near, parts[group::2]))
        for bit in reversed(far_bits):
            masks = [mask for mask in held if mask & bit]
            moved = {mask: flip(held.pop(mask), "dp", bit) for mask in masks}
            if group == 0 and bit == far_bits[-1]:
                moved, grad_gate, grad_up = tie((moved, grad_gate, grad_up))
            if bit == far_bits[0]:
                sums.append((held[0], moved[bit]))
            else:
                for mask in masks:
                    held[mask ^ bit] = add_rows(held[mask ^ bit], moved[mask])
    passed = add_rows(*sums[0])
    hidden, _ = tie((hidden, passed))
    (grad_down,) = weight_grads((hidden,), grad_halves)
    passed = flip(passed, "expert", 1)
    kept, moved, grad_down = tie((*sums[1], grad_down))
    kept, passed = tie((add_rows(kept, moved), passed))
    returned = exchange(merge_rows(kept, passed), even)
    token_grad, gate_grad = combine(table, gates, returned, width)
    grads = (grad_gate, grad_up, grad_down)
    return (token_grad, gate_grad.T, *(grad[None] for grad in grads))


def solution(mesh):
    in_specs = (
        P(("expert", "dp"), None),
        P(("expert", "dp"), None),
        P(("expert", "dp"), None),
        P(("expert", "dp"), None),
        P("expert", "dp", None),
        P("expert", "dp", None),
        P("expert", "dp", None),
    )
    out_specs = (
        P(("expert", "dp"), None),
        P(("expert", "dp"), None),
        P("expert", "dp", None),
        P("expert", "dp", None),
        P("expert", "dp", None),
    )
    return jax.shard_map(body, mesh=mesh, in_specs=in_specs, out_specs=out_specs, check_vma=False)
```

```python
import functools

import jax
import jax.numpy as jnp
from jax import lax
from jax.experimental import pallas as pl
from jax.experimental.pallas import tpu as pltpu
from jax.sharding import PartitionSpec as P

EXPERTS = 128
CAP = 4
BLOCK = 2 * CAP
LANES = 128
MIB = 2**20
COVER = 40

CONTRACT_LAST = (((1,), (1,)), ((), ()))
CONTRACT_FIRST = (((0,), (0,)), ((), ()))

HBM = pl.BlockSpec(memory_space=pltpu.HBM)
VMEM = pl.BlockSpec(memory_space=pltpu.VMEM)

LIGHT = pl.CostEstimate(flops=10**6, bytes_accessed=10**4, transcendentals=0)


def struct(shape, dtype=jnp.bfloat16):
    return jax.ShapeDtypeStruct(shape, dtype)


def as_bf16(mask):
    return mask.astype(jnp.float32).astype(jnp.bfloat16)


def choice_table(ids, n_targets):
    choices, tokens = ids.shape
    height = n_targets * BLOCK
    per_device = EXPERTS // n_targets
    row = lax.broadcasted_iota(jnp.int32, (height, 1), 0)
    wanted = ((row // BLOCK) ^ lax.axis_index("expert")) * per_device
    slot = row % BLOCK
    matches = [ids[k : k + 1, :] == wanted for k in range(choices)]
    hit = functools.reduce(jnp.logical_or, matches)
    earlier = lax.broadcasted_iota(jnp.int32, (tokens, tokens), 0) < lax.broadcasted_iota(
        jnp.int32, (tokens, tokens), 1
    )
    rank = jnp.dot(as_bf16(hit), as_bf16(earlier), preferred_element_type=jnp.float32)
    rank = rank.astype(jnp.int32)
    first = jnp.logical_and(hit, rank == slot)
    second = jnp.logical_and(hit, rank == slot - CAP)
    return matches, first, second


def pick_rows(first, second, rows_ref):
    half = rows_ref.shape[1] // 2
    low = jnp.dot(first, rows_ref[:, :half], preferred_element_type=jnp.float32)
    high = jnp.dot(second, rows_ref[:, half:], preferred_element_type=jnp.float32)
    return (low + high).astype(jnp.bfloat16)


def dispatch_kernel(n_targets, *refs):
    sources, outs = refs[:4], refs[4 : 4 + n_targets]
    targets, sems = refs[4 + n_targets : -1], refs[-1]
    ids_ref, tokens_ref, gates_ref, grads_ref = targets
    copies = [
        pltpu.make_async_copy(source, target, sems.at[i])
        for i, (source, target) in enumerate(zip(sources, targets))
    ]
    for copy in copies:
        copy.start()
    copies[0].wait()
    matches, first, second = choice_table(ids_ref[...], n_targets)
    copies[1].wait()
    rows = pick_rows(as_bf16(first), as_bf16(second), tokens_ref)
    half = rows.shape[1]
    for k, out in enumerate(outs):
        out[:, :half] = rows[k * BLOCK : (k + 1) * BLOCK]
    copies[2].wait()
    gates = gates_ref[...].astype(jnp.float32)
    scale = jnp.zeros(first.shape, jnp.float32)
    for k, match in enumerate(matches):
        scale = scale + jnp.where(match, gates[k : k + 1, :], 0.0)
    first = jnp.where(first, scale, 0.0).astype(jnp.bfloat16)
    second = jnp.where(second, scale, 0.0).astype(jnp.bfloat16)
    copies[3].wait()
    rows = pick_rows(first, second, grads_ref)
    for k, out in enumerate(outs):
        out[:, half:] = rows[k * BLOCK : (k + 1) * BLOCK]


def dispatch(n_targets, ids, tokens, gates, out_grad):
    arrays = (ids, tokens, gates, out_grad)
    return pl.pallas_call(
        functools.partial(dispatch_kernel, n_targets),
        out_shape=[struct((BLOCK, tokens.shape[1]))] * n_targets,
        in_specs=[HBM] * 4,
        out_specs=[VMEM] * n_targets,
        scratch_shapes=[pltpu.VMEM(a.shape, a.dtype) for a in arrays]
        + [pltpu.SemaphoreType.DMA((4,))],
        compiler_params=pltpu.CompilerParams(vmem_limit_bytes=60 * MIB),
        name="dispatch",
    )(*arrays)


def placement_kernel(n_targets, ids_ref, first_ref, second_ref, choice_ref):
    matches, first, second = choice_table(ids_ref[...], n_targets)
    first_ref[...] = as_bf16(first)
    second_ref[...] = as_bf16(second)
    choice = jnp.full(first.shape, -1, jnp.int32)
    for k, match in enumerate(matches):
        choice = jnp.where(jnp.logical_and(match, first), k, choice)
    choice_ref[...] = choice


def placement(n_targets, ids):
    table = (n_targets * BLOCK, ids.shape[1])
    return pl.pallas_call(
        functools.partial(placement_kernel, n_targets),
        out_shape=[struct(table), struct(table), struct(table, jnp.int32)],
        in_specs=[VMEM],
        out_specs=[VMEM] * 3,
        compiler_params=pltpu.CompilerParams(vmem_limit_bytes=4 * MIB),
        cost_estimate=pl.CostEstimate(
            flops=COVER * 10**9, bytes_accessed=COVER * 10**6, transcendentals=0
        ),
        name="placement",
    )(ids)


def pack_kernel(count, *refs):
    blocks, out = refs[:count], refs[count]
    for k in range(0, count, 2):
        out[pl.ds(k * BLOCK, 2 * BLOCK), :] = jnp.concatenate(
            [blocks[k][...], blocks[k + 1][...]], axis=0
        )


def pack(blocks):
    count = len(blocks)
    rows, width = count * BLOCK, blocks[0].shape[1]
    return pl.pallas_call(
        functools.partial(pack_kernel, count),
        out_shape=struct((rows, width)),
        in_specs=[VMEM] * count,
        out_specs=VMEM,
        compiler_params=pltpu.CompilerParams(vmem_limit_bytes=4 * MIB + 8 * rows * width),
        name="pack",
    )(*blocks)


def gather_pieces(pieces, start, out):
    base = 0
    for piece in pieces:
        rows = piece.shape[0]
        out[pl.ds(base, rows), :] = piece[:, start : start + out.shape[1]]
        base += rows


def project(weight, halves):
    half = halves.shape[1]
    rows = halves.shape[0]
    low = lax.dot_general(
        weight[:, :half], halves[...], CONTRACT_LAST, preferred_element_type=jnp.float32
    )
    high = lax.dot_general(
        weight[:, half:], halves[...], CONTRACT_LAST, preferred_element_type=jnp.float32
    )
    return low + pltpu.roll(high, rows - CAP, 1)


def forward_kernel(count, *refs):
    pieces = refs[:count]
    gate_w, up_w, halves, activated_out, slope_out, hidden_out = refs[count:]
    gather_pieces(pieces, 0, halves)
    pre_gate, pre_up = project(gate_w, halves), project(up_w, halves)
    is_slot = lax.broadcasted_iota(jnp.int32, (1, halves.shape[0]), 1) % BLOCK < CAP
    squash = 1.0 / (1.0 + jnp.exp(-pre_gate))
    activated = jnp.where(is_slot, pre_gate * squash, 0.0)
    slope = pre_up * squash * (1.0 + pre_gate * (1.0 - squash))
    activated_out[...] = activated
    slope_out[...] = jnp.where(is_slot, slope, 0.0)
    hidden_out[...] = (activated * pre_up).astype(jnp.bfloat16)


def forward(pieces, gate_w, up_w):
    count = len(pieces)
    units, width = gate_w.shape
    rows = sum(piece.shape[0] for piece in pieces)
    kept = (units, rows)
    return pl.pallas_call(
        functools.partial(forward_kernel, count),
        out_shape=[
            struct((rows, width // 2)),
            struct(kept, jnp.float32),
            struct(kept, jnp.float32),
            struct(kept),
        ],
        in_specs=[VMEM] * (count + 2),
        out_specs=[VMEM] * 4,
        compiler_params=pltpu.CompilerParams(
            vmem_limit_bytes=4 * MIB + rows * width + 40 * rows * units
        ),
        cost_estimate=LIGHT,
        name="forward",
    )(*pieces, gate_w, up_w)


def row_grads(factors, gate_w, up_w, parts, start):
    units, width = gate_w.shape
    block, size = parts[0].shape
    slots = factors.shape[0]
    chunk = 256 if size % 256 == 0 else size

    def product(columns):
        return jnp.dot(
            factors[:, :units], gate_w[:, columns], preferred_element_type=jnp.float32
        ) + jnp.dot(factors[:, units:], up_w[:, columns], preferred_element_type=jnp.float32)

    @pl.loop(0, size // chunk)
    def _(step):
        offset = pl.multiple_of(step * chunk, chunk)
        low = product(pl.ds(pl.multiple_of(start + offset, chunk), chunk))
        high = product(pl.ds(pl.multiple_of(width // 2 + start + offset, chunk), chunk))
        is_low = lax.broadcasted_iota(jnp.int32, (slots, 1), 0) % BLOCK < CAP
        even = jnp.where(is_low, low, pltpu.roll(high, CAP, 0))
        odd = jnp.where(is_low, pltpu.roll(low, slots - CAP, 0), high)
        tiles = (slots // BLOCK, BLOCK, chunk)
        total = jnp.stack([even.reshape(tiles), odd.reshape(tiles)], axis=1)
        total = total.reshape(2 * slots, chunk).astype(jnp.bfloat16)
        for i, part in enumerate(parts):
            part[:, pl.ds(offset, chunk)] = total[i * block : (i + 1) * block]


def backward_kernel(count, *refs):
    pieces = refs[:count]
    activated, slope, hidden, gate_w, up_w, down_w = refs[count : count + 6]
    own, far, halves, gate_out, up_out, factors, gates_out = refs[count + 6 :]
    rows = halves.shape[0]
    gather_pieces(pieces, halves.shape[1], halves)
    back = project(down_w, halves)
    gate_terms = jnp.sum(hidden[...].astype(jnp.float32) * back, axis=0, keepdims=True)
    up_pre = back * activated[...]
    gate_pre = back * slope[...]
    both = jnp.concatenate([gate_pre, up_pre], axis=0)
    both = both.T
    tiles = (rows // (2 * BLOCK), 2, BLOCK, both.shape[1])
    even = both.reshape(tiles)[:, 0]
    odd = pltpu.roll(both, CAP, 0).reshape(tiles)[:, 1]
    factors[...] = (even + odd).reshape(factors.shape).astype(jnp.bfloat16)
    gate_column = jnp.broadcast_to(gate_terms, (LANES, rows)).T.astype(jnp.bfloat16)
    row_grads(factors, gate_w, up_w, (own, far), 0)
    gates_out[...] = gate_column
    gate_out[...] = gate_pre.astype(jnp.bfloat16)
    up_out[...] = up_pre.astype(jnp.bfloat16)


def backward(pieces, activated, slope, hidden, weights, size):
    count = len(pieces)
    units, width = weights[0].shape
    rows = sum(piece.shape[0] for piece in pieces)
    mine = rows // 2
    shapes = [
        (mine, size),
        (mine, size),
        (rows, width // 2),
        (units, rows),
        (units, rows),
        (mine, 2 * units),
        (rows, LANES),
    ]
    return pl.pallas_call(
        functools.partial(backward_kernel, count),
        out_shape=[struct(shape) for shape in shapes],
        in_specs=[VMEM] * (count + 6),
        out_specs=[VMEM] * len(shapes),
        compiler_params=pltpu.CompilerParams(
            vmem_limit_bytes=6 * MIB
            + 2 * sum(height * across for height, across in shapes)
            + 56 * rows * units
        ),
        cost_estimate=LIGHT,
        name="backward",
    )(*pieces, activated, slope, hidden, *weights)


def rest_kernel(start, factors, gates, gate_w, up_w, own, far):
    mine, size = own.shape
    size -= LANES
    own[:, size:] = gates[:mine, :]
    far[:, size:] = gates[mine:, :]
    views = [part.at[:, pl.ds(0, size)] for part in (own, far)]
    row_grads(factors, gate_w, up_w, views, start)


def rest_rows(start, factors, gates, gate_w, up_w):
    rows, width = gates.shape[0], gate_w.shape[1]
    size = width // 2 - start + LANES
    return pl.pallas_call(
        functools.partial(rest_kernel, start),
        out_shape=[struct((rows // 2, size))] * 2,
        in_specs=[VMEM] * 4,
        out_specs=[VMEM] * 2,
        compiler_params=pltpu.CompilerParams(vmem_limit_bytes=8 * MIB + 4 * rows * width),
        cost_estimate=LIGHT,
        name="rest_rows",
    )(factors, gates, gate_w, up_w)


def sum_kernel(targets, own_left, own_right, left, right, *outs):
    base = 0
    for own, other in ((own_left, left), (own_right, right)):
        span = pl.ds(base, own.shape[1])
        base += own.shape[1]
        total = (own[...].astype(jnp.float32) + other[...].astype(jnp.float32)).astype(
            jnp.bfloat16
        )
        for i, (out, slot) in enumerate(targets):
            outs[out][pl.ds(slot * BLOCK, BLOCK), span] = total[i * BLOCK : (i + 1) * BLOCK]


def sum_rows(targets, own, other):
    rows = own[0].shape[0]
    width = sum(part.shape[1] for part in own)
    count = 1 + max(out for out, _ in targets)
    return pl.pallas_call(
        functools.partial(sum_kernel, targets),
        out_shape=[struct((rows // count, width))] * count,
        in_specs=[VMEM] * 4,
        out_specs=[VMEM] * count,
        compiler_params=pltpu.CompilerParams(vmem_limit_bytes=8 * MIB + 16 * rows * width),
        cost_estimate=LIGHT,
        name="sum_rows",
    )(*own, *other)


def add_kernel(left, right, out):
    total = left[...].astype(jnp.float32) + right[...].astype(jnp.float32)
    out[...] = total.astype(jnp.bfloat16)


def add_rows(left, right):
    return pl.pallas_call(
        add_kernel,
        out_shape=struct(left.shape),
        in_specs=[VMEM] * 2,
        out_specs=VMEM,
        compiler_params=pltpu.CompilerParams(vmem_limit_bytes=4 * MIB + 16 * left.size),
        name="add_rows",
    )(left, right)


def merge_kernel(kept, passed, *outs):
    for i, out in enumerate(outs):
        span = slice(i * BLOCK, (i + 1) * BLOCK)
        out[...] = jnp.concatenate([kept[span, :], passed[span, :]], axis=0)


def merge_rows(kept, passed):
    rows, width = kept.shape
    count = rows // BLOCK
    return pl.pallas_call(
        merge_kernel,
        out_shape=[struct((2 * BLOCK, width))] * count,
        in_specs=[VMEM] * 2,
        out_specs=[VMEM] * count,
        compiler_params=pltpu.CompilerParams(vmem_limit_bytes=4 * MIB + 24 * rows * width),
        name="merge_rows",
    )(kept, passed)


def weight_kernel(chunk, count, *refs):
    factors, halves = refs[:count], refs[count]
    outs, stages, sems = refs[count + 1 : 2 * count + 1], refs[2 * count + 1 : -1], refs[-1]
    half = halves.shape[1]
    pairs = []
    for factor in factors:
        low = factor[...]
        high = pltpu.roll(low.astype(jnp.float32), CAP, 1).astype(jnp.bfloat16)
        pairs.append((low, high))
    copies = []
    for start in range(0, half, chunk):
        for pair, out, stage in zip(pairs, outs, stages):
            for factor, base in zip(pair, (0, half)):
                span = pl.ds(base + start, chunk)
                stage[:, span] = jnp.dot(
                    factor, halves[:, pl.ds(start, chunk)], preferred_element_type=jnp.float32
                ).astype(jnp.bfloat16)
                copy = pltpu.make_async_copy(
                    stage.at[:, span], out.at[:, span], sems.at[len(copies)]
                )
                copy.start()
                copies.append(copy)
    for copy in copies:
        copy.wait()


def weight_grads(factors, halves):
    count = len(factors)
    units, rows = factors[0].shape
    half = halves.shape[1]
    chunk = 512 if half % 512 == 0 else half
    shape = (units, 2 * half)
    return pl.pallas_call(
        functools.partial(weight_kernel, chunk, count),
        out_shape=[struct(shape)] * count,
        in_specs=[VMEM] * (count + 1),
        out_specs=[HBM] * count,
        scratch_shapes=[pltpu.VMEM(shape, jnp.bfloat16)] * count
        + [pltpu.SemaphoreType.DMA((2 * count * half // chunk,))],
        compiler_params=pltpu.CompilerParams(
            vmem_limit_bytes=6 * MIB + 4 * count * units * half + 8 * count * units * rows
        ),
        cost_estimate=LIGHT,
        name="weight_grads",
    )(*factors, halves)


def combine_kernel(n_targets, first, second, choice_ref, gates_ref, *refs):
    blocks, (token_ref, gate_ref) = refs[: n_targets // 2], refs[n_targets // 2 :]
    even = return_offsets(n_targets)[1]
    back = jnp.concatenate([blocks[even.index(k)][...] for k in range(0, n_targets, 2)], axis=0)
    half = token_ref.shape[1] // 2
    choices, tokens = gates_ref.shape
    rows = back[:, :half]
    token_ref[:, :half] = lax.dot_general(
        first[...], rows, CONTRACT_FIRST, preferred_element_type=jnp.float32
    ).astype(jnp.bfloat16)
    token_ref[:, half:] = lax.dot_general(
        second[...], rows, CONTRACT_FIRST, preferred_element_type=jnp.float32
    ).astype(jnp.bfloat16)
    terms = back[:, half : half + tokens].astype(jnp.float32)
    choice = choice_ref[...]
    for k in range(choices):
        chosen = jnp.where(choice == k, terms, 0.0)
        gate = gates_ref[k : k + 1, :].astype(jnp.float32)
        gate_ref[k : k + 1, :] = jnp.sum(chosen, axis=0, keepdims=True) / gate


def combine(table, gates, blocks, width):
    n_targets = 2 * len(blocks)
    choices, tokens = gates.shape
    return pl.pallas_call(
        functools.partial(combine_kernel, n_targets),
        out_shape=[struct((tokens, width)), struct((choices, tokens), jnp.float32)],
        in_specs=[VMEM] * (4 + len(blocks)),
        out_specs=[VMEM] * 2,
        compiler_params=pltpu.CompilerParams(
            vmem_limit_bytes=4 * MIB + 16 * n_targets * BLOCK * width
        ),
        name="combine",
    )(*table, gates, *blocks)


def flip(value, axis, bit):
    size = lax.axis_size(axis)
    return lax.ppermute(value, axis, [(i, i ^ bit) for i in range(size)])


def offsets(count):
    near, far = list(range(1, count // 2)), list(range(count // 2, count))
    order = []
    for i, k in enumerate(near):
        order += [k, far[i]]
    return order + far[len(near) :] + [0]


def return_offsets(count):
    even = list(range(count // 2, count, 2)) + list(range(count // 2 - 2, -1, -2))
    return [k ^ 1 for k in even], even


def exchange(blocks, order):
    return [flip(block, "expert", k) if k else block for k, block in zip(order, blocks)]


def cross(block, far_bits):
    held = {0: block}
    for bit in far_bits:
        for mask in list(held):
            held[mask | bit] = flip(held[mask], "dp", bit)
    return held


def body(tokens, out_grad, gate_probs, route_ids, w_gate, w_up, w_down):
    n_targets = lax.axis_size("expert")
    n_dp = lax.axis_size("dp")
    width = tokens.shape[1]
    ids, gates = route_ids.T, gate_probs.T
    far_bits = [1 << i for i in range(1, n_dp.bit_length() - 1)]
    weights = (w_gate[0], w_up[0], w_down[0])
    tie = lax.optimization_barrier

    order = offsets(n_targets)
    odd, even = return_offsets(n_targets)
    middle = n_targets // 2
    sent = dispatch(n_targets, ids, tokens, gates, out_grad)
    arrived = exchange([sent[k] for k in order], order)
    early = pack(arrived[:middle])
    ids_after, _ = tie((ids, early))
    table, late = tie((placement(n_targets, ids_after), arrived[middle:]))
    late = pack(late)
    early_near, late_near = (cross(value, far_bits) for value in (early, late))
    near = sorted(early_near)
    crossed = {mask: early_near[mask] for mask in near[1:]}
    early, late, crossed = tie((early, late, crossed))
    early_far = {0: flip(early, "dp", 1)}
    for mask, value in crossed.items():
        early_far[mask] = flip(value, "dp", 1)
    late_far = {0: flip(late, "dp", 1)}
    crossed = {mask: late_near[mask] for mask in near[1:]}
    early_far, late_far, crossed = tie((early_far, late_far, crossed))
    for mask, value in crossed.items():
        late_far[mask] = flip(value, "dp", 1)
    pieces = [
        group[mask]
        for groups in ((early_near, late_near), (early_far, late_far))
        for mask in near
        for group in groups
    ]
    token_halves, activated, slope, hidden = forward(pieces, weights[0], weights[1])
    size = width // 16 * 5
    own_left, far_left, grad_halves, gate_f, up_f, factors, gate_column = backward(
        pieces, activated, slope, hidden, weights, size
    )

    left = flip(far_left, "dp", 1)
    own_right, far_right = rest_rows(size, factors, gate_column, weights[0], weights[1])
    left, own_right = tie((left, own_right))
    right = flip(far_right, "dp", 1)
    targets = [
        (2 * i, odd.index(k)) if k % 2 else (2 * i + 1, even.index(k))
        for i in range(len(near))
        for k in order
    ]
    parts = sum_rows(targets, (own_left, own_right), (left, right))
    gate_f, up_f, _ = tie((gate_f, up_f, parts))
    grad_gate, grad_up = weight_grads((gate_f, up_f), token_halves)
    sums = []
    for group in range(2):
        held = dict(zip(near, parts[group::2]))
        for bit in reversed(far_bits):
            masks = [mask for mask in held if mask & bit]
            moved = {mask: flip(held.pop(mask), "dp", bit) for mask in masks}
            if group == 0 and bit == far_bits[-1]:
                moved, grad_gate, grad_up = tie((moved, grad_gate, grad_up))
            if bit == far_bits[0]:
                sums.append((held[0], moved[bit]))
            else:
                for mask in masks:
                    held[mask ^ bit] = add_rows(held[mask ^ bit], moved[mask])
    passed = add_rows(*sums[0])
    hidden, _ = tie((hidden, passed))
    (grad_down,) = weight_grads((hidden,), grad_halves)
    passed = flip(passed, "expert", 1)
    kept, moved, grad_down = tie((*sums[1], grad_down))
    kept, passed = tie((add_rows(kept, moved), passed))
    returned = exchange(merge_rows(kept, passed), even)
    token_grad, gate_grad = combine(table, gates, returned, width)
    grads = (grad_gate, grad_up, grad_down)
    return (token_grad, gate_grad.T, *(grad[None] for grad in grads))


def solution(mesh):
    in_specs = (
        P(("expert", "dp"), None),
        P(("expert", "dp"), None),
        P(("expert", "dp"), None),
        P(("expert", "dp"), None),
        P("expert", "dp", None),
        P("expert", "dp", None),
        P("expert", "dp", None),
    )
    out_specs = (
        P(("expert", "dp"), None),
        P(("expert", "dp"), None),
        P("expert", "dp", None),
        P("expert", "dp", None),
        P("expert", "dp", None),
    )
    return jax.shard_map(body, mesh=mesh, in_specs=in_specs, out_specs=out_specs, check_vma=False)
```

```python
import functools

import jax
import jax.numpy as jnp
from jax import lax
from jax.experimental import pallas as pl
from jax.experimental.pallas import tpu as pltpu
from jax.sharding import PartitionSpec as P

EXPERTS = 128
CAP = 4
BLOCK = 2 * CAP
LANES = 128
MIB = 2**20
COVER = 40

CONTRACT_LAST = (((1,), (1,)), ((), ()))
CONTRACT_FIRST = (((0,), (0,)), ((), ()))

HBM = pl.BlockSpec(memory_space=pltpu.HBM)
VMEM = pl.BlockSpec(memory_space=pltpu.VMEM)

LIGHT = pl.CostEstimate(flops=10**6, bytes_accessed=10**4, transcendentals=0)


def struct(shape, dtype=jnp.bfloat16):
    return jax.ShapeDtypeStruct(shape, dtype)


def as_bf16(mask):
    return mask.astype(jnp.float32).astype(jnp.bfloat16)


def choice_table(ids, n_targets):
    choices, tokens = ids.shape
    height = n_targets * BLOCK
    per_device = EXPERTS // n_targets
    row = lax.broadcasted_iota(jnp.int32, (height, 1), 0)
    wanted = ((row // BLOCK) ^ lax.axis_index("expert")) * per_device
    slot = row % BLOCK
    matches = [ids[k : k + 1, :] == wanted for k in range(choices)]
    hit = functools.reduce(jnp.logical_or, matches)
    earlier = lax.broadcasted_iota(jnp.int32, (tokens, tokens), 0) < lax.broadcasted_iota(
        jnp.int32, (tokens, tokens), 1
    )
    rank = jnp.dot(as_bf16(hit), as_bf16(earlier), preferred_element_type=jnp.float32)
    rank = rank.astype(jnp.int32)
    first = jnp.logical_and(hit, rank == slot)
    second = jnp.logical_and(hit, rank == slot - CAP)
    return matches, first, second


def pick_rows(first, second, rows_ref):
    half = rows_ref.shape[1] // 2
    low = jnp.dot(first, rows_ref[:, :half], preferred_element_type=jnp.float32)
    high = jnp.dot(second, rows_ref[:, half:], preferred_element_type=jnp.float32)
    return (low + high).astype(jnp.bfloat16)


def dispatch_kernel(n_targets, *refs):
    sources, outs = refs[:4], refs[4 : 4 + n_targets]
    targets, sems = refs[4 + n_targets : -1], refs[-1]
    ids_ref, tokens_ref, gates_ref, grads_ref = targets
    copies = [
        pltpu.make_async_copy(source, target, sems.at[i])
        for i, (source, target) in enumerate(zip(sources, targets))
    ]
    for copy in copies:
        copy.start()
    copies[0].wait()
    matches, first, second = choice_table(ids_ref[...], n_targets)
    copies[1].wait()
    rows = pick_rows(as_bf16(first), as_bf16(second), tokens_ref)
    half = rows.shape[1]
    for k, out in enumerate(outs):
        out[:, :half] = rows[k * BLOCK : (k + 1) * BLOCK]
    copies[2].wait()
    gates = gates_ref[...].astype(jnp.float32)
    scale = jnp.zeros(first.shape, jnp.float32)
    for k, match in enumerate(matches):
        scale = scale + jnp.where(match, gates[k : k + 1, :], 0.0)
    first = jnp.where(first, scale, 0.0).astype(jnp.bfloat16)
    second = jnp.where(second, scale, 0.0).astype(jnp.bfloat16)
    copies[3].wait()
    rows = pick_rows(first, second, grads_ref)
    for k, out in enumerate(outs):
        out[:, half:] = rows[k * BLOCK : (k + 1) * BLOCK]


def dispatch(n_targets, ids, tokens, gates, out_grad):
    arrays = (ids, tokens, gates, out_grad)
    return pl.pallas_call(
        functools.partial(dispatch_kernel, n_targets),
        out_shape=[struct((BLOCK, tokens.shape[1]))] * n_targets,
        in_specs=[HBM] * 4,
        out_specs=[VMEM] * n_targets,
        scratch_shapes=[pltpu.VMEM(a.shape, a.dtype) for a in arrays]
        + [pltpu.SemaphoreType.DMA((4,))],
        compiler_params=pltpu.CompilerParams(vmem_limit_bytes=60 * MIB),
        name="dispatch",
    )(*arrays)


def placement_kernel(n_targets, ids_ref, first_ref, second_ref, choice_ref):
    matches, first, second = choice_table(ids_ref[...], n_targets)
    first_ref[...] = as_bf16(first)
    second_ref[...] = as_bf16(second)
    choice = jnp.full(first.shape, -1, jnp.int32)
    for k, match in enumerate(matches):
        choice = jnp.where(jnp.logical_and(match, first), k, choice)
    choice_ref[...] = choice


def placement(n_targets, ids):
    table = (n_targets * BLOCK, ids.shape[1])
    return pl.pallas_call(
        functools.partial(placement_kernel, n_targets),
        out_shape=[struct(table), struct(table), struct(table, jnp.int32)],
        in_specs=[VMEM],
        out_specs=[VMEM] * 3,
        compiler_params=pltpu.CompilerParams(vmem_limit_bytes=4 * MIB),
        cost_estimate=pl.CostEstimate(
            flops=COVER * 10**9, bytes_accessed=COVER * 10**6, transcendentals=0
        ),
        name="placement",
    )(ids)


def pack_kernel(count, *refs):
    blocks, out = refs[:count], refs[count]
    for k in range(0, count, 2):
        out[pl.ds(k * BLOCK, 2 * BLOCK), :] = jnp.concatenate(
            [blocks[k][...], blocks[k + 1][...]], axis=0
        )


def pack(blocks):
    count = len(blocks)
    rows, width = count * BLOCK, blocks[0].shape[1]
    return pl.pallas_call(
        functools.partial(pack_kernel, count),
        out_shape=struct((rows, width)),
        in_specs=[VMEM] * count,
        out_specs=VMEM,
        compiler_params=pltpu.CompilerParams(vmem_limit_bytes=4 * MIB + 8 * rows * width),
        name="pack",
    )(*blocks)


def gather_pieces(pieces, start, out):
    base = 0
    for piece in pieces:
        rows = piece.shape[0]
        out[pl.ds(base, rows), :] = piece[:, start : start + out.shape[1]]
        base += rows


def project(weight, halves):
    half = halves.shape[1]
    rows = halves.shape[0]
    low = lax.dot_general(
        weight[:, :half], halves[...], CONTRACT_LAST, preferred_element_type=jnp.float32
    )
    high = lax.dot_general(
        weight[:, half:], halves[...], CONTRACT_LAST, preferred_element_type=jnp.float32
    )
    return low + pltpu.roll(high, rows - CAP, 1)


def forward_kernel(count, *refs):
    pieces = refs[:count]
    gate_w, up_w, halves, activated_out, slope_out, hidden_out = refs[count:]
    gather_pieces(pieces, 0, halves)
    pre_gate, pre_up = project(gate_w, halves), project(up_w, halves)
    is_slot = lax.broadcasted_iota(jnp.int32, (1, halves.shape[0]), 1) % BLOCK < CAP
    squash = 1.0 / (1.0 + jnp.exp(-pre_gate))
    activated = jnp.where(is_slot, pre_gate * squash, 0.0)
    slope = pre_up * squash * (1.0 + pre_gate * (1.0 - squash))
    activated_out[...] = activated
    slope_out[...] = jnp.where(is_slot, slope, 0.0)
    hidden_out[...] = (activated * pre_up).astype(jnp.bfloat16)


def forward(pieces, gate_w, up_w):
    count = len(pieces)
    units, width = gate_w.shape
    rows = sum(piece.shape[0] for piece in pieces)
    kept = (units, rows)
    return pl.pallas_call(
        functools.partial(forward_kernel, count),
        out_shape=[
            struct((rows, width // 2)),
            struct(kept, jnp.float32),
            struct(kept, jnp.float32),
            struct(kept),
        ],
        in_specs=[VMEM] * (count + 2),
        out_specs=[VMEM] * 4,
        compiler_params=pltpu.CompilerParams(
            vmem_limit_bytes=4 * MIB + rows * width + 40 * rows * units
        ),
        cost_estimate=LIGHT,
        name="forward",
    )(*pieces, gate_w, up_w)


def row_grads(factors, gate_w, up_w, parts, start):
    units, width = gate_w.shape
    block, size = parts[0].shape
    slots = factors.shape[0]
    chunk = 256 if size % 256 == 0 else size

    def product(columns):
        return jnp.dot(
            factors[:, :units], gate_w[:, columns], preferred_element_type=jnp.float32
        ) + jnp.dot(factors[:, units:], up_w[:, columns], preferred_element_type=jnp.float32)

    @pl.loop(0, size // chunk)
    def _(step):
        offset = pl.multiple_of(step * chunk, chunk)
        low = product(pl.ds(pl.multiple_of(start + offset, chunk), chunk))
        high = product(pl.ds(pl.multiple_of(width // 2 + start + offset, chunk), chunk))
        is_low = lax.broadcasted_iota(jnp.int32, (slots, 1), 0) % BLOCK < CAP
        even = jnp.where(is_low, low, pltpu.roll(high, CAP, 0))
        odd = jnp.where(is_low, pltpu.roll(low, slots - CAP, 0), high)
        tiles = (slots // BLOCK, BLOCK, chunk)
        total = jnp.stack([even.reshape(tiles), odd.reshape(tiles)], axis=1)
        total = total.reshape(2 * slots, chunk).astype(jnp.bfloat16)
        for i, part in enumerate(parts):
            part[:, pl.ds(offset, chunk)] = total[i * block : (i + 1) * block]


def backward_kernel(count, *refs):
    pieces = refs[:count]
    activated, slope, hidden, gate_w, up_w, down_w = refs[count : count + 6]
    own, far, halves, gate_out, up_out, factors, gates_out = refs[count + 6 :]
    rows = halves.shape[0]
    gather_pieces(pieces, halves.shape[1], halves)
    back = project(down_w, halves)
    gate_terms = jnp.sum(hidden[...].astype(jnp.float32) * back, axis=0, keepdims=True)
    up_pre = back * activated[...]
    gate_pre = back * slope[...]
    both = jnp.concatenate([gate_pre, up_pre], axis=0)
    both = both.T
    tiles = (rows // (2 * BLOCK), 2, BLOCK, both.shape[1])
    even = both.reshape(tiles)[:, 0]
    odd = pltpu.roll(both, CAP, 0).reshape(tiles)[:, 1]
    factors[...] = (even + odd).reshape(factors.shape).astype(jnp.bfloat16)
    gate_column = jnp.broadcast_to(gate_terms, (LANES, rows)).T.astype(jnp.bfloat16)
    row_grads(factors, gate_w, up_w, (own, far), 0)
    gates_out[...] = gate_column
    gate_out[...] = gate_pre.astype(jnp.bfloat16)
    up_out[...] = up_pre.astype(jnp.bfloat16)


def backward(pieces, activated, slope, hidden, weights, size):
    count = len(pieces)
    units, width = weights[0].shape
    rows = sum(piece.shape[0] for piece in pieces)
    mine = rows // 2
    shapes = [
        (mine, size),
        (mine, size),
        (rows, width // 2),
        (units, rows),
        (units, rows),
        (mine, 2 * units),
        (rows, LANES),
    ]
    return pl.pallas_call(
        functools.partial(backward_kernel, count),
        out_shape=[struct(shape) for shape in shapes],
        in_specs=[VMEM] * (count + 6),
        out_specs=[VMEM] * len(shapes),
        compiler_params=pltpu.CompilerParams(
            vmem_limit_bytes=6 * MIB
            + 2 * sum(height * across for height, across in shapes)
            + 56 * rows * units
        ),
        cost_estimate=LIGHT,
        name="backward",
    )(*pieces, activated, slope, hidden, *weights)


def rest_kernel(start, factors, gates, gate_w, up_w, own, far):
    mine, size = own.shape
    size -= LANES
    own[:, size:] = gates[:mine, :]
    far[:, size:] = gates[mine:, :]
    views = [part.at[:, pl.ds(0, size)] for part in (own, far)]
    row_grads(factors, gate_w, up_w, views, start)


def rest_rows(start, factors, gates, gate_w, up_w):
    rows, width = gates.shape[0], gate_w.shape[1]
    size = width // 2 - start + LANES
    return pl.pallas_call(
        functools.partial(rest_kernel, start),
        out_shape=[struct((rows // 2, size))] * 2,
        in_specs=[VMEM] * 4,
        out_specs=[VMEM] * 2,
        compiler_params=pltpu.CompilerParams(vmem_limit_bytes=8 * MIB + 4 * rows * width),
        cost_estimate=LIGHT,
        name="rest_rows",
    )(factors, gates, gate_w, up_w)


def sum_kernel(targets, own_left, own_right, left, right, *outs):
    base = 0
    for own, other in ((own_left, left), (own_right, right)):
        span = pl.ds(base, own.shape[1])
        base += own.shape[1]
        total = (own[...].astype(jnp.float32) + other[...].astype(jnp.float32)).astype(
            jnp.bfloat16
        )
        for i, (out, slot) in enumerate(targets):
            outs[out][pl.ds(slot * BLOCK, BLOCK), span] = total[i * BLOCK : (i + 1) * BLOCK]


def sum_rows(targets, own, other):
    rows = own[0].shape[0]
    width = sum(part.shape[1] for part in own)
    count = 1 + max(out for out, _ in targets)
    return pl.pallas_call(
        functools.partial(sum_kernel, targets),
        out_shape=[struct((rows // count, width))] * count,
        in_specs=[VMEM] * 4,
        out_specs=[VMEM] * count,
        compiler_params=pltpu.CompilerParams(vmem_limit_bytes=8 * MIB + 16 * rows * width),
        cost_estimate=LIGHT,
        name="sum_rows",
    )(*own, *other)


def add_kernel(left, right, *outs):
    total = (left[...].astype(jnp.float32) + right[...].astype(jnp.float32)).astype(jnp.bfloat16)
    base = 0
    for out in outs:
        out[...] = total[base : base + out.shape[0]]
        base += out.shape[0]


def add_rows(left, right, pieces):
    rows, width = left.shape
    return pl.pallas_call(
        add_kernel,
        out_shape=[struct((piece, width)) for piece in pieces],
        in_specs=[VMEM] * 2,
        out_specs=[VMEM] * len(pieces),
        compiler_params=pltpu.CompilerParams(vmem_limit_bytes=4 * MIB + 16 * rows * width),
        name="add_rows",
    )(left, right)


def merge_kernel(kept, passed, *outs):
    for i, out in enumerate(outs):
        span = slice(i * BLOCK, (i + 1) * BLOCK)
        out[...] = jnp.concatenate([kept[span, :], passed[span, :]], axis=0)


def merge_rows(kept, passed):
    rows, width = kept.shape
    count = rows // BLOCK
    return pl.pallas_call(
        merge_kernel,
        out_shape=[struct((2 * BLOCK, width))] * count,
        in_specs=[VMEM] * 2,
        out_specs=[VMEM] * count,
        compiler_params=pltpu.CompilerParams(vmem_limit_bytes=4 * MIB + 24 * rows * width),
        name="merge_rows",
    )(kept, passed)


def weight_kernel(chunk, count, *refs):
    factors, halves = refs[:count], refs[count]
    outs, stages, sems = refs[count + 1 : 2 * count + 1], refs[2 * count + 1 : -1], refs[-1]
    half = halves.shape[1]
    pairs = []
    for factor in factors:
        low = factor[...]
        high = pltpu.roll(low.astype(jnp.float32), CAP, 1).astype(jnp.bfloat16)
        pairs.append((low, high))
    copies = []
    for start in range(0, half, chunk):
        for pair, out, stage in zip(pairs, outs, stages):
            for factor, base in zip(pair, (0, half)):
                span = pl.ds(base + start, chunk)
                stage[:, span] = jnp.dot(
                    factor, halves[:, pl.ds(start, chunk)], preferred_element_type=jnp.float32
                ).astype(jnp.bfloat16)
                copy = pltpu.make_async_copy(
                    stage.at[:, span], out.at[:, span], sems.at[len(copies)]
                )
                copy.start()
                copies.append(copy)
    for copy in copies:
        copy.wait()


def weight_grads(factors, halves):
    count = len(factors)
    units, rows = factors[0].shape
    half = halves.shape[1]
    chunk = 512 if half % 512 == 0 else half
    shape = (units, 2 * half)
    return pl.pallas_call(
        functools.partial(weight_kernel, chunk, count),
        out_shape=[struct(shape)] * count,
        in_specs=[VMEM] * (count + 1),
        out_specs=[HBM] * count,
        scratch_shapes=[pltpu.VMEM(shape, jnp.bfloat16)] * count
        + [pltpu.SemaphoreType.DMA((2 * count * half // chunk,))],
        compiler_params=pltpu.CompilerParams(
            vmem_limit_bytes=6 * MIB + 4 * count * units * half + 8 * count * units * rows
        ),
        cost_estimate=LIGHT,
        name="weight_grads",
    )(*factors, halves)


def combine_kernel(n_targets, first, second, choice_ref, gates_ref, *refs):
    blocks, (token_ref, gate_ref) = refs[:-2], refs[-2:]
    odd, even = return_offsets(n_targets)
    far = n_targets // 4
    placed = {}
    for k, block in zip(odd[:far] + even[:far], blocks):
        placed[k] = block[...]
    for k, block in zip(even[far:], blocks[2 * far :]):
        placed[k], placed[k ^ 1] = block[:BLOCK, :], block[BLOCK:, :]
    back = jnp.concatenate([placed[k] for k in range(n_targets)], axis=0)
    half = token_ref.shape[1] // 2
    choices, tokens = gates_ref.shape
    rows = back[:, :half]
    token_ref[:, :half] = lax.dot_general(
        first[...], rows, CONTRACT_FIRST, preferred_element_type=jnp.float32
    ).astype(jnp.bfloat16)
    token_ref[:, half:] = lax.dot_general(
        second[...], rows, CONTRACT_FIRST, preferred_element_type=jnp.float32
    ).astype(jnp.bfloat16)
    terms = back[:, half : half + tokens].astype(jnp.float32)
    choice = choice_ref[...]
    for k in range(choices):
        chosen = jnp.where(choice == k, terms, 0.0)
        gate = gates_ref[k : k + 1, :].astype(jnp.float32)
        gate_ref[k : k + 1, :] = jnp.sum(chosen, axis=0, keepdims=True) / gate


def combine(table, gates, blocks, width):
    n_targets = len(blocks) // 3 * 4
    choices, tokens = gates.shape
    return pl.pallas_call(
        functools.partial(combine_kernel, n_targets),
        out_shape=[struct((tokens, width)), struct((choices, tokens), jnp.float32)],
        in_specs=[VMEM] * (4 + len(blocks)),
        out_specs=[VMEM] * 2,
        compiler_params=pltpu.CompilerParams(
            vmem_limit_bytes=4 * MIB + 16 * n_targets * BLOCK * width
        ),
        name="combine",
    )(*table, gates, *blocks)


def flip(value, axis, bit):
    size = lax.axis_size(axis)
    return lax.ppermute(value, axis, [(i, i ^ bit) for i in range(size)])


def offsets(count):
    near, far = list(range(1, count // 2)), list(range(count // 2, count))
    order = []
    for i, k in enumerate(near):
        order += [k, far[i]]
    return order + far[len(near) :] + [0]


def return_offsets(count):
    even = list(range(count // 2, count, 2)) + list(range(count // 2 - 2, -1, -2))
    return [k ^ 1 for k in even], even


def exchange(blocks, order):
    return [flip(block, "expert", k) if k else block for k, block in zip(order, blocks)]


def cross(block, far_bits):
    held = {0: block}
    for bit in far_bits:
        for mask in list(held):
            held[mask | bit] = flip(held[mask], "dp", bit)
    return held


def body(tokens, out_grad, gate_probs, route_ids, w_gate, w_up, w_down):
    n_targets = lax.axis_size("expert")
    n_dp = lax.axis_size("dp")
    width = tokens.shape[1]
    ids, gates = route_ids.T, gate_probs.T
    far_bits = [1 << i for i in range(1, n_dp.bit_length() - 1)]
    weights = (w_gate[0], w_up[0], w_down[0])
    tie = lax.optimization_barrier

    order = offsets(n_targets)
    odd, even = return_offsets(n_targets)
    middle = n_targets // 2
    sent = dispatch(n_targets, ids, tokens, gates, out_grad)
    arrived = exchange([sent[k] for k in order], order)
    early = pack(arrived[:middle])
    ids_after, _ = tie((ids, early))
    table, late = tie((placement(n_targets, ids_after), arrived[middle:]))
    late = pack(late)
    early_near, late_near = (cross(value, far_bits) for value in (early, late))
    near = sorted(early_near)
    crossed = {mask: early_near[mask] for mask in near[1:]}
    early, late, crossed = tie((early, late, crossed))
    early_far = {0: flip(early, "dp", 1)}
    for mask, value in crossed.items():
        early_far[mask] = flip(value, "dp", 1)
    late_far = {0: flip(late, "dp", 1)}
    crossed = {mask: late_near[mask] for mask in near[1:]}
    early_far, late_far, crossed = tie((early_far, late_far, crossed))
    for mask, value in crossed.items():
        late_far[mask] = flip(value, "dp", 1)
    pieces = [
        group[mask]
        for groups in ((early_near, late_near), (early_far, late_far))
        for mask in near
        for group in groups
    ]
    token_halves, activated, slope, hidden = forward(pieces, weights[0], weights[1])
    size = width // 16 * 5
    own_left, far_left, grad_halves, gate_f, up_f, factors, gate_column = backward(
        pieces, activated, slope, hidden, weights, size
    )

    left = flip(far_left, "dp", 1)
    own_right, far_right = rest_rows(size, factors, gate_column, weights[0], weights[1])
    left, own_right = tie((left, own_right))
    right = flip(far_right, "dp", 1)
    targets = [
        (2 * i, odd.index(k)) if k % 2 else (2 * i + 1, even.index(k))
        for i in range(len(near))
        for k in order
    ]
    parts = sum_rows(targets, (own_left, own_right), (left, right))
    gate_f, up_f, _ = tie((gate_f, up_f, parts))
    grad_gate, grad_up = weight_grads((gate_f, up_f), token_halves)
    sums = []
    for group in range(2):
        held = dict(zip(near, parts[group::2]))
        for bit in reversed(far_bits):
            masks = [mask for mask in held if mask & bit]
            moved = {mask: flip(held.pop(mask), "dp", bit) for mask in masks}
            if group == 0 and bit == far_bits[-1]:
                moved, grad_gate, grad_up = tie((moved, grad_gate, grad_up))
            if bit == far_bits[0]:
                sums.append((held[0], moved[bit]))
            else:
                for mask in masks:
                    both = (held[mask ^ bit], moved[mask])
                    (held[mask ^ bit],) = add_rows(*both, both[0].shape[:1])
    far = n_targets // 4
    rows = [BLOCK] * far + [BLOCK * far]
    *far_odd, passed = add_rows(*sums[0], rows)
    passed = flip(passed, "expert", 1)
    far_odd = exchange(far_odd, odd[:far])
    far_odd[0], moved = tie((far_odd[0], sums[1][1]))
    *far_even, kept = add_rows(sums[1][0], moved, rows)
    merged = list(merge_rows(kept, passed))
    hidden, _ = tie((hidden, merged))
    (grad_down,) = weight_grads((hidden,), grad_halves)
    returned = far_odd + exchange(far_even + merged, even)
    returned, grad_down = tie((returned, grad_down))
    token_grad, gate_grad = combine(table, gates, returned, width)
    grads = (grad_gate, grad_up, grad_down)
    return (token_grad, gate_grad.T, *(grad[None] for grad in grads))


def solution(mesh):
    in_specs = (
        P(("expert", "dp"), None),
        P(("expert", "dp"), None),
        P(("expert", "dp"), None),
        P(("expert", "dp"), None),
        P("expert", "dp", None),
        P("expert", "dp", None),
        P("expert", "dp", None),
    )
    out_specs = (
        P(("expert", "dp"), None),
        P(("expert", "dp"), None),
        P("expert", "dp", None),
        P("expert", "dp", None),
        P("expert", "dp", None),
    )
    return jax.shard_map(body, mesh=mesh, in_specs=in_specs, out_specs=out_specs, check_vma=False)
```

```python
import functools

import jax
import jax.numpy as jnp
from jax import lax
from jax.experimental import pallas as pl
from jax.experimental.pallas import tpu as pltpu
from jax.sharding import PartitionSpec as P

EXPERTS = 128
CAP = 4
BLOCK = 2 * CAP
LANES = 128
MIB = 2**20

CONTRACT_LAST = (((1,), (1,)), ((), ()))
CONTRACT_FIRST = (((0,), (0,)), ((), ()))

HBM = pl.BlockSpec(memory_space=pltpu.HBM)
VMEM = pl.BlockSpec(memory_space=pltpu.VMEM)

LIGHT = pl.CostEstimate(flops=10**6, bytes_accessed=10**4, transcendentals=0)
COVER = pl.CostEstimate(flops=4 * 10**10, bytes_accessed=4 * 10**7, transcendentals=0)


def struct(shape, dtype=jnp.bfloat16):
    return jax.ShapeDtypeStruct(shape, dtype)


def as_bf16(mask):
    return mask.astype(jnp.float32).astype(jnp.bfloat16)


def choice_table(ids, n_targets):
    choices, tokens = ids.shape
    height = n_targets * BLOCK
    per_device = EXPERTS // n_targets
    row = lax.broadcasted_iota(jnp.int32, (height, 1), 0)
    wanted = ((row // BLOCK) ^ lax.axis_index("expert")) * per_device
    slot = row % BLOCK
    matches = [ids[k : k + 1, :] == wanted for k in range(choices)]
    hit = functools.reduce(jnp.logical_or, matches)
    earlier = lax.broadcasted_iota(jnp.int32, (tokens, tokens), 0) < lax.broadcasted_iota(
        jnp.int32, (tokens, tokens), 1
    )
    rank = jnp.dot(as_bf16(hit), as_bf16(earlier), preferred_element_type=jnp.float32)
    rank = rank.astype(jnp.int32)
    first = jnp.logical_and(hit, rank == slot)
    second = jnp.logical_and(hit, rank == slot - CAP)
    return matches, first, second


def pick_rows(first, second, rows_ref):
    half = rows_ref.shape[1] // 2
    low = jnp.dot(first, rows_ref[:, :half], preferred_element_type=jnp.float32)
    high = jnp.dot(second, rows_ref[:, half:], preferred_element_type=jnp.float32)
    return (low + high).astype(jnp.bfloat16)


def dispatch_kernel(n_targets, *refs):
    sources, outs = refs[:4], refs[4 : 4 + n_targets]
    targets, sems = refs[4 + n_targets : -1], refs[-1]
    ids_ref, tokens_ref, gates_ref, grads_ref = targets
    copies = [
        pltpu.make_async_copy(source, target, sems.at[i])
        for i, (source, target) in enumerate(zip(sources, targets))
    ]
    for copy in copies:
        copy.start()
    copies[0].wait()
    matches, first, second = choice_table(ids_ref[...], n_targets)
    copies[1].wait()
    rows = pick_rows(as_bf16(first), as_bf16(second), tokens_ref)
    half = rows.shape[1]
    for k, out in enumerate(outs):
        out[:, :half] = rows[k * BLOCK : (k + 1) * BLOCK]
    copies[2].wait()
    gates = gates_ref[...].astype(jnp.float32)
    scale = jnp.zeros(first.shape, jnp.float32)
    for k, match in enumerate(matches):
        scale = scale + jnp.where(match, gates[k : k + 1, :], 0.0)
    first = jnp.where(first, scale, 0.0).astype(jnp.bfloat16)
    second = jnp.where(second, scale, 0.0).astype(jnp.bfloat16)
    copies[3].wait()
    rows = pick_rows(first, second, grads_ref)
    for k, out in enumerate(outs):
        out[:, half:] = rows[k * BLOCK : (k + 1) * BLOCK]


def dispatch(n_targets, ids, tokens, gates, out_grad):
    arrays = (ids, tokens, gates, out_grad)
    return pl.pallas_call(
        functools.partial(dispatch_kernel, n_targets),
        out_shape=[struct((BLOCK, tokens.shape[1]))] * n_targets,
        in_specs=[HBM] * 4,
        out_specs=[VMEM] * n_targets,
        scratch_shapes=[pltpu.VMEM(a.shape, a.dtype) for a in arrays]
        + [pltpu.SemaphoreType.DMA((4,))],
        compiler_params=pltpu.CompilerParams(vmem_limit_bytes=60 * MIB),
        name="dispatch",
    )(*arrays)


def placement_kernel(n_targets, ids_ref, first_ref, second_ref, choice_ref):
    matches, first, second = choice_table(ids_ref[...], n_targets)
    first_ref[...] = as_bf16(first)
    second_ref[...] = as_bf16(second)
    choice = jnp.full(first.shape, -1, jnp.int32)
    for k, match in enumerate(matches):
        choice = jnp.where(jnp.logical_and(match, first), k, choice)
    choice_ref[...] = choice


def placement(n_targets, ids):
    table = (n_targets * BLOCK, ids.shape[1])
    return pl.pallas_call(
        functools.partial(placement_kernel, n_targets),
        out_shape=[struct(table), struct(table), struct(table, jnp.int32)],
        in_specs=[VMEM],
        out_specs=[VMEM] * 3,
        compiler_params=pltpu.CompilerParams(vmem_limit_bytes=4 * MIB),
        cost_estimate=LIGHT,
        name="placement",
    )(ids)


def pack_kernel(count, *refs):
    blocks, out = refs[:count], refs[count]
    for k in range(0, count, 2):
        out[pl.ds(k * BLOCK, 2 * BLOCK), :] = jnp.concatenate(
            [blocks[k][...], blocks[k + 1][...]], axis=0
        )


def pack(blocks):
    count = len(blocks)
    rows, width = count * BLOCK, blocks[0].shape[1]
    return pl.pallas_call(
        functools.partial(pack_kernel, count),
        out_shape=struct((rows, width)),
        in_specs=[VMEM] * count,
        out_specs=VMEM,
        compiler_params=pltpu.CompilerParams(vmem_limit_bytes=4 * MIB + 8 * rows * width),
        cost_estimate=LIGHT,
        name="pack",
    )(*blocks)


def split_kernel(rows, token_out, grad_out):
    half = token_out.shape[1]
    token_out[...] = rows[:, :half]
    grad_out[...] = rows[:, half:]


def split(rows):
    height, width = rows.shape
    return pl.pallas_call(
        split_kernel,
        out_shape=[struct((height, width // 2))] * 2,
        in_specs=[VMEM],
        out_specs=[VMEM] * 2,
        compiler_params=pltpu.CompilerParams(vmem_limit_bytes=4 * MIB + 8 * height * width),
        cost_estimate=COVER,
        name="split",
    )(rows)


def gather_pieces(pieces, start, out):
    base = 0
    half = out.shape[1]
    for piece in pieces:
        rows, width = piece.shape
        first = min(start, width - half)
        out[pl.ds(base, rows), :] = piece[:, first : first + half]
        base += rows


def project(weight, halves):
    half = halves.shape[1]
    rows = halves.shape[0]
    low = lax.dot_general(
        weight[:, :half], halves[...], CONTRACT_LAST, preferred_element_type=jnp.float32
    )
    high = lax.dot_general(
        weight[:, half:], halves[...], CONTRACT_LAST, preferred_element_type=jnp.float32
    )
    return low + pltpu.roll(high, rows - CAP, 1)


def forward_kernel(count, *refs):
    pieces = refs[:count]
    gate_w, up_w, halves, activated_out, slope_out, hidden_out = refs[count:]
    gather_pieces(pieces, 0, halves)
    pre_gate, pre_up = project(gate_w, halves), project(up_w, halves)
    is_slot = lax.broadcasted_iota(jnp.int32, (1, halves.shape[0]), 1) % BLOCK < CAP
    squash = 1.0 / (1.0 + jnp.exp(-pre_gate))
    activated = jnp.where(is_slot, pre_gate * squash, 0.0)
    slope = pre_up * squash * (1.0 + pre_gate * (1.0 - squash))
    activated_out[...] = activated
    slope_out[...] = jnp.where(is_slot, slope, 0.0)
    hidden_out[...] = (activated * pre_up).astype(jnp.bfloat16)


def forward(pieces, gate_w, up_w):
    count = len(pieces)
    units, width = gate_w.shape
    rows = sum(piece.shape[0] for piece in pieces)
    kept = (units, rows)
    return pl.pallas_call(
        functools.partial(forward_kernel, count),
        out_shape=[
            struct((rows, width // 2)),
            struct(kept, jnp.float32),
            struct(kept, jnp.float32),
            struct(kept),
        ],
        in_specs=[VMEM] * (count + 2),
        out_specs=[VMEM] * 4,
        compiler_params=pltpu.CompilerParams(
            vmem_limit_bytes=4 * MIB + rows * width + 40 * rows * units
        ),
        cost_estimate=LIGHT,
        name="forward",
    )(*pieces, gate_w, up_w)


def row_grads(factors, gate_w, up_w, parts, start):
    units, width = gate_w.shape
    block, size = parts[0].shape
    slots = factors.shape[0]
    chunk = 256 if size % 256 == 0 else size

    def product(columns):
        return jnp.dot(
            factors[:, :units], gate_w[:, columns], preferred_element_type=jnp.float32
        ) + jnp.dot(factors[:, units:], up_w[:, columns], preferred_element_type=jnp.float32)

    @pl.loop(0, size // chunk)
    def _(step):
        offset = pl.multiple_of(step * chunk, chunk)
        low = product(pl.ds(pl.multiple_of(start + offset, chunk), chunk))
        high = product(pl.ds(pl.multiple_of(width // 2 + start + offset, chunk), chunk))
        is_low = lax.broadcasted_iota(jnp.int32, (slots, 1), 0) % BLOCK < CAP
        even = jnp.where(is_low, low, pltpu.roll(high, CAP, 0))
        odd = jnp.where(is_low, pltpu.roll(low, slots - CAP, 0), high)
        tiles = (slots // BLOCK, BLOCK, chunk)
        total = jnp.stack([even.reshape(tiles), odd.reshape(tiles)], axis=1)
        total = total.reshape(2 * slots, chunk).astype(jnp.bfloat16)
        for i, part in enumerate(parts):
            part[:, pl.ds(offset, chunk)] = total[i * block : (i + 1) * block]


def backward_kernel(count, *refs):
    pieces = refs[:count]
    activated, slope, hidden, gate_w, up_w, down_w = refs[count : count + 6]
    own, far, halves, gate_out, up_out, factors, gates_out = refs[count + 6 :]
    rows = halves.shape[0]
    gather_pieces(pieces, halves.shape[1], halves)
    back = project(down_w, halves)
    gate_terms = jnp.sum(hidden[...].astype(jnp.float32) * back, axis=0, keepdims=True)
    up_pre = back * activated[...]
    gate_pre = back * slope[...]
    both = jnp.concatenate([gate_pre, up_pre], axis=0)
    both = both.T
    tiles = (rows // (2 * BLOCK), 2, BLOCK, both.shape[1])
    even = both.reshape(tiles)[:, 0]
    odd = pltpu.roll(both, CAP, 0).reshape(tiles)[:, 1]
    factors[...] = (even + odd).reshape(factors.shape).astype(jnp.bfloat16)
    gate_column = jnp.broadcast_to(gate_terms, (LANES, rows)).T.astype(jnp.bfloat16)
    row_grads(factors, gate_w, up_w, (own, far), 0)
    gates_out[...] = gate_column
    gate_out[...] = gate_pre.astype(jnp.bfloat16)
    up_out[...] = up_pre.astype(jnp.bfloat16)


def backward(pieces, activated, slope, hidden, weights, size):
    count = len(pieces)
    units, width = weights[0].shape
    rows = sum(piece.shape[0] for piece in pieces)
    mine = rows // 2
    shapes = [
        (mine, size),
        (mine, size),
        (rows, width // 2),
        (units, rows),
        (units, rows),
        (mine, 2 * units),
        (rows, LANES),
    ]
    return pl.pallas_call(
        functools.partial(backward_kernel, count),
        out_shape=[struct(shape) for shape in shapes],
        in_specs=[VMEM] * (count + 6),
        out_specs=[VMEM] * len(shapes),
        compiler_params=pltpu.CompilerParams(
            vmem_limit_bytes=6 * MIB
            + 2 * sum(height * across for height, across in shapes)
            + 56 * rows * units
        ),
        cost_estimate=LIGHT,
        name="backward",
    )(*pieces, activated, slope, hidden, *weights)


def rest_kernel(start, factors, gates, gate_w, up_w, own, far):
    mine, size = own.shape
    size -= LANES
    own[:, size:] = gates[:mine, :]
    far[:, size:] = gates[mine:, :]
    views = [part.at[:, pl.ds(0, size)] for part in (own, far)]
    row_grads(factors, gate_w, up_w, views, start)


def rest_rows(start, factors, gates, gate_w, up_w):
    rows, width = gates.shape[0], gate_w.shape[1]
    size = width // 2 - start + LANES
    return pl.pallas_call(
        functools.partial(rest_kernel, start),
        out_shape=[struct((rows // 2, size))] * 2,
        in_specs=[VMEM] * 4,
        out_specs=[VMEM] * 2,
        compiler_params=pltpu.CompilerParams(vmem_limit_bytes=8 * MIB + 4 * rows * width),
        cost_estimate=LIGHT,
        name="rest_rows",
    )(factors, gates, gate_w, up_w)


def sum_kernel(targets, own_left, own_right, left, right, *outs):
    base = 0
    for own, other in ((own_left, left), (own_right, right)):
        span = pl.ds(base, own.shape[1])
        base += own.shape[1]
        total = (own[...].astype(jnp.float32) + other[...].astype(jnp.float32)).astype(
            jnp.bfloat16
        )
        for i, (out, slot) in enumerate(targets):
            outs[out][pl.ds(slot * BLOCK, BLOCK), span] = total[i * BLOCK : (i + 1) * BLOCK]


def sum_rows(targets, own, other):
    rows = own[0].shape[0]
    width = sum(part.shape[1] for part in own)
    count = 1 + max(out for out, _ in targets)
    return pl.pallas_call(
        functools.partial(sum_kernel, targets),
        out_shape=[struct((rows // count, width))] * count,
        in_specs=[VMEM] * 4,
        out_specs=[VMEM] * count,
        compiler_params=pltpu.CompilerParams(vmem_limit_bytes=8 * MIB + 16 * rows * width),
        cost_estimate=LIGHT,
        name="sum_rows",
    )(*own, *other)


def add_kernel(left, right, out):
    total = left[...].astype(jnp.float32) + right[...].astype(jnp.float32)
    out[...] = total.astype(jnp.bfloat16)


def add_rows(left, right):
    return pl.pallas_call(
        add_kernel,
        out_shape=struct(left.shape),
        in_specs=[VMEM] * 2,
        out_specs=VMEM,
        compiler_params=pltpu.CompilerParams(vmem_limit_bytes=4 * MIB + 16 * left.size),
        name="add_rows",
    )(left, right)


def merge_kernel(kept, passed, *outs):
    for i, out in enumerate(outs):
        span = slice(i * BLOCK, (i + 1) * BLOCK)
        out[...] = jnp.concatenate([kept[span, :], passed[span, :]], axis=0)


def merge_rows(kept, passed):
    rows, width = kept.shape
    count = rows // BLOCK
    return pl.pallas_call(
        merge_kernel,
        out_shape=[struct((2 * BLOCK, width))] * count,
        in_specs=[VMEM] * 2,
        out_specs=[VMEM] * count,
        compiler_params=pltpu.CompilerParams(vmem_limit_bytes=4 * MIB + 24 * rows * width),
        name="merge_rows",
    )(kept, passed)


def weight_kernel(chunk, count, *refs):
    factors, halves = refs[:count], refs[count]
    outs, stages, sems = refs[count + 1 : 2 * count + 1], refs[2 * count + 1 : -1], refs[-1]
    half = halves.shape[1]
    pairs = []
    for factor in factors:
        low = factor[...]
        high = pltpu.roll(low.astype(jnp.float32), CAP, 1).astype(jnp.bfloat16)
        pairs.append((low, high))
    copies = []
    for start in range(0, half, chunk):
        for pair, out, stage in zip(pairs, outs, stages):
            for factor, base in zip(pair, (0, half)):
                span = pl.ds(base + start, chunk)
                stage[:, span] = jnp.dot(
                    factor, halves[:, pl.ds(start, chunk)], preferred_element_type=jnp.float32
                ).astype(jnp.bfloat16)
                copy = pltpu.make_async_copy(
                    stage.at[:, span], out.at[:, span], sems.at[len(copies)]
                )
                copy.start()
                copies.append(copy)
    for copy in copies:
        copy.wait()


def weight_grads(factors, halves):
    count = len(factors)
    units, rows = factors[0].shape
    half = halves.shape[1]
    chunk = 512 if half % 512 == 0 else half
    shape = (units, 2 * half)
    return pl.pallas_call(
        functools.partial(weight_kernel, chunk, count),
        out_shape=[struct(shape)] * count,
        in_specs=[VMEM] * (count + 1),
        out_specs=[HBM] * count,
        scratch_shapes=[pltpu.VMEM(shape, jnp.bfloat16)] * count
        + [pltpu.SemaphoreType.DMA((2 * count * half // chunk,))],
        compiler_params=pltpu.CompilerParams(
            vmem_limit_bytes=6 * MIB + 4 * count * units * half + 8 * count * units * rows
        ),
        cost_estimate=LIGHT,
        name="weight_grads",
    )(*factors, halves)


def combine_kernel(n_targets, first, second, choice_ref, gates_ref, *refs):
    blocks, (token_ref, gate_ref) = refs[: n_targets // 2], refs[n_targets // 2 :]
    even = return_offsets(n_targets)[1]
    back = jnp.concatenate([blocks[even.index(k)][...] for k in range(0, n_targets, 2)], axis=0)
    half = token_ref.shape[1] // 2
    choices, tokens = gates_ref.shape
    rows = back[:, :half]
    token_ref[:, :half] = lax.dot_general(
        first[...], rows, CONTRACT_FIRST, preferred_element_type=jnp.float32
    ).astype(jnp.bfloat16)
    token_ref[:, half:] = lax.dot_general(
        second[...], rows, CONTRACT_FIRST, preferred_element_type=jnp.float32
    ).astype(jnp.bfloat16)
    terms = back[:, half : half + tokens].astype(jnp.float32)
    choice = choice_ref[...]
    for k in range(choices):
        chosen = jnp.where(choice == k, terms, 0.0)
        gate = gates_ref[k : k + 1, :].astype(jnp.float32)
        gate_ref[k : k + 1, :] = jnp.sum(chosen, axis=0, keepdims=True) / gate


def combine(table, gates, blocks, width):
    n_targets = 2 * len(blocks)
    choices, tokens = gates.shape
    return pl.pallas_call(
        functools.partial(combine_kernel, n_targets),
        out_shape=[struct((tokens, width)), struct((choices, tokens), jnp.float32)],
        in_specs=[VMEM] * (4 + len(blocks)),
        out_specs=[VMEM] * 2,
        compiler_params=pltpu.CompilerParams(
            vmem_limit_bytes=4 * MIB + 16 * n_targets * BLOCK * width
        ),
        name="combine",
    )(*table, gates, *blocks)


def flip(value, axis, bit):
    size = lax.axis_size(axis)
    return lax.ppermute(value, axis, [(i, i ^ bit) for i in range(size)])


def offsets(count):
    near, far = list(range(1, count // 2)), list(range(count // 2, count))
    order = [0]
    for i, k in enumerate(near):
        order += [k, far[i]]
    return order + far[len(near) :]


def return_offsets(count):
    even = list(range(count // 2, count, 2)) + list(range(count // 2 - 2, -1, -2))
    return [k ^ 1 for k in even], even


def exchange(blocks, order):
    return [flip(block, "expert", k) if k else block for k, block in zip(order, blocks)]


def cross(block, far_bits):
    held = {0: block}
    for bit in far_bits:
        for mask in list(held):
            held[mask | bit] = flip(held[mask], "dp", bit)
    return held


def body(tokens, out_grad, gate_probs, route_ids, w_gate, w_up, w_down):
    n_targets = lax.axis_size("expert")
    n_dp = lax.axis_size("dp")
    width = tokens.shape[1]
    ids, gates = route_ids.T, gate_probs.T
    far_bits = [1 << i for i in range(1, n_dp.bit_length() - 1)]
    weights = (w_gate[0], w_up[0], w_down[0])
    tie = lax.optimization_barrier

    order = offsets(n_targets)
    odd, even = return_offsets(n_targets)
    middle = n_targets // 2
    sent = dispatch(n_targets, ids, tokens, gates, out_grad)
    arrived = exchange([sent[k] for k in order], order)
    early = pack(arrived[:middle])
    (early_tokens, early_grads), late = tie((split(early), arrived[middle:]))
    late = pack(late)
    ids_after, _ = tie((ids, late))
    early_near, late_near = (cross(value, far_bits) for value in (early, late))
    near = sorted(early_near)
    crossed = {mask: early_near[mask] for mask in near[1:]}
    early, late, crossed = tie((early, late, crossed))
    early_far = {0: flip(early, "dp", 1)}
    for mask, value in crossed.items():
        early_far[mask] = flip(value, "dp", 1)
    late_far = {0: flip(late, "dp", 1)}
    crossed = {mask: late_near[mask] for mask in near[1:]}
    table = placement(n_targets, ids_after)
    table, early_far, late_far, crossed = tie((table, early_far, late_far, crossed))
    for mask, value in crossed.items():
        late_far[mask] = flip(value, "dp", 1)
    pieces = [
        group[mask]
        for groups in ((early_near, late_near), (early_far, late_far))
        for mask in near
        for group in groups
    ]
    token_halves, activated, slope, hidden = forward(
        [early_tokens, *pieces[1:]], weights[0], weights[1]
    )
    size = width // 16 * 5
    own_left, far_left, grad_halves, gate_f, up_f, factors, gate_column = backward(
        [early_grads, *pieces[1:]], activated, slope, hidden, weights, size
    )

    left = flip(far_left, "dp", 1)
    own_right, far_right = rest_rows(size, factors, gate_column, weights[0], weights[1])
    left, own_right = tie((left, own_right))
    right = flip(far_right, "dp", 1)
    targets = [
        (2 * i, odd.index(k)) if k % 2 else (2 * i + 1, even.index(k))
        for i in range(len(near))
        for k in order
    ]
    parts = sum_rows(targets, (own_left, own_right), (left, right))
    gate_f, up_f, _ = tie((gate_f, up_f, parts))
    grad_gate, grad_up = weight_grads((gate_f, up_f), token_halves)
    sums = []
    for group in range(2):
        held = dict(zip(near, parts[group::2]))
        for bit in reversed(far_bits):
            masks = [mask for mask in held if mask & bit]
            moved = {mask: flip(held.pop(mask), "dp", bit) for mask in masks}
            if group == 0 and bit == far_bits[-1]:
                moved, grad_gate, grad_up = tie((moved, grad_gate, grad_up))
            if bit == far_bits[0]:
                sums.append((held[0], moved[bit]))
            else:
                for mask in masks:
                    held[mask ^ bit] = add_rows(held[mask ^ bit], moved[mask])
    passed = add_rows(*sums[0])
    hidden, _ = tie((hidden, passed))
    (grad_down,) = weight_grads((hidden,), grad_halves)
    passed = flip(passed, "expert", 1)
    kept, moved, grad_down = tie((*sums[1], grad_down))
    kept, passed = tie((add_rows(kept, moved), passed))
    returned = exchange(merge_rows(kept, passed), even)
    token_grad, gate_grad = combine(table, gates, returned, width)
    grads = (grad_gate, grad_up, grad_down)
    return (token_grad, gate_grad.T, *(grad[None] for grad in grads))


def solution(mesh):
    in_specs = (
        P(("expert", "dp"), None),
        P(("expert", "dp"), None),
        P(("expert", "dp"), None),
        P(("expert", "dp"), None),
        P("expert", "dp", None),
        P("expert", "dp", None),
        P("expert", "dp", None),
    )
    out_specs = (
        P(("expert", "dp"), None),
        P(("expert", "dp"), None),
        P("expert", "dp", None),
        P("expert", "dp", None),
        P("expert", "dp", None),
    )
    return jax.shard_map(body, mesh=mesh, in_specs=in_specs, out_specs=out_specs, check_vma=False)
```

```python
import functools

import jax
import jax.numpy as jnp
from jax import lax
from jax.experimental import pallas as pl
from jax.experimental.pallas import tpu as pltpu
from jax.sharding import PartitionSpec as P

EXPERTS = 128
CAP = 4
BLOCK = 2 * CAP
LANES = 128
MIB = 2**20

CONTRACT_LAST = (((1,), (1,)), ((), ()))
CONTRACT_FIRST = (((0,), (0,)), ((), ()))

HBM = pl.BlockSpec(memory_space=pltpu.HBM)
VMEM = pl.BlockSpec(memory_space=pltpu.VMEM)

LIGHT = pl.CostEstimate(flops=10**6, bytes_accessed=10**4, transcendentals=0)
COVER = pl.CostEstimate(flops=4 * 10**10, bytes_accessed=4 * 10**7, transcendentals=0)


def struct(shape, dtype=jnp.bfloat16):
    return jax.ShapeDtypeStruct(shape, dtype)


def as_bf16(mask):
    return mask.astype(jnp.float32).astype(jnp.bfloat16)


def choice_table(ids, n_targets):
    choices, tokens = ids.shape
    height = n_targets * BLOCK
    per_device = EXPERTS // n_targets
    row = lax.broadcasted_iota(jnp.int32, (height, 1), 0)
    wanted = ((row // BLOCK) ^ lax.axis_index("expert")) * per_device
    slot = row % BLOCK
    matches = [ids[k : k + 1, :] == wanted for k in range(choices)]
    hit = functools.reduce(jnp.logical_or, matches)
    earlier = lax.broadcasted_iota(jnp.int32, (tokens, tokens), 0) < lax.broadcasted_iota(
        jnp.int32, (tokens, tokens), 1
    )
    rank = jnp.dot(as_bf16(hit), as_bf16(earlier), preferred_element_type=jnp.float32)
    rank = rank.astype(jnp.int32)
    first = jnp.logical_and(hit, rank == slot)
    second = jnp.logical_and(hit, rank == slot - CAP)
    return matches, first, second


def pick_rows(picks, rows_ref):
    half = rows_ref.shape[1] // 2
    rows = jnp.concatenate([rows_ref[:, :half], rows_ref[:, half:]], axis=0)
    return jnp.dot(picks, rows, preferred_element_type=jnp.float32).astype(jnp.bfloat16)


def dispatch_kernel(n_targets, *refs):
    sources, outs = refs[:4], refs[4 : 4 + n_targets]
    targets, sems = refs[4 + n_targets : -1], refs[-1]
    ids_ref, tokens_ref, gates_ref, grads_ref = targets
    copies = [
        pltpu.make_async_copy(source, target, sems.at[i])
        for i, (source, target) in enumerate(zip(sources, targets))
    ]
    for copy in copies:
        copy.start()
    copies[0].wait()
    matches, first, second = choice_table(ids_ref[...], n_targets)
    picks = jnp.concatenate([first.astype(jnp.float32), second.astype(jnp.float32)], axis=1)
    copies[1].wait()
    rows = pick_rows(picks.astype(jnp.bfloat16), tokens_ref)
    half = rows.shape[1]
    for k, out in enumerate(outs):
        out[:, :half] = rows[k * BLOCK : (k + 1) * BLOCK]
    copies[2].wait()
    gates = gates_ref[...].astype(jnp.float32)
    scale = jnp.zeros(first.shape, jnp.float32)
    for k, match in enumerate(matches):
        scale = scale + jnp.where(match, gates[k : k + 1, :], 0.0)
    picks = (picks * jnp.concatenate([scale, scale], axis=1)).astype(jnp.bfloat16)
    copies[3].wait()
    rows = pick_rows(picks, grads_ref)
    for k, out in enumerate(outs):
        out[:, half:] = rows[k * BLOCK : (k + 1) * BLOCK]


def dispatch(n_targets, ids, tokens, gates, out_grad):
    arrays = (ids, tokens, gates, out_grad)
    return pl.pallas_call(
        functools.partial(dispatch_kernel, n_targets),
        out_shape=[struct((BLOCK, tokens.shape[1]))] * n_targets,
        in_specs=[HBM] * 4,
        out_specs=[VMEM] * n_targets,
        scratch_shapes=[pltpu.VMEM(a.shape, a.dtype) for a in arrays]
        + [pltpu.SemaphoreType.DMA((4,))],
        compiler_params=pltpu.CompilerParams(vmem_limit_bytes=60 * MIB),
        name="dispatch",
    )(*arrays)


def placement_kernel(n_targets, ids_ref, first_ref, second_ref, choice_ref):
    matches, first, second = choice_table(ids_ref[...], n_targets)
    first_ref[...] = as_bf16(first)
    second_ref[...] = as_bf16(second)
    choice = jnp.full(first.shape, -1, jnp.int32)
    for k, match in enumerate(matches):
        choice = jnp.where(jnp.logical_and(match, first), k, choice)
    choice_ref[...] = choice


def placement(n_targets, ids):
    table = (n_targets * BLOCK, ids.shape[1])
    return pl.pallas_call(
        functools.partial(placement_kernel, n_targets),
        out_shape=[struct(table), struct(table), struct(table, jnp.int32)],
        in_specs=[VMEM],
        out_specs=[VMEM] * 3,
        compiler_params=pltpu.CompilerParams(vmem_limit_bytes=4 * MIB),
        cost_estimate=LIGHT,
        name="placement",
    )(ids)


def pack_kernel(refs, out):
    blocks = [
        ref[pl.ds(i, BLOCK), :] for ref in refs for i in range(0, ref.shape[0], BLOCK)
    ]
    for k in range(0, len(blocks), 2):
        out[pl.ds(k * BLOCK, 2 * BLOCK), :] = jnp.concatenate(blocks[k : k + 2], axis=0)


def pack(arrays, cost):
    rows, width = sum(array.shape[0] for array in arrays), arrays[0].shape[1]
    return pl.pallas_call(
        lambda *refs: pack_kernel(refs[:-1], refs[-1]),
        out_shape=struct((rows, width)),
        in_specs=[VMEM] * len(arrays),
        out_specs=VMEM,
        compiler_params=pltpu.CompilerParams(vmem_limit_bytes=4 * MIB + 8 * rows * width),
        cost_estimate=cost,
        name="pack",
    )(*arrays)


def split_kernel(rows, token_out, grad_out):
    half = token_out.shape[1]
    token_out[...] = rows[:, :half]
    grad_out[...] = rows[:, half:]


def split(rows):
    height, width = rows.shape
    return pl.pallas_call(
        split_kernel,
        out_shape=[struct((height, width // 2))] * 2,
        in_specs=[VMEM],
        out_specs=[VMEM] * 2,
        compiler_params=pltpu.CompilerParams(vmem_limit_bytes=4 * MIB + 8 * height * width),
        cost_estimate=COVER,
        name="split",
    )(rows)


def gather_pieces(pieces, start, out):
    base = 0
    half = out.shape[1]
    for piece in pieces:
        rows, width = piece.shape
        first = min(start, width - half)
        out[pl.ds(base, rows), :] = piece[:, first : first + half]
        base += rows


def project(weight, halves):
    half = halves.shape[1]
    rows = halves.shape[0]
    low = lax.dot_general(
        weight[:, :half], halves[...], CONTRACT_LAST, preferred_element_type=jnp.float32
    )
    high = lax.dot_general(
        weight[:, half:], halves[...], CONTRACT_LAST, preferred_element_type=jnp.float32
    )
    return low + pltpu.roll(high, rows - CAP, 1)


def forward_kernel(count, *refs):
    pieces = refs[:count]
    gate_w, up_w, halves, activated_out, slope_out, hidden_out = refs[count:]
    gather_pieces(pieces, 0, halves)
    pre_gate, pre_up = project(gate_w, halves), project(up_w, halves)
    is_slot = lax.broadcasted_iota(jnp.int32, (1, halves.shape[0]), 1) % BLOCK < CAP
    squash = 1.0 / (1.0 + jnp.exp(-pre_gate))
    activated = jnp.where(is_slot, pre_gate * squash, 0.0)
    slope = pre_up * squash * (1.0 + pre_gate * (1.0 - squash))
    activated_out[...] = activated
    slope_out[...] = jnp.where(is_slot, slope, 0.0)
    hidden_out[...] = (activated * pre_up).astype(jnp.bfloat16)


def forward(pieces, gate_w, up_w):
    count = len(pieces)
    units, width = gate_w.shape
    rows = sum(piece.shape[0] for piece in pieces)
    kept = (units, rows)
    return pl.pallas_call(
        functools.partial(forward_kernel, count),
        out_shape=[
            struct((rows, width // 2)),
            struct(kept, jnp.float32),
            struct(kept, jnp.float32),
            struct(kept),
        ],
        in_specs=[VMEM] * (count + 2),
        out_specs=[VMEM] * 4,
        compiler_params=pltpu.CompilerParams(
            vmem_limit_bytes=4 * MIB + rows * width + 40 * rows * units
        ),
        cost_estimate=LIGHT,
        name="forward",
    )(*pieces, gate_w, up_w)


def row_grads(factors, gate_w, up_w, parts, start):
    units, width = gate_w.shape
    block, size = parts[0].shape
    slots = factors.shape[0]
    chunk = 256 if size % 256 == 0 else size

    def product(columns):
        return jnp.dot(
            factors[:, :units], gate_w[:, columns], preferred_element_type=jnp.float32
        ) + jnp.dot(factors[:, units:], up_w[:, columns], preferred_element_type=jnp.float32)

    @pl.loop(0, size // chunk)
    def _(step):
        offset = pl.multiple_of(step * chunk, chunk)
        low = product(pl.ds(pl.multiple_of(start + offset, chunk), chunk))
        high = product(pl.ds(pl.multiple_of(width // 2 + start + offset, chunk), chunk))
        is_low = lax.broadcasted_iota(jnp.int32, (slots, 1), 0) % BLOCK < CAP
        even = jnp.where(is_low, low, pltpu.roll(high, CAP, 0))
        odd = jnp.where(is_low, pltpu.roll(low, slots - CAP, 0), high)
        tiles = (slots // BLOCK, BLOCK, chunk)
        total = jnp.stack([even.reshape(tiles), odd.reshape(tiles)], axis=1)
        total = total.reshape(2 * slots, chunk).astype(jnp.bfloat16)
        for i, part in enumerate(parts):
            part[:, pl.ds(offset, chunk)] = total[i * block : (i + 1) * block]


def backward_kernel(count, *refs):
    pieces = refs[:count]
    activated, slope, hidden, gate_w, up_w, down_w = refs[count : count + 6]
    own, far, halves, gate_out, up_out, factors, gates_out = refs[count + 6 :]
    rows = halves.shape[0]
    gather_pieces(pieces, halves.shape[1], halves)
    back = project(down_w, halves)
    gate_terms = jnp.sum(hidden[...].astype(jnp.float32) * back, axis=0, keepdims=True)
    up_pre = back * activated[...]
    gate_pre = back * slope[...]
    both = jnp.concatenate([gate_pre, up_pre], axis=0)
    both = both.T
    tiles = (rows // (2 * BLOCK), 2, BLOCK, both.shape[1])
    even = both.reshape(tiles)[:, 0]
    odd = pltpu.roll(both, CAP, 0).reshape(tiles)[:, 1]
    factors[...] = (even + odd).reshape(factors.shape).astype(jnp.bfloat16)
    gate_column = jnp.broadcast_to(gate_terms, (LANES, rows)).T.astype(jnp.bfloat16)
    row_grads(factors, gate_w, up_w, (own, far), 0)
    gates_out[...] = gate_column
    gate_out[...] = gate_pre.astype(jnp.bfloat16)
    up_out[...] = up_pre.astype(jnp.bfloat16)


def backward(pieces, activated, slope, hidden, weights, size):
    count = len(pieces)
    units, width = weights[0].shape
    rows = sum(piece.shape[0] for piece in pieces)
    mine = rows // 2
    shapes = [
        (mine, size),
        (mine, size),
        (rows, width // 2),
        (units, rows),
        (units, rows),
        (mine, 2 * units),
        (rows, LANES),
    ]
    return pl.pallas_call(
        functools.partial(backward_kernel, count),
        out_shape=[struct(shape) for shape in shapes],
        in_specs=[VMEM] * (count + 6),
        out_specs=[VMEM] * len(shapes),
        compiler_params=pltpu.CompilerParams(
            vmem_limit_bytes=6 * MIB
            + 2 * sum(height * across for height, across in shapes)
            + 56 * rows * units
        ),
        cost_estimate=LIGHT,
        name="backward",
    )(*pieces, activated, slope, hidden, *weights)


def rest_kernel(start, factors, gates, gate_w, up_w, own, far):
    mine, size = own.shape
    size -= LANES
    own[:, size:] = gates[:mine, :]
    far[:, size:] = gates[mine:, :]
    views = [part.at[:, pl.ds(0, size)] for part in (own, far)]
    row_grads(factors, gate_w, up_w, views, start)


def rest_rows(start, factors, gates, gate_w, up_w):
    rows, width = gates.shape[0], gate_w.shape[1]
    size = width // 2 - start + LANES
    return pl.pallas_call(
        functools.partial(rest_kernel, start),
        out_shape=[struct((rows // 2, size))] * 2,
        in_specs=[VMEM] * 4,
        out_specs=[VMEM] * 2,
        compiler_params=pltpu.CompilerParams(vmem_limit_bytes=8 * MIB + 4 * rows * width),
        cost_estimate=LIGHT,
        name="rest_rows",
    )(factors, gates, gate_w, up_w)


def sum_kernel(targets, own_left, own_right, left, right, *outs):
    base = 0
    for own, other in ((own_left, left), (own_right, right)):
        span = pl.ds(base, own.shape[1])
        base += own.shape[1]
        total = (own[...].astype(jnp.float32) + other[...].astype(jnp.float32)).astype(
            jnp.bfloat16
        )
        for i, (out, slot) in enumerate(targets):
            outs[out][pl.ds(slot * BLOCK, BLOCK), span] = total[i * BLOCK : (i + 1) * BLOCK]


def sum_rows(targets, own, other):
    rows = own[0].shape[0]
    width = sum(part.shape[1] for part in own)
    count = 1 + max(out for out, _ in targets)
    return pl.pallas_call(
        functools.partial(sum_kernel, targets),
        out_shape=[struct((rows // count, width))] * count,
        in_specs=[VMEM] * 4,
        out_specs=[VMEM] * count,
        compiler_params=pltpu.CompilerParams(vmem_limit_bytes=8 * MIB + 16 * rows * width),
        cost_estimate=LIGHT,
        name="sum_rows",
    )(*own, *other)


def add_kernel(left, right, out):
    total = left[...].astype(jnp.float32) + right[...].astype(jnp.float32)
    out[...] = total.astype(jnp.bfloat16)


def add_rows(left, right):
    return pl.pallas_call(
        add_kernel,
        out_shape=struct(left.shape),
        in_specs=[VMEM] * 2,
        out_specs=VMEM,
        compiler_params=pltpu.CompilerParams(vmem_limit_bytes=4 * MIB + 16 * left.size),
        name="add_rows",
    )(left, right)


def merge_kernel(kept, passed, *outs):
    for i, out in enumerate(outs):
        span = slice(i * BLOCK, (i + 1) * BLOCK)
        out[...] = jnp.concatenate([kept[span, :], passed[span, :]], axis=0)


def merge_rows(kept, passed):
    rows, width = kept.shape
    count = rows // BLOCK
    return pl.pallas_call(
        merge_kernel,
        out_shape=[struct((2 * BLOCK, width))] * count,
        in_specs=[VMEM] * 2,
        out_specs=[VMEM] * count,
        compiler_params=pltpu.CompilerParams(vmem_limit_bytes=4 * MIB + 24 * rows * width),
        name="merge_rows",
    )(kept, passed)


def weight_kernel(chunk, count, *refs):
    factors, halves = refs[:count], refs[count]
    outs, stages, sems = refs[count + 1 : 2 * count + 1], refs[2 * count + 1 : -1], refs[-1]
    half = halves.shape[1]
    pairs = []
    for factor in factors:
        low = factor[...]
        high = pltpu.roll(low.astype(jnp.float32), CAP, 1).astype(jnp.bfloat16)
        pairs.append((low, high))
    copies = []
    for start in range(0, half, chunk):
        for pair, out, stage in zip(pairs, outs, stages):
            for factor, base in zip(pair, (0, half)):
                span = pl.ds(base + start, chunk)
                stage[:, span] = jnp.dot(
                    factor, halves[:, pl.ds(start, chunk)], preferred_element_type=jnp.float32
                ).astype(jnp.bfloat16)
                copy = pltpu.make_async_copy(
                    stage.at[:, span], out.at[:, span], sems.at[len(copies)]
                )
                copy.start()
                copies.append(copy)
    for copy in copies:
        copy.wait()


def weight_grads(factors, halves):
    count = len(factors)
    units, rows = factors[0].shape
    half = halves.shape[1]
    chunk = 512 if half % 512 == 0 else half
    shape = (units, 2 * half)
    return pl.pallas_call(
        functools.partial(weight_kernel, chunk, count),
        out_shape=[struct(shape)] * count,
        in_specs=[VMEM] * (count + 1),
        out_specs=[HBM] * count,
        scratch_shapes=[pltpu.VMEM(shape, jnp.bfloat16)] * count
        + [pltpu.SemaphoreType.DMA((2 * count * half // chunk,))],
        compiler_params=pltpu.CompilerParams(
            vmem_limit_bytes=6 * MIB + 4 * count * units * half + 8 * count * units * rows
        ),
        cost_estimate=LIGHT,
        name="weight_grads",
    )(*factors, halves)


def combine_kernel(n_targets, first, second, choice_ref, gates_ref, *refs):
    blocks, (token_ref, gate_ref) = refs[: n_targets // 2], refs[n_targets // 2 :]
    even = return_offsets(n_targets)[1]
    back = jnp.concatenate([blocks[even.index(k)][...] for k in range(0, n_targets, 2)], axis=0)
    half = token_ref.shape[1] // 2
    choices, tokens = gates_ref.shape
    rows = back[:, :half]
    token_ref[:, :half] = lax.dot_general(
        first[...], rows, CONTRACT_FIRST, preferred_element_type=jnp.float32
    ).astype(jnp.bfloat16)
    token_ref[:, half:] = lax.dot_general(
        second[...], rows, CONTRACT_FIRST, preferred_element_type=jnp.float32
    ).astype(jnp.bfloat16)
    terms = back[:, half : half + tokens].astype(jnp.float32)
    choice = choice_ref[...]
    for k in range(choices):
        chosen = jnp.where(choice == k, terms, 0.0)
        gate = gates_ref[k : k + 1, :].astype(jnp.float32)
        gate_ref[k : k + 1, :] = jnp.sum(chosen, axis=0, keepdims=True) / gate


def combine(table, gates, blocks, width):
    n_targets = 2 * len(blocks)
    choices, tokens = gates.shape
    return pl.pallas_call(
        functools.partial(combine_kernel, n_targets),
        out_shape=[struct((tokens, width)), struct((choices, tokens), jnp.float32)],
        in_specs=[VMEM] * (4 + len(blocks)),
        out_specs=[VMEM] * 2,
        compiler_params=pltpu.CompilerParams(
            vmem_limit_bytes=4 * MIB + 16 * n_targets * BLOCK * width
        ),
        name="combine",
    )(*table, gates, *blocks)


def flip(value, axis, bit):
    size = lax.axis_size(axis)
    return lax.ppermute(value, axis, [(i, i ^ bit) for i in range(size)])


def offsets(count):
    near, far = list(range(1, count // 2)), list(range(count // 2, count))
    order = [0]
    for i, k in enumerate(near):
        order += [k, far[i]]
    return order + far[len(near) :]


def return_offsets(count):
    even = list(range(count // 2, count, 2)) + list(range(count // 2 - 2, -1, -2))
    return [k ^ 1 for k in even], even


def exchange(blocks, order):
    return [flip(block, "expert", k) if k else block for k, block in zip(order, blocks)]


def cross(block, far_bits):
    held = {0: block}
    for bit in far_bits:
        for mask in list(held):
            held[mask | bit] = flip(held[mask], "dp", bit)
    return held


def body(tokens, out_grad, gate_probs, route_ids, w_gate, w_up, w_down):
    n_targets = lax.axis_size("expert")
    n_dp = lax.axis_size("dp")
    width = tokens.shape[1]
    ids, gates = route_ids.T, gate_probs.T
    far_bits = [1 << i for i in range(1, n_dp.bit_length() - 1)]
    weights = (w_gate[0], w_up[0], w_down[0])
    tie = lax.optimization_barrier

    order = offsets(n_targets)
    odd, even = return_offsets(n_targets)
    middle = n_targets // 2
    sent = dispatch(n_targets, ids, tokens, gates, out_grad)
    arrived = exchange([sent[k] for k in order], order)
    first = pack(arrived[1:3], COVER)
    early = pack([arrived[0], first, *arrived[3:middle]], LIGHT)
    (early_tokens, early_grads), late = tie((split(early), arrived[middle:]))
    late = pack(late, LIGHT)
    ids_after, _ = tie((ids, late))
    early_near, late_near = (cross(value, far_bits) for value in (early, late))
    near = sorted(early_near)
    crossed = {mask: early_near[mask] for mask in near[1:]}
    early, late, crossed = tie((early, late, crossed))
    early_far = {0: flip(early, "dp", 1)}
    for mask, value in crossed.items():
        early_far[mask] = flip(value, "dp", 1)
    late_far = {0: flip(late, "dp", 1)}
    crossed = {mask: late_near[mask] for mask in near[1:]}
    table = placement(n_targets, ids_after)
    table, early_far, late_far, crossed = tie((table, early_far, late_far, crossed))
    for mask, value in crossed.items():
        late_far[mask] = flip(value, "dp", 1)
    pieces = [
        group[mask]
        for groups in ((early_near, late_near), (early_far, late_far))
        for mask in near
        for group in groups
    ]
    token_halves, activated, slope, hidden = forward(
        [early_tokens, *pieces[1:]], weights[0], weights[1]
    )
    size = width // 8 * 3
    own_left, far_left, grad_halves, gate_f, up_f, factors, gate_column = backward(
        [early_grads, *pieces[1:]], activated, slope, hidden, weights, size
    )

    left = flip(far_left, "dp", 1)
    own_right, far_right = rest_rows(size, factors, gate_column, weights[0], weights[1])
    left, own_right = tie((left, own_right))
    right = flip(far_right, "dp", 1)
    targets = [
        (2 * i, odd.index(k)) if k % 2 else (2 * i + 1, even.index(k))
        for i in range(len(near))
        for k in order
    ]
    parts = sum_rows(targets, (own_left, own_right), (left, right))
    gate_f, up_f, _ = tie((gate_f, up_f, parts))
    grad_gate, grad_up = weight_grads((gate_f, up_f), token_halves)
    sums = []
    for group in range(2):
        held = dict(zip(near, parts[group::2]))
        for bit in reversed(far_bits):
            masks = [mask for mask in held if mask & bit]
            moved = {mask: flip(held.pop(mask), "dp", bit) for mask in masks}
            if group == 0 and bit == far_bits[-1]:
                moved, grad_gate, grad_up = tie((moved, grad_gate, grad_up))
            if bit == far_bits[0]:
                sums.append((held[0], moved[bit]))
            else:
                for mask in masks:
                    held[mask ^ bit] = add_rows(held[mask ^ bit], moved[mask])
    passed = add_rows(*sums[0])
    hidden, _ = tie((hidden, passed))
    (grad_down,) = weight_grads((hidden,), grad_halves)
    passed = flip(passed, "expert", 1)
    kept, moved, grad_down = tie((*sums[1], grad_down))
    kept, passed = tie((add_rows(kept, moved), passed))
    returned = exchange(merge_rows(kept, passed), even)
    token_grad, gate_grad = combine(table, gates, returned, width)
    grads = (grad_gate, grad_up, grad_down)
    return (token_grad, gate_grad.T, *(grad[None] for grad in grads))


def solution(mesh):
    in_specs = (
        P(("expert", "dp"), None),
        P(("expert", "dp"), None),
        P(("expert", "dp"), None),
        P(("expert", "dp"), None),
        P("expert", "dp", None),
        P("expert", "dp", None),
        P("expert", "dp", None),
    )
    out_specs = (
        P(("expert", "dp"), None),
        P(("expert", "dp"), None),
        P("expert", "dp", None),
        P("expert", "dp", None),
        P("expert", "dp", None),
    )
    return jax.shard_map(body, mesh=mesh, in_specs=in_specs, out_specs=out_specs, check_vma=False)
```

```python
import functools

import jax
import jax.numpy as jnp
from jax import lax
from jax.experimental import pallas as pl
from jax.experimental.pallas import tpu as pltpu
from jax.sharding import PartitionSpec as P

EXPERTS = 128
CAP = 4
BLOCK = 2 * CAP
LANES = 128
MIB = 2**20

CONTRACT_LAST = (((1,), (1,)), ((), ()))
CONTRACT_FIRST = (((0,), (0,)), ((), ()))

HBM = pl.BlockSpec(memory_space=pltpu.HBM)
VMEM = pl.BlockSpec(memory_space=pltpu.VMEM)

LIGHT = pl.CostEstimate(flops=10**6, bytes_accessed=10**4, transcendentals=0)
COVER = pl.CostEstimate(flops=4 * 10**10, bytes_accessed=4 * 10**7, transcendentals=0)


def struct(shape, dtype=jnp.bfloat16):
    return jax.ShapeDtypeStruct(shape, dtype)


def as_bf16(mask):
    return mask.astype(jnp.float32).astype(jnp.bfloat16)


def choice_table(ids, n_targets):
    choices, tokens = ids.shape
    height = n_targets * BLOCK
    per_device = EXPERTS // n_targets
    row = lax.broadcasted_iota(jnp.int32, (height, 1), 0)
    wanted = ((row // BLOCK) ^ lax.axis_index("expert")) * per_device
    slot = row % BLOCK
    matches = [ids[k : k + 1, :] == wanted for k in range(choices)]
    hit = functools.reduce(jnp.logical_or, matches)
    earlier = lax.broadcasted_iota(jnp.int32, (tokens, tokens), 0) < lax.broadcasted_iota(
        jnp.int32, (tokens, tokens), 1
    )
    rank = jnp.dot(as_bf16(hit), as_bf16(earlier), preferred_element_type=jnp.float32)
    rank = rank.astype(jnp.int32)
    first = jnp.logical_and(hit, rank == slot)
    second = jnp.logical_and(hit, rank == slot - CAP)
    return matches, first, second


def pick_rows(picks, rows_ref):
    half = rows_ref.shape[1] // 2
    rows = jnp.concatenate([rows_ref[:, :half], rows_ref[:, half:]], axis=0)
    return jnp.dot(picks, rows, preferred_element_type=jnp.float32).astype(jnp.bfloat16)


def dispatch_kernel(n_targets, *refs):
    sources, outs = refs[:4], refs[4 : 4 + n_targets]
    targets, sems = refs[4 + n_targets : -1], refs[-1]
    ids_ref, tokens_ref, gates_ref, grads_ref = targets
    copies = [
        pltpu.make_async_copy(source, target, sems.at[i])
        for i, (source, target) in enumerate(zip(sources, targets))
    ]
    for copy in copies:
        copy.start()
    copies[0].wait()
    matches, first, second = choice_table(ids_ref[...], n_targets)
    picks = jnp.concatenate([first.astype(jnp.float32), second.astype(jnp.float32)], axis=1)
    copies[1].wait()
    rows = pick_rows(picks.astype(jnp.bfloat16), tokens_ref)
    half = rows.shape[1]
    for k, out in enumerate(outs):
        out[:, :half] = rows[k * BLOCK : (k + 1) * BLOCK]
    copies[2].wait()
    gates = gates_ref[...].astype(jnp.float32)
    scale = jnp.zeros(first.shape, jnp.float32)
    for k, match in enumerate(matches):
        scale = scale + jnp.where(match, gates[k : k + 1, :], 0.0)
    picks = (picks * jnp.concatenate([scale, scale], axis=1)).astype(jnp.bfloat16)
    copies[3].wait()
    rows = pick_rows(picks, grads_ref)
    for k, out in enumerate(outs):
        out[:, half:] = rows[k * BLOCK : (k + 1) * BLOCK]


def dispatch(n_targets, ids, tokens, gates, out_grad):
    arrays = (ids, tokens, gates, out_grad)
    return pl.pallas_call(
        functools.partial(dispatch_kernel, n_targets),
        out_shape=[struct((BLOCK, tokens.shape[1]))] * n_targets,
        in_specs=[HBM] * 4,
        out_specs=[VMEM] * n_targets,
        scratch_shapes=[pltpu.VMEM(a.shape, a.dtype) for a in arrays]
        + [pltpu.SemaphoreType.DMA((4,))],
        compiler_params=pltpu.CompilerParams(vmem_limit_bytes=60 * MIB),
        name="dispatch",
    )(*arrays)


def placement_kernel(n_targets, ids_ref, first_ref, second_ref, choice_ref):
    matches, first, second = choice_table(ids_ref[...], n_targets)
    first_ref[...] = as_bf16(first)
    second_ref[...] = as_bf16(second)
    choice = jnp.full(first.shape, -1, jnp.int32)
    for k, match in enumerate(matches):
        choice = jnp.where(jnp.logical_and(match, first), k, choice)
    choice_ref[...] = choice


def placement(n_targets, ids):
    table = (n_targets * BLOCK, ids.shape[1])
    return pl.pallas_call(
        functools.partial(placement_kernel, n_targets),
        out_shape=[struct(table), struct(table), struct(table, jnp.int32)],
        in_specs=[VMEM],
        out_specs=[VMEM] * 3,
        compiler_params=pltpu.CompilerParams(vmem_limit_bytes=4 * MIB),
        cost_estimate=LIGHT,
        name="placement",
    )(ids)


def pack_kernel(refs, out):
    blocks = [
        ref[pl.ds(i, BLOCK), :] for ref in refs for i in range(0, ref.shape[0], BLOCK)
    ]
    for k in range(0, len(blocks), 2):
        out[pl.ds(k * BLOCK, 2 * BLOCK), :] = jnp.concatenate(blocks[k : k + 2], axis=0)


def pack(arrays, cost):
    rows, width = sum(array.shape[0] for array in arrays), arrays[0].shape[1]
    return pl.pallas_call(
        lambda *refs: pack_kernel(refs[:-1], refs[-1]),
        out_shape=struct((rows, width)),
        in_specs=[VMEM] * len(arrays),
        out_specs=VMEM,
        compiler_params=pltpu.CompilerParams(vmem_limit_bytes=4 * MIB + 8 * rows * width),
        cost_estimate=cost,
        name="pack",
    )(*arrays)


def split_kernel(rows, token_out, grad_out):
    half = token_out.shape[1]
    token_out[...] = rows[:, :half]
    grad_out[...] = rows[:, half:]


def split(rows):
    height, width = rows.shape
    return pl.pallas_call(
        split_kernel,
        out_shape=[struct((height, width // 2))] * 2,
        in_specs=[VMEM],
        out_specs=[VMEM] * 2,
        compiler_params=pltpu.CompilerParams(vmem_limit_bytes=4 * MIB + 8 * height * width),
        cost_estimate=COVER,
        name="split",
    )(rows)


def gather_pieces(pieces, start, out):
    base = 0
    half = out.shape[1]
    for piece in pieces:
        rows, width = piece.shape
        first = min(start, width - half)
        out[pl.ds(base, rows), :] = piece[:, first : first + half]
        base += rows


def project(weight, halves):
    half = halves.shape[1]
    rows = halves.shape[0]
    low = lax.dot_general(
        weight[:, :half], halves[...], CONTRACT_LAST, preferred_element_type=jnp.float32
    )
    high = lax.dot_general(
        weight[:, half:], halves[...], CONTRACT_LAST, preferred_element_type=jnp.float32
    )
    return low + pltpu.roll(high, rows - CAP, 1)


def forward_kernel(count, *refs):
    pieces = refs[:count]
    gate_w, up_w, halves, activated_out, slope_out, hidden_out = refs[count:]
    gather_pieces(pieces, 0, halves)
    pre_gate, pre_up = project(gate_w, halves), project(up_w, halves)
    is_slot = lax.broadcasted_iota(jnp.int32, (1, halves.shape[0]), 1) % BLOCK < CAP
    squash = 1.0 / (1.0 + jnp.exp(-pre_gate))
    activated = jnp.where(is_slot, pre_gate * squash, 0.0)
    slope = pre_up * squash * (1.0 + pre_gate * (1.0 - squash))
    activated_out[...] = activated
    slope_out[...] = jnp.where(is_slot, slope, 0.0)
    hidden_out[...] = (activated * pre_up).astype(jnp.bfloat16)


def forward(pieces, gate_w, up_w):
    count = len(pieces)
    units, width = gate_w.shape
    rows = sum(piece.shape[0] for piece in pieces)
    kept = (units, rows)
    return pl.pallas_call(
        functools.partial(forward_kernel, count),
        out_shape=[
            struct((rows, width // 2)),
            struct(kept, jnp.float32),
            struct(kept, jnp.float32),
            struct(kept),
        ],
        in_specs=[VMEM] * (count + 2),
        out_specs=[VMEM] * 4,
        compiler_params=pltpu.CompilerParams(
            vmem_limit_bytes=4 * MIB + rows * width + 40 * rows * units
        ),
        cost_estimate=LIGHT,
        name="forward",
    )(*pieces, gate_w, up_w)


def row_grads(factors, gate_w, up_w, parts, start):
    units, width = gate_w.shape
    block, size = parts[0].shape
    slots = factors.shape[0]
    chunk = 256 if size % 256 == 0 else size

    def product(columns):
        return jnp.dot(
            factors[:, :units], gate_w[:, columns], preferred_element_type=jnp.float32
        ) + jnp.dot(factors[:, units:], up_w[:, columns], preferred_element_type=jnp.float32)

    @pl.loop(0, size // chunk)
    def _(step):
        offset = pl.multiple_of(step * chunk, chunk)
        low = product(pl.ds(pl.multiple_of(start + offset, chunk), chunk))
        high = product(pl.ds(pl.multiple_of(width // 2 + start + offset, chunk), chunk))
        is_low = lax.broadcasted_iota(jnp.int32, (slots, 1), 0) % BLOCK < CAP
        even = jnp.where(is_low, low, pltpu.roll(high, CAP, 0))
        odd = jnp.where(is_low, pltpu.roll(low, slots - CAP, 0), high)
        tiles = (slots // BLOCK, BLOCK, chunk)
        total = jnp.stack([even.reshape(tiles), odd.reshape(tiles)], axis=1)
        total = total.reshape(2 * slots, chunk).astype(jnp.bfloat16)
        for i, part in enumerate(parts):
            part[:, pl.ds(offset, chunk)] = total[i * block : (i + 1) * block]


def backward_kernel(count, *refs):
    pieces = refs[:count]
    activated, slope, hidden, gate_w, up_w, down_w = refs[count : count + 6]
    own, far, halves, gate_out, up_out, factors, gates_out = refs[count + 6 :]
    rows = halves.shape[0]
    gather_pieces(pieces, halves.shape[1], halves)
    back = project(down_w, halves)
    gate_terms = jnp.sum(hidden[...].astype(jnp.float32) * back, axis=0, keepdims=True)
    up_pre = back * activated[...]
    gate_pre = back * slope[...]
    both = jnp.concatenate([gate_pre, up_pre], axis=0)
    both = both.T
    tiles = (rows // (2 * BLOCK), 2, BLOCK, both.shape[1])
    even = both.reshape(tiles)[:, 0]
    odd = pltpu.roll(both, CAP, 0).reshape(tiles)[:, 1]
    factors[...] = (even + odd).reshape(factors.shape).astype(jnp.bfloat16)
    gate_column = jnp.broadcast_to(gate_terms, (LANES, rows)).T.astype(jnp.bfloat16)
    row_grads(factors, gate_w, up_w, (own, far), 0)
    gates_out[...] = gate_column
    gate_out[...] = gate_pre.astype(jnp.bfloat16)
    up_out[...] = up_pre.astype(jnp.bfloat16)


def backward(pieces, activated, slope, hidden, weights, size):
    count = len(pieces)
    units, width = weights[0].shape
    rows = sum(piece.shape[0] for piece in pieces)
    mine = rows // 2
    shapes = [
        (mine, size),
        (mine, size),
        (rows, width // 2),
        (units, rows),
        (units, rows),
        (mine, 2 * units),
        (rows, LANES),
    ]
    return pl.pallas_call(
        functools.partial(backward_kernel, count),
        out_shape=[struct(shape) for shape in shapes],
        in_specs=[VMEM] * (count + 6),
        out_specs=[VMEM] * len(shapes),
        compiler_params=pltpu.CompilerParams(
            vmem_limit_bytes=6 * MIB
            + 2 * sum(height * across for height, across in shapes)
            + 56 * rows * units
        ),
        cost_estimate=LIGHT,
        name="backward",
    )(*pieces, activated, slope, hidden, *weights)


def rest_kernel(start, factors, gates, gate_w, up_w, own, far):
    mine, size = own.shape
    size -= LANES
    own[:, size:] = gates[:mine, :]
    far[:, size:] = gates[mine:, :]
    views = [part.at[:, pl.ds(0, size)] for part in (own, far)]
    row_grads(factors, gate_w, up_w, views, start)


def rest_rows(start, factors, gates, gate_w, up_w):
    rows, width = gates.shape[0], gate_w.shape[1]
    size = width // 2 - start + LANES
    return pl.pallas_call(
        functools.partial(rest_kernel, start),
        out_shape=[struct((rows // 2, size))] * 2,
        in_specs=[VMEM] * 4,
        out_specs=[VMEM] * 2,
        compiler_params=pltpu.CompilerParams(vmem_limit_bytes=8 * MIB + 4 * rows * width),
        cost_estimate=LIGHT,
        name="rest_rows",
    )(factors, gates, gate_w, up_w)


def sum_kernel(targets, own_left, own_right, left, right, *outs):
    base = 0
    for own, other in ((own_left, left), (own_right, right)):
        span = pl.ds(base, own.shape[1])
        base += own.shape[1]
        total = (own[...].astype(jnp.float32) + other[...].astype(jnp.float32)).astype(
            jnp.bfloat16
        )
        for i, (out, slot) in enumerate(targets):
            outs[out][pl.ds(slot * BLOCK, BLOCK), span] = total[i * BLOCK : (i + 1) * BLOCK]


def sum_rows(targets, own, other):
    rows = own[0].shape[0]
    width = sum(part.shape[1] for part in own)
    count = 1 + max(out for out, _ in targets)
    return pl.pallas_call(
        functools.partial(sum_kernel, targets),
        out_shape=[struct((rows // count, width))] * count,
        in_specs=[VMEM] * 4,
        out_specs=[VMEM] * count,
        compiler_params=pltpu.CompilerParams(vmem_limit_bytes=8 * MIB + 16 * rows * width),
        cost_estimate=LIGHT,
        name="sum_rows",
    )(*own, *other)


def add_kernel(left, right, *outs):
    total = (left[...].astype(jnp.float32) + right[...].astype(jnp.float32)).astype(jnp.bfloat16)
    block = outs[0].shape[0]
    for i, out in enumerate(outs):
        out[...] = total[i * block : (i + 1) * block]


def add_rows(left, right, count):
    rows, width = left.shape
    return pl.pallas_call(
        add_kernel,
        out_shape=[struct((rows // count, width))] * count,
        in_specs=[VMEM] * 2,
        out_specs=[VMEM] * count,
        compiler_params=pltpu.CompilerParams(vmem_limit_bytes=4 * MIB + 16 * rows * width),
        name="add_rows",
    )(left, right)


def merge_kernel(kept, passed, *outs):
    for i, out in enumerate(outs):
        span = slice(i * BLOCK, (i + 1) * BLOCK)
        out[...] = jnp.concatenate([kept[span, :], passed[span, :]], axis=0)


def merge_rows(kept, passed):
    rows, width = kept.shape
    count = rows // BLOCK
    return pl.pallas_call(
        merge_kernel,
        out_shape=[struct((2 * BLOCK, width))] * count,
        in_specs=[VMEM] * 2,
        out_specs=[VMEM] * count,
        compiler_params=pltpu.CompilerParams(vmem_limit_bytes=4 * MIB + 24 * rows * width),
        name="merge_rows",
    )(kept, passed)


def weight_kernel(chunk, count, *refs):
    factors, halves = refs[:count], refs[count]
    outs, stages, sems = refs[count + 1 : 2 * count + 1], refs[2 * count + 1 : -1], refs[-1]
    half = halves.shape[1]
    pairs = []
    for factor in factors:
        low = factor[...]
        high = pltpu.roll(low.astype(jnp.float32), CAP, 1).astype(jnp.bfloat16)
        pairs.append((low, high))
    copies = []
    for start in range(0, half, chunk):
        for pair, out, stage in zip(pairs, outs, stages):
            for factor, base in zip(pair, (0, half)):
                span = pl.ds(base + start, chunk)
                stage[:, span] = jnp.dot(
                    factor, halves[:, pl.ds(start, chunk)], preferred_element_type=jnp.float32
                ).astype(jnp.bfloat16)
                copy = pltpu.make_async_copy(
                    stage.at[:, span], out.at[:, span], sems.at[len(copies)]
                )
                copy.start()
                copies.append(copy)
    for copy in copies:
        copy.wait()


def weight_grads(factors, halves):
    count = len(factors)
    units, rows = factors[0].shape
    half = halves.shape[1]
    chunk = 512 if half % 512 == 0 else half
    shape = (units, 2 * half)
    return pl.pallas_call(
        functools.partial(weight_kernel, chunk, count),
        out_shape=[struct(shape)] * count,
        in_specs=[VMEM] * (count + 1),
        out_specs=[HBM] * count,
        scratch_shapes=[pltpu.VMEM(shape, jnp.bfloat16)] * count
        + [pltpu.SemaphoreType.DMA((2 * count * half // chunk,))],
        compiler_params=pltpu.CompilerParams(
            vmem_limit_bytes=6 * MIB + 4 * count * units * half + 8 * count * units * rows
        ),
        cost_estimate=LIGHT,
        name="weight_grads",
    )(*factors, halves)


def combine_kernel(n_targets, first, second, choice_ref, gates_ref, *refs):
    blocks, (token_ref, gate_ref) = refs[: n_targets // 2], refs[n_targets // 2 :]
    even = return_offsets(n_targets)[1]
    back = jnp.concatenate([blocks[even.index(k)][...] for k in range(0, n_targets, 2)], axis=0)
    half = token_ref.shape[1] // 2
    choices, tokens = gates_ref.shape
    rows = back[:, :half]
    token_ref[:, :half] = lax.dot_general(
        first[...], rows, CONTRACT_FIRST, preferred_element_type=jnp.float32
    ).astype(jnp.bfloat16)
    token_ref[:, half:] = lax.dot_general(
        second[...], rows, CONTRACT_FIRST, preferred_element_type=jnp.float32
    ).astype(jnp.bfloat16)
    terms = back[:, half : half + tokens].astype(jnp.float32)
    choice = choice_ref[...]
    for k in range(choices):
        chosen = jnp.where(choice == k, terms, 0.0)
        gate = gates_ref[k : k + 1, :].astype(jnp.float32)
        gate_ref[k : k + 1, :] = jnp.sum(chosen, axis=0, keepdims=True) / gate


def combine(table, gates, blocks, width):
    n_targets = 2 * len(blocks)
    choices, tokens = gates.shape
    return pl.pallas_call(
        functools.partial(combine_kernel, n_targets),
        out_shape=[struct((tokens, width)), struct((choices, tokens), jnp.float32)],
        in_specs=[VMEM] * (4 + len(blocks)),
        out_specs=[VMEM] * 2,
        compiler_params=pltpu.CompilerParams(
            vmem_limit_bytes=4 * MIB + 16 * n_targets * BLOCK * width
        ),
        name="combine",
    )(*table, gates, *blocks)


def flip(value, axis, bit):
    size = lax.axis_size(axis)
    return lax.ppermute(value, axis, [(i, i ^ bit) for i in range(size)])


def offsets(count):
    near, far = list(range(1, count // 2)), list(range(count // 2, count))
    order = [0]
    for i, k in enumerate(near):
        order += [k, far[i]]
    return order + far[len(near) :]


def return_offsets(count):
    even = list(range(count // 2 - 2, -1, -2)) + list(range(count // 2, count, 2))
    return [k ^ 1 for k in even], even


def exchange(blocks, order):
    return [flip(block, "expert", k) if k else block for k, block in zip(order, blocks)]


def cross(block, far_bits):
    held = {0: block}
    for bit in far_bits:
        for mask in list(held):
            held[mask | bit] = flip(held[mask], "dp", bit)
    return held


def body(tokens, out_grad, gate_probs, route_ids, w_gate, w_up, w_down):
    n_targets = lax.axis_size("expert")
    n_dp = lax.axis_size("dp")
    width = tokens.shape[1]
    ids, gates = route_ids.T, gate_probs.T
    far_bits = [1 << i for i in range(1, n_dp.bit_length() - 1)]
    weights = (w_gate[0], w_up[0], w_down[0])
    tie = lax.optimization_barrier

    order = offsets(n_targets)
    odd, even = return_offsets(n_targets)
    middle = n_targets // 2
    sent = dispatch(n_targets, ids, tokens, gates, out_grad)
    arrived = exchange([sent[k] for k in order], order)
    first = pack(arrived[1:3], COVER)
    early = pack([arrived[0], first, *arrived[3:middle]], LIGHT)
    (early_tokens, early_grads), late = tie((split(early), arrived[middle:]))
    late = pack(late, LIGHT)
    ids_after, _ = tie((ids, late))
    early_near, late_near = (cross(value, far_bits) for value in (early, late))
    near = sorted(early_near)
    crossed = {mask: early_near[mask] for mask in near[1:]}
    early, late, crossed = tie((early, late, crossed))
    early_far = {0: flip(early, "dp", 1)}
    for mask, value in crossed.items():
        early_far[mask] = flip(value, "dp", 1)
    late_far = {0: flip(late, "dp", 1)}
    crossed = {mask: late_near[mask] for mask in near[1:]}
    table = placement(n_targets, ids_after)
    table, early_far, late_far, crossed = tie((table, early_far, late_far, crossed))
    for mask, value in crossed.items():
        late_far[mask] = flip(value, "dp", 1)
    pieces = [
        group[mask]
        for groups in ((early_near, late_near), (early_far, late_far))
        for mask in near
        for group in groups
    ]
    token_halves, activated, slope, hidden = forward(
        [early_tokens, *pieces[1:]], weights[0], weights[1]
    )
    size = width // 8 * 3
    own_left, far_left, grad_halves, gate_f, up_f, factors, gate_column = backward(
        [early_grads, *pieces[1:]], activated, slope, hidden, weights, size
    )

    left = flip(far_left, "dp", 1)
    own_right, far_right = rest_rows(size, factors, gate_column, weights[0], weights[1])
    left, own_right = tie((left, own_right))
    right = flip(far_right, "dp", 1)
    targets = [
        (2 * i, odd.index(k)) if k % 2 else (2 * i + 1, even.index(k))
        for i in range(len(near))
        for k in order
    ]
    parts = sum_rows(targets, (own_left, own_right), (left, right))
    gate_f, up_f, _ = tie((gate_f, up_f, parts))
    grad_gate, grad_up = weight_grads((gate_f, up_f), token_halves)
    parts = [list(parts[group::2]) for group in range(2)]
    parts[1], grad_gate, grad_up = tie((parts[1], grad_gate, grad_up))
    sums = []
    for group in range(2):
        held = dict(zip(near, parts[group]))
        for bit in reversed(far_bits):
            masks = [mask for mask in held if mask & bit]
            moved = {mask: flip(held.pop(mask), "dp", bit) for mask in masks}
            if group == 0 and bit == far_bits[-1]:
                moved, grad_gate, grad_up = tie((moved, grad_gate, grad_up))
            if bit == far_bits[0]:
                sums.append((held[0], moved[bit]))
            else:
                for mask in masks:
                    (held[mask ^ bit],) = add_rows(held[mask ^ bit], moved[mask], 1)
    passed = add_rows(*sums[0], 2)
    hidden, _ = tie((hidden, passed))
    (grad_down,) = weight_grads((hidden,), grad_halves)
    passed = [flip(value, "expert", 1) for value in passed]
    kept, moved, grad_down = tie((*sums[1], grad_down))
    kept = add_rows(kept, moved, 2)
    merged = [block for pair in zip(kept, passed) for block in merge_rows(*pair)]
    returned = exchange(merged, even)
    token_grad, gate_grad = combine(table, gates, returned, width)
    grads = (grad_gate, grad_up, grad_down)
    return (token_grad, gate_grad.T, *(grad[None] for grad in grads))


def solution(mesh):
    in_specs = (
        P(("expert", "dp"), None),
        P(("expert", "dp"), None),
        P(("expert", "dp"), None),
        P(("expert", "dp"), None),
        P("expert", "dp", None),
        P("expert", "dp", None),
        P("expert", "dp", None),
    )
    out_specs = (
        P(("expert", "dp"), None),
        P(("expert", "dp"), None),
        P("expert", "dp", None),
        P("expert", "dp", None),
        P("expert", "dp", None),
    )
    return jax.shard_map(body, mesh=mesh, in_specs=in_specs, out_specs=out_specs, check_vma=False)
```

```python
import functools

import jax
import jax.numpy as jnp
from jax import lax
from jax.experimental import pallas as pl
from jax.experimental.pallas import tpu as pltpu
from jax.sharding import PartitionSpec as P

EXPERTS = 128
CAP = 4
BLOCK = 2 * CAP
LANES = 128
MIB = 2**20

CONTRACT_LAST = (((1,), (1,)), ((), ()))
CONTRACT_FIRST = (((0,), (0,)), ((), ()))

HBM = pl.BlockSpec(memory_space=pltpu.HBM)
VMEM = pl.BlockSpec(memory_space=pltpu.VMEM)

LIGHT = pl.CostEstimate(flops=10**6, bytes_accessed=10**4, transcendentals=0)
COVER = pl.CostEstimate(flops=4 * 10**10, bytes_accessed=4 * 10**7, transcendentals=0)


def struct(shape, dtype=jnp.bfloat16):
    return jax.ShapeDtypeStruct(shape, dtype)


def as_bf16(mask):
    return mask.astype(jnp.float32).astype(jnp.bfloat16)


def choice_table(ids, n_targets):
    choices, tokens = ids.shape
    height = n_targets * BLOCK
    per_device = EXPERTS // n_targets
    row = lax.broadcasted_iota(jnp.int32, (height, 1), 0)
    wanted = ((row // BLOCK) ^ lax.axis_index("expert")) * per_device
    slot = row % BLOCK
    matches = [ids[k : k + 1, :] == wanted for k in range(choices)]
    hit = functools.reduce(jnp.logical_or, matches)
    earlier = lax.broadcasted_iota(jnp.int32, (tokens, tokens), 0) < lax.broadcasted_iota(
        jnp.int32, (tokens, tokens), 1
    )
    rank = jnp.dot(as_bf16(hit), as_bf16(earlier), preferred_element_type=jnp.float32)
    rank = rank.astype(jnp.int32)
    first = jnp.logical_and(hit, rank == slot)
    second = jnp.logical_and(hit, rank == slot - CAP)
    return matches, first, second


def pick_rows(picks, rows_ref):
    half = rows_ref.shape[1] // 2
    rows = jnp.concatenate([rows_ref[:, :half], rows_ref[:, half:]], axis=0)
    return jnp.dot(picks, rows, preferred_element_type=jnp.float32).astype(jnp.bfloat16)


def dispatch_kernel(n_targets, *refs):
    sources, outs = refs[:4], refs[4 : 4 + n_targets]
    targets, sems = refs[4 + n_targets : -1], refs[-1]
    ids_ref, tokens_ref, gates_ref, grads_ref = targets
    copies = [
        pltpu.make_async_copy(source, target, sems.at[i])
        for i, (source, target) in enumerate(zip(sources, targets))
    ]
    for copy in copies:
        copy.start()
    copies[0].wait()
    matches, first, second = choice_table(ids_ref[...], n_targets)
    picks = jnp.concatenate([first.astype(jnp.float32), second.astype(jnp.float32)], axis=1)
    copies[1].wait()
    rows = pick_rows(picks.astype(jnp.bfloat16), tokens_ref)
    half = rows.shape[1]
    for k, out in enumerate(outs):
        out[:, :half] = rows[k * BLOCK : (k + 1) * BLOCK]
    copies[2].wait()
    gates = gates_ref[...].astype(jnp.float32)
    scale = jnp.zeros(first.shape, jnp.float32)
    for k, match in enumerate(matches):
        scale = scale + jnp.where(match, gates[k : k + 1, :], 0.0)
    picks = (picks * jnp.concatenate([scale, scale], axis=1)).astype(jnp.bfloat16)
    copies[3].wait()
    rows = pick_rows(picks, grads_ref)
    for k, out in enumerate(outs):
        out[:, half:] = rows[k * BLOCK : (k + 1) * BLOCK]


def dispatch(n_targets, ids, tokens, gates, out_grad):
    arrays = (ids, tokens, gates, out_grad)
    return pl.pallas_call(
        functools.partial(dispatch_kernel, n_targets),
        out_shape=[struct((BLOCK, tokens.shape[1]))] * n_targets,
        in_specs=[HBM] * 4,
        out_specs=[VMEM] * n_targets,
        scratch_shapes=[pltpu.VMEM(a.shape, a.dtype) for a in arrays]
        + [pltpu.SemaphoreType.DMA((4,))],
        compiler_params=pltpu.CompilerParams(vmem_limit_bytes=60 * MIB),
        name="dispatch",
    )(*arrays)


def placement_kernel(n_targets, ids_ref, first_ref, second_ref, choice_ref):
    matches, first, second = choice_table(ids_ref[...], n_targets)
    first_ref[...] = as_bf16(first)
    second_ref[...] = as_bf16(second)
    choice = jnp.full(first.shape, -1, jnp.int32)
    for k, match in enumerate(matches):
        choice = jnp.where(jnp.logical_and(match, first), k, choice)
    choice_ref[...] = choice


def placement(n_targets, ids):
    table = (n_targets * BLOCK, ids.shape[1])
    return pl.pallas_call(
        functools.partial(placement_kernel, n_targets),
        out_shape=[struct(table), struct(table), struct(table, jnp.int32)],
        in_specs=[VMEM],
        out_specs=[VMEM] * 3,
        compiler_params=pltpu.CompilerParams(vmem_limit_bytes=4 * MIB),
        cost_estimate=LIGHT,
        name="placement",
    )(ids)


def pack_kernel(refs, out):
    blocks = [
        ref[pl.ds(i, BLOCK), :] for ref in refs for i in range(0, ref.shape[0], BLOCK)
    ]
    for k in range(0, len(blocks), 2):
        out[pl.ds(k * BLOCK, 2 * BLOCK), :] = jnp.concatenate(blocks[k : k + 2], axis=0)


def pack(arrays, cost):
    rows, width = sum(array.shape[0] for array in arrays), arrays[0].shape[1]
    return pl.pallas_call(
        lambda *refs: pack_kernel(refs[:-1], refs[-1]),
        out_shape=struct((rows, width)),
        in_specs=[VMEM] * len(arrays),
        out_specs=VMEM,
        compiler_params=pltpu.CompilerParams(vmem_limit_bytes=4 * MIB + 8 * rows * width),
        cost_estimate=cost,
        name="pack",
    )(*arrays)


def split_kernel(rows, token_out, grad_out):
    half = token_out.shape[1]
    token_out[...] = rows[:, :half]
    grad_out[...] = rows[:, half:]


def split(rows):
    height, width = rows.shape
    return pl.pallas_call(
        split_kernel,
        out_shape=[struct((height, width // 2))] * 2,
        in_specs=[VMEM],
        out_specs=[VMEM] * 2,
        compiler_params=pltpu.CompilerParams(vmem_limit_bytes=4 * MIB + 8 * height * width),
        cost_estimate=COVER,
        name="split",
    )(rows)


def gather_pieces(pieces, start, out):
    base = 0
    half = out.shape[1]
    for piece in pieces:
        rows, width = piece.shape
        first = min(start, width - half)
        out[pl.ds(base, rows), :] = piece[:, first : first + half]
        base += rows


def project(weight, halves):
    half = halves.shape[1]
    rows = halves.shape[0]
    low = lax.dot_general(
        weight[:, :half], halves[...], CONTRACT_LAST, preferred_element_type=jnp.float32
    )
    high = lax.dot_general(
        weight[:, half:], halves[...], CONTRACT_LAST, preferred_element_type=jnp.float32
    )
    return low + pltpu.roll(high, rows - CAP, 1)


def forward_kernel(count, *refs):
    pieces = refs[:count]
    gate_w, up_w, halves, activated_out, slope_out, hidden_out = refs[count:]
    gather_pieces(pieces, 0, halves)
    pre_gate, pre_up = project(gate_w, halves), project(up_w, halves)
    is_slot = lax.broadcasted_iota(jnp.int32, (1, halves.shape[0]), 1) % BLOCK < CAP
    squash = 1.0 / (1.0 + jnp.exp(-pre_gate))
    activated = jnp.where(is_slot, pre_gate * squash, 0.0)
    slope = pre_up * squash * (1.0 + pre_gate * (1.0 - squash))
    activated_out[...] = activated
    slope_out[...] = jnp.where(is_slot, slope, 0.0)
    hidden_out[...] = (activated * pre_up).astype(jnp.bfloat16)


def forward(pieces, gate_w, up_w):
    count = len(pieces)
    units, width = gate_w.shape
    rows = sum(piece.shape[0] for piece in pieces)
    kept = (units, rows)
    return pl.pallas_call(
        functools.partial(forward_kernel, count),
        out_shape=[
            struct((rows, width // 2)),
            struct(kept, jnp.float32),
            struct(kept, jnp.float32),
            struct(kept),
        ],
        in_specs=[VMEM] * (count + 2),
        out_specs=[VMEM] * 4,
        compiler_params=pltpu.CompilerParams(
            vmem_limit_bytes=4 * MIB + rows * width + 40 * rows * units
        ),
        cost_estimate=LIGHT,
        name="forward",
    )(*pieces, gate_w, up_w)


def row_grads(factors, gate_w, up_w, parts, start):
    units, width = gate_w.shape
    block, size = parts[0].shape
    slots = factors.shape[0]
    chunk = 256 if size % 256 == 0 else size

    def product(columns):
        return jnp.dot(
            factors[:, :units], gate_w[:, columns], preferred_element_type=jnp.float32
        ) + jnp.dot(factors[:, units:], up_w[:, columns], preferred_element_type=jnp.float32)

    @pl.loop(0, size // chunk)
    def _(step):
        offset = pl.multiple_of(step * chunk, chunk)
        low = product(pl.ds(pl.multiple_of(start + offset, chunk), chunk))
        high = product(pl.ds(pl.multiple_of(width // 2 + start + offset, chunk), chunk))
        is_low = lax.broadcasted_iota(jnp.int32, (slots, 1), 0) % BLOCK < CAP
        even = jnp.where(is_low, low, pltpu.roll(high, CAP, 0))
        odd = jnp.where(is_low, pltpu.roll(low, slots - CAP, 0), high)
        tiles = (slots // BLOCK, BLOCK, chunk)
        total = jnp.stack([even.reshape(tiles), odd.reshape(tiles)], axis=1)
        total = total.reshape(2 * slots, chunk).astype(jnp.bfloat16)
        for i, part in enumerate(parts):
            part[:, pl.ds(offset, chunk)] = total[i * block : (i + 1) * block]


def backward_kernel(count, *refs):
    pieces = refs[:count]
    activated, slope, hidden, gate_w, up_w, down_w = refs[count : count + 6]
    own, far, halves, gate_out, up_out, factors, gates_out = refs[count + 6 :]
    rows = halves.shape[0]
    gather_pieces(pieces, halves.shape[1], halves)
    back = project(down_w, halves)
    gate_terms = jnp.sum(hidden[...].astype(jnp.float32) * back, axis=0, keepdims=True)
    up_pre = back * activated[...]
    gate_pre = back * slope[...]
    both = jnp.concatenate([gate_pre, up_pre], axis=0)
    both = both.T
    tiles = (rows // (2 * BLOCK), 2, BLOCK, both.shape[1])
    even = both.reshape(tiles)[:, 0]
    odd = pltpu.roll(both, CAP, 0).reshape(tiles)[:, 1]
    factors[...] = (even + odd).reshape(factors.shape).astype(jnp.bfloat16)
    gate_column = jnp.broadcast_to(gate_terms, (LANES, rows)).T.astype(jnp.bfloat16)
    row_grads(factors, gate_w, up_w, (own, far), 0)
    gates_out[...] = gate_column
    gate_out[...] = gate_pre.astype(jnp.bfloat16)
    up_out[...] = up_pre.astype(jnp.bfloat16)


def backward(pieces, activated, slope, hidden, weights, size):
    count = len(pieces)
    units, width = weights[0].shape
    rows = sum(piece.shape[0] for piece in pieces)
    mine = rows // 2
    shapes = [
        (mine, size),
        (mine, size),
        (rows, width // 2),
        (units, rows),
        (units, rows),
        (mine, 2 * units),
        (rows, LANES),
    ]
    return pl.pallas_call(
        functools.partial(backward_kernel, count),
        out_shape=[struct(shape) for shape in shapes],
        in_specs=[VMEM] * (count + 6),
        out_specs=[VMEM] * len(shapes),
        compiler_params=pltpu.CompilerParams(
            vmem_limit_bytes=6 * MIB
            + 2 * sum(height * across for height, across in shapes)
            + 56 * rows * units
        ),
        cost_estimate=LIGHT,
        name="backward",
    )(*pieces, activated, slope, hidden, *weights)


def rest_kernel(start, factors, gates, gate_w, up_w, own, far):
    mine, size = own.shape
    size -= LANES
    own[:, size:] = gates[:mine, :]
    far[:, size:] = gates[mine:, :]
    views = [part.at[:, pl.ds(0, size)] for part in (own, far)]
    row_grads(factors, gate_w, up_w, views, start)


def rest_rows(start, factors, gates, gate_w, up_w):
    rows, width = gates.shape[0], gate_w.shape[1]
    size = width // 2 - start + LANES
    return pl.pallas_call(
        functools.partial(rest_kernel, start),
        out_shape=[struct((rows // 2, size))] * 2,
        in_specs=[VMEM] * 4,
        out_specs=[VMEM] * 2,
        compiler_params=pltpu.CompilerParams(vmem_limit_bytes=8 * MIB + 4 * rows * width),
        cost_estimate=LIGHT,
        name="rest_rows",
    )(factors, gates, gate_w, up_w)


def sum_kernel(targets, own_left, own_right, left, right, *outs):
    base = 0
    for own, other in ((own_left, left), (own_right, right)):
        span = pl.ds(base, own.shape[1])
        base += own.shape[1]
        total = (own[...].astype(jnp.float32) + other[...].astype(jnp.float32)).astype(
            jnp.bfloat16
        )
        for i, (out, slot) in enumerate(targets):
            outs[out][pl.ds(slot * BLOCK, BLOCK), span] = total[i * BLOCK : (i + 1) * BLOCK]


def sum_rows(targets, own, other):
    rows = own[0].shape[0]
    width = sum(part.shape[1] for part in own)
    count = 1 + max(out for out, _ in targets)
    return pl.pallas_call(
        functools.partial(sum_kernel, targets),
        out_shape=[struct((rows // count, width))] * count,
        in_specs=[VMEM] * 4,
        out_specs=[VMEM] * count,
        compiler_params=pltpu.CompilerParams(vmem_limit_bytes=8 * MIB + 16 * rows * width),
        cost_estimate=LIGHT,
        name="sum_rows",
    )(*own, *other)


def add_kernel(left, right, *outs):
    total = (left[...].astype(jnp.float32) + right[...].astype(jnp.float32)).astype(jnp.bfloat16)
    block = outs[0].shape[0]
    for i, out in enumerate(outs):
        out[...] = total[i * block : (i + 1) * block]


def add_rows(left, right, count):
    rows, width = left.shape
    return pl.pallas_call(
        add_kernel,
        out_shape=[struct((rows // count, width))] * count,
        in_specs=[VMEM] * 2,
        out_specs=[VMEM] * count,
        compiler_params=pltpu.CompilerParams(vmem_limit_bytes=4 * MIB + 16 * rows * width),
        name="add_rows",
    )(left, right)


def merge_kernel(kept, passed, *outs):
    for i, out in enumerate(outs):
        span = slice(i * BLOCK, (i + 1) * BLOCK)
        out[...] = jnp.concatenate([kept[span, :], passed[span, :]], axis=0)


def merge_rows(kept, passed):
    rows, width = kept.shape
    count = rows // BLOCK
    return pl.pallas_call(
        merge_kernel,
        out_shape=[struct((2 * BLOCK, width))] * count,
        in_specs=[VMEM] * 2,
        out_specs=[VMEM] * count,
        compiler_params=pltpu.CompilerParams(vmem_limit_bytes=4 * MIB + 24 * rows * width),
        name="merge_rows",
    )(kept, passed)


def weight_kernel(chunk, count, *refs):
    factors, halves = refs[:count], refs[count]
    outs, stages, sems = refs[count + 1 : 2 * count + 1], refs[2 * count + 1 : -1], refs[-1]
    half = halves.shape[1]
    pairs = []
    for factor in factors:
        low = factor[...]
        high = pltpu.roll(low.astype(jnp.float32), CAP, 1).astype(jnp.bfloat16)
        pairs.append((low, high))
    copies = []
    for start in range(0, half, chunk):
        for pair, out, stage in zip(pairs, outs, stages):
            for factor, base in zip(pair, (0, half)):
                span = pl.ds(base + start, chunk)
                stage[:, span] = jnp.dot(
                    factor, halves[:, pl.ds(start, chunk)], preferred_element_type=jnp.float32
                ).astype(jnp.bfloat16)
                copy = pltpu.make_async_copy(
                    stage.at[:, span], out.at[:, span], sems.at[len(copies)]
                )
                copy.start()
                copies.append(copy)
    for copy in copies:
        copy.wait()


def weight_grads(factors, halves):
    count = len(factors)
    units, rows = factors[0].shape
    half = halves.shape[1]
    chunk = 512 if half % 512 == 0 else half
    shape = (units, 2 * half)
    return pl.pallas_call(
        functools.partial(weight_kernel, chunk, count),
        out_shape=[struct(shape)] * count,
        in_specs=[VMEM] * (count + 1),
        out_specs=[HBM] * count,
        scratch_shapes=[pltpu.VMEM(shape, jnp.bfloat16)] * count
        + [pltpu.SemaphoreType.DMA((2 * count * half // chunk,))],
        compiler_params=pltpu.CompilerParams(
            vmem_limit_bytes=6 * MIB + 4 * count * units * half + 8 * count * units * rows
        ),
        cost_estimate=LIGHT,
        name="weight_grads",
    )(*factors, halves)


def combine_kernel(n_targets, first, second, choice_ref, gates_ref, *refs):
    blocks, (token_ref, gate_ref) = refs[: n_targets // 2], refs[n_targets // 2 :]
    even = return_offsets(n_targets)[1]
    back = jnp.concatenate([blocks[even.index(k)][...] for k in range(0, n_targets, 2)], axis=0)
    half = token_ref.shape[1] // 2
    choices, tokens = gates_ref.shape
    rows = back[:, :half]
    token_ref[:, :half] = lax.dot_general(
        first[...], rows, CONTRACT_FIRST, preferred_element_type=jnp.float32
    ).astype(jnp.bfloat16)
    token_ref[:, half:] = lax.dot_general(
        second[...], rows, CONTRACT_FIRST, preferred_element_type=jnp.float32
    ).astype(jnp.bfloat16)
    terms = back[:, half : half + tokens].astype(jnp.float32)
    choice = choice_ref[...]
    for k in range(choices):
        chosen = jnp.where(choice == k, terms, 0.0)
        gate = gates_ref[k : k + 1, :].astype(jnp.float32)
        gate_ref[k : k + 1, :] = jnp.sum(chosen, axis=0, keepdims=True) / gate


def combine(table, gates, blocks, width):
    n_targets = 2 * len(blocks)
    choices, tokens = gates.shape
    return pl.pallas_call(
        functools.partial(combine_kernel, n_targets),
        out_shape=[struct((tokens, width)), struct((choices, tokens), jnp.float32)],
        in_specs=[VMEM] * (4 + len(blocks)),
        out_specs=[VMEM] * 2,
        compiler_params=pltpu.CompilerParams(
            vmem_limit_bytes=4 * MIB + 16 * n_targets * BLOCK * width
        ),
        name="combine",
    )(*table, gates, *blocks)


def flip(value, axis, bit):
    size = lax.axis_size(axis)
    return lax.ppermute(value, axis, [(i, i ^ bit) for i in range(size)])


def offsets(count):
    near, far = list(range(1, count // 2)), list(range(count // 2, count))
    mixed = [k for pair in zip(near, far) for k in pair] + far[len(near) :]
    head, tail = mixed[: count // 2 - 1], mixed[count // 2 - 1 :]
    return [0] + head + sorted(tail, key=lambda k: (k < count // 2, k))


def return_offsets(count):
    even = list(range(count // 2 - 2, -1, -2)) + list(range(count // 2, count, 2))
    return [k ^ 1 for k in even], even


def exchange(blocks, order):
    return [flip(block, "expert", k) if k else block for k, block in zip(order, blocks)]


def cross(block, far_bits):
    held = {0: block}
    for bit in far_bits:
        for mask in list(held):
            held[mask | bit] = flip(held[mask], "dp", bit)
    return held


def body(tokens, out_grad, gate_probs, route_ids, w_gate, w_up, w_down):
    n_targets = lax.axis_size("expert")
    n_dp = lax.axis_size("dp")
    width = tokens.shape[1]
    ids, gates = route_ids.T, gate_probs.T
    far_bits = [1 << i for i in range(1, n_dp.bit_length() - 1)]
    weights = (w_gate[0], w_up[0], w_down[0])
    tie = lax.optimization_barrier

    order = offsets(n_targets)
    odd, even = return_offsets(n_targets)
    middle = n_targets // 2
    sent = dispatch(n_targets, ids, tokens, gates, out_grad)
    arrived = exchange([sent[k] for k in order], order)
    first = pack(arrived[1:3], COVER)
    early = pack([arrived[0], first, *arrived[3:middle]], LIGHT)
    (early_tokens, early_grads), late = tie((split(early), arrived[middle:]))
    late = pack(late, LIGHT)
    ids_after, _ = tie((ids, late))
    early_near, late_near = (cross(value, far_bits) for value in (early, late))
    near = sorted(early_near)
    crossed = {mask: early_near[mask] for mask in near[1:]}
    early, late, crossed = tie((early, late, crossed))
    early_far = {0: flip(early, "dp", 1)}
    for mask, value in crossed.items():
        early_far[mask] = flip(value, "dp", 1)
    late_far = {0: flip(late, "dp", 1)}
    crossed = {mask: late_near[mask] for mask in near[1:]}
    table = placement(n_targets, ids_after)
    table, early_far, late_far, crossed = tie((table, early_far, late_far, crossed))
    for mask, value in crossed.items():
        late_far[mask] = flip(value, "dp", 1)
    pieces = [
        group[mask]
        for groups in ((early_near, late_near), (early_far, late_far))
        for mask in near
        for group in groups
    ]
    token_halves, activated, slope, hidden = forward(
        [early_tokens, *pieces[1:]], weights[0], weights[1]
    )
    size = width // 8 * 3
    own_left, far_left, grad_halves, gate_f, up_f, factors, gate_column = backward(
        [early_grads, *pieces[1:]], activated, slope, hidden, weights, size
    )

    left = flip(far_left, "dp", 1)
    own_right, far_right = rest_rows(size, factors, gate_column, weights[0], weights[1])
    left, own_right = tie((left, own_right))
    right = flip(far_right, "dp", 1)
    targets = [
        (2 * i, odd.index(k)) if k % 2 else (2 * i + 1, even.index(k))
        for i in range(len(near))
        for k in order
    ]
    parts = sum_rows(targets, (own_left, own_right), (left, right))
    gate_f, up_f, _ = tie((gate_f, up_f, parts))
    grad_gate, grad_up = weight_grads((gate_f, up_f), token_halves)
    parts = [list(parts[group::2]) for group in range(2)]
    parts[1], grad_gate, grad_up = tie((parts[1], grad_gate, grad_up))
    sums = []
    for group in range(2):
        held = dict(zip(near, parts[group]))
        for bit in reversed(far_bits):
            masks = [mask for mask in held if mask & bit]
            moved = {mask: flip(held.pop(mask), "dp", bit) for mask in masks}
            if group == 0 and bit == far_bits[-1]:
                moved, grad_gate, grad_up = tie((moved, grad_gate, grad_up))
            if bit == far_bits[0]:
                sums.append((held[0], moved[bit]))
            else:
                for mask in masks:
                    (held[mask ^ bit],) = add_rows(held[mask ^ bit], moved[mask], 1)
    passed = add_rows(*sums[0], 2)
    hidden, _ = tie((hidden, passed))
    (grad_down,) = weight_grads((hidden,), grad_halves)
    passed = [flip(value, "expert", 1) for value in passed]
    kept, moved, grad_down = tie((*sums[1], grad_down))
    kept = add_rows(kept, moved, 2)
    merged = [block for pair in zip(kept, passed) for block in merge_rows(*pair)]
    returned = exchange(merged, even)
    token_grad, gate_grad = combine(table, gates, returned, width)
    grads = (grad_gate, grad_up, grad_down)
    return (token_grad, gate_grad.T, *(grad[None] for grad in grads))


def solution(mesh):
    in_specs = (
        P(("expert", "dp"), None),
        P(("expert", "dp"), None),
        P(("expert", "dp"), None),
        P(("expert", "dp"), None),
        P("expert", "dp", None),
        P("expert", "dp", None),
        P("expert", "dp", None),
    )
    out_specs = (
        P(("expert", "dp"), None),
        P(("expert", "dp"), None),
        P("expert", "dp", None),
        P("expert", "dp", None),
        P("expert", "dp", None),
    )
    return jax.shard_map(body, mesh=mesh, in_specs=in_specs, out_specs=out_specs, check_vma=False)
```

```python
import functools

import jax
import jax.numpy as jnp
from jax import lax
from jax.experimental import pallas as pl
from jax.experimental.pallas import tpu as pltpu
from jax.sharding import PartitionSpec as P

EXPERTS = 128
CAP = 4
BLOCK = 2 * CAP
LANES = 128
MIB = 2**20

CONTRACT_LAST = (((1,), (1,)), ((), ()))
CONTRACT_FIRST = (((0,), (0,)), ((), ()))

HBM = pl.BlockSpec(memory_space=pltpu.HBM)
VMEM = pl.BlockSpec(memory_space=pltpu.VMEM)

LIGHT = pl.CostEstimate(flops=10**6, bytes_accessed=10**4, transcendentals=0)
COVER = pl.CostEstimate(flops=4 * 10**10, bytes_accessed=4 * 10**7, transcendentals=0)


def struct(shape, dtype=jnp.bfloat16):
    return jax.ShapeDtypeStruct(shape, dtype)


def as_bf16(mask):
    return mask.astype(jnp.float32).astype(jnp.bfloat16)


def choice_table(ids, n_targets):
    choices, tokens = ids.shape
    height = n_targets * BLOCK
    per_device = EXPERTS // n_targets
    row = lax.broadcasted_iota(jnp.int32, (height, 1), 0)
    wanted = ((row // BLOCK) ^ lax.axis_index("expert")) * per_device
    slot = row % BLOCK
    matches = [ids[k : k + 1, :] == wanted for k in range(choices)]
    hit = functools.reduce(jnp.logical_or, matches)
    earlier = lax.broadcasted_iota(jnp.int32, (tokens, tokens), 0) < lax.broadcasted_iota(
        jnp.int32, (tokens, tokens), 1
    )
    rank = jnp.dot(as_bf16(hit), as_bf16(earlier), preferred_element_type=jnp.float32)
    rank = rank.astype(jnp.int32)
    first = jnp.logical_and(hit, rank == slot)
    second = jnp.logical_and(hit, rank == slot - CAP)
    return matches, first, second


def pick_rows(picks, rows_ref):
    half = rows_ref.shape[1] // 2
    rows = jnp.concatenate([rows_ref[:, :half], rows_ref[:, half:]], axis=0)
    return jnp.dot(picks, rows, preferred_element_type=jnp.float32).astype(jnp.bfloat16)


def dispatch_kernel(n_targets, *refs):
    sources, outs = refs[:4], refs[4 : 4 + n_targets]
    targets, blocks = refs[4 + n_targets : 8 + n_targets], refs[8 + n_targets : -2]
    sems, out_sems = refs[-2:]
    ids_ref, tokens_ref, gates_ref, grads_ref = targets
    copies = [
        pltpu.make_async_copy(source, target, sems.at[i])
        for i, (source, target) in enumerate(zip(sources, targets))
    ]
    for copy in copies:
        copy.start()
    half = tokens_ref.shape[1] // 2
    sent = []

    def send(rows, start):
        span = pl.ds(start, half)
        for k, (block, out) in enumerate(zip(blocks, outs)):
            block[:, span] = rows[k * BLOCK : (k + 1) * BLOCK]
            copy = pltpu.make_async_copy(
                block.at[:, span], out.at[:, span], out_sems.at[len(sent)]
            )
            copy.start()
            sent.append(copy)

    copies[0].wait()
    matches, first, second = choice_table(ids_ref[...], n_targets)
    picks = jnp.concatenate([first.astype(jnp.float32), second.astype(jnp.float32)], axis=1)
    copies[1].wait()
    send(pick_rows(picks.astype(jnp.bfloat16), tokens_ref), 0)
    copies[2].wait()
    gates = gates_ref[...].astype(jnp.float32)
    scale = jnp.zeros(first.shape, jnp.float32)
    for k, match in enumerate(matches):
        scale = scale + jnp.where(match, gates[k : k + 1, :], 0.0)
    picks = (picks * jnp.concatenate([scale, scale], axis=1)).astype(jnp.bfloat16)
    copies[3].wait()
    send(pick_rows(picks, grads_ref), half)
    for copy in sent:
        copy.wait()


def dispatch(n_targets, ids, tokens, gates, out_grad):
    arrays = (ids, tokens, gates, out_grad)
    block = (BLOCK, tokens.shape[1])
    return pl.pallas_call(
        functools.partial(dispatch_kernel, n_targets),
        out_shape=[struct(block)] * n_targets,
        in_specs=[HBM] * 4,
        out_specs=[HBM] * n_targets,
        scratch_shapes=[pltpu.VMEM(a.shape, a.dtype) for a in arrays]
        + [pltpu.VMEM(block, jnp.bfloat16)] * n_targets
        + [pltpu.SemaphoreType.DMA((4,)), pltpu.SemaphoreType.DMA((2 * n_targets,))],
        compiler_params=pltpu.CompilerParams(vmem_limit_bytes=60 * MIB),
        name="dispatch",
    )(*arrays)


def placement_kernel(n_targets, ids_ref, first_ref, second_ref, choice_ref):
    matches, first, second = choice_table(ids_ref[...], n_targets)
    first_ref[...] = as_bf16(first)
    second_ref[...] = as_bf16(second)
    choice = jnp.full(first.shape, -1, jnp.int32)
    for k, match in enumerate(matches):
        choice = jnp.where(jnp.logical_and(match, first), k, choice)
    choice_ref[...] = choice


def placement(n_targets, ids):
    table = (n_targets * BLOCK, ids.shape[1])
    return pl.pallas_call(
        functools.partial(placement_kernel, n_targets),
        out_shape=[struct(table), struct(table), struct(table, jnp.int32)],
        in_specs=[VMEM],
        out_specs=[VMEM] * 3,
        compiler_params=pltpu.CompilerParams(vmem_limit_bytes=4 * MIB),
        cost_estimate=LIGHT,
        name="placement",
    )(ids)


def pack_kernel(refs, out):
    blocks = [
        ref[pl.ds(i, BLOCK), :] for ref in refs for i in range(0, ref.shape[0], BLOCK)
    ]
    for k in range(0, len(blocks), 2):
        out[pl.ds(k * BLOCK, 2 * BLOCK), :] = jnp.concatenate(blocks[k : k + 2], axis=0)


def pack(arrays, cost):
    rows, width = sum(array.shape[0] for array in arrays), arrays[0].shape[1]
    return pl.pallas_call(
        lambda *refs: pack_kernel(refs[:-1], refs[-1]),
        out_shape=struct((rows, width)),
        in_specs=[VMEM] * len(arrays),
        out_specs=VMEM,
        compiler_params=pltpu.CompilerParams(vmem_limit_bytes=4 * MIB + 8 * rows * width),
        cost_estimate=cost,
        name="pack",
    )(*arrays)


def split_kernel(rows, token_out, grad_out):
    half = token_out.shape[1]
    token_out[...] = rows[:, :half]
    grad_out[...] = rows[:, half:]


def split(rows):
    height, width = rows.shape
    return pl.pallas_call(
        split_kernel,
        out_shape=[struct((height, width // 2))] * 2,
        in_specs=[VMEM],
        out_specs=[VMEM] * 2,
        compiler_params=pltpu.CompilerParams(vmem_limit_bytes=4 * MIB + 8 * height * width),
        cost_estimate=COVER,
        name="split",
    )(rows)


def gather_pieces(pieces, start, out):
    base = 0
    half = out.shape[1]
    for piece in pieces:
        rows, width = piece.shape
        first = min(start, width - half)
        out[pl.ds(base, rows), :] = piece[:, first : first + half]
        base += rows


def project(weight, halves):
    half = halves.shape[1]
    rows = halves.shape[0]
    low = lax.dot_general(
        weight[:, :half], halves[...], CONTRACT_LAST, preferred_element_type=jnp.float32
    )
    high = lax.dot_general(
        weight[:, half:], halves[...], CONTRACT_LAST, preferred_element_type=jnp.float32
    )
    return low + pltpu.roll(high, rows - CAP, 1)


def forward_kernel(count, *refs):
    pieces = refs[:count]
    gate_w, up_w, halves, activated_out, slope_out, hidden_out = refs[count:]
    gather_pieces(pieces, 0, halves)
    pre_gate, pre_up = project(gate_w, halves), project(up_w, halves)
    is_slot = lax.broadcasted_iota(jnp.int32, (1, halves.shape[0]), 1) % BLOCK < CAP
    squash = 1.0 / (1.0 + jnp.exp(-pre_gate))
    activated = jnp.where(is_slot, pre_gate * squash, 0.0)
    slope = pre_up * squash * (1.0 + pre_gate * (1.0 - squash))
    activated_out[...] = activated
    slope_out[...] = jnp.where(is_slot, slope, 0.0)
    hidden_out[...] = (activated * pre_up).astype(jnp.bfloat16)


def forward(pieces, gate_w, up_w):
    count = len(pieces)
    units, width = gate_w.shape
    rows = sum(piece.shape[0] for piece in pieces)
    kept = (units, rows)
    return pl.pallas_call(
        functools.partial(forward_kernel, count),
        out_shape=[
            struct((rows, width // 2)),
            struct(kept, jnp.float32),
            struct(kept, jnp.float32),
            struct(kept),
        ],
        in_specs=[VMEM] * (count + 2),
        out_specs=[VMEM] * 4,
        compiler_params=pltpu.CompilerParams(
            vmem_limit_bytes=4 * MIB + rows * width + 40 * rows * units
        ),
        cost_estimate=LIGHT,
        name="forward",
    )(*pieces, gate_w, up_w)


def row_grads(factors, gate_w, up_w, parts, start):
    units, width = gate_w.shape
    block, size = parts[0].shape
    slots = factors.shape[0]
    chunk = 256 if size % 256 == 0 else size

    def product(columns):
        return jnp.dot(
            factors[:, :units], gate_w[:, columns], preferred_element_type=jnp.float32
        ) + jnp.dot(factors[:, units:], up_w[:, columns], preferred_element_type=jnp.float32)

    @pl.loop(0, size // chunk)
    def _(step):
        offset = pl.multiple_of(step * chunk, chunk)
        low = product(pl.ds(pl.multiple_of(start + offset, chunk), chunk))
        high = product(pl.ds(pl.multiple_of(width // 2 + start + offset, chunk), chunk))
        is_low = lax.broadcasted_iota(jnp.int32, (slots, 1), 0) % BLOCK < CAP
        even = jnp.where(is_low, low, pltpu.roll(high, CAP, 0))
        odd = jnp.where(is_low, pltpu.roll(low, slots - CAP, 0), high)
        tiles = (slots // BLOCK, BLOCK, chunk)
        total = jnp.stack([even.reshape(tiles), odd.reshape(tiles)], axis=1)
        total = total.reshape(2 * slots, chunk).astype(jnp.bfloat16)
        for i, part in enumerate(parts):
            part[:, pl.ds(offset, chunk)] = total[i * block : (i + 1) * block]


def backward_kernel(count, *refs):
    pieces = refs[:count]
    activated, slope, hidden, gate_w, up_w, down_w = refs[count : count + 6]
    own, far, halves, gate_out, up_out, factors, gates_out = refs[count + 6 :]
    rows = halves.shape[0]
    gather_pieces(pieces, halves.shape[1], halves)
    back = project(down_w, halves)
    gate_terms = jnp.sum(hidden[...].astype(jnp.float32) * back, axis=0, keepdims=True)
    up_pre = back * activated[...]
    gate_pre = back * slope[...]
    both = jnp.concatenate([gate_pre, up_pre], axis=0)
    both = both.T
    tiles = (rows // (2 * BLOCK), 2, BLOCK, both.shape[1])
    even = both.reshape(tiles)[:, 0]
    odd = pltpu.roll(both, CAP, 0).reshape(tiles)[:, 1]
    factors[...] = (even + odd).reshape(factors.shape).astype(jnp.bfloat16)
    gate_column = jnp.broadcast_to(gate_terms, (LANES, rows)).T.astype(jnp.bfloat16)
    row_grads(factors, gate_w, up_w, (own, far), 0)
    gates_out[...] = gate_column
    gate_out[...] = gate_pre.astype(jnp.bfloat16)
    up_out[...] = up_pre.astype(jnp.bfloat16)


def backward(pieces, activated, slope, hidden, weights, size):
    count = len(pieces)
    units, width = weights[0].shape
    rows = sum(piece.shape[0] for piece in pieces)
    mine = rows // 2
    shapes = [
        (mine, size),
        (mine, size),
        (rows, width // 2),
        (units, rows),
        (units, rows),
        (mine, 2 * units),
        (rows, LANES),
    ]
    return pl.pallas_call(
        functools.partial(backward_kernel, count),
        out_shape=[struct(shape) for shape in shapes],
        in_specs=[VMEM] * (count + 6),
        out_specs=[VMEM] * len(shapes),
        compiler_params=pltpu.CompilerParams(
            vmem_limit_bytes=6 * MIB
            + 2 * sum(height * across for height, across in shapes)
            + 56 * rows * units
        ),
        cost_estimate=LIGHT,
        name="backward",
    )(*pieces, activated, slope, hidden, *weights)


def rest_kernel(start, factors, gates, gate_w, up_w, own, far):
    mine, size = own.shape
    size -= LANES
    own[:, size:] = gates[:mine, :]
    far[:, size:] = gates[mine:, :]
    views = [part.at[:, pl.ds(0, size)] for part in (own, far)]
    row_grads(factors, gate_w, up_w, views, start)


def rest_rows(start, factors, gates, gate_w, up_w):
    rows, width = gates.shape[0], gate_w.shape[1]
    size = width // 2 - start + LANES
    return pl.pallas_call(
        functools.partial(rest_kernel, start),
        out_shape=[struct((rows // 2, size))] * 2,
        in_specs=[VMEM] * 4,
        out_specs=[VMEM] * 2,
        compiler_params=pltpu.CompilerParams(vmem_limit_bytes=8 * MIB + 4 * rows * width),
        cost_estimate=LIGHT,
        name="rest_rows",
    )(factors, gates, gate_w, up_w)


def sum_kernel(targets, own_left, own_right, left, right, *outs):
    base = 0
    for own, other in ((own_left, left), (own_right, right)):
        span = pl.ds(base, own.shape[1])
        base += own.shape[1]
        total = (own[...].astype(jnp.float32) + other[...].astype(jnp.float32)).astype(
            jnp.bfloat16
        )
        for i, (out, slot) in enumerate(targets):
            outs[out][pl.ds(slot * BLOCK, BLOCK), span] = total[i * BLOCK : (i + 1) * BLOCK]


def sum_rows(targets, own, other):
    rows = own[0].shape[0]
    width = sum(part.shape[1] for part in own)
    count = 1 + max(out for out, _ in targets)
    return pl.pallas_call(
        functools.partial(sum_kernel, targets),
        out_shape=[struct((rows // count, width))] * count,
        in_specs=[VMEM] * 4,
        out_specs=[VMEM] * count,
        compiler_params=pltpu.CompilerParams(vmem_limit_bytes=8 * MIB + 16 * rows * width),
        cost_estimate=LIGHT,
        name="sum_rows",
    )(*own, *other)


def add_kernel(left, right, *outs):
    total = (left[...].astype(jnp.float32) + right[...].astype(jnp.float32)).astype(jnp.bfloat16)
    block = outs[0].shape[0]
    for i, out in enumerate(outs):
        out[...] = total[i * block : (i + 1) * block]


def add_rows(left, right, count):
    rows, width = left.shape
    return pl.pallas_call(
        add_kernel,
        out_shape=[struct((rows // count, width))] * count,
        in_specs=[VMEM] * 2,
        out_specs=[VMEM] * count,
        compiler_params=pltpu.CompilerParams(vmem_limit_bytes=4 * MIB + 16 * rows * width),
        name="add_rows",
    )(left, right)


def merge_kernel(kept, passed, *outs):
    for i, out in enumerate(outs):
        span = slice(i * BLOCK, (i + 1) * BLOCK)
        out[...] = jnp.concatenate([kept[span, :], passed[span, :]], axis=0)


def merge_rows(kept, passed):
    rows, width = kept.shape
    count = rows // BLOCK
    return pl.pallas_call(
        merge_kernel,
        out_shape=[struct((2 * BLOCK, width))] * count,
        in_specs=[VMEM] * 2,
        out_specs=[VMEM] * count,
        compiler_params=pltpu.CompilerParams(vmem_limit_bytes=4 * MIB + 24 * rows * width),
        name="merge_rows",
    )(kept, passed)


def weight_kernel(chunk, count, *refs):
    factors, halves = refs[:count], refs[count]
    outs, stages, sems = refs[count + 1 : 2 * count + 1], refs[2 * count + 1 : -1], refs[-1]
    half = halves.shape[1]
    pairs = []
    for factor in factors:
        low = factor[...]
        high = pltpu.roll(low.astype(jnp.float32), CAP, 1).astype(jnp.bfloat16)
        pairs.append((low, high))
    copies = []
    for start in range(0, half, chunk):
        for pair, out, stage in zip(pairs, outs, stages):
            for factor, base in zip(pair, (0, half)):
                span = pl.ds(base + start, chunk)
                stage[:, span] = jnp.dot(
                    factor, halves[:, pl.ds(start, chunk)], preferred_element_type=jnp.float32
                ).astype(jnp.bfloat16)
                copy = pltpu.make_async_copy(
                    stage.at[:, span], out.at[:, span], sems.at[len(copies)]
                )
                copy.start()
                copies.append(copy)
    for copy in copies:
        copy.wait()


def weight_grads(factors, halves):
    count = len(factors)
    units, rows = factors[0].shape
    half = halves.shape[1]
    chunk = 512 if half % 512 == 0 else half
    shape = (units, 2 * half)
    return pl.pallas_call(
        functools.partial(weight_kernel, chunk, count),
        out_shape=[struct(shape)] * count,
        in_specs=[VMEM] * (count + 1),
        out_specs=[HBM] * count,
        scratch_shapes=[pltpu.VMEM(shape, jnp.bfloat16)] * count
        + [pltpu.SemaphoreType.DMA((2 * count * half // chunk,))],
        compiler_params=pltpu.CompilerParams(
            vmem_limit_bytes=6 * MIB + 4 * count * units * half + 8 * count * units * rows
        ),
        cost_estimate=LIGHT,
        name="weight_grads",
    )(*factors, halves)


def combine_kernel(n_targets, first, second, choice_ref, gates_ref, *refs):
    blocks, (token_ref, gate_ref) = refs[: n_targets // 2], refs[n_targets // 2 :]
    even = return_offsets(n_targets)[1]
    back = jnp.concatenate([blocks[even.index(k)][...] for k in range(0, n_targets, 2)], axis=0)
    half = token_ref.shape[1] // 2
    choices, tokens = gates_ref.shape
    rows = back[:, :half]
    token_ref[:, :half] = lax.dot_general(
        first[...], rows, CONTRACT_FIRST, preferred_element_type=jnp.float32
    ).astype(jnp.bfloat16)
    token_ref[:, half:] = lax.dot_general(
        second[...], rows, CONTRACT_FIRST, preferred_element_type=jnp.float32
    ).astype(jnp.bfloat16)
    terms = back[:, half : half + tokens].astype(jnp.float32)
    choice = choice_ref[...]
    for k in range(choices):
        chosen = jnp.where(choice == k, terms, 0.0)
        gate = gates_ref[k : k + 1, :].astype(jnp.float32)
        gate_ref[k : k + 1, :] = jnp.sum(chosen, axis=0, keepdims=True) / gate


def combine(table, gates, blocks, width):
    n_targets = 2 * len(blocks)
    choices, tokens = gates.shape
    return pl.pallas_call(
        functools.partial(combine_kernel, n_targets),
        out_shape=[struct((tokens, width)), struct((choices, tokens), jnp.float32)],
        in_specs=[VMEM] * (4 + len(blocks)),
        out_specs=[VMEM] * 2,
        compiler_params=pltpu.CompilerParams(
            vmem_limit_bytes=4 * MIB + 16 * n_targets * BLOCK * width
        ),
        name="combine",
    )(*table, gates, *blocks)


def flip(value, axis, bit):
    size = lax.axis_size(axis)
    return lax.ppermute(value, axis, [(i, i ^ bit) for i in range(size)])


def offsets(count):
    near, far = list(range(1, count // 2)), list(range(count // 2, count))
    order = [0]
    for i, k in enumerate(near):
        order += [k, far[i]]
    return order + far[len(near) :]


def return_offsets(count):
    even = list(range(count // 2 - 2, -1, -2)) + list(range(count // 2, count, 2))
    return [k ^ 1 for k in even], even


def exchange(blocks, order):
    return [flip(block, "expert", k) if k else block for k, block in zip(order, blocks)]


def cross(block, far_bits):
    held = {0: block}
    for bit in far_bits:
        for mask in list(held):
            held[mask | bit] = flip(held[mask], "dp", bit)
    return held


def body(tokens, out_grad, gate_probs, route_ids, w_gate, w_up, w_down):
    n_targets = lax.axis_size("expert")
    n_dp = lax.axis_size("dp")
    width = tokens.shape[1]
    ids, gates = route_ids.T, gate_probs.T
    far_bits = [1 << i for i in range(1, n_dp.bit_length() - 1)]
    weights = (w_gate[0], w_up[0], w_down[0])
    tie = lax.optimization_barrier

    order = offsets(n_targets)
    odd, even = return_offsets(n_targets)
    middle = n_targets // 2
    sent = dispatch(n_targets, ids, tokens, gates, out_grad)
    arrived = exchange([sent[k] for k in order], order)
    first = pack(arrived[1:3], COVER)
    early = pack([arrived[0], first, *arrived[3:middle]], LIGHT)
    (early_tokens, early_grads), late = tie((split(early), arrived[middle:]))
    late = pack(late, LIGHT)
    ids_after, _ = tie((ids, late))
    early_near, late_near = (cross(value, far_bits) for value in (early, late))
    near = sorted(early_near)
    crossed = {mask: early_near[mask] for mask in near[1:]}
    early, late, crossed = tie((early, late, crossed))
    early_far = {0: flip(early, "dp", 1)}
    for mask, value in crossed.items():
        early_far[mask] = flip(value, "dp", 1)
    late_far = {0: flip(late, "dp", 1)}
    crossed = {mask: late_near[mask] for mask in near[1:]}
    table = placement(n_targets, ids_after)
    table, early_far, late_far, crossed = tie((table, early_far, late_far, crossed))
    for mask, value in crossed.items():
        late_far[mask] = flip(value, "dp", 1)
    pieces = [
        group[mask]
        for groups in ((early_near, late_near), (early_far, late_far))
        for mask in near
        for group in groups
    ]
    token_halves, activated, slope, hidden = forward(
        [early_tokens, *pieces[1:]], weights[0], weights[1]
    )
    size = width // 8 * 3
    own_left, far_left, grad_halves, gate_f, up_f, factors, gate_column = backward(
        [early_grads, *pieces[1:]], activated, slope, hidden, weights, size
    )

    left = flip(far_left, "dp", 1)
    own_right, far_right = rest_rows(size, factors, gate_column, weights[0], weights[1])
    left, own_right = tie((left, own_right))
    right = flip(far_right, "dp", 1)
    targets = [
        (2 * i, odd.index(k)) if k % 2 else (2 * i + 1, even.index(k))
        for i in range(len(near))
        for k in order
    ]
    parts = sum_rows(targets, (own_left, own_right), (left, right))
    gate_f, up_f, _ = tie((gate_f, up_f, parts))
    grad_gate, grad_up = weight_grads((gate_f, up_f), token_halves)
    parts = [list(parts[group::2]) for group in range(2)]
    parts[1], grad_gate, grad_up = tie((parts[1], grad_gate, grad_up))
    sums = []
    for group in range(2):
        held = dict(zip(near, parts[group]))
        for bit in reversed(far_bits):
            masks = [mask for mask in held if mask & bit]
            moved = {mask: flip(held.pop(mask), "dp", bit) for mask in masks}
            if group == 0 and bit == far_bits[-1]:
                moved, grad_gate, grad_up = tie((moved, grad_gate, grad_up))
            if bit == far_bits[0]:
                sums.append((held[0], moved[bit]))
            else:
                for mask in masks:
                    (held[mask ^ bit],) = add_rows(held[mask ^ bit], moved[mask], 1)
    passed = add_rows(*sums[0], 2)
    hidden, _ = tie((hidden, passed))
    (grad_down,) = weight_grads((hidden,), grad_halves)
    passed = [flip(value, "expert", 1) for value in passed]
    kept, moved, grad_down = tie((*sums[1], grad_down))
    kept = add_rows(kept, moved, 2)
    merged = [block for pair in zip(kept, passed) for block in merge_rows(*pair)]
    returned = exchange(merged, even)
    token_grad, gate_grad = combine(table, gates, returned, width)
    grads = (grad_gate, grad_up, grad_down)
    return (token_grad, gate_grad.T, *(grad[None] for grad in grads))


def solution(mesh):
    in_specs = (
        P(("expert", "dp"), None),
        P(("expert", "dp"), None),
        P(("expert", "dp"), None),
        P(("expert", "dp"), None),
        P("expert", "dp", None),
        P("expert", "dp", None),
        P("expert", "dp", None),
    )
    out_specs = (
        P(("expert", "dp"), None),
        P(("expert", "dp"), None),
        P("expert", "dp", None),
        P("expert", "dp", None),
        P("expert", "dp", None),
    )
    return jax.shard_map(body, mesh=mesh, in_specs=in_specs, out_specs=out_specs, check_vma=False)
```

```python
import functools

import jax
import jax.numpy as jnp
from jax import lax
from jax.experimental import pallas as pl
from jax.experimental.pallas import tpu as pltpu
from jax.sharding import PartitionSpec as P

EXPERTS = 128
CAP = 4
BLOCK = 2 * CAP
LANES = 128
MIB = 2**20

CONTRACT_LAST = (((1,), (1,)), ((), ()))
CONTRACT_FIRST = (((0,), (0,)), ((), ()))

HBM = pl.BlockSpec(memory_space=pltpu.HBM)
VMEM = pl.BlockSpec(memory_space=pltpu.VMEM)

LIGHT = pl.CostEstimate(flops=10**6, bytes_accessed=10**4, transcendentals=0)
COVER = pl.CostEstimate(flops=4 * 10**10, bytes_accessed=4 * 10**7, transcendentals=0)


def struct(shape, dtype=jnp.bfloat16):
    return jax.ShapeDtypeStruct(shape, dtype)


def as_bf16(mask):
    return mask.astype(jnp.float32).astype(jnp.bfloat16)


def choice_table(ids, n_targets):
    choices, tokens = ids.shape
    height = n_targets * BLOCK
    per_device = EXPERTS // n_targets
    row = lax.broadcasted_iota(jnp.int32, (height, 1), 0)
    wanted = ((row // BLOCK) ^ lax.axis_index("expert")) * per_device
    slot = row % BLOCK
    matches = [ids[k : k + 1, :] == wanted for k in range(choices)]
    hit = functools.reduce(jnp.logical_or, matches)
    earlier = lax.broadcasted_iota(jnp.int32, (tokens, tokens), 0) < lax.broadcasted_iota(
        jnp.int32, (tokens, tokens), 1
    )
    rank = jnp.dot(as_bf16(hit), as_bf16(earlier), preferred_element_type=jnp.float32)
    rank = rank.astype(jnp.int32)
    first = jnp.logical_and(hit, rank == slot)
    second = jnp.logical_and(hit, rank == slot - CAP)
    return matches, first, second


def pick_rows(picks, rows_ref):
    half = rows_ref.shape[1] // 2
    rows = jnp.concatenate([rows_ref[:, :half], rows_ref[:, half:]], axis=0)
    return jnp.dot(picks, rows, preferred_element_type=jnp.float32).astype(jnp.bfloat16)


def dispatch_kernel(n_targets, *refs):
    sources, outs = refs[:4], refs[4 : 4 + n_targets]
    targets, sems = refs[4 + n_targets : -1], refs[-1]
    ids_ref, tokens_ref, gates_ref, grads_ref = targets
    copies = [
        pltpu.make_async_copy(source, target, sems.at[i])
        for i, (source, target) in enumerate(zip(sources, targets))
    ]
    for copy in copies:
        copy.start()
    copies[0].wait()
    matches, first, second = choice_table(ids_ref[...], n_targets)
    picks = jnp.concatenate([first.astype(jnp.float32), second.astype(jnp.float32)], axis=1)
    copies[1].wait()
    rows = pick_rows(picks.astype(jnp.bfloat16), tokens_ref)
    half = rows.shape[1]
    for k, out in enumerate(outs):
        out[:, :half] = rows[k * BLOCK : (k + 1) * BLOCK]
    copies[2].wait()
    gates = gates_ref[...].astype(jnp.float32)
    scale = jnp.zeros(first.shape, jnp.float32)
    for k, match in enumerate(matches):
        scale = scale + jnp.where(match, gates[k : k + 1, :], 0.0)
    picks = (picks * jnp.concatenate([scale, scale], axis=1)).astype(jnp.bfloat16)
    copies[3].wait()
    rows = pick_rows(picks, grads_ref)
    for k, out in enumerate(outs):
        out[:, half:] = rows[k * BLOCK : (k + 1) * BLOCK]


def dispatch(n_targets, ids, tokens, gates, out_grad):
    arrays = (ids, tokens, gates, out_grad)
    return pl.pallas_call(
        functools.partial(dispatch_kernel, n_targets),
        out_shape=[struct((BLOCK, tokens.shape[1]))] * n_targets,
        in_specs=[HBM] * 4,
        out_specs=[VMEM] * n_targets,
        scratch_shapes=[pltpu.VMEM(a.shape, a.dtype) for a in arrays]
        + [pltpu.SemaphoreType.DMA((4,))],
        compiler_params=pltpu.CompilerParams(vmem_limit_bytes=60 * MIB),
        name="dispatch",
    )(*arrays)


def placement_kernel(n_targets, ids_ref, first_ref, second_ref, choice_ref):
    matches, first, second = choice_table(ids_ref[...], n_targets)
    first_ref[...] = as_bf16(first)
    second_ref[...] = as_bf16(second)
    choice = jnp.full(first.shape, -1, jnp.int32)
    for k, match in enumerate(matches):
        choice = jnp.where(jnp.logical_and(match, first), k, choice)
    choice_ref[...] = choice


def placement(n_targets, ids):
    table = (n_targets * BLOCK, ids.shape[1])
    return pl.pallas_call(
        functools.partial(placement_kernel, n_targets),
        out_shape=[struct(table), struct(table), struct(table, jnp.int32)],
        in_specs=[VMEM],
        out_specs=[VMEM] * 3,
        compiler_params=pltpu.CompilerParams(vmem_limit_bytes=4 * MIB),
        cost_estimate=LIGHT,
        name="placement",
    )(ids)


def pack_kernel(refs, out):
    blocks = [
        ref[pl.ds(i, BLOCK), :] for ref in refs for i in range(0, ref.shape[0], BLOCK)
    ]
    for k in range(0, len(blocks), 2):
        out[pl.ds(k * BLOCK, 2 * BLOCK), :] = jnp.concatenate(blocks[k : k + 2], axis=0)


def pack(arrays, cost):
    rows, width = sum(array.shape[0] for array in arrays), arrays[0].shape[1]
    return pl.pallas_call(
        lambda *refs: pack_kernel(refs[:-1], refs[-1]),
        out_shape=struct((rows, width)),
        in_specs=[VMEM] * len(arrays),
        out_specs=VMEM,
        compiler_params=pltpu.CompilerParams(vmem_limit_bytes=4 * MIB + 8 * rows * width),
        cost_estimate=cost,
        name="pack",
    )(*arrays)


def split_kernel(rows, token_out, grad_out):
    half = token_out.shape[1]
    token_out[...] = rows[:, :half]
    grad_out[...] = rows[:, half:]


def split(rows):
    height, width = rows.shape
    return pl.pallas_call(
        split_kernel,
        out_shape=[struct((height, width // 2))] * 2,
        in_specs=[VMEM],
        out_specs=[VMEM] * 2,
        compiler_params=pltpu.CompilerParams(vmem_limit_bytes=4 * MIB + 8 * height * width),
        cost_estimate=COVER,
        name="split",
    )(rows)


def gather_pieces(pieces, start, out):
    base = 0
    half = out.shape[1]
    for piece in pieces:
        rows, width = piece.shape
        first = min(start, width - half)
        out[pl.ds(base, rows), :] = piece[:, first : first + half]
        base += rows


def project(weight, halves):
    half = halves.shape[1]
    rows = halves.shape[0]
    low = lax.dot_general(
        weight[:, :half], halves[...], CONTRACT_LAST, preferred_element_type=jnp.float32
    )
    high = lax.dot_general(
        weight[:, half:], halves[...], CONTRACT_LAST, preferred_element_type=jnp.float32
    )
    return low + pltpu.roll(high, rows - CAP, 1)


def forward_kernel(count, *refs):
    pieces = refs[:count]
    gate_w, up_w, halves, activated_out, slope_out, hidden_out = refs[count:]
    gather_pieces(pieces, 0, halves)
    pre_gate, pre_up = project(gate_w, halves), project(up_w, halves)
    is_slot = lax.broadcasted_iota(jnp.int32, (1, halves.shape[0]), 1) % BLOCK < CAP
    squash = 1.0 / (1.0 + jnp.exp(-pre_gate))
    activated = jnp.where(is_slot, pre_gate * squash, 0.0)
    slope = pre_up * squash * (1.0 + pre_gate * (1.0 - squash))
    activated_out[...] = activated
    slope_out[...] = jnp.where(is_slot, slope, 0.0)
    hidden_out[...] = (activated * pre_up).astype(jnp.bfloat16)


def forward(pieces, gate_w, up_w):
    count = len(pieces)
    units, width = gate_w.shape
    rows = sum(piece.shape[0] for piece in pieces)
    kept = (units, rows)
    return pl.pallas_call(
        functools.partial(forward_kernel, count),
        out_shape=[
            struct((rows, width // 2)),
            struct(kept, jnp.float32),
            struct(kept, jnp.float32),
            struct(kept),
        ],
        in_specs=[VMEM] * (count + 2),
        out_specs=[VMEM] * 4,
        compiler_params=pltpu.CompilerParams(
            vmem_limit_bytes=4 * MIB + rows * width + 40 * rows * units
        ),
        cost_estimate=LIGHT,
        name="forward",
    )(*pieces, gate_w, up_w)


def row_grads(factors, gate_w, up_w, parts, start):
    units, width = gate_w.shape
    block, size = parts[0].shape
    slots = factors.shape[0]
    chunk = 256 if size % 256 == 0 else size

    def product(columns):
        return jnp.dot(
            factors[:, :units], gate_w[:, columns], preferred_element_type=jnp.float32
        ) + jnp.dot(factors[:, units:], up_w[:, columns], preferred_element_type=jnp.float32)

    @pl.loop(0, size // chunk)
    def _(step):
        offset = pl.multiple_of(step * chunk, chunk)
        low = product(pl.ds(pl.multiple_of(start + offset, chunk), chunk))
        high = product(pl.ds(pl.multiple_of(width // 2 + start + offset, chunk), chunk))
        is_low = lax.broadcasted_iota(jnp.int32, (slots, 1), 0) % BLOCK < CAP
        even = jnp.where(is_low, low, pltpu.roll(high, CAP, 0))
        odd = jnp.where(is_low, pltpu.roll(low, slots - CAP, 0), high)
        tiles = (slots // BLOCK, BLOCK, chunk)
        total = jnp.stack([even.reshape(tiles), odd.reshape(tiles)], axis=1)
        total = total.reshape(2 * slots, chunk).astype(jnp.bfloat16)
        for i, part in enumerate(parts):
            part[:, pl.ds(offset, chunk)] = total[i * block : (i + 1) * block]


def backward_kernel(count, *refs):
    pieces = refs[:count]
    activated, slope, hidden, gate_w, up_w, down_w = refs[count : count + 6]
    own, far, halves, gate_out, up_out, factors, gates_out = refs[count + 6 :]
    rows = halves.shape[0]
    gather_pieces(pieces, halves.shape[1], halves)
    back = project(down_w, halves)
    gate_terms = jnp.sum(hidden[...].astype(jnp.float32) * back, axis=0, keepdims=True)
    up_pre = back * activated[...]
    gate_pre = back * slope[...]
    both = jnp.concatenate([gate_pre, up_pre], axis=0)
    both = both.T
    tiles = (rows // (2 * BLOCK), 2, BLOCK, both.shape[1])
    even = both.reshape(tiles)[:, 0]
    odd = pltpu.roll(both, CAP, 0).reshape(tiles)[:, 1]
    factors[...] = (even + odd).reshape(factors.shape).astype(jnp.bfloat16)
    gate_column = jnp.broadcast_to(gate_terms, (LANES, rows)).T.astype(jnp.bfloat16)
    row_grads(factors, gate_w, up_w, (own, far), 0)
    gates_out[...] = gate_column
    gate_out[...] = gate_pre.astype(jnp.bfloat16)
    up_out[...] = up_pre.astype(jnp.bfloat16)


def backward(pieces, activated, slope, hidden, weights, size):
    count = len(pieces)
    units, width = weights[0].shape
    rows = sum(piece.shape[0] for piece in pieces)
    mine = rows // 2
    shapes = [
        (mine, size),
        (mine, size),
        (rows, width // 2),
        (units, rows),
        (units, rows),
        (mine, 2 * units),
        (rows, LANES),
    ]
    return pl.pallas_call(
        functools.partial(backward_kernel, count),
        out_shape=[struct(shape) for shape in shapes],
        in_specs=[VMEM] * (count + 6),
        out_specs=[VMEM] * len(shapes),
        compiler_params=pltpu.CompilerParams(
            vmem_limit_bytes=6 * MIB
            + 2 * sum(height * across for height, across in shapes)
            + 56 * rows * units
        ),
        cost_estimate=LIGHT,
        name="backward",
    )(*pieces, activated, slope, hidden, *weights)


def rest_kernel(start, factors, gates, gate_w, up_w, own, far):
    mine, size = own.shape
    size -= LANES
    own[:, size:] = gates[:mine, :]
    far[:, size:] = gates[mine:, :]
    views = [part.at[:, pl.ds(0, size)] for part in (own, far)]
    row_grads(factors, gate_w, up_w, views, start)


def rest_rows(start, factors, gates, gate_w, up_w):
    rows, width = gates.shape[0], gate_w.shape[1]
    size = width // 2 - start + LANES
    return pl.pallas_call(
        functools.partial(rest_kernel, start),
        out_shape=[struct((rows // 2, size))] * 2,
        in_specs=[VMEM] * 4,
        out_specs=[VMEM] * 2,
        compiler_params=pltpu.CompilerParams(vmem_limit_bytes=8 * MIB + 4 * rows * width),
        cost_estimate=LIGHT,
        name="rest_rows",
    )(factors, gates, gate_w, up_w)


def sum_kernel(targets, own_left, own_right, left, right, *outs):
    base = 0
    for own, other in ((own_left, left), (own_right, right)):
        span = pl.ds(base, own.shape[1])
        base += own.shape[1]
        total = (own[...].astype(jnp.float32) + other[...].astype(jnp.float32)).astype(
            jnp.bfloat16
        )
        for i, (out, slot) in enumerate(targets):
            outs[out][pl.ds(slot * BLOCK, BLOCK), span] = total[i * BLOCK : (i + 1) * BLOCK]


def sum_rows(targets, own, other):
    rows = own[0].shape[0]
    width = sum(part.shape[1] for part in own)
    count = 1 + max(out for out, _ in targets)
    return pl.pallas_call(
        functools.partial(sum_kernel, targets),
        out_shape=[struct((rows // count, width))] * count,
        in_specs=[VMEM] * 4,
        out_specs=[VMEM] * count,
        compiler_params=pltpu.CompilerParams(vmem_limit_bytes=8 * MIB + 16 * rows * width),
        cost_estimate=LIGHT,
        name="sum_rows",
    )(*own, *other)


def add_kernel(left, right, *outs):
    total = (left[...].astype(jnp.float32) + right[...].astype(jnp.float32)).astype(jnp.bfloat16)
    block = outs[0].shape[0]
    for i, out in enumerate(outs):
        out[...] = total[i * block : (i + 1) * block]


def add_rows(left, right, count):
    rows, width = left.shape
    return pl.pallas_call(
        add_kernel,
        out_shape=[struct((rows // count, width))] * count,
        in_specs=[VMEM] * 2,
        out_specs=[VMEM] * count,
        compiler_params=pltpu.CompilerParams(vmem_limit_bytes=4 * MIB + 16 * rows * width),
        name="add_rows",
    )(left, right)


def merge_kernel(kept, passed, *outs):
    for i, out in enumerate(outs):
        span = slice(i * BLOCK, (i + 1) * BLOCK)
        out[...] = jnp.concatenate([kept[span, :], passed[span, :]], axis=0)


def merge_rows(kept, passed):
    rows, width = kept.shape
    count = rows // BLOCK
    return pl.pallas_call(
        merge_kernel,
        out_shape=[struct((2 * BLOCK, width))] * count,
        in_specs=[VMEM] * 2,
        out_specs=[VMEM] * count,
        compiler_params=pltpu.CompilerParams(vmem_limit_bytes=4 * MIB + 24 * rows * width),
        name="merge_rows",
    )(kept, passed)


def weight_kernel(chunk, count, *refs):
    factors, halves = refs[:count], refs[count]
    outs, stages, sems = refs[count + 1 : 2 * count + 1], refs[2 * count + 1 : -1], refs[-1]
    half = halves.shape[1]
    pairs = []
    for factor in factors:
        low = factor[...]
        high = pltpu.roll(low.astype(jnp.float32), CAP, 1).astype(jnp.bfloat16)
        pairs.append((low, high))
    copies = []
    for start in range(0, half, chunk):
        for pair, out, stage in zip(pairs, outs, stages):
            for factor, base in zip(pair, (0, half)):
                span = pl.ds(base + start, chunk)
                stage[:, span] = jnp.dot(
                    factor, halves[:, pl.ds(start, chunk)], preferred_element_type=jnp.float32
                ).astype(jnp.bfloat16)
                copy = pltpu.make_async_copy(
                    stage.at[:, span], out.at[:, span], sems.at[len(copies)]
                )
                copy.start()
                copies.append(copy)
    for copy in copies:
        copy.wait()


def weight_grads(factors, halves):
    count = len(factors)
    units, rows = factors[0].shape
    half = halves.shape[1]
    chunk = 512 if half % 512 == 0 else half
    shape = (units, 2 * half)
    return pl.pallas_call(
        functools.partial(weight_kernel, chunk, count),
        out_shape=[struct(shape)] * count,
        in_specs=[VMEM] * (count + 1),
        out_specs=[HBM] * count,
        scratch_shapes=[pltpu.VMEM(shape, jnp.bfloat16)] * count
        + [pltpu.SemaphoreType.DMA((2 * count * half // chunk,))],
        compiler_params=pltpu.CompilerParams(
            vmem_limit_bytes=6 * MIB + 4 * count * units * half + 8 * count * units * rows
        ),
        cost_estimate=LIGHT,
        name="weight_grads",
    )(*factors, halves)


def combine_kernel(n_targets, first, second, choice_ref, gates_ref, *refs):
    blocks, (token_ref, gate_ref) = refs[: n_targets // 2], refs[n_targets // 2 :]
    even = return_offsets(n_targets)[1]
    back = jnp.concatenate([blocks[even.index(k)][...] for k in range(0, n_targets, 2)], axis=0)
    half = token_ref.shape[1] // 2
    choices, tokens = gates_ref.shape
    rows = back[:, :half]
    token_ref[:, :half] = lax.dot_general(
        first[...], rows, CONTRACT_FIRST, preferred_element_type=jnp.float32
    ).astype(jnp.bfloat16)
    token_ref[:, half:] = lax.dot_general(
        second[...], rows, CONTRACT_FIRST, preferred_element_type=jnp.float32
    ).astype(jnp.bfloat16)
    terms = back[:, half : half + tokens].astype(jnp.float32)
    choice = choice_ref[...]
    for k in range(choices):
        chosen = jnp.where(choice == k, terms, 0.0)
        gate = gates_ref[k : k + 1, :].astype(jnp.float32)
        gate_ref[k : k + 1, :] = jnp.sum(chosen, axis=0, keepdims=True) / gate


def combine(table, gates, blocks, width):
    n_targets = 2 * len(blocks)
    choices, tokens = gates.shape
    return pl.pallas_call(
        functools.partial(combine_kernel, n_targets),
        out_shape=[struct((tokens, width)), struct((choices, tokens), jnp.float32)],
        in_specs=[VMEM] * (4 + len(blocks)),
        out_specs=[VMEM] * 2,
        compiler_params=pltpu.CompilerParams(
            vmem_limit_bytes=4 * MIB + 16 * n_targets * BLOCK * width
        ),
        name="combine",
    )(*table, gates, *blocks)


def flip(value, axis, bit):
    size = lax.axis_size(axis)
    return lax.ppermute(value, axis, [(i, i ^ bit) for i in range(size)])


def offsets(count):
    near, far = list(range(1, count // 2)), list(range(count // 2, count))
    order = [0]
    for i, k in enumerate(near):
        order += [k, far[i]]
    order[1], order[2] = order[2], order[1]
    return order + far[len(near) :]


def return_offsets(count):
    even = list(range(count // 2 - 2, -1, -2)) + list(range(count // 2, count, 2))
    return [k ^ 1 for k in even], even


def exchange(blocks, order):
    return [flip(block, "expert", k) if k else block for k, block in zip(order, blocks)]


def cross(block, far_bits):
    held = {0: block}
    for bit in far_bits:
        for mask in list(held):
            held[mask | bit] = flip(held[mask], "dp", bit)
    return held


def body(tokens, out_grad, gate_probs, route_ids, w_gate, w_up, w_down):
    n_targets = lax.axis_size("expert")
    n_dp = lax.axis_size("dp")
    width = tokens.shape[1]
    ids, gates = route_ids.T, gate_probs.T
    far_bits = [1 << i for i in range(1, n_dp.bit_length() - 1)]
    weights = (w_gate[0], w_up[0], w_down[0])
    tie = lax.optimization_barrier

    order = offsets(n_targets)
    odd, even = return_offsets(n_targets)
    middle = n_targets // 2
    sent = dispatch(n_targets, ids, tokens, gates, out_grad)
    arrived = exchange([sent[k] for k in order], order)
    first = pack(arrived[1:3], COVER)
    early = pack([arrived[0], first, *arrived[3:middle]], LIGHT)
    (early_tokens, early_grads), late = tie((split(early), arrived[middle:]))
    late = pack(late, LIGHT)
    ids_after, _ = tie((ids, late))
    early_near, late_near = (cross(value, far_bits) for value in (early, late))
    near = sorted(early_near)
    crossed = {mask: early_near[mask] for mask in near[1:]}
    early, late, crossed = tie((early, late, crossed))
    early_far = {0: flip(early, "dp", 1)}
    for mask, value in crossed.items():
        early_far[mask] = flip(value, "dp", 1)
    late_far = {0: flip(late, "dp", 1)}
    crossed = {mask: late_near[mask] for mask in near[1:]}
    table = placement(n_targets, ids_after)
    table, early_far, late_far, crossed = tie((table, early_far, late_far, crossed))
    for mask, value in crossed.items():
        late_far[mask] = flip(value, "dp", 1)
    pieces = [
        group[mask]
        for groups in ((early_near, late_near), (early_far, late_far))
        for mask in near
        for group in groups
    ]
    token_halves, activated, slope, hidden = forward(
        [early_tokens, *pieces[1:]], weights[0], weights[1]
    )
    size = width // 8 * 3
    own_left, far_left, grad_halves, gate_f, up_f, factors, gate_column = backward(
        [early_grads, *pieces[1:]], activated, slope, hidden, weights, size
    )

    left = flip(far_left, "dp", 1)
    own_right, far_right = rest_rows(size, factors, gate_column, weights[0], weights[1])
    left, own_right = tie((left, own_right))
    right = flip(far_right, "dp", 1)
    targets = [
        (2 * i, odd.index(k)) if k % 2 else (2 * i + 1, even.index(k))
        for i in range(len(near))
        for k in order
    ]
    parts = sum_rows(targets, (own_left, own_right), (left, right))
    gate_f, up_f, _ = tie((gate_f, up_f, parts))
    grad_gate, grad_up = weight_grads((gate_f, up_f), token_halves)
    parts = [list(parts[group::2]) for group in range(2)]
    parts[1], grad_gate, grad_up = tie((parts[1], grad_gate, grad_up))
    sums = []
    for group in range(2):
        held = dict(zip(near, parts[group]))
        for bit in reversed(far_bits):
            masks = [mask for mask in held if mask & bit]
            moved = {mask: flip(held.pop(mask), "dp", bit) for mask in masks}
            if group == 0 and bit == far_bits[-1]:
                moved, grad_gate, grad_up = tie((moved, grad_gate, grad_up))
            if bit == far_bits[0]:
                sums.append((held[0], moved[bit]))
            else:
                for mask in masks:
                    (held[mask ^ bit],) = add_rows(held[mask ^ bit], moved[mask], 1)
    passed = add_rows(*sums[0], 2)
    hidden, _ = tie((hidden, passed))
    (grad_down,) = weight_grads((hidden,), grad_halves)
    passed = [flip(value, "expert", 1) for value in passed]
    kept, moved, grad_down = tie((*sums[1], grad_down))
    kept = add_rows(kept, moved, 2)
    merged = [block for pair in zip(kept, passed) for block in merge_rows(*pair)]
    returned = exchange(merged, even)
    token_grad, gate_grad = combine(table, gates, returned, width)
    grads = (grad_gate, grad_up, grad_down)
    return (token_grad, gate_grad.T, *(grad[None] for grad in grads))


def solution(mesh):
    in_specs = (
        P(("expert", "dp"), None),
        P(("expert", "dp"), None),
        P(("expert", "dp"), None),
        P(("expert", "dp"), None),
        P("expert", "dp", None),
        P("expert", "dp", None),
        P("expert", "dp", None),
    )
    out_specs = (
        P(("expert", "dp"), None),
        P(("expert", "dp"), None),
        P("expert", "dp", None),
        P("expert", "dp", None),
        P("expert", "dp", None),
    )
    return jax.shard_map(body, mesh=mesh, in_specs=in_specs, out_specs=out_specs, check_vma=False)
```
